32 devices in a mesh: seq: 4 (over z), blk: 8 (over y, x, core).
Axes of the slice: x: 2, y: 2, z: 4, core: 2. Of those that a mesh axis runs over, the one named last changes fastest.
Arguments:
- tokens: bfloat16 [4, 4096, 1024], P('seq', 'blk'), may hold values from -16 to 16
- image_sides: int32 [4, 16], P('seq'), may hold values from 0 to 48, as said below
- ln1_gain: float32 [1024], replicated, may hold values from 0.1 to 1.9
- ln1_bias: float32 [1024], replicated, may hold values from -1.8 to 1.8
- qkv_weight: bfloat16 [1024, 3072], replicated, may hold values from -0.1875 to 0.1875
- qv_bias: float32 [2048], replicated, may hold values from -3 to 3
- proj_weight: bfloat16 [1024, 1024], replicated, may hold values from -0.75 to 0.75
- proj_bias: float32 [1024], replicated, may hold values from -1.8 to 1.8
- ln2_gain: float32 [1024], replicated, may hold values from 0.1 to 1.9
- ln2_bias: float32 [1024], replicated, may hold values from -1.8 to 1.8
- up_weight: bfloat16 [1024, 4096], replicated, may hold values from -0.1875 to 0.1875
- up_bias: float32 [4096], replicated, may hold values from -3 to 3
- down_weight: bfloat16 [4096, 1024], replicated, may hold values from -0.09375 to 0.09375
- down_bias: float32 [1024], replicated, may hold values from -1.8 to 1.8
- conv_weight: bfloat16 [9216, 256], replicated, may hold values from -0.0625 to 0.0625
- bn_gain: float32 [256], replicated, may hold values from 0.1 to 1.9
- bn_bias: float32 [256], replicated, may hold values from -3 to 3
- out_grad: bfloat16 [4, 4096, 1024], P('seq', 'blk'), may hold values from -6 to 6
- pup_grad: bfloat16 [4, 4096, 1024], P('seq', 'blk'), may hold values from -6 to 6
Outputs:
- block_out: bfloat16 [4, 4096, 1024], P('seq', 'blk')
- pup_out: bfloat16 [4, 4096, 1024], P('seq', 'blk')
- tokens_grad: float32 [4, 4096, 1024], P('seq', 'blk')
- ln1_gain_grad: float32 [1024], P('blk')
- ln1_bias_grad: float32 [1024], P('blk')
- qkv_weight_grad: float32 [1024, 3072], P('blk')
- qv_bias_grad: float32 [2048], P('blk')
- proj_weight_grad: float32 [1024, 1024], P('blk')
- proj_bias_grad: float32 [1024], P('blk')
- ln2_gain_grad: float32 [1024], P('blk')
- ln2_bias_grad: float32 [1024], P('blk')
- up_weight_grad: float32 [1024, 4096], P('blk')
- up_bias_grad: float32 [4096], P('blk')
- down_weight_grad: float32 [4096, 1024], P('blk')
- down_bias_grad: float32 [1024], P('blk')
- conv_weight_grad: float32 [9216, 256], P('blk')
- bn_gain_grad: float32 [256], P('blk')
- bn_bias_grad: float32 [256], P('blk')
The draws below stay inside these ranges and needn't reach their ends.
Inputs may be any that keep to these rules, and one draw needn't show every extreme that they name: `image_sides`: each row lists the sides of the images packed into one sequence, each 16, 32 or 48, then zeros; the squares of a row's nonzero sides sum to 4096, and every row holds an image of side 3 * 16.
All inputs are finite; a program needn't handle non-finite values.
Results may differ from the reference program's by a relative error of at most 0.017.
Values may be sent and summed in bfloat16 or wider, within the bound.
A program may use at most 704 MiB of HBM per device.

```python
import jax
import jax.numpy as jnp
from jax import lax

D = 1024
HEADS = 16
HEAD = 64
FF = 4096
C = 256
UNIT = 16
LEN = 4096
SEQS = 4
MAXIMG = 16


def draw_tokens(key, part):
    key = jax.random.fold_in(key, 11)
    row_total = SEQS * LEN
    place_share = (jnp.arange(SEQS, dtype=jnp.float32)[:, None] * LEN + jnp.arange(LEN, dtype=jnp.float32)[None, :]) / (row_total - 1)
    base_values = jnp.clip(jax.random.normal(key, (SEQS, LEN, D), jnp.float32), -5.0, 5.0)
    rising = 1.0 + 2.0 * place_share
    return (base_values * rising[:, :, None]).astype(jnp.bfloat16)


def draw_image_sides(key, part):
    key = jax.random.fold_in(key, 7)
    unit_total = LEN // (UNIT * UNIT)
    slot_total = MAXIMG

    def one_row(row_key):
        side_key, rotation_key = jax.random.split(row_key)
        side_units = jax.random.randint(side_key, (slot_total,), 1, 4).astype(jnp.int32)
        side_units = side_units.at[0].set(3)
        running = jnp.cumsum(side_units * side_units).astype(jnp.int32)
        kept_mask = running <= unit_total
        kept_count = jnp.sum(kept_mask.astype(jnp.int32)).astype(jnp.int32)
        filled = jnp.sum(jnp.where(kept_mask, side_units * side_units, 0)).astype(jnp.int32)
        image_count = (kept_count + unit_total - filled).astype(jnp.int32)
        slot_index = jnp.arange(slot_total, dtype=jnp.int32)
        listed = jnp.where(kept_mask, side_units, jnp.where(slot_index < image_count, 1, 0)).astype(jnp.int32)
        rotation = jax.random.randint(rotation_key, (), 0, image_count).astype(jnp.int32)
        source_index = ((slot_index + rotation) % image_count).astype(jnp.int32)
        turned = jnp.where(slot_index < image_count, jnp.take(listed, source_index), 0).astype(jnp.int32)
        return (turned * UNIT).astype(jnp.int32)
    return jax.vmap(one_row)(jax.random.split(key, SEQS))


def level_of(rng, dims, shards, low, top_value):
    level, own = 1.0, jax.random.fold_in(rng, 6)
    for position, parts in shards:
        draws = jnp.exp(jax.random.uniform(jax.random.fold_in(own, position), (parts,), jnp.float32, low / len(shards), top_value / len(shards)))
        level = level * jnp.repeat(draws, dims[position] // parts).reshape([-1 if axis == position else 1 for axis in range(len(dims))])
    return level


def noise(own_key, extent, width, reach, cuts=(), kind=jnp.bfloat16):
    values = jax.random.normal(own_key, extent, jnp.float32) * width
    if len(cuts) > 0:
        values = level_of(own_key, extent, cuts, -0.22, 0.18) * values
    return jnp.clip(values, min=-reach, max=reach).astype(kind)


def setup_inputs(seed: int = 0) -> dict:
    splits = jax.random.split(jax.random.key(seed), 20)
    return {
        "tokens": draw_tokens(jax.random.fold_in(splits[19], 71), 0),
        "image_sides": draw_image_sides(jax.random.fold_in(splits[19], 71), 0),
        "ln1_gain": jnp.clip(1.0 + 0.18 * jax.random.normal(splits[2], (D,), jnp.float32), 0.1, 1.9),
        "ln1_bias": noise(splits[3], (D,), 0.3, 1.8, (), jnp.float32),
        "qkv_weight": noise(splits[4], (D, 3 * D), D ** -0.5, 0.1875),
        "qv_bias": noise(splits[5], (2 * D,), 0.5, 3.0, (), jnp.float32),
        "proj_weight": noise(splits[6], (D, D), (D // 16) ** -0.5, 0.75),
        "proj_bias": noise(splits[7], (D,), 0.3, 1.8, (), jnp.float32),
        "ln2_gain": jnp.clip(1.0 + 0.18 * jax.random.normal(splits[8], (D,), jnp.float32), 0.1, 1.9),
        "ln2_bias": noise(splits[9], (D,), 0.3, 1.8, (), jnp.float32),
        "up_weight": noise(splits[10], (D, FF), D ** -0.5, 0.1875),
        "up_bias": noise(splits[11], (FF,), 0.5, 3.0, (), jnp.float32),
        "down_weight": noise(splits[12], (FF, D), FF ** -0.5, 0.09375),
        "down_bias": noise(splits[13], (D,), 0.3, 1.8, (), jnp.float32),
        "conv_weight": noise(splits[14], (9 * D, C), (9 * D) ** -0.5, 0.0625),
        "bn_gain": jnp.clip(1.0 + 0.18 * jax.random.normal(splits[15], (C,), jnp.float32), 0.1, 1.9),
        "bn_bias": noise(splits[16], (C,), 0.5, 3.0, (), jnp.float32),
        "out_grad": noise(splits[17], (SEQS, LEN, D), 1.0, 6.0, ((0, 4), (1, 8))),
        "pup_grad": noise(splits[18], (SEQS, LEN, 4 * C), 1.0, 6.0, ((0, 4), (1, 8))),
    }


@jax.custom_vjp
def low(v):
    return lax.optimization_barrier(v.astype(jnp.bfloat16)).astype(jnp.float32)

@jax.custom_vjp
def low_back(v):
    return v

def low_keep(v):
    return (low(v), None)

def low_pass(kept, grad):
    return (grad,)

def back_keep(v):
    return (v, None)

def back_low(kept, grad):
    return (low(grad),)
low.defvjp(low_keep, low_pass)
low_back.defvjp(back_keep, back_low)
highest = lax.Precision.HIGHEST
norm_eps = 1e-06
batch_eps = 1e-05
masked_score = -1e+30

def product(left, right):
    return jnp.dot(left, right, precision=highest, preferred_element_type=jnp.float32)

def image_info(image_sides, positions):
    image_areas = image_sides * image_sides
    image_ends = jnp.cumsum(image_areas).astype(jnp.int32)
    image_starts = (image_ends - image_areas).astype(jnp.int32)
    segment = lax.optimization_barrier(jnp.sum((image_ends[None, :] <= positions[:, None]).astype(jnp.int32), axis=1)).astype(jnp.int32)
    picked = segment[:, None] == jnp.arange(image_sides.shape[0], dtype=jnp.int32)[None, :]
    image_width = lax.optimization_barrier(jnp.sum(jnp.where(picked, image_sides[None, :], 0), axis=1)).astype(jnp.int32)
    image_width = jnp.maximum(image_width, 1).astype(jnp.int32)
    image_begin = lax.optimization_barrier(jnp.sum(jnp.where(picked, image_starts[None, :], 0), axis=1)).astype(jnp.int32)
    offset = (positions - image_begin).astype(jnp.int32)
    row_index = (offset // image_width).astype(jnp.int32)
    col_index = (offset - row_index * image_width).astype(jnp.int32)
    return (segment, image_width, row_index, col_index)

def neighbour_rows(source, centre, image_width, row_index, col_index, direction):
    pieces = []
    for row_step in (-1, 0, 1):
        for col_step in (-1, 0, 1):
            row_move = direction * row_step
            col_move = direction * col_step
            inside = (row_index + row_move >= 0) & (row_index + row_move < image_width) & (col_index + col_move >= 0) & (col_index + col_move < image_width)
            where_from = jnp.clip(centre + row_move * image_width + col_move, 0, source.shape[0] - 1).astype(jnp.int32)
            fetched = jnp.take(source, where_from, axis=0)
            pieces.append(jnp.where(inside[:, None], fetched, jnp.zeros((), source.dtype)))
    return jnp.stack(pieces, axis=1)

def upsample(source, centre, image_width, row_index, col_index):
    picked_rows = {}

    def neighbour(row_step, col_step):
        if (row_step, col_step) not in picked_rows:
            row_move = jnp.where((row_index + row_step >= 0) & (row_index + row_step < image_width), row_step, 0).astype(jnp.int32)
            col_move = jnp.where((col_index + col_step >= 0) & (col_index + col_step < image_width), col_step, 0).astype(jnp.int32)
            where_from = (centre + row_move * image_width + col_move).astype(jnp.int32)
            picked_rows[row_step, col_step] = jnp.take(source, where_from, axis=0)
        return picked_rows[row_step, col_step]
    quarters = []
    for row_step in (-1, 1):
        for col_step in (-1, 1):
            quarters.append(0.5625 * neighbour(0, 0) + 0.1875 * neighbour(row_step, 0) + 0.1875 * neighbour(0, col_step) + 0.0625 * neighbour(row_step, col_step))
    return jnp.concatenate(quarters, axis=1)

def layer_norm(values, gain_vec, bias_vec):
    centred = values - lax.optimization_barrier(jnp.mean(values, axis=-1, keepdims=True))
    spread = lax.optimization_barrier(jnp.mean(centred * centred, axis=-1, keepdims=True))
    return centred * lax.rsqrt(spread + norm_eps) * gain_vec + bias_vec

def attend(queries, keys_in, values_in, segment):
    length = queries.shape[0]
    block_rows = min(512, length)
    block_count = length // block_rows
    query_heads = queries.reshape(block_count, block_rows, HEADS, HEAD)
    key_heads = keys_in.reshape(length, HEADS, HEAD)
    value_heads = values_in.reshape(length, HEADS, HEAD)
    query_segment = segment.reshape(block_count, block_rows)

    def one_block(operands):
        query_part, segment_part = operands
        scores = jnp.einsum('qhd,khd->hqk', query_part, key_heads, precision=highest, preferred_element_type=jnp.float32)
        scores = low_back(scores)
        allowed = (segment_part[:, None] == segment[None, :])[None]
        scores = jnp.where(allowed, scores, masked_score)
        row_peak = lax.optimization_barrier(jnp.max(scores, axis=-1, keepdims=True))
        row_total = lax.optimization_barrier(jnp.sum(jnp.where(allowed, jnp.exp(scores - row_peak), 0.0), axis=-1, keepdims=True))
        weights = jnp.where(allowed, jnp.exp(scores - (row_peak + jnp.log(row_total))), 0.0)
        weights = low(weights)
        return jnp.einsum('hqk,khd->qhd', weights, value_heads, precision=highest, preferred_element_type=jnp.float32)
    output = lax.map(jax.checkpoint(one_block), (query_heads, query_segment))
    return output.reshape(length, HEADS * HEAD)

def encoder_block(inputs, segment, block_params):
    ln1_gain, ln1_bias, qkv_weight, qv_bias, proj_weight, proj_bias, ln2_gain, ln2_bias, up_weight, up_bias, down_weight, down_bias = block_params
    hidden_one = low(layer_norm(inputs, ln1_gain, ln1_bias))
    joined = product(hidden_one, qkv_weight)
    query_scale = HEAD ** (-0.5)
    queries = low(low_back((joined[:, :D] + qv_bias[:D]) * query_scale))
    keys_in = low(low_back(joined[:, D:2 * D]))
    values_in = low(low_back(joined[:, 2 * D:] + qv_bias[D:]))
    attended = low(low_back(attend(queries, keys_in, values_in, segment)))
    after_attn = inputs + low_back(product(attended, proj_weight) + proj_bias)
    hidden_two = low(layer_norm(after_attn, ln2_gain, ln2_bias))
    raised = low_back(product(hidden_two, up_weight) + up_bias)
    activated = low(jax.nn.gelu(raised, approximate=False))
    return after_attn + low_back(product(activated, down_weight) + down_bias)

def reference(tokens, image_sides, ln1_gain, ln1_bias, qkv_weight, qv_bias, proj_weight, proj_bias, ln2_gain, ln2_bias, up_weight, up_bias, down_weight, down_bias, conv_weight, bn_gain, bn_bias, out_grad, pup_grad):
    block_params = tuple((item.astype(jnp.float32) for item in (ln1_gain, ln1_bias, qkv_weight, qv_bias, proj_weight, proj_bias, ln2_gain, ln2_bias, up_weight, up_bias, down_weight, down_bias)))
    conv_matrix = conv_weight.astype(jnp.float32)
    batch_gain = bn_gain.astype(jnp.float32)
    batch_bias = bn_bias.astype(jnp.float32)
    inputs_all = tokens.astype(jnp.float32)

    def forward(inputs_all, block_params, conv_matrix, batch_gain, batch_bias):

        def one_sequence(operands):
            inputs, sides_row = operands
            positions = jnp.arange(inputs.shape[0], dtype=jnp.int32)
            segment, image_width, row_index, col_index = image_info(sides_row, positions)
            block_value = encoder_block(inputs, segment, block_params)
            gathered = neighbour_rows(low(block_value), positions, image_width, row_index, col_index, 1)
            conv_out = low_back(product(gathered.reshape(gathered.shape[0], 9 * D), conv_matrix))
            return (block_value, conv_out)
        block_all, conv_all = lax.map(one_sequence, (inputs_all, image_sides))
        batch_mean = lax.optimization_barrier(jnp.mean(conv_all, axis=(0, 1)))
        batch_var = lax.optimization_barrier(jnp.mean(conv_all * conv_all, axis=(0, 1))) - batch_mean * batch_mean
        conv_normed = (conv_all - batch_mean) * lax.rsqrt(batch_var + batch_eps)
        activation = low(jax.nn.gelu(conv_normed * batch_gain + batch_bias, approximate=False))

        def one_upsample(operands):
            act_rows, sides_row = operands
            positions = jnp.arange(act_rows.shape[0], dtype=jnp.int32)
            segment, image_width, row_index, col_index = image_info(sides_row, positions)
            return upsample(act_rows, positions, image_width, row_index, col_index)
        pup_all = lax.map(one_upsample, (activation, image_sides))
        return (block_all, pup_all)
    primal, pullback = jax.vjp(forward, inputs_all, block_params, conv_matrix, batch_gain, batch_bias)
    tokens_grad, block_grads, conv_grad, gain_grad, bias_grad = pullback((out_grad.astype(jnp.float32), pup_grad.astype(jnp.float32)))
    return (primal[0].astype(jnp.bfloat16), primal[1].astype(jnp.bfloat16), tokens_grad, block_grads[0], block_grads[1], block_grads[2], block_grads[3], block_grads[4], block_grads[5], block_grads[6], block_grads[7], block_grads[8], block_grads[9], block_grads[10], block_grads[11], conv_grad, gain_grad, bias_grad)
```

```python
import functools

import jax
import jax.numpy as jnp
from jax import lax
from jax.experimental import pallas as pl
from jax.experimental.pallas import tpu as pltpu
from jax.sharding import PartitionSpec as P

D = 1024
HEADS = 16
HEAD = 64
FF = 4096
C = 256
REACH = 4
UNIT = 16
BLOCK = UNIT * UNIT
IMAGE_BLOCKS = (1, 4, 9)
RIM = 64
WIDE_RIM = 128
LOG2E = 1.4426950408889634
MESH = pl.DeviceIdType.MESH

norm_eps = 1e-06
batch_eps = 1e-05
masked_score = -1e30
f32 = jnp.float32
bf16 = jnp.bfloat16

NT = (((1,), (1,)), ((), ()))
TN = (((0,), (0,)), ((), ()))


def dot(left, right):
    return jnp.dot(left, right, preferred_element_type=f32)


def dot_nt(left, right):
    return lax.dot_general(left, right, NT, preferred_element_type=f32)


def dot_tn(left, right):
    return lax.dot_general(left, right, TN, preferred_element_type=f32)


def whole(shape):
    zeros = (0,) * len(shape)
    return pl.BlockSpec(shape, lambda *_: zeros)


def params(megabytes, **more):
    return pltpu.CompilerParams(vmem_limit_bytes=megabytes << 20, **more)


def cost(flops, moved, transcendentals=0):
    return pl.CostEstimate(
        flops=int(flops), bytes_accessed=int(moved), transcendentals=int(transcendentals)
    )


def image_info(image_sides, positions):
    image_areas = image_sides * image_sides
    image_ends = jnp.cumsum(image_areas).astype(jnp.int32)
    image_starts = (image_ends - image_areas).astype(jnp.int32)
    segment = jnp.sum((image_ends[None, :] <= positions[:, None]).astype(jnp.int32), axis=1).astype(
        jnp.int32
    )
    picked = segment[:, None] == jnp.arange(image_sides.shape[0], dtype=jnp.int32)[None, :]
    image_width = jnp.sum(jnp.where(picked, image_sides[None, :], 0), axis=1).astype(jnp.int32)
    image_width = jnp.maximum(image_width, 1).astype(jnp.int32)
    image_begin = jnp.sum(jnp.where(picked, image_starts[None, :], 0), axis=1).astype(jnp.int32)
    offset = (positions - image_begin).astype(jnp.int32)
    row_index = (offset // image_width).astype(jnp.int32)
    col_index = (offset - row_index * image_width).astype(jnp.int32)
    return (segment, image_width, row_index, col_index, image_begin)


def edge_flags(image_sides, positions):
    _, width, row, col, _ = image_info(image_sides, positions)
    flags = jnp.stack([row > 0, row < width - 1, col > 0, col < width - 1], axis=1)
    return jnp.concatenate([flags, flags], axis=1).astype(f32)


def layer_stats(values):
    mean = jnp.mean(values, axis=-1, keepdims=True)
    centred = values - mean
    scale_inv = lax.rsqrt(jnp.mean(centred * centred, axis=-1, keepdims=True) + norm_eps)
    return centred * scale_inv, scale_inv


def layer_backward(grad_out, normed, scale_inv, gain):
    scaled = grad_out * gain
    inner = (
        scaled
        - jnp.mean(scaled, axis=-1, keepdims=True)
        - normed * jnp.mean(scaled * normed, axis=-1, keepdims=True)
    )
    return scale_inv * inner


def column_sums(values):
    return jnp.sum(values, axis=0, keepdims=True)


def gelu_parts(values):
    cumulative = 0.5 + 0.5 * lax.erf(values * 0.7071067811865476)
    weighted = values * (0.3989422804014327 * jnp.exp(values * values * -0.5))
    return cumulative, weighted


def qkv_kernel(x_ref, gain_ref, bias_ref, wq_ref, wk_ref, wv_ref, bq_ref, bv_ref, h_ref, out_ref):
    @pl.when(pl.program_id(0) == 0)
    def _():
        normed, _ = layer_stats(x_ref[...].astype(f32))
        h_ref[...] = (normed * gain_ref[...] + bias_ref[...]).astype(bf16)

    hidden = h_ref[...]
    query = ((dot(hidden, wq_ref[...]) + bq_ref[...]) * (HEAD**-0.5 * LOG2E)).astype(bf16)
    key = dot(hidden, wk_ref[...]).astype(bf16)
    value = (dot(hidden, wv_ref[...]) + bv_ref[...]).astype(bf16)
    for part in range(2):
        lanes = slice(128 * part, 128 * part + 128)
        out_ref[part, :, 0:128] = query[:, lanes]
        out_ref[part, :, 128:256] = key[:, lanes]
        out_ref[part, :, 256:384] = value[:, lanes]


def project_qkv(x, gain, bias, weight, qv_bias):
    rows = x.shape[0]
    groups = D // 128
    return pl.pallas_call(
        qkv_kernel,
        grid=(groups // 2,),
        in_specs=[
            whole((rows, D)),
            whole((1, D)),
            whole((1, D)),
            pl.BlockSpec((D, 256), lambda i: (0, i)),
            pl.BlockSpec((D, 256), lambda i: (0, 4 + i)),
            pl.BlockSpec((D, 256), lambda i: (0, 8 + i)),
            pl.BlockSpec((1, 256), lambda i: (0, i)),
            pl.BlockSpec((1, 256), lambda i: (0, 4 + i)),
        ],
        out_specs=[whole((rows, D)), pl.BlockSpec((2, rows, 384), lambda i: (i, 0, 0))],
        out_shape=[
            jax.ShapeDtypeStruct((rows, D), bf16),
            jax.ShapeDtypeStruct((groups, rows, 384), bf16),
        ],
        compiler_params=params(40),
        cost_estimate=cost(2 * rows * D * 3 * D, 12 << 20),
        name="norm_qkv",
    )(x, gain, bias, weight, weight, weight, qv_bias, qv_bias)


def attention_kernel(starts, counts, qkv, o_ref, lse_ref, value_t):
    step = pl.program_id(0)

    @pl.when(step == 0)
    def _():
        value_t[...] = qkv[:, 256:384].T

    own = pl.ds(pl.multiple_of(step * BLOCK, BLOCK), BLOCK)
    query = qkv[own, 0:128]
    lane = lax.broadcasted_iota(jnp.int32, (BLOCK, 128), 1)
    zero = jnp.zeros_like(query)
    queries = [jnp.where(lane < HEAD, query, zero), jnp.where(lane >= HEAD, query, zero)]
    first, count = starts[step], counts[step]
    for blocks in IMAGE_BLOCKS:

        @pl.when(count == blocks)
        def _(blocks=blocks):
            image = pl.ds(pl.multiple_of(first * BLOCK, BLOCK), blocks * BLOCK)
            keys = qkv[image, 128:256]
            scores = [dot_nt(keys, part) for part in queries]
            outs, logs = [], []
            for head in range(2):
                peak = jnp.max(scores[head], axis=0, keepdims=True)
                grown = jnp.exp2(scores[head] - peak)
                total = jnp.sum(grown, axis=0, keepdims=True)
                rows = slice(HEAD * head, HEAD * head + HEAD)
                outs.append(dot(value_t[rows, image], grown.astype(bf16)) * (1.0 / total))
                logs.append(peak + jnp.log2(total))
            o_ref[...] = jnp.concatenate(outs, axis=0).T.astype(bf16)
            lse_ref[...] = jnp.concatenate(logs + [jnp.zeros((6, BLOCK), f32)], axis=0)


def attention(starts, counts, qkv):
    length = qkv.shape[0]
    pairs = 100 * 2 * BLOCK * BLOCK
    return pl.pallas_call(
        attention_kernel,
        grid_spec=pltpu.PrefetchScalarGridSpec(
            num_scalar_prefetch=2,
            grid=(length // BLOCK,),
            in_specs=[whole((length, 384))],
            out_specs=[
                pl.BlockSpec((BLOCK, 128), lambda i, *_: (i, 0)),
                pl.BlockSpec((8, BLOCK), lambda i, *_: (0, i)),
            ],
            scratch_shapes=[pltpu.VMEM((128, length), bf16)],
        ),
        out_shape=[
            jax.ShapeDtypeStruct((length, 128), bf16),
            jax.ShapeDtypeStruct((8, length), f32),
        ],
        compiler_params=params(40),
        cost_estimate=cost(4 * HEAD * pairs, 5 << 20, pairs),
        name="attention",
    )(starts, counts, qkv)


def attention_grad_kernel(
    starts, counts, qkv, do_ref, o_ref, lse, out_ref, query_m, do_m, key_t, dq_t, delta
):
    step = pl.program_id(0)
    length = do_ref.shape[0]
    lane = lax.broadcasted_iota(jnp.int32, (BLOCK, 128), 1)
    low = lane < HEAD

    @pl.when(step == 0)
    def _():
        key_t[...] = qkv[:, 128:256].T
        dq_t[...] = jnp.zeros_like(dq_t)

        def prepare(i, _):
            rows = pl.ds(pl.multiple_of(i * BLOCK, BLOCK), BLOCK)
            grad = do_ref[rows, :]
            product = (grad.astype(f32) * o_ref[rows, :].astype(f32)).T
            delta[0:1, rows] = jnp.sum(product[:HEAD], axis=0, keepdims=True)
            delta[1:2, rows] = jnp.sum(product[HEAD:], axis=0, keepdims=True)
            query = qkv[rows, 0:128]
            zero = jnp.zeros_like(query)
            query_m[0, rows, :] = jnp.where(low, query, zero)
            query_m[1, rows, :] = jnp.where(low, zero, query)
            do_m[0, rows, :] = jnp.where(low, grad, zero)
            do_m[1, rows, :] = jnp.where(low, zero, grad)
            return 0

        lax.fori_loop(0, length // BLOCK, prepare, 0)

    own = pl.ds(pl.multiple_of(step * BLOCK, BLOCK), BLOCK)
    key = qkv[own, 128:256]
    value = qkv[own, 256:384]
    first, count = starts[step], counts[step]
    for blocks in IMAGE_BLOCKS:

        @pl.when(count == blocks)
        def _(blocks=blocks):
            image = pl.ds(pl.multiple_of(first * BLOCK, BLOCK), blocks * BLOCK)
            dk = dv = None
            for head in range(2):
                rows = slice(HEAD * head, HEAD * head + HEAD)
                query, grad = query_m[head, image, :], do_m[head, image, :]
                scores = dot_nt(key, query)
                value_grad = dot_nt(value, grad)
                weights = jnp.exp2(scores - lse[head : head + 1, image])
                score_grad = (weights * (value_grad - delta[head : head + 1, image])).astype(bf16)
                dv_part = dot(weights.astype(bf16), grad)
                dk_part = dot(score_grad, query)
                dv = dv_part if dv is None else dv + dv_part
                dk = dk_part if dk is None else dk + dk_part
                dq_t[rows, image] += dot(key_t[rows, own], score_grad)
            out_ref[own, 128:256] = (dk * (1.0 / LOG2E)).astype(bf16)
            out_ref[own, 256:384] = dv.astype(bf16)

    @pl.when(step == pl.num_programs(0) - 1)
    def _():
        def finish(i, _):
            rows = pl.ds(pl.multiple_of(i * BLOCK, BLOCK), BLOCK)
            out_ref[rows, 0:128] = dq_t[:, rows].T.astype(bf16) * jnp.asarray(HEAD**-0.5, bf16)
            return 0

        lax.fori_loop(0, length // BLOCK, finish, 0)


def attention_grad(starts, counts, qkv, do, o, lse):
    length = qkv.shape[0]
    pairs = 100 * 2 * BLOCK * BLOCK
    return pl.pallas_call(
        attention_grad_kernel,
        grid_spec=pltpu.PrefetchScalarGridSpec(
            num_scalar_prefetch=2,
            grid=(length // BLOCK,),
            in_specs=[
                whole((length, 384)),
                whole((length, 128)),
                whole((length, 128)),
                whole((8, length)),
            ],
            out_specs=whole((length, 384)),
            scratch_shapes=[
                pltpu.VMEM((2, length, 128), bf16),
                pltpu.VMEM((2, length, 128), bf16),
                pltpu.VMEM((128, length), bf16),
                pltpu.VMEM((128, length), f32),
                pltpu.VMEM((8, length), f32),
            ],
        ),
        out_shape=jax.ShapeDtypeStruct((length, 384), bf16),
        compiler_params=params(56),
        cost_estimate=cost(10 * HEAD * pairs, 12 << 20, pairs),
        name="attention_grad",
    )(starts, counts, qkv, do, o, lse)


FF_TILE = 512


def mlp_kernel(
    o_ref, x_ref, wp_ref, pb_ref, gain_ref, bias_ref, wu_ref, ub_ref, wd_ref, db_ref,
    x1_ref, h_ref, act_ref, slope_ref, out_ref, total,
):
    step = pl.program_id(0)

    @pl.when(step == 0)
    def _():
        attended = jnp.concatenate([o_ref[i] for i in range(o_ref.shape[0])], axis=1)
        x1 = x_ref[...].astype(f32) + dot(attended, wp_ref[...]) + pb_ref[...]
        x1_ref[...] = x1
        normed, _ = layer_stats(x1)
        h_ref[...] = (normed * gain_ref[...] + bias_ref[...]).astype(bf16)
        total[...] = x1 + db_ref[...]

    raised = dot(h_ref[...], wu_ref[...]) + ub_ref[...]
    cumulative, weighted = gelu_parts(raised)
    act = (raised * cumulative).astype(bf16)
    act_ref[...] = act
    slope_ref[...] = (cumulative + weighted).astype(bf16)
    total[...] += dot(act, wd_ref[...])

    @pl.when(step == pl.num_programs(0) - 1)
    def _():
        out_ref[...] = total[...].astype(bf16)


def mlp(o, x, wp, pb, gain, bias, wu, ub, wd, db):
    rows = x.shape[0]
    groups = o.shape[0]
    tile = FF_TILE
    return pl.pallas_call(
        mlp_kernel,
        grid=(FF // tile,),
        in_specs=[
            whole((groups, rows, 128)),
            whole((rows, D)),
            whole((D, D)),
            whole((1, D)),
            whole((1, D)),
            whole((1, D)),
            pl.BlockSpec((D, tile), lambda i: (0, i)),
            pl.BlockSpec((1, tile), lambda i: (0, i)),
            pl.BlockSpec((tile, D), lambda i: (i, 0)),
            whole((1, D)),
        ],
        out_specs=[
            whole((rows, D)),
            whole((rows, D)),
            pl.BlockSpec((rows, tile), lambda i: (0, i)),
            pl.BlockSpec((rows, tile), lambda i: (0, i)),
            whole((rows, D)),
        ],
        out_shape=[
            jax.ShapeDtypeStruct((rows, D), f32),
            jax.ShapeDtypeStruct((rows, D), bf16),
            jax.ShapeDtypeStruct((rows, FF), bf16),
            jax.ShapeDtypeStruct((rows, FF), bf16),
            jax.ShapeDtypeStruct((rows, D), bf16),
        ],
        scratch_shapes=[pltpu.VMEM((rows, D), f32)],
        compiler_params=params(56),
        cost_estimate=cost(2 * rows * D * (D + 2 * FF), 34 << 20, rows * FF),
        name="proj_norm_mlp",
    )(o, x, wp, pb, gain, bias, wu, ub, wd, db)


def mlp_grad_kernel(
    dy_ref, act_ref, slope_ref, wd_ref, wu_ref, x1_ref, h_ref, gain_ref, wp_ref, o_ref,
    dwd_ref, dwu_ref, dub_ref, dx1_ref, do_ref, dwp_ref, sums_ref, dm, h_t, total,
):
    step = pl.program_id(0)

    @pl.when(step == 0)
    def _():
        dm[...] = dy_ref[...].astype(bf16)
        h_t[...] = h_ref[...].T
        total[...] = jnp.zeros_like(total)

    down_in = dm[...]
    act_grad = dot_nt(down_in, wd_ref[...])
    raised_grad = act_grad * slope_ref[...].astype(f32)
    raised_low = raised_grad.astype(bf16)
    dub_ref[...] = column_sums(raised_low.astype(f32))
    dwd_ref[...] = dot_tn(act_ref[...], down_in).astype(bf16)
    dwu_ref[...] = dot(h_t[...], raised_low).astype(bf16)
    total[...] += dot_nt(raised_low, wu_ref[...])

    @pl.when(step == pl.num_programs(0) - 1)
    def _():
        grad = total[...]
        normed, scale_inv = layer_stats(x1_ref[...])
        dx1 = dy_ref[...] + layer_backward(grad, normed, scale_inv, gain_ref[...])
        dx1_ref[...] = dx1
        low = dx1.astype(bf16)
        sums_ref[0:1, :] = column_sums(low.astype(f32))
        sums_ref[1:2, :] = column_sums(grad * normed)
        sums_ref[2:3, :] = column_sums(grad)
        sums_ref[3:4, :] = column_sums(dm[...].astype(f32))
        sums_ref[4:8, :] = jnp.zeros((4, D), f32)
        attended = jnp.concatenate([o_ref[i] for i in range(o_ref.shape[0])], axis=1)
        dwp_ref[...] = dot_tn(attended, low).astype(bf16)
        attended_grad = dot_nt(low, wp_ref[...]).astype(bf16)
        for i in range(do_ref.shape[0]):
            do_ref[i] = attended_grad[:, 128 * i : 128 * i + 128]


def mlp_grad(dy, act, slope, wd, wu, x1, h, gain, wp, o):
    rows = dy.shape[0]
    groups = o.shape[0]
    tile = FF_TILE
    return pl.pallas_call(
        mlp_grad_kernel,
        grid=(FF // tile,),
        in_specs=[
            whole((rows, D)),
            pl.BlockSpec((rows, tile), lambda i: (0, i)),
            pl.BlockSpec((rows, tile), lambda i: (0, i)),
            pl.BlockSpec((tile, D), lambda i: (i, 0)),
            pl.BlockSpec((D, tile), lambda i: (0, i)),
            whole((rows, D)),
            whole((rows, D)),
            whole((1, D)),
            whole((D, D)),
            whole((groups, rows, 128)),
        ],
        out_specs=[
            pl.BlockSpec((tile, D), lambda i: (i, 0)),
            pl.BlockSpec((D, tile), lambda i: (0, i)),
            pl.BlockSpec((1, tile), lambda i: (0, i)),
            whole((rows, D)),
            whole((groups, rows, 128)),
            whole((D, D)),
            whole((8, D)),
        ],
        out_shape=[
            jax.ShapeDtypeStruct((FF, D), bf16),
            jax.ShapeDtypeStruct((D, FF), bf16),
            jax.ShapeDtypeStruct((1, FF), f32),
            jax.ShapeDtypeStruct((rows, D), f32),
            jax.ShapeDtypeStruct((groups, rows, 128), bf16),
            jax.ShapeDtypeStruct((D, D), bf16),
            jax.ShapeDtypeStruct((8, D), f32),
        ],
        scratch_shapes=[
            pltpu.VMEM((rows, D), bf16),
            pltpu.VMEM((D, rows), bf16),
            pltpu.VMEM((rows, D), f32),
        ],
        compiler_params=params(60),
        cost_estimate=cost(2 * rows * D * (2 * D + 4 * FF), 60 << 20),
        name="mlp_norm_proj_grad",
    )(dy, act, slope, wd, wu, x1, h, gain, wp, o)


def qkv_grad_kernel(
    g_ref, wq_ref, wk_ref, wv_ref, h_ref, dx1_ref, x_ref, gain_ref,
    dw_ref, dqb_ref, dvb_ref, dx_ref, sums_ref, h_t, total,
):
    step = pl.program_id(0)

    @pl.when(step == 0)
    def _():
        h_t[...] = h_ref[...].T
        total[...] = jnp.zeros_like(total)

    for part, w_ref in enumerate((wq_ref, wk_ref, wv_ref)):
        lanes = slice(128 * part, 128 * part + 128)
        grad = jnp.concatenate([g_ref[0, :, lanes], g_ref[1, :, lanes]], axis=1)
        total[...] += dot_nt(grad, w_ref[...])
        dw_ref[part] = dot(h_t[...], grad).astype(bf16)
        if part == 0:
            dqb_ref[...] = column_sums(grad.astype(f32))
        if part == 2:
            dvb_ref[...] = column_sums(grad.astype(f32))

    @pl.when(step == pl.num_programs(0) - 1)
    def _():
        grad = total[...]
        normed, scale_inv = layer_stats(x_ref[...].astype(f32))
        dx_ref[...] = dx1_ref[...] + layer_backward(grad, normed, scale_inv, gain_ref[...])
        sums_ref[0:1, :] = column_sums(grad * normed)
        sums_ref[1:2, :] = column_sums(grad)
        sums_ref[2:8, :] = jnp.zeros((6, D), f32)


def qkv_grad(g, weight, h, dx1, x, gain):
    rows = x.shape[0]
    groups = D // 128
    return pl.pallas_call(
        qkv_grad_kernel,
        grid=(groups // 2,),
        in_specs=[
            pl.BlockSpec((2, rows, 384), lambda i: (i, 0, 0)),
            pl.BlockSpec((D, 256), lambda i: (0, i)),
            pl.BlockSpec((D, 256), lambda i: (0, 4 + i)),
            pl.BlockSpec((D, 256), lambda i: (0, 8 + i)),
            whole((rows, D)),
            whole((rows, D)),
            whole((rows, D)),
            whole((1, D)),
        ],
        out_specs=[
            pl.BlockSpec((3, D, 256), lambda i: (0, 0, i)),
            pl.BlockSpec((1, 256), lambda i: (0, i)),
            pl.BlockSpec((1, 256), lambda i: (0, i)),
            whole((rows, D)),
            whole((8, D)),
        ],
        out_shape=[
            jax.ShapeDtypeStruct((3, D, D), bf16),
            jax.ShapeDtypeStruct((1, D), f32),
            jax.ShapeDtypeStruct((1, D), f32),
            jax.ShapeDtypeStruct((rows, D), f32),
            jax.ShapeDtypeStruct((8, D), f32),
        ],
        scratch_shapes=[pltpu.VMEM((D, rows), bf16), pltpu.VMEM((rows, D), f32)],
        compiler_params=params(48),
        cost_estimate=cost(4 * rows * D * 3 * D, 24 << 20),
        name="qkv_norm_grad",
    )(g, weight, weight, weight, h, dx1, x, gain)


def row_segments(rows, rim):
    count = rows // BLOCK
    pieces = []
    for block in range(count):
        first = block * BLOCK - (rim if block == 0 else 0)
        last = (block + 1) * BLOCK + (rim if block == count - 1 else 0)
        pieces.append((first, last - first, block))
    return pieces


def shifted_rows(start, shift, size):
    return pl.ds(pl.multiple_of(start + shift, UNIT), size)


def conv_kernel(widths, x_ref, top_ref, bottom_ref, flags, w_ref, z_ref, sums_ref, x_ext, left, right, centre):
    step = pl.program_id(0)
    rows = x_ref.shape[0]
    extent = rows + 2 * RIM

    @pl.when(step == 0)
    def _():
        x_ext[0:RIM, :] = top_ref[...]
        x_ext[RIM : RIM + rows, :] = x_ref[...]
        x_ext[RIM + rows :, :] = bottom_ref[...]
        left[...] = jnp.zeros_like(left)
        right[...] = jnp.zeros_like(right)

    source = x_ext[...]
    left[8 : 8 + extent, :] = dot(source, w_ref[0:D, :])
    right[8 : 8 + extent, :] = dot(source, w_ref[2 * D : 3 * D, :])
    centre[...] = (
        dot(source, w_ref[D : 2 * D, :])
        + flags[:, 2:3] * left[7 : 7 + extent, :]
        + flags[:, 3:4] * right[9 : 9 + extent, :]
    )
    for first, size, block in row_segments(rows, 0):
        own = slice(first, first + size)
        width = widths[block]
        for tap in range(3):

            @pl.when(step == tap)
            def _(tap=tap, first=first, size=size, own=own, width=width):
                found = centre[shifted_rows(RIM + first, (tap - 1) * width, size), :]
                if tap == 0:
                    z_ref[own, :] = flags[RIM + first : RIM + first + size, 0:1] * found
                elif tap == 1:
                    z_ref[own, :] += found
                else:
                    z_ref[own, :] += flags[RIM + first : RIM + first + size, 1:2] * found

    @pl.when(step == 2)
    def _():
        z = z_ref[...]
        sums_ref[0:1, :] = column_sums(z)
        sums_ref[1:2, :] = column_sums(z * z)
        sums_ref[2:8, :] = jnp.zeros((6, C), f32)


def conv(widths, x, top, bottom, flags, weight):
    rows = x.shape[0]
    extent = rows + 2 * RIM
    return pl.pallas_call(
        conv_kernel,
        grid_spec=pltpu.PrefetchScalarGridSpec(
            num_scalar_prefetch=1,
            grid=(3,),
            in_specs=[
                whole((rows, D)),
                whole((RIM, D)),
                whole((RIM, D)),
                whole((extent, 8)),
                pl.BlockSpec((3 * D, C), lambda i, *_: (i, 0)),
            ],
            out_specs=[whole((rows, C)), whole((8, C))],
            scratch_shapes=[
                pltpu.VMEM((extent, D), bf16),
                pltpu.VMEM((extent + 16, C), f32),
                pltpu.VMEM((extent + 16, C), f32),
                pltpu.VMEM((extent, C), f32),
            ],
        ),
        out_shape=[jax.ShapeDtypeStruct((rows, C), f32), jax.ShapeDtypeStruct((8, C), f32)],
        compiler_params=params(40),
        cost_estimate=cost(2 * extent * 9 * D * C, 8 << 20),
        name="conv",
    )(widths, x, top, bottom, flags, weight)


def spread_kernel(widths, g_ref, top_ref, bottom_ref, flags, out_ref, upper, lower, g_ext):
    rows = g_ref.shape[0]
    extent = rows + 2 * WIDE_RIM
    g_ext[0:WIDE_RIM, :] = top_ref[...].astype(f32)
    g_ext[WIDE_RIM : WIDE_RIM + rows, :] = g_ref[...].astype(f32)
    g_ext[WIDE_RIM + rows :, :] = bottom_ref[...].astype(f32)
    inner = slice(8, extent - 8)
    has_left, has_right = flags[inner, 2:3], flags[inner, 3:4]
    for i, target in enumerate((upper, lower)):
        near = g_ext[:, 2 * i * C : (2 * i + 1) * C]
        far = g_ext[:, (2 * i + 1) * C : (2 * i + 2) * C]
        target[0:8, :] = jnp.zeros((8, C), f32)
        target[extent - 8 :, :] = jnp.zeros((8, C), f32)
        target[inner, :] = (
            (1.0 - 0.25 * has_left) * near[inner, :]
            + (1.0 - 0.25 * has_right) * far[inner, :]
            + 0.25 * has_right * g_ext[9 : extent - 7, 2 * i * C : (2 * i + 1) * C]
            + 0.25 * has_left * g_ext[7 : extent - 9, (2 * i + 1) * C : (2 * i + 2) * C]
        )
    for first, size, block in row_segments(rows, RIM):
        width = widths[block]
        here = WIDE_RIM + first
        has_up, has_down = flags[here : here + size, 0:1], flags[here : here + size, 1:2]
        out_ref[RIM + first : RIM + first + size, :] = (
            (1.0 - 0.25 * has_up) * upper[here : here + size, :]
            + (1.0 - 0.25 * has_down) * lower[here : here + size, :]
            + 0.25 * has_down * upper[shifted_rows(here, width, size), :]
            + 0.25 * has_up * lower[shifted_rows(here, -width, size), :]
        )


def spread(widths, g, top, bottom, flags):
    rows = g.shape[0]
    extent = rows + 2 * WIDE_RIM
    return pl.pallas_call(
        spread_kernel,
        grid_spec=pltpu.PrefetchScalarGridSpec(
            num_scalar_prefetch=1,
            grid=(1,),
            in_specs=[
                whole((rows, D)),
                whole((WIDE_RIM, D)),
                whole((WIDE_RIM, D)),
                whole((extent, 8)),
            ],
            out_specs=whole((rows + 2 * RIM, C)),
            scratch_shapes=[
                pltpu.VMEM((extent, C), f32),
                pltpu.VMEM((extent, C), f32),
                pltpu.VMEM((extent, D), f32),
            ],
        ),
        out_shape=jax.ShapeDtypeStruct((rows + 2 * RIM, C), f32),
        compiler_params=params(40),
        cost_estimate=cost(20 * extent * D, 3 << 20),
        name="upsample_grad",
    )(widths, g, top, bottom, flags)


def batch_kernel(
    widths, z_ref, top_ref, bottom_ref, dact_ref, flags, mean_ref, inv_ref, gain_ref, bias_ref,
    up_ref, normed_ref, dbn_ref, sums_ref, act, mixed,
):
    rows = z_ref.shape[0]
    z = jnp.concatenate([top_ref[...], z_ref[...], bottom_ref[...]], axis=0)
    normed = (z - mean_ref[...]) * inv_ref[...]
    normed_ref[...] = normed
    pre = normed * gain_ref[...] + bias_ref[...]
    cumulative, weighted = gelu_parts(pre)
    act[...] = (pre * cumulative).astype(bf16).astype(f32)
    dbn = dact_ref[...] * (cumulative + weighted)
    dbn_ref[...] = dbn
    own = slice(RIM, RIM + rows)
    sums_ref[0:1, :] = column_sums(dbn[own, :])
    sums_ref[1:2, :] = column_sums(dbn[own, :] * normed[own, :])
    sums_ref[2:8, :] = jnp.zeros((6, C), f32)
    for first, size, block in row_segments(rows, 0):
        width = widths[block]
        here = RIM + first
        outer = slice(here - 8, here + size + 8)
        for i in range(2):
            has = flags[outer, i : i + 1]
            mixed[...] = (1.0 - 0.25 * has) * act[outer, :] + 0.25 * has * act[
                pl.ds(pl.multiple_of(here - 8 + (2 * i - 1) * width, 8), size + 16), :
            ]
            for j in range(2):
                has = flags[here : here + size, 2 + j : 3 + j]
                up_ref[first : first + size, (2 * i + j) * C : (2 * i + j + 1) * C] = (
                    (1.0 - 0.25 * has) * mixed[8 : 8 + size, :]
                    + 0.25 * has * mixed[7 + 2 * j : 7 + 2 * j + size, :]
                ).astype(bf16)


def batch(widths, z, top, bottom, dact, flags, mean, inv, gain, bias):
    rows = z.shape[0]
    extent = rows + 2 * RIM
    return pl.pallas_call(
        batch_kernel,
        grid_spec=pltpu.PrefetchScalarGridSpec(
            num_scalar_prefetch=1,
            grid=(1,),
            in_specs=[
                whole((rows, C)),
                whole((RIM, C)),
                whole((RIM, C)),
                whole((extent, C)),
                whole((extent, 8)),
                whole((1, C)),
                whole((1, C)),
                whole((1, C)),
                whole((1, C)),
            ],
            out_specs=[
                whole((rows, D)),
                whole((extent, C)),
                whole((extent, C)),
                whole((8, C)),
            ],
            scratch_shapes=[pltpu.VMEM((extent, C), f32), pltpu.VMEM((BLOCK + 16, C), f32)],
        ),
        out_shape=[
            jax.ShapeDtypeStruct((rows, D), bf16),
            jax.ShapeDtypeStruct((extent, C), f32),
            jax.ShapeDtypeStruct((extent, C), f32),
            jax.ShapeDtypeStruct((8, C), f32),
        ],
        compiler_params=params(40),
        cost_estimate=cost(60 * extent * C, 4 << 20),
        name="batch_norm",
    )(widths, z, top, bottom, dact, flags, mean, inv, gain, bias)


def conv_grad_kernel(
    widths, dbn_ref, normed_ref, flags, scale_ref, shift_ref, slope_ref, w_ref, x_ref, og_ref,
    dw_ref, dy_ref, moved, taps, x_t, total,
):
    step = pl.program_id(0)
    rows = x_ref.shape[0]
    extent = rows + 2 * RIM

    @pl.when(step == 0)
    def _():
        dz = scale_ref[...] * (dbn_ref[...] - shift_ref[...] - normed_ref[...] * slope_ref[...])
        dz = dz.astype(bf16).astype(f32)
        x_t[...] = x_ref[...].T
        total[...] = og_ref[...].astype(f32)
        moved[0, 0:8, :] = jnp.zeros((8, C), f32)
        moved[0, 8 + extent :, :] = jnp.zeros((8, C), f32)
        moved[0, 8 : 8 + extent, :] = dz
        moved[1, 8 : 8 + extent, :] = flags[:, 3:4] * moved[0, 9 : 9 + extent, :]
        moved[2, 8 : 8 + extent, :] = flags[:, 2:3] * moved[0, 7 : 7 + extent, :]
        for first, size, block in row_segments(rows, 0):
            width = widths[block]
            here = RIM + first
            for row in range(3):
                for col, slot in enumerate((1, 0, 2)):
                    found = moved[slot, pl.ds(pl.multiple_of(8 + here + (1 - row) * width, 8), size), :]
                    if row == 0:
                        found = flags[here : here + size, 1:2] * found
                    if row == 2:
                        found = flags[here : here + size, 0:1] * found
                    taps[3 * row + col, first : first + size, :] = found.astype(bf16)

    tap = taps[step]
    dw_ref[...] = dot(x_t[...], tap).astype(bf16)
    total[...] += dot_nt(tap, w_ref[...])

    @pl.when(step == pl.num_programs(0) - 1)
    def _():
        dy_ref[...] = total[...]


def conv_grad(widths, dbn, normed, flags, scale, shift, slope, weight, x, out_grad):
    rows = x.shape[0]
    extent = rows + 2 * RIM
    return pl.pallas_call(
        conv_grad_kernel,
        grid_spec=pltpu.PrefetchScalarGridSpec(
            num_scalar_prefetch=1,
            grid=(9,),
            in_specs=[
                whole((extent, C)),
                whole((extent, C)),
                whole((extent, 8)),
                whole((1, C)),
                whole((1, C)),
                whole((1, C)),
                pl.BlockSpec((D, C), lambda i, *_: (i, 0)),
                whole((rows, D)),
                whole((rows, D)),
            ],
            out_specs=[pl.BlockSpec((D, C), lambda i, *_: (i, 0)), whole((rows, D))],
            scratch_shapes=[
                pltpu.VMEM((3, extent + 16, C), f32),
                pltpu.VMEM((9, rows, C), bf16),
                pltpu.VMEM((D, rows), bf16),
                pltpu.VMEM((rows, D), f32),
            ],
        ),
        out_shape=[jax.ShapeDtypeStruct((9 * D, C), bf16), jax.ShapeDtypeStruct((rows, D), f32)],
        compiler_params=params(48),
        cost_estimate=cost(4 * rows * 9 * D * C, 16 << 20),
        name="conv_grad",
    )(widths, dbn, normed, flags, scale, shift, slope, weight, x, out_grad)


def small_sum_kernel(scatter, blks, seqs, x_ref, out_ref, first, second, sends, receives, sends2, receives2):
    blk, seq = lax.axis_index("blk"), lax.axis_index("seq")
    barrier = pltpu.get_barrier_semaphore()
    for step in range(1, blks):
        pl.semaphore_signal(
            barrier, inc=1, device_id={"blk": lax.rem(blk + step, blks)}, device_id_type=MESH
        )
    for step in range(1, seqs):
        pl.semaphore_signal(
            barrier, inc=1, device_id={"seq": lax.rem(seq + step, seqs)}, device_id_type=MESH
        )
    pl.semaphore_wait(barrier, blks + seqs - 2)
    copies = []
    for step in range(1, blks):
        to = lax.rem(blk + step, blks)
        copy = pltpu.make_async_remote_copy(
            src_ref=x_ref.at[to] if scatter else x_ref.at[0],
            dst_ref=first.at[blk],
            send_sem=sends.at[step],
            recv_sem=receives.at[step],
            device_id={"blk": to},
            device_id_type=MESH,
        )
        copy.start()
        copies.append(copy)
    first[blk] = x_ref[blk] if scatter else x_ref[0]
    for copy in copies:
        copy.wait()
    total = first[0]
    for i in range(1, blks):
        total = total + first[i]
    second[seq] = total
    copies = []
    for step in range(1, seqs):
        copy = pltpu.make_async_remote_copy(
            src_ref=second.at[seq],
            dst_ref=second.at[seq],
            send_sem=sends2.at[step],
            recv_sem=receives2.at[step],
            device_id={"seq": lax.rem(seq + step, seqs)},
            device_id_type=MESH,
        )
        copy.start()
        copies.append(copy)
    for copy in copies:
        copy.wait()
    total = second[0]
    for i in range(1, seqs):
        total = total + second[i]
    out_ref[...] = total


def small_sum(x, scatter, collective_id):
    blks, seqs = lax.axis_size("blk"), lax.axis_size("seq")
    part = x.shape[1:]
    return pl.pallas_call(
        functools.partial(small_sum_kernel, scatter, blks, seqs),
        in_specs=[pl.BlockSpec(memory_space=pltpu.VMEM)],
        out_specs=pl.BlockSpec(memory_space=pltpu.VMEM),
        out_shape=jax.ShapeDtypeStruct(part, f32),
        scratch_shapes=[
            pltpu.VMEM((blks, *part), f32),
            pltpu.VMEM((seqs, *part), f32),
            pltpu.SemaphoreType.DMA((blks,)),
            pltpu.SemaphoreType.DMA((blks,)),
            pltpu.SemaphoreType.DMA((seqs,)),
            pltpu.SemaphoreType.DMA((seqs,)),
        ],
        compiler_params=params(16, collective_id=collective_id, has_side_effects=True),
        name="small_sum",
    )(x)


def shifted(value, axis, steps):
    count = lax.axis_size(axis)
    leading, last = (max(0, -steps), min(count, count - steps))
    return lax.ppermute(value, axis, [(source, source + steps) for source in range(leading, last)])


def near_blocks(sides_row, keys_own, values_own):
    rows = keys_own.shape[0]
    place, length = lax.axis_index("blk"), rows * lax.axis_size("blk")
    centre = jnp.arange(rows, dtype=jnp.int32)
    segment = image_info(sides_row, place * rows + centre)[0]
    found = []
    for offset in range(-REACH, REACH + 1):
        keys, values = (keys_own, values_own) if offset == 0 else shifted((keys_own, values_own), "blk", -offset)
        positions = (place + offset) * rows + centre
        inside = (positions >= 0) & (positions < length)
        allowed = (segment[:, None] == image_info(sides_row, positions)[0][None, :]) & inside[None, :]
        found.append((offset, keys.reshape(rows, HEADS, HEAD), values.reshape(rows, HEADS, HEAD), allowed))
    return found


def near_scores(queries, keys, allowed):
    scores = jnp.einsum("qhd,khd->hqk", queries, keys, preferred_element_type=f32)
    return jnp.where(allowed[None], scores, masked_score)


def near_attention(near, queries):
    rows = queries.shape[0]
    peak = jnp.full((HEADS, rows), masked_score, f32)
    total = jnp.zeros((HEADS, rows), f32)
    for _, keys, _, allowed in near:
        scores = near_scores(queries, keys, allowed)
        new_peak = jnp.maximum(peak, jnp.max(scores, axis=-1))
        grown = jnp.where(allowed[None], jnp.exp2(scores - new_peak[..., None]), 0.0)
        total = total * jnp.exp2(peak - new_peak) + jnp.sum(grown, axis=-1)
        peak = new_peak
    lse = peak + jnp.log2(total)
    out = jnp.zeros((rows, HEADS, HEAD), f32)
    for _, keys, values, allowed in near:
        scores = near_scores(queries, keys, allowed)
        weights = jnp.where(allowed[None], jnp.exp2(scores - lse[..., None]), 0.0).astype(bf16)
        out = out + jnp.einsum("hqk,khd->qhd", weights, values, preferred_element_type=f32)
    return out.reshape(rows, D).astype(bf16), lse


def near_attention_grad(near, queries, lse, out, grad):
    rows = queries.shape[0]
    grad_heads = grad.reshape(rows, HEADS, HEAD)
    delta = jnp.sum((grad.astype(f32) * out.astype(f32)).reshape(rows, HEADS, HEAD), axis=-1).T
    dq = jnp.zeros((rows, HEADS, HEAD), f32)
    dk = jnp.zeros((rows, HEADS, HEAD), f32)
    dv = jnp.zeros((rows, HEADS, HEAD), f32)
    for offset, keys, values, allowed in near:
        scores = near_scores(queries, keys, allowed)
        weights = jnp.where(allowed[None], jnp.exp2(scores - lse[..., None]), 0.0)
        value_grad = jnp.einsum("qhd,khd->hqk", grad_heads, values, preferred_element_type=f32)
        score_grad = (weights * (value_grad - delta[..., None])).astype(bf16)
        dq = dq + jnp.einsum("hqk,khd->qhd", score_grad, keys, preferred_element_type=f32)
        dk_part = jnp.einsum("hqk,qhd->khd", score_grad, queries, preferred_element_type=f32)
        dv_part = jnp.einsum(
            "hqk,qhd->khd", weights.astype(bf16), grad_heads, preferred_element_type=f32
        )
        if offset:
            dk_part, dv_part = shifted((dk_part.astype(bf16), dv_part.astype(bf16)), "blk", offset)
        dk = dk + dk_part.astype(f32)
        dv = dv + dv_part.astype(f32)
    dq = dq.reshape(rows, D).astype(bf16) * jnp.asarray(HEAD**-0.5, bf16)
    dk = (dk * (1.0 / LOG2E)).reshape(rows, D).astype(bf16)
    return dq, dk, dv.reshape(rows, D).astype(bf16)


def in_groups(*parts):
    rows = parts[0].shape[0]
    stacked = jnp.stack([part.reshape(rows, D // 128, 128) for part in parts], axis=2)
    return stacked.transpose(1, 0, 2, 3).reshape(D // 128, rows, 128 * len(parts))


def from_groups(groups, part):
    picked = groups[:, :, 128 * part : 128 * part + 128]
    return picked.transpose(1, 0, 2).reshape(groups.shape[1], D)


def rims(rows_own, width):
    count = lax.axis_size("blk")
    top = lax.ppermute(rows_own[-width:], "blk", [(i, i + 1) for i in range(count - 1)])
    bottom = lax.ppermute(rows_own[:width], "blk", [(i + 1, i) for i in range(count - 1)])
    return top, bottom


def line(vector):
    return vector.reshape(1, -1)


def shards(
    tokens,
    image_sides,
    ln1_gain,
    ln1_bias,
    qkv_weight,
    qv_bias,
    proj_weight,
    proj_bias,
    ln2_gain,
    ln2_bias,
    up_weight,
    up_bias,
    down_weight,
    down_bias,
    conv_weight,
    bn_gain,
    bn_bias,
    out_grad,
    pup_grad,
):
    x = tokens[0]
    sides_row = image_sides[0]
    rows = x.shape[0]
    blks, seqs = lax.axis_size("blk"), lax.axis_size("seq")
    place = lax.axis_index("blk")
    length = rows * blks
    samples = length * seqs
    by_heads = HEADS // 2 == blks

    block_starts = jnp.arange(length // BLOCK, dtype=jnp.int32) * BLOCK
    _, block_width, _, _, block_begin = image_info(sides_row, block_starts)
    starts = (block_begin // BLOCK).astype(jnp.int32)
    counts = (block_width * block_width // BLOCK).astype(jnp.int32)
    own_blocks = rows // BLOCK
    widths = lax.dynamic_slice_in_dim(block_width, place * own_blocks, own_blocks)
    wide_positions = place * rows + jnp.arange(-WIDE_RIM, rows + WIDE_RIM, dtype=jnp.int32)
    wide_flags = edge_flags(sides_row, wide_positions)
    flags = wide_flags[WIDE_RIM - RIM : WIDE_RIM + rows + RIM]

    g = pup_grad[0]
    g_top, g_bottom = rims(g, WIDE_RIM)
    dact = spread(widths, g, g_top, g_bottom, wide_flags)

    h1, qkv_groups = project_qkv(x, line(ln1_gain), line(ln1_bias), qkv_weight, line(qv_bias))
    if by_heads:
        qkv = lax.all_to_all(qkv_groups, "blk", 0, 0, tiled=True).reshape(length, 384)
        o_heads, lse = attention(starts, counts, qkv)
        o_groups = lax.all_to_all(o_heads.reshape(blks, rows, 128), "blk", 0, 0, tiled=True)
    else:
        queries = from_groups(qkv_groups, 0).reshape(rows, HEADS, HEAD)
        near = near_blocks(sides_row, from_groups(qkv_groups, 1), from_groups(qkv_groups, 2))
        attended, lse = near_attention(near, queries)
        o_groups = in_groups(attended)
    x1, h2, act, slope, block_low = mlp(
        o_groups, x, proj_weight, line(proj_bias), line(ln2_gain), line(ln2_bias),
        up_weight, line(up_bias), down_weight, line(down_bias),
    )
    top, bottom = rims(block_low, RIM)
    z, z_sums = conv(widths, block_low, top, bottom, flags, conv_weight)
    z_top, z_bottom = rims(z, RIM)
    z_sums = small_sum(z_sums[None], False, 1)
    mean = z_sums[0:1] / samples
    inv = lax.rsqrt(z_sums[1:2] / samples - mean * mean + batch_eps)
    pup_out, normed, dbn, bn_sums = batch(
        widths, z, z_top, z_bottom, dact, flags, mean, inv, line(bn_gain), line(bn_bias)
    )
    bn_sums = small_sum(bn_sums[None], False, 2)

    conv_weight_grad, dy = conv_grad(
        widths, dbn, normed, flags, inv * line(bn_gain), bn_sums[0:1] / samples, bn_sums[1:2] / samples,
        conv_weight, block_low, out_grad[0],
    )
    down_grad, up_grad, up_bias_grad, dx1, do_groups, proj_grad, mlp_sums = mlp_grad(
        dy, act, slope, down_weight, up_weight, x1, h2, line(ln2_gain), proj_weight, o_groups
    )
    if by_heads:
        do_heads = lax.all_to_all(do_groups, "blk", 0, 0, tiled=True).reshape(length, 128)
        dqkv = attention_grad(starts, counts, qkv, do_heads, o_heads, lse)
        dqkv_groups = lax.all_to_all(dqkv.reshape(blks, rows, 384), "blk", 0, 0, tiled=True)
    else:
        grads = near_attention_grad(near, queries, lse, attended, from_groups(do_groups, 0))
        dqkv_groups = in_groups(*grads)
    qkv_weight_grad, dqb, dvb, tokens_grad, qkv_sums = qkv_grad(
        dqkv_groups, qkv_weight, h1, dx1, x, line(ln1_gain)
    )

    def scattered(grad):
        part = lax.psum_scatter(grad, "blk", scatter_dimension=0, tiled=True)
        return lax.psum(part, "seq").astype(f32)

    down_grad, up_grad, proj_grad, conv_weight_grad = [
        scattered(grad) for grad in (down_grad, up_grad, proj_grad, conv_weight_grad)
    ]
    qkv_weight_grad = scattered(qkv_weight_grad.transpose(1, 0, 2).reshape(D, 3 * D))
    vectors = [
        qkv_sums[0], qkv_sums[1], dqb[0], dvb[0], mlp_sums[0], mlp_sums[1], mlp_sums[2], mlp_sums[3],
    ]
    piece = D // blks
    qv_grad = jnp.concatenate([dqb[0], dvb[0]])
    stacked = jnp.concatenate(
        [vector.reshape(blks, -1) for vector in vectors[:2] + vectors[4:] + [qv_grad, up_bias_grad[0]]], axis=1
    )
    summed = small_sum(stacked[:, None, :], True, 3)[0]
    cuts = [piece] * 6 + [2 * piece, 4 * piece]
    small = []
    at = 0
    for cut in cuts:
        small.append(summed[at : at + cut])
        at += cut
    ln1_g, ln1_b, proj_b, ln2_g, ln2_b, down_b, qv_b, up_b = small
    channel_piece = C // blks
    gain_slice = lax.dynamic_slice_in_dim(bn_sums[1], place * channel_piece, channel_piece)
    bias_slice = lax.dynamic_slice_in_dim(bn_sums[0], place * channel_piece, channel_piece)
    return (
        block_low[None],
        pup_out[None],
        tokens_grad[None],
        ln1_g,
        ln1_b,
        qkv_weight_grad,
        qv_b,
        proj_grad,
        proj_b,
        ln2_g,
        ln2_b,
        up_grad,
        up_b,
        down_grad,
        down_b,
        conv_weight_grad,
        gain_slice,
        bias_slice,
    )


def solution(mesh):
    replicated = P()
    packed = P("seq", "blk", None)
    placed = (packed, P("seq", None)) + (replicated,) * 15 + (packed, packed)
    rows, vector = P("blk", None), P("blk")
    return jax.shard_map(
        shards,
        mesh=mesh,
        in_specs=placed,
        out_specs=(
            packed, packed, packed, vector, vector, rows, vector, rows, vector, vector, vector, rows,
            vector, rows, vector, rows, vector, vector,
        ),
        check_vma=False,
    )
```

```python
import functools

import jax
import jax.numpy as jnp
from jax import lax
from jax.experimental import pallas as pl
from jax.experimental.pallas import tpu as pltpu
from jax.sharding import PartitionSpec as P

D = 1024
HEADS = 16
HEAD = 64
FF = 4096
C = 256
REACH = 4
UNIT = 16
BLOCK = UNIT * UNIT
IMAGE_BLOCKS = (1, 4, 9)
RIM = 64
WIDE_RIM = 128
LOG2E = 1.4426950408889634
MESH = pl.DeviceIdType.MESH

norm_eps = 1e-06
batch_eps = 1e-05
masked_score = -1e30
f32 = jnp.float32
bf16 = jnp.bfloat16

NT = (((1,), (1,)), ((), ()))
TN = (((0,), (0,)), ((), ()))


def dot(left, right):
    return jnp.dot(left, right, preferred_element_type=f32)


def dot_nt(left, right):
    return lax.dot_general(left, right, NT, preferred_element_type=f32)


def dot_tn(left, right):
    return lax.dot_general(left, right, TN, preferred_element_type=f32)


def whole(shape):
    zeros = (0,) * len(shape)
    return pl.BlockSpec(shape, lambda *_: zeros)


def params(megabytes, **more):
    return pltpu.CompilerParams(vmem_limit_bytes=megabytes << 20, **more)


def cost(flops, moved, transcendentals=0):
    return pl.CostEstimate(
        flops=int(flops), bytes_accessed=int(moved), transcendentals=int(transcendentals)
    )


def image_info(image_sides, positions):
    image_areas = image_sides * image_sides
    image_ends = jnp.cumsum(image_areas).astype(jnp.int32)
    image_starts = (image_ends - image_areas).astype(jnp.int32)
    segment = jnp.sum((image_ends[None, :] <= positions[:, None]).astype(jnp.int32), axis=1).astype(
        jnp.int32
    )
    picked = segment[:, None] == jnp.arange(image_sides.shape[0], dtype=jnp.int32)[None, :]
    image_width = jnp.sum(jnp.where(picked, image_sides[None, :], 0), axis=1).astype(jnp.int32)
    image_width = jnp.maximum(image_width, 1).astype(jnp.int32)
    image_begin = jnp.sum(jnp.where(picked, image_starts[None, :], 0), axis=1).astype(jnp.int32)
    offset = (positions - image_begin).astype(jnp.int32)
    row_index = (offset // image_width).astype(jnp.int32)
    col_index = (offset - row_index * image_width).astype(jnp.int32)
    return (segment, image_width, row_index, col_index, image_begin)


def edge_flags(image_sides, positions):
    _, width, row, col, _ = image_info(image_sides, positions)
    flags = jnp.stack([row > 0, row < width - 1, col > 0, col < width - 1], axis=1)
    return jnp.concatenate([flags, flags], axis=1).astype(f32)


def layer_stats(values):
    mean = jnp.mean(values, axis=-1, keepdims=True)
    centred = values - mean
    scale_inv = lax.rsqrt(jnp.mean(centred * centred, axis=-1, keepdims=True) + norm_eps)
    return centred * scale_inv, scale_inv


def layer_backward(grad_out, normed, scale_inv, gain):
    scaled = grad_out * gain
    inner = (
        scaled
        - jnp.mean(scaled, axis=-1, keepdims=True)
        - normed * jnp.mean(scaled * normed, axis=-1, keepdims=True)
    )
    return scale_inv * inner


def column_sums(values):
    return jnp.sum(values, axis=0, keepdims=True)


def gelu_parts(values):
    cumulative = 0.5 + 0.5 * lax.erf(values * 0.7071067811865476)
    weighted = values * (0.3989422804014327 * jnp.exp(values * values * -0.5))
    return cumulative, weighted


def qkv_kernel(x_ref, gain_ref, bias_ref, wq_ref, wk_ref, wv_ref, bq_ref, bv_ref, h_ref, out_ref):
    @pl.when(pl.program_id(0) == 0)
    def _():
        normed, _ = layer_stats(x_ref[...].astype(f32))
        h_ref[...] = (normed * gain_ref[...] + bias_ref[...]).astype(bf16)

    hidden = h_ref[...]
    query = ((dot(hidden, wq_ref[...]) + bq_ref[...]) * (HEAD**-0.5 * LOG2E)).astype(bf16)
    key = dot(hidden, wk_ref[...]).astype(bf16)
    value = (dot(hidden, wv_ref[...]) + bv_ref[...]).astype(bf16)
    for part in range(2):
        lanes = slice(128 * part, 128 * part + 128)
        out_ref[part, :, 0:128] = query[:, lanes]
        out_ref[part, :, 128:256] = key[:, lanes]
        out_ref[part, :, 256:384] = value[:, lanes]


def project_qkv(x, gain, bias, weight, qv_bias):
    rows = x.shape[0]
    groups = D // 128
    return pl.pallas_call(
        qkv_kernel,
        grid=(groups // 2,),
        in_specs=[
            whole((rows, D)),
            whole((1, D)),
            whole((1, D)),
            pl.BlockSpec((D, 256), lambda i: (0, i)),
            pl.BlockSpec((D, 256), lambda i: (0, 4 + i)),
            pl.BlockSpec((D, 256), lambda i: (0, 8 + i)),
            pl.BlockSpec((1, 256), lambda i: (0, i)),
            pl.BlockSpec((1, 256), lambda i: (0, 4 + i)),
        ],
        out_specs=[whole((rows, D)), pl.BlockSpec((2, rows, 384), lambda i: (i, 0, 0))],
        out_shape=[
            jax.ShapeDtypeStruct((rows, D), bf16),
            jax.ShapeDtypeStruct((groups, rows, 384), bf16),
        ],
        compiler_params=params(40),
        cost_estimate=cost(2 * rows * D * 3 * D, 12 << 20),
        name="norm_qkv",
    )(x, gain, bias, weight, weight, weight, qv_bias, qv_bias)


def attention_kernel(starts, counts, qkv, o_ref, lse_ref, value_t):
    step = pl.program_id(0)

    @pl.when(step == 0)
    def _():
        value_t[...] = qkv[:, 256:384].T

    own = pl.ds(pl.multiple_of(step * BLOCK, BLOCK), BLOCK)
    query = qkv[own, 0:128]
    lane = lax.broadcasted_iota(jnp.int32, (BLOCK, 128), 1)
    zero = jnp.zeros_like(query)
    queries = [jnp.where(lane < HEAD, query, zero), jnp.where(lane >= HEAD, query, zero)]
    first, count = starts[step], counts[step]
    for blocks in IMAGE_BLOCKS:

        @pl.when(count == blocks)
        def _(blocks=blocks):
            image = pl.ds(pl.multiple_of(first * BLOCK, BLOCK), blocks * BLOCK)
            keys = qkv[image, 128:256]
            scores = [dot_nt(keys, part) for part in queries]
            outs, logs = [], []
            for head in range(2):
                peak = jnp.max(scores[head], axis=0, keepdims=True)
                grown = jnp.exp2(scores[head] - peak)
                total = jnp.sum(grown, axis=0, keepdims=True)
                rows = slice(HEAD * head, HEAD * head + HEAD)
                outs.append(dot(value_t[rows, image], grown.astype(bf16)) * (1.0 / total))
                logs.append(peak + jnp.log2(total))
            o_ref[...] = jnp.concatenate(outs, axis=0).T.astype(bf16)
            lse_ref[...] = jnp.concatenate(logs + [jnp.zeros((6, BLOCK), f32)], axis=0)


def attention(starts, counts, qkv):
    length = qkv.shape[0]
    pairs = 100 * 2 * BLOCK * BLOCK
    return pl.pallas_call(
        attention_kernel,
        grid_spec=pltpu.PrefetchScalarGridSpec(
            num_scalar_prefetch=2,
            grid=(length // BLOCK,),
            in_specs=[whole((length, 384))],
            out_specs=[
                pl.BlockSpec((BLOCK, 128), lambda i, *_: (i, 0)),
                pl.BlockSpec((8, BLOCK), lambda i, *_: (0, i)),
            ],
            scratch_shapes=[pltpu.VMEM((128, length), bf16)],
        ),
        out_shape=[
            jax.ShapeDtypeStruct((length, 128), bf16),
            jax.ShapeDtypeStruct((8, length), f32),
        ],
        compiler_params=params(40),
        cost_estimate=cost(4 * HEAD * pairs, 5 << 20, pairs),
        name="attention",
    )(starts, counts, qkv)


def attention_grad_kernel(
    starts, counts, qkv, do_ref, o_ref, lse, out_ref, query_m, do_m, key_t, dq_t, delta
):
    step = pl.program_id(0)
    length = do_ref.shape[0]
    lane = lax.broadcasted_iota(jnp.int32, (BLOCK, 128), 1)
    low = lane < HEAD

    @pl.when(step == 0)
    def _():
        key_t[...] = qkv[:, 128:256].T
        dq_t[...] = jnp.zeros_like(dq_t)

        def prepare(i, _):
            rows = pl.ds(pl.multiple_of(i * BLOCK, BLOCK), BLOCK)
            grad = do_ref[rows, :]
            product = (grad.astype(f32) * o_ref[rows, :].astype(f32)).T
            delta[0:1, rows] = jnp.sum(product[:HEAD], axis=0, keepdims=True)
            delta[1:2, rows] = jnp.sum(product[HEAD:], axis=0, keepdims=True)
            query = qkv[rows, 0:128]
            zero = jnp.zeros_like(query)
            query_m[0, rows, :] = jnp.where(low, query, zero)
            query_m[1, rows, :] = jnp.where(low, zero, query)
            do_m[0, rows, :] = jnp.where(low, grad, zero)
            do_m[1, rows, :] = jnp.where(low, zero, grad)
            return 0

        lax.fori_loop(0, length // BLOCK, prepare, 0)

    own = pl.ds(pl.multiple_of(step * BLOCK, BLOCK), BLOCK)
    key = qkv[own, 128:256]
    value = qkv[own, 256:384]
    first, count = starts[step], counts[step]
    for blocks in IMAGE_BLOCKS:

        @pl.when(count == blocks)
        def _(blocks=blocks):
            image = pl.ds(pl.multiple_of(first * BLOCK, BLOCK), blocks * BLOCK)
            dk = dv = None
            for head in range(2):
                rows = slice(HEAD * head, HEAD * head + HEAD)
                query, grad = query_m[head, image, :], do_m[head, image, :]
                scores = dot_nt(key, query)
                value_grad = dot_nt(value, grad)
                weights = jnp.exp2(scores - lse[head : head + 1, image])
                score_grad = (weights * (value_grad - delta[head : head + 1, image])).astype(bf16)
                dv_part = dot(weights.astype(bf16), grad)
                dk_part = dot(score_grad, query)
                dv = dv_part if dv is None else dv + dv_part
                dk = dk_part if dk is None else dk + dk_part
                dq_t[rows, image] += dot(key_t[rows, own], score_grad)
            out_ref[own, 128:256] = (dk * (1.0 / LOG2E)).astype(bf16)
            out_ref[own, 256:384] = dv.astype(bf16)

    @pl.when(step == pl.num_programs(0) - 1)
    def _():
        def finish(i, _):
            rows = pl.ds(pl.multiple_of(i * BLOCK, BLOCK), BLOCK)
            out_ref[rows, 0:128] = dq_t[:, rows].T.astype(bf16) * jnp.asarray(HEAD**-0.5, bf16)
            return 0

        lax.fori_loop(0, length // BLOCK, finish, 0)


def attention_grad(starts, counts, qkv, do, o, lse):
    length = qkv.shape[0]
    pairs = 100 * 2 * BLOCK * BLOCK
    return pl.pallas_call(
        attention_grad_kernel,
        grid_spec=pltpu.PrefetchScalarGridSpec(
            num_scalar_prefetch=2,
            grid=(length // BLOCK,),
            in_specs=[
                whole((length, 384)),
                whole((length, 128)),
                whole((length, 128)),
                whole((8, length)),
            ],
            out_specs=whole((length, 384)),
            scratch_shapes=[
                pltpu.VMEM((2, length, 128), bf16),
                pltpu.VMEM((2, length, 128), bf16),
                pltpu.VMEM((128, length), bf16),
                pltpu.VMEM((128, length), f32),
                pltpu.VMEM((8, length), f32),
            ],
        ),
        out_shape=jax.ShapeDtypeStruct((length, 384), bf16),
        compiler_params=params(56),
        cost_estimate=cost(10 * HEAD * pairs, 12 << 20, pairs),
        name="attention_grad",
    )(starts, counts, qkv, do, o, lse)


FF_TILE = 512


def mlp_kernel(
    o_ref, x_ref, wp_ref, pb_ref, gain_ref, bias_ref, wu_ref, ub_ref, wd_ref, db_ref,
    x1_ref, h_ref, act_ref, slope_ref, out_ref, total,
):
    step = pl.program_id(0)

    @pl.when(step == 0)
    def _():
        attended = jnp.concatenate([o_ref[i] for i in range(o_ref.shape[0])], axis=1)
        x1 = x_ref[...].astype(f32) + dot(attended, wp_ref[...]) + pb_ref[...]
        x1_ref[...] = x1
        normed, _ = layer_stats(x1)
        h_ref[...] = (normed * gain_ref[...] + bias_ref[...]).astype(bf16)
        total[...] = x1 + db_ref[...]

    raised = dot(h_ref[...], wu_ref[...]) + ub_ref[...]
    cumulative, weighted = gelu_parts(raised)
    act = (raised * cumulative).astype(bf16)
    act_ref[...] = act
    slope_ref[...] = (cumulative + weighted).astype(bf16)
    total[...] += dot(act, wd_ref[...])

    @pl.when(step == pl.num_programs(0) - 1)
    def _():
        out_ref[...] = total[...].astype(bf16)


def mlp(o, x, wp, pb, gain, bias, wu, ub, wd, db):
    rows = x.shape[0]
    groups = o.shape[0]
    tile = FF_TILE
    return pl.pallas_call(
        mlp_kernel,
        grid=(FF // tile,),
        in_specs=[
            whole((groups, rows, 128)),
            whole((rows, D)),
            whole((D, D)),
            whole((1, D)),
            whole((1, D)),
            whole((1, D)),
            pl.BlockSpec((D, tile), lambda i: (0, i)),
            pl.BlockSpec((1, tile), lambda i: (0, i)),
            pl.BlockSpec((tile, D), lambda i: (i, 0)),
            whole((1, D)),
        ],
        out_specs=[
            whole((rows, D)),
            whole((rows, D)),
            pl.BlockSpec((rows, tile), lambda i: (0, i)),
            pl.BlockSpec((rows, tile), lambda i: (0, i)),
            whole((rows, D)),
        ],
        out_shape=[
            jax.ShapeDtypeStruct((rows, D), f32),
            jax.ShapeDtypeStruct((rows, D), bf16),
            jax.ShapeDtypeStruct((rows, FF), bf16),
            jax.ShapeDtypeStruct((rows, FF), bf16),
            jax.ShapeDtypeStruct((rows, D), bf16),
        ],
        scratch_shapes=[pltpu.VMEM((rows, D), f32)],
        compiler_params=params(56),
        cost_estimate=cost(2 * rows * D * (D + 2 * FF), 34 << 20, rows * FF),
        name="proj_norm_mlp",
    )(o, x, wp, pb, gain, bias, wu, ub, wd, db)


def mlp_grad_kernel(
    dy_ref, act_ref, slope_ref, wd_ref, wu_ref, x1_ref, h_ref, gain_ref, wp_ref, o_ref,
    dwd_ref, dwu_ref, dub_ref, dx1_ref, do_ref, dwp_ref, sums_ref, dm, h_t, total,
):
    step = pl.program_id(0)

    @pl.when(step == 0)
    def _():
        dm[...] = dy_ref[...].astype(bf16)
        h_t[...] = h_ref[...].T
        total[...] = jnp.zeros_like(total)

    down_in = dm[...]
    act_grad = dot_nt(down_in, wd_ref[...])
    raised_grad = act_grad * slope_ref[...].astype(f32)
    raised_low = raised_grad.astype(bf16)
    dub_ref[...] = column_sums(raised_low.astype(f32))
    dwd_ref[...] = dot_tn(act_ref[...], down_in).astype(bf16)
    dwu_ref[...] = dot(h_t[...], raised_low).astype(bf16)
    total[...] += dot_nt(raised_low, wu_ref[...])

    @pl.when(step == pl.num_programs(0) - 1)
    def _():
        grad = total[...]
        normed, scale_inv = layer_stats(x1_ref[...])
        dx1 = dy_ref[...] + layer_backward(grad, normed, scale_inv, gain_ref[...])
        dx1_ref[...] = dx1
        low = dx1.astype(bf16)
        sums_ref[0:1, :] = column_sums(low.astype(f32))
        sums_ref[1:2, :] = column_sums(grad * normed)
        sums_ref[2:3, :] = column_sums(grad)
        sums_ref[3:4, :] = column_sums(dm[...].astype(f32))
        sums_ref[4:8, :] = jnp.zeros((4, D), f32)
        attended = jnp.concatenate([o_ref[i] for i in range(o_ref.shape[0])], axis=1)
        dwp_ref[...] = dot_tn(attended, low).astype(bf16)
        attended_grad = dot_nt(low, wp_ref[...]).astype(bf16)
        for i in range(do_ref.shape[0]):
            do_ref[i] = attended_grad[:, 128 * i : 128 * i + 128]


def mlp_grad(dy, act, slope, wd, wu, x1, h, gain, wp, o):
    rows = dy.shape[0]
    groups = o.shape[0]
    tile = FF_TILE
    return pl.pallas_call(
        mlp_grad_kernel,
        grid=(FF // tile,),
        in_specs=[
            whole((rows, D)),
            pl.BlockSpec((rows, tile), lambda i: (0, i)),
            pl.BlockSpec((rows, tile), lambda i: (0, i)),
            pl.BlockSpec((tile, D), lambda i: (i, 0)),
            pl.BlockSpec((D, tile), lambda i: (0, i)),
            whole((rows, D)),
            whole((rows, D)),
            whole((1, D)),
            whole((D, D)),
            whole((groups, rows, 128)),
        ],
        out_specs=[
            pl.BlockSpec((tile, D), lambda i: (i, 0)),
            pl.BlockSpec((D, tile), lambda i: (0, i)),
            pl.BlockSpec((1, tile), lambda i: (0, i)),
            whole((rows, D)),
            whole((groups, rows, 128)),
            whole((D, D)),
            whole((8, D)),
        ],
        out_shape=[
            jax.ShapeDtypeStruct((FF, D), bf16),
            jax.ShapeDtypeStruct((D, FF), bf16),
            jax.ShapeDtypeStruct((1, FF), f32),
            jax.ShapeDtypeStruct((rows, D), f32),
            jax.ShapeDtypeStruct((groups, rows, 128), bf16),
            jax.ShapeDtypeStruct((D, D), bf16),
            jax.ShapeDtypeStruct((8, D), f32),
        ],
        scratch_shapes=[
            pltpu.VMEM((rows, D), bf16),
            pltpu.VMEM((D, rows), bf16),
            pltpu.VMEM((rows, D), f32),
        ],
        compiler_params=params(60),
        cost_estimate=cost(2 * rows * D * (2 * D + 4 * FF), 60 << 20),
        name="mlp_norm_proj_grad",
    )(dy, act, slope, wd, wu, x1, h, gain, wp, o)


def qkv_grad_kernel(
    g_ref, wq_ref, wk_ref, wv_ref, h_ref, dx1_ref, x_ref, gain_ref,
    dw_ref, dqb_ref, dvb_ref, dx_ref, sums_ref, h_t, total,
):
    step = pl.program_id(0)

    @pl.when(step == 0)
    def _():
        h_t[...] = h_ref[...].T
        total[...] = jnp.zeros_like(total)

    for part, w_ref in enumerate((wq_ref, wk_ref, wv_ref)):
        lanes = slice(128 * part, 128 * part + 128)
        grad = jnp.concatenate([g_ref[0, :, lanes], g_ref[1, :, lanes]], axis=1)
        total[...] += dot_nt(grad, w_ref[...])
        dw_ref[part] = dot(h_t[...], grad).astype(bf16)
        if part == 0:
            dqb_ref[...] = column_sums(grad.astype(f32))
        if part == 2:
            dvb_ref[...] = column_sums(grad.astype(f32))

    @pl.when(step == pl.num_programs(0) - 1)
    def _():
        grad = total[...]
        normed, scale_inv = layer_stats(x_ref[...].astype(f32))
        dx_ref[...] = dx1_ref[...] + layer_backward(grad, normed, scale_inv, gain_ref[...])
        sums_ref[0:1, :] = column_sums(grad * normed)
        sums_ref[1:2, :] = column_sums(grad)
        sums_ref[2:8, :] = jnp.zeros((6, D), f32)


def qkv_grad(g, weight, h, dx1, x, gain):
    rows = x.shape[0]
    groups = D // 128
    return pl.pallas_call(
        qkv_grad_kernel,
        grid=(groups // 2,),
        in_specs=[
            pl.BlockSpec((2, rows, 384), lambda i: (i, 0, 0)),
            pl.BlockSpec((D, 256), lambda i: (0, i)),
            pl.BlockSpec((D, 256), lambda i: (0, 4 + i)),
            pl.BlockSpec((D, 256), lambda i: (0, 8 + i)),
            whole((rows, D)),
            whole((rows, D)),
            whole((rows, D)),
            whole((1, D)),
        ],
        out_specs=[
            pl.BlockSpec((3, D, 256), lambda i: (0, 0, i)),
            pl.BlockSpec((1, 256), lambda i: (0, i)),
            pl.BlockSpec((1, 256), lambda i: (0, i)),
            whole((rows, D)),
            whole((8, D)),
        ],
        out_shape=[
            jax.ShapeDtypeStruct((3, D, D), bf16),
            jax.ShapeDtypeStruct((1, D), f32),
            jax.ShapeDtypeStruct((1, D), f32),
            jax.ShapeDtypeStruct((rows, D), f32),
            jax.ShapeDtypeStruct((8, D), f32),
        ],
        scratch_shapes=[pltpu.VMEM((D, rows), bf16), pltpu.VMEM((rows, D), f32)],
        compiler_params=params(48),
        cost_estimate=cost(4 * rows * D * 3 * D, 24 << 20),
        name="qkv_norm_grad",
    )(g, weight, weight, weight, h, dx1, x, gain)


def row_segments(rows, rim):
    count = rows // BLOCK
    pieces = []
    for block in range(count):
        first = block * BLOCK - (rim if block == 0 else 0)
        last = (block + 1) * BLOCK + (rim if block == count - 1 else 0)
        pieces.append((first, last - first, block))
    return pieces


def shifted_rows(start, shift, size):
    return pl.ds(pl.multiple_of(start + shift, UNIT), size)


def conv_kernel(widths, x_ref, top_ref, bottom_ref, flags, w_ref, z_ref, sums_ref, x_ext, left, right, centre):
    step = pl.program_id(0)
    rows = x_ref.shape[0]
    extent = rows + 2 * RIM

    @pl.when(step == 0)
    def _():
        x_ext[0:RIM, :] = top_ref[...]
        x_ext[RIM : RIM + rows, :] = x_ref[...]
        x_ext[RIM + rows :, :] = bottom_ref[...]
        left[...] = jnp.zeros_like(left)
        right[...] = jnp.zeros_like(right)

    source = x_ext[...]
    left[8 : 8 + extent, :] = dot(source, w_ref[0:D, :])
    right[8 : 8 + extent, :] = dot(source, w_ref[2 * D : 3 * D, :])
    centre[...] = (
        dot(source, w_ref[D : 2 * D, :])
        + flags[:, 2:3] * left[7 : 7 + extent, :]
        + flags[:, 3:4] * right[9 : 9 + extent, :]
    )
    for first, size, block in row_segments(rows, 0):
        own = slice(first, first + size)
        width = widths[block]
        for tap in range(3):

            @pl.when(step == tap)
            def _(tap=tap, first=first, size=size, own=own, width=width):
                found = centre[shifted_rows(RIM + first, (tap - 1) * width, size), :]
                if tap == 0:
                    z_ref[own, :] = flags[RIM + first : RIM + first + size, 0:1] * found
                elif tap == 1:
                    z_ref[own, :] += found
                else:
                    z_ref[own, :] += flags[RIM + first : RIM + first + size, 1:2] * found

    @pl.when(step == 2)
    def _():
        z = z_ref[...]
        sums_ref[0:1, :] = column_sums(z)
        sums_ref[1:2, :] = column_sums(z * z)
        sums_ref[2:8, :] = jnp.zeros((6, C), f32)


def conv(widths, x, top, bottom, flags, weight):
    rows = x.shape[0]
    extent = rows + 2 * RIM
    return pl.pallas_call(
        conv_kernel,
        grid_spec=pltpu.PrefetchScalarGridSpec(
            num_scalar_prefetch=1,
            grid=(3,),
            in_specs=[
                whole((rows, D)),
                whole((RIM, D)),
                whole((RIM, D)),
                whole((extent, 8)),
                pl.BlockSpec((3 * D, C), lambda i, *_: (i, 0)),
            ],
            out_specs=[whole((rows, C)), whole((8, C))],
            scratch_shapes=[
                pltpu.VMEM((extent, D), bf16),
                pltpu.VMEM((extent + 16, C), f32),
                pltpu.VMEM((extent + 16, C), f32),
                pltpu.VMEM((extent, C), f32),
            ],
        ),
        out_shape=[jax.ShapeDtypeStruct((rows, C), f32), jax.ShapeDtypeStruct((8, C), f32)],
        compiler_params=params(40),
        cost_estimate=cost(2 * extent * 9 * D * C, 8 << 20),
        name="conv",
    )(widths, x, top, bottom, flags, weight)


def spread_kernel(widths, g_ref, top_ref, bottom_ref, flags, out_ref, upper, lower, g_ext):
    rows = g_ref.shape[0]
    extent = rows + 2 * WIDE_RIM
    g_ext[0:WIDE_RIM, :] = top_ref[...].astype(f32)
    g_ext[WIDE_RIM : WIDE_RIM + rows, :] = g_ref[...].astype(f32)
    g_ext[WIDE_RIM + rows :, :] = bottom_ref[...].astype(f32)
    inner = slice(8, extent - 8)
    has_left, has_right = flags[inner, 2:3], flags[inner, 3:4]
    for i, target in enumerate((upper, lower)):
        near = g_ext[:, 2 * i * C : (2 * i + 1) * C]
        far = g_ext[:, (2 * i + 1) * C : (2 * i + 2) * C]
        target[0:8, :] = jnp.zeros((8, C), f32)
        target[extent - 8 :, :] = jnp.zeros((8, C), f32)
        target[inner, :] = (
            (1.0 - 0.25 * has_left) * near[inner, :]
            + (1.0 - 0.25 * has_right) * far[inner, :]
            + 0.25 * has_right * g_ext[9 : extent - 7, 2 * i * C : (2 * i + 1) * C]
            + 0.25 * has_left * g_ext[7 : extent - 9, (2 * i + 1) * C : (2 * i + 2) * C]
        )
    for first, size, block in row_segments(rows, RIM):
        width = widths[block]
        here = WIDE_RIM + first
        has_up, has_down = flags[here : here + size, 0:1], flags[here : here + size, 1:2]
        out_ref[RIM + first : RIM + first + size, :] = (
            (1.0 - 0.25 * has_up) * upper[here : here + size, :]
            + (1.0 - 0.25 * has_down) * lower[here : here + size, :]
            + 0.25 * has_down * upper[shifted_rows(here, width, size), :]
            + 0.25 * has_up * lower[shifted_rows(here, -width, size), :]
        )


def spread(widths, g, top, bottom, flags):
    rows = g.shape[0]
    extent = rows + 2 * WIDE_RIM
    return pl.pallas_call(
        spread_kernel,
        grid_spec=pltpu.PrefetchScalarGridSpec(
            num_scalar_prefetch=1,
            grid=(1,),
            in_specs=[
                whole((rows, D)),
                whole((WIDE_RIM, D)),
                whole((WIDE_RIM, D)),
                whole((extent, 8)),
            ],
            out_specs=whole((rows + 2 * RIM, C)),
            scratch_shapes=[
                pltpu.VMEM((extent, C), f32),
                pltpu.VMEM((extent, C), f32),
                pltpu.VMEM((extent, D), f32),
            ],
        ),
        out_shape=jax.ShapeDtypeStruct((rows + 2 * RIM, C), f32),
        compiler_params=params(40),
        cost_estimate=cost(20 * extent * D, 3 << 20),
        name="upsample_grad",
    )(widths, g, top, bottom, flags)


def batch_kernel(
    widths, z_ref, top_ref, bottom_ref, dact_ref, flags, mean_ref, inv_ref, gain_ref, bias_ref,
    up_ref, normed_ref, dbn_ref, sums_ref, act, mixed,
):
    rows = z_ref.shape[0]
    z = jnp.concatenate([top_ref[...], z_ref[...], bottom_ref[...]], axis=0)
    normed = (z - mean_ref[...]) * inv_ref[...]
    normed_ref[...] = normed
    pre = normed * gain_ref[...] + bias_ref[...]
    cumulative, weighted = gelu_parts(pre)
    act[...] = (pre * cumulative).astype(bf16).astype(f32)
    dbn = dact_ref[...] * (cumulative + weighted)
    dbn_ref[...] = dbn
    own = slice(RIM, RIM + rows)
    sums_ref[0:1, :] = column_sums(dbn[own, :])
    sums_ref[1:2, :] = column_sums(dbn[own, :] * normed[own, :])
    sums_ref[2:8, :] = jnp.zeros((6, C), f32)
    for first, size, block in row_segments(rows, 0):
        width = widths[block]
        here = RIM + first
        outer = slice(here - 8, here + size + 8)
        for i in range(2):
            has = flags[outer, i : i + 1]
            mixed[...] = (1.0 - 0.25 * has) * act[outer, :] + 0.25 * has * act[
                pl.ds(pl.multiple_of(here - 8 + (2 * i - 1) * width, 8), size + 16), :
            ]
            for j in range(2):
                has = flags[here : here + size, 2 + j : 3 + j]
                up_ref[first : first + size, (2 * i + j) * C : (2 * i + j + 1) * C] = (
                    (1.0 - 0.25 * has) * mixed[8 : 8 + size, :]
                    + 0.25 * has * mixed[7 + 2 * j : 7 + 2 * j + size, :]
                ).astype(bf16)


def batch(widths, z, top, bottom, dact, flags, mean, inv, gain, bias):
    rows = z.shape[0]
    extent = rows + 2 * RIM
    return pl.pallas_call(
        batch_kernel,
        grid_spec=pltpu.PrefetchScalarGridSpec(
            num_scalar_prefetch=1,
            grid=(1,),
            in_specs=[
                whole((rows, C)),
                whole((RIM, C)),
                whole((RIM, C)),
                whole((extent, C)),
                whole((extent, 8)),
                whole((1, C)),
                whole((1, C)),
                whole((1, C)),
                whole((1, C)),
            ],
            out_specs=[
                whole((rows, D)),
                whole((extent, C)),
                whole((extent, C)),
                whole((8, C)),
            ],
            scratch_shapes=[pltpu.VMEM((extent, C), f32), pltpu.VMEM((BLOCK + 16, C), f32)],
        ),
        out_shape=[
            jax.ShapeDtypeStruct((rows, D), bf16),
            jax.ShapeDtypeStruct((extent, C), f32),
            jax.ShapeDtypeStruct((extent, C), f32),
            jax.ShapeDtypeStruct((8, C), f32),
        ],
        compiler_params=params(40),
        cost_estimate=cost(60 * extent * C, 4 << 20),
        name="batch_norm",
    )(widths, z, top, bottom, dact, flags, mean, inv, gain, bias)


def conv_grad_kernel(
    widths, dbn_ref, normed_ref, flags, scale_ref, shift_ref, slope_ref, w_ref, x_ref, og_ref,
    dw_ref, dy_ref, moved, taps, x_t, total,
):
    step = pl.program_id(0)
    rows = x_ref.shape[0]
    extent = rows + 2 * RIM

    @pl.when(step == 0)
    def _():
        dz = scale_ref[...] * (dbn_ref[...] - shift_ref[...] - normed_ref[...] * slope_ref[...])
        dz = dz.astype(bf16).astype(f32)
        x_t[...] = x_ref[...].T
        total[...] = og_ref[...].astype(f32)
        moved[0, 0:8, :] = jnp.zeros((8, C), f32)
        moved[0, 8 + extent :, :] = jnp.zeros((8, C), f32)
        moved[0, 8 : 8 + extent, :] = dz
        moved[1, 8 : 8 + extent, :] = flags[:, 3:4] * moved[0, 9 : 9 + extent, :]
        moved[2, 8 : 8 + extent, :] = flags[:, 2:3] * moved[0, 7 : 7 + extent, :]
        for first, size, block in row_segments(rows, 0):
            width = widths[block]
            here = RIM + first
            for row in range(3):
                for col, slot in enumerate((1, 0, 2)):
                    found = moved[slot, pl.ds(pl.multiple_of(8 + here + (1 - row) * width, 8), size), :]
                    if row == 0:
                        found = flags[here : here + size, 1:2] * found
                    if row == 2:
                        found = flags[here : here + size, 0:1] * found
                    taps[3 * row + col, first : first + size, :] = found.astype(bf16)

    tap = taps[step]
    dw_ref[...] = dot(x_t[...], tap).astype(bf16)
    total[...] += dot_nt(tap, w_ref[...])

    @pl.when(step == pl.num_programs(0) - 1)
    def _():
        dy_ref[...] = total[...]


def conv_grad(widths, dbn, normed, flags, scale, shift, slope, weight, x, out_grad):
    rows = x.shape[0]
    extent = rows + 2 * RIM
    return pl.pallas_call(
        conv_grad_kernel,
        grid_spec=pltpu.PrefetchScalarGridSpec(
            num_scalar_prefetch=1,
            grid=(9,),
            in_specs=[
                whole((extent, C)),
                whole((extent, C)),
                whole((extent, 8)),
                whole((1, C)),
                whole((1, C)),
                whole((1, C)),
                pl.BlockSpec((D, C), lambda i, *_: (i, 0)),
                whole((rows, D)),
                whole((rows, D)),
            ],
            out_specs=[pl.BlockSpec((D, C), lambda i, *_: (i, 0)), whole((rows, D))],
            scratch_shapes=[
                pltpu.VMEM((3, extent + 16, C), f32),
                pltpu.VMEM((9, rows, C), bf16),
                pltpu.VMEM((D, rows), bf16),
                pltpu.VMEM((rows, D), f32),
            ],
        ),
        out_shape=[jax.ShapeDtypeStruct((9 * D, C), bf16), jax.ShapeDtypeStruct((rows, D), f32)],
        compiler_params=params(48),
        cost_estimate=cost(4 * rows * 9 * D * C, 16 << 20),
        name="conv_grad",
    )(widths, dbn, normed, flags, scale, shift, slope, weight, x, out_grad)


def small_sum_kernel(scatter, blks, seqs, x_ref, out_ref, first, second, sends, receives, sends2, receives2):
    blk, seq = lax.axis_index("blk"), lax.axis_index("seq")
    barrier = pltpu.get_barrier_semaphore()
    for step in range(1, blks):
        pl.semaphore_signal(
            barrier, inc=1, device_id={"blk": lax.rem(blk + step, blks)}, device_id_type=MESH
        )
    for step in range(1, seqs):
        pl.semaphore_signal(
            barrier, inc=1, device_id={"seq": lax.rem(seq + step, seqs)}, device_id_type=MESH
        )
    pl.semaphore_wait(barrier, blks + seqs - 2)
    copies = []
    for step in range(1, blks):
        to = lax.rem(blk + step, blks)
        copy = pltpu.make_async_remote_copy(
            src_ref=x_ref.at[to] if scatter else x_ref.at[0],
            dst_ref=first.at[blk],
            send_sem=sends.at[step],
            recv_sem=receives.at[step],
            device_id={"blk": to},
            device_id_type=MESH,
        )
        copy.start()
        copies.append(copy)
    first[blk] = x_ref[blk] if scatter else x_ref[0]
    for copy in copies:
        copy.wait()
    total = first[0]
    for i in range(1, blks):
        total = total + first[i]
    second[seq] = total
    copies = []
    for step in range(1, seqs):
        copy = pltpu.make_async_remote_copy(
            src_ref=second.at[seq],
            dst_ref=second.at[seq],
            send_sem=sends2.at[step],
            recv_sem=receives2.at[step],
            device_id={"seq": lax.rem(seq + step, seqs)},
            device_id_type=MESH,
        )
        copy.start()
        copies.append(copy)
    for copy in copies:
        copy.wait()
    total = second[0]
    for i in range(1, seqs):
        total = total + second[i]
    out_ref[...] = total


def small_sum(x, scatter, collective_id):
    blks, seqs = lax.axis_size("blk"), lax.axis_size("seq")
    part = x.shape[1:]
    return pl.pallas_call(
        functools.partial(small_sum_kernel, scatter, blks, seqs),
        in_specs=[pl.BlockSpec(memory_space=pltpu.VMEM)],
        out_specs=pl.BlockSpec(memory_space=pltpu.VMEM),
        out_shape=jax.ShapeDtypeStruct(part, f32),
        scratch_shapes=[
            pltpu.VMEM((blks, *part), f32),
            pltpu.VMEM((seqs, *part), f32),
            pltpu.SemaphoreType.DMA((blks,)),
            pltpu.SemaphoreType.DMA((blks,)),
            pltpu.SemaphoreType.DMA((seqs,)),
            pltpu.SemaphoreType.DMA((seqs,)),
        ],
        compiler_params=params(16, collective_id=collective_id, has_side_effects=True),
        name="small_sum",
    )(x)


LAG = 2
PIECE_ROWS = 64


def reduce_kernel(seqs, units, *refs):
    count = 1 + max(unit[0] for unit in units)
    ins, outs = refs[:count], refs[count:2 * count]
    own, near, side, last, below, above = [refs[(2 + i) * count:(3 + i) * count] for i in range(6)]
    (load_sem, s1, r1, s2, r2, s3, r3, sb, rb, sa, ra, out_sem) = refs[8 * count:]
    blk, seq = lax.axis_index("blk"), lax.axis_index("seq")
    core, x, y = blk % 2, (blk // 2) % 2, blk // 4
    pair, over_x, over_y = (blk + 1 - 2 * core, blk + 2 - 4 * x, blk + 4 - 8 * y)
    root = 1
    barrier = pltpu.get_barrier_semaphore()
    for peer in (pair, over_x, over_y):
        pl.semaphore_signal(barrier, inc=1, device_id={"blk": peer}, device_id_type=MESH)
    @pl.when(seq > 0)
    def _():
        pl.semaphore_signal(barrier, inc=1, device_id={"seq": seq - 1}, device_id_type=MESH)
    @pl.when(seq < seqs - 1)
    def _():
        pl.semaphore_signal(barrier, inc=1, device_id={"seq": seq + 1}, device_id_type=MESH)
    ends = jnp.where(seq > 0, 1, 0) + jnp.where(seq < seqs - 1, 1, 0)
    pl.semaphore_wait(barrier, 3 + ends)

    def send(src, dst, ssem, rsem, peer):
        return pltpu.make_async_remote_copy(src_ref=src, dst_ref=dst, send_sem=ssem, recv_sem=rsem, device_id=peer, device_id_type=MESH)

    def load(u):
        a, part, rows, cols = units[u]
        return pltpu.make_async_copy(ins[a].at[part, :, core, rows, cols], own[a].at[part, :, rows, cols], load_sem.at[u])
    def first(u):
        a, part, rows, cols = units[u]
        return send(ins[a].at[part, :, 1 - core, rows, cols], near[a].at[part, :, rows, cols], s1.at[u], r1.at[u], {"blk": pair})
    def second(u):
        a, part, rows, cols = units[u]
        if u % 2 == 0:
            src = [own[a].at[part, pl.ds(1 - x + 2 * i, 1), rows, cols] for i in range(2)]
            peer = over_x
        else:
            src = [own[a].at[part, pl.ds(2 * (1 - y) + i, 1), rows, cols] for i in range(2)]
            peer = over_y
        return [send(src[i], side[a].at[part, pl.ds(i,1), rows, cols], s2.at[u, i], r2.at[u, i], {"blk": peer}) for i in range(2)]
    def third(u):
        a, part, rows, cols = units[u]
        if u % 2 == 0:
            src, peer = 2 * (1 - y) + x, over_y
        else:
            src, peer = 2 * y + 1 - x, over_x
        return send(own[a].at[part, src, rows, cols], last[a].at[part, rows, cols], s3.at[u], r3.at[u], {"blk": peer})
    mine = 2 * y + x
    def result(u):
        a, part, rows, cols = units[u]
        return own[a].at[part, mine, rows, cols]
    def down(u):
        a, part, rows, cols = units[u]
        return send(result(u), above[a].at[part, rows, cols], sa.at[u], ra.at[u], {"seq": seq - 1})
    def up(u):
        a, part, rows, cols = units[u]
        return send(result(u), below[a].at[part, rows, cols], sb.at[u], rb.at[u], {"seq": seq + 1})
    def store(u):
        a, part, rows, cols = units[u]
        return pltpu.make_async_copy(result(u), outs[a].at[part, rows, cols], out_sem.at[u])

    def add_to(target, *sources):
        total = target[...].astype(f32)
        for source in sources:
            total = total + source[...].astype(f32)
        target[...] = total.astype(target.dtype)

    def stage_near(u):
        a, part, rows, cols = units[u]
        load(u).wait()
        first(u).wait_recv()
        for i in range(4):
            add_to(own[a].at[part, i, rows, cols], near[a].at[part, i, rows, cols])
        for copy in second(u): copy.start()
    def stage_side(u):
        a, part, rows, cols = units[u]
        for i, copy in enumerate(second(u)):
            copy.wait_recv()
            keep = 2 * i + x if u % 2 == 0 else 2 * y + i
            add_to(own[a].at[part, keep, rows, cols], side[a].at[part, i, rows, cols])
        third(u).start()
    def stage_last(u):
        a, part, rows, cols = units[u]
        third(u).wait_recv()
        add_to(result(u), last[a].at[part, rows, cols])
        @pl.when(seq < root)
        def _():
            up(u).start()
        @pl.when(seq == seqs - 1)
        def _():
            down(u).start()
    def stage_chain(u, place):
        a, part, rows, cols = units[u]
        @pl.when(seq == place)
        def _():
            down(u).wait_recv()
            add_to(result(u), above[a].at[part, rows, cols])
            down(u).start()
    def stage_root(u):
        a, part, rows, cols = units[u]
        @pl.when(seq == root)
        def _():
            up(u).wait_recv()
            down(u).wait_recv()
            add_to(result(u), below[a].at[part, rows, cols], above[a].at[part, rows, cols])
            up(u).start()
            down(u).start()
            store(u).start()
    def stage_spread(u, place):
        a, part, rows, cols = units[u]
        @pl.when(seq == place)
        def _():
            if place < root:
                down(u).wait_recv()
                up(u).wait_send()
                result(u)[...] = above[a].at[part, rows, cols][...]
            else:
                up(u).wait_recv()
                down(u).wait_send()
                result(u)[...] = below[a].at[part, rows, cols][...]
                if place < seqs - 1: up(u).start()
            store(u).start()

    stages = [(0, stage_near), (LAG, stage_side), (2 * LAG, stage_last)]
    at = 3 * LAG
    for place in range(seqs - 2, root, -1):
        stages.append((at, functools.partial(stage_chain, place=place))); at += LAG
    stages.append((at, stage_root)); at += LAG
    for place in range(root): stages.append((at, functools.partial(stage_spread, place=place)))
    for place in range(root + 1, seqs):
        stages.append((at, functools.partial(stage_spread, place=place))); at += LAG
    for u in range(len(units)):
        load(u).start()
        first(u).start()
    for t in range(len(units) + stages[-1][0]):
        for lag, stage in reversed(stages):
            if 0 <= t - lag < len(units): stage(t - lag)
    for u in range(len(units)):
        first(u).wait_send()
        for copy in second(u): copy.wait_send()
        third(u).wait_send()
        @pl.when(seq == root)
        def _():
            down(u).wait_send()
            up(u).wait_send()
        @pl.when((seq > root) & (seq < seqs - 1))
        def _():
            up(u).wait_send()
        store(u).wait()


def cuts(size, piece):
    return [slice(first, min(size, first + piece)) for first in range(0, size, piece)]


def reduce_grads(arrays, collective_id):
    shapes = [(array.shape[0],) + array.shape[3:] for array in arrays]
    units = []
    for index, (parts, rows, columns) in enumerate(shapes):
        piece = PIECE_ROWS if columns >= D else 3 * PIECE_ROWS
        for part in range(parts):
            for row in cuts(rows, piece):
                for column in cuts(columns, D):
                    units.append((index, part, row, column))
    count, total = len(arrays), len(units)
    scratch = []
    for lead in ((4,), (4,), (2,), (), (), ()):
        scratch += [
            pltpu.VMEM((shape[0],) + lead + shape[1:], array.dtype)
            for shape, array in zip(shapes, arrays)
        ]
    for lanes in (1, 1, 1, 2, 2, 1, 1, 1, 1, 1, 1, 1):
        scratch.append(pltpu.SemaphoreType.DMA((total, 2) if lanes == 2 else (total,)))
    anywhere = pl.BlockSpec(memory_space=pl.ANY)
    return pl.pallas_call(
        functools.partial(reduce_kernel, lax.axis_size("seq"), units),
        in_specs=[anywhere] * count,
        out_specs=[anywhere] * count,
        out_shape=[
            jax.ShapeDtypeStruct(shape, array.dtype) for shape, array in zip(shapes, arrays)
        ],
        scratch_shapes=scratch,
        compiler_params=params(60, collective_id=collective_id, has_side_effects=True),
        name="reduce_grads",
    )(*arrays)


def shifted(value, axis, steps):
    count = lax.axis_size(axis)
    leading, last = (max(0, -steps), min(count, count - steps))
    return lax.ppermute(value, axis, [(source, source + steps) for source in range(leading, last)])


def near_blocks(sides_row, keys_own, values_own):
    rows = keys_own.shape[0]
    place, length = lax.axis_index("blk"), rows * lax.axis_size("blk")
    centre = jnp.arange(rows, dtype=jnp.int32)
    segment = image_info(sides_row, place * rows + centre)[0]
    found = []
    for offset in range(-REACH, REACH + 1):
        keys, values = (keys_own, values_own) if offset == 0 else shifted((keys_own, values_own), "blk", -offset)
        positions = (place + offset) * rows + centre
        inside = (positions >= 0) & (positions < length)
        allowed = (segment[:, None] == image_info(sides_row, positions)[0][None, :]) & inside[None, :]
        found.append((offset, keys.reshape(rows, HEADS, HEAD), values.reshape(rows, HEADS, HEAD), allowed))
    return found


def near_scores(queries, keys, allowed):
    scores = jnp.einsum("qhd,khd->hqk", queries, keys, preferred_element_type=f32)
    return jnp.where(allowed[None], scores, masked_score)


def near_attention(near, queries):
    rows = queries.shape[0]
    peak = jnp.full((HEADS, rows), masked_score, f32)
    total = jnp.zeros((HEADS, rows), f32)
    for _, keys, _, allowed in near:
        scores = near_scores(queries, keys, allowed)
        new_peak = jnp.maximum(peak, jnp.max(scores, axis=-1))
        grown = jnp.where(allowed[None], jnp.exp2(scores - new_peak[..., None]), 0.0)
        total = total * jnp.exp2(peak - new_peak) + jnp.sum(grown, axis=-1)
        peak = new_peak
    lse = peak + jnp.log2(total)
    out = jnp.zeros((rows, HEADS, HEAD), f32)
    for _, keys, values, allowed in near:
        scores = near_scores(queries, keys, allowed)
        weights = jnp.where(allowed[None], jnp.exp2(scores - lse[..., None]), 0.0).astype(bf16)
        out = out + jnp.einsum("hqk,khd->qhd", weights, values, preferred_element_type=f32)
    return out.reshape(rows, D).astype(bf16), lse


def near_attention_grad(near, queries, lse, out, grad):
    rows = queries.shape[0]
    grad_heads = grad.reshape(rows, HEADS, HEAD)
    delta = jnp.sum((grad.astype(f32) * out.astype(f32)).reshape(rows, HEADS, HEAD), axis=-1).T
    dq = jnp.zeros((rows, HEADS, HEAD), f32)
    dk = jnp.zeros((rows, HEADS, HEAD), f32)
    dv = jnp.zeros((rows, HEADS, HEAD), f32)
    for offset, keys, values, allowed in near:
        scores = near_scores(queries, keys, allowed)
        weights = jnp.where(allowed[None], jnp.exp2(scores - lse[..., None]), 0.0)
        value_grad = jnp.einsum("qhd,khd->hqk", grad_heads, values, preferred_element_type=f32)
        score_grad = (weights * (value_grad - delta[..., None])).astype(bf16)
        dq = dq + jnp.einsum("hqk,khd->qhd", score_grad, keys, preferred_element_type=f32)
        dk_part = jnp.einsum("hqk,qhd->khd", score_grad, queries, preferred_element_type=f32)
        dv_part = jnp.einsum(
            "hqk,qhd->khd", weights.astype(bf16), grad_heads, preferred_element_type=f32
        )
        if offset:
            dk_part, dv_part = shifted((dk_part.astype(bf16), dv_part.astype(bf16)), "blk", offset)
        dk = dk + dk_part.astype(f32)
        dv = dv + dv_part.astype(f32)
    dq = dq.reshape(rows, D).astype(bf16) * jnp.asarray(HEAD**-0.5, bf16)
    dk = (dk * (1.0 / LOG2E)).reshape(rows, D).astype(bf16)
    return dq, dk, dv.reshape(rows, D).astype(bf16)


def in_groups(*parts):
    rows = parts[0].shape[0]
    stacked = jnp.stack([part.reshape(rows, D // 128, 128) for part in parts], axis=2)
    return stacked.transpose(1, 0, 2, 3).reshape(D // 128, rows, 128 * len(parts))


def from_groups(groups, part):
    picked = groups[:, :, 128 * part : 128 * part + 128]
    return picked.transpose(1, 0, 2).reshape(groups.shape[1], D)


def rims(rows_own, width):
    count = lax.axis_size("blk")
    top = lax.ppermute(rows_own[-width:], "blk", [(i, i + 1) for i in range(count - 1)])
    bottom = lax.ppermute(rows_own[:width], "blk", [(i + 1, i) for i in range(count - 1)])
    return top, bottom


def line(vector):
    return vector.reshape(1, -1)


def shards(
    tokens,
    image_sides,
    ln1_gain,
    ln1_bias,
    qkv_weight,
    qv_bias,
    proj_weight,
    proj_bias,
    ln2_gain,
    ln2_bias,
    up_weight,
    up_bias,
    down_weight,
    down_bias,
    conv_weight,
    bn_gain,
    bn_bias,
    out_grad,
    pup_grad,
):
    x = tokens[0]
    sides_row = image_sides[0]
    rows = x.shape[0]
    blks, seqs = lax.axis_size("blk"), lax.axis_size("seq")
    place = lax.axis_index("blk")
    length = rows * blks
    samples = length * seqs
    by_heads = HEADS // 2 == blks

    block_starts = jnp.arange(length // BLOCK, dtype=jnp.int32) * BLOCK
    _, block_width, _, _, block_begin = image_info(sides_row, block_starts)
    starts = (block_begin // BLOCK).astype(jnp.int32)
    counts = (block_width * block_width // BLOCK).astype(jnp.int32)
    own_blocks = rows // BLOCK
    widths = lax.dynamic_slice_in_dim(block_width, place * own_blocks, own_blocks)
    wide_positions = place * rows + jnp.arange(-WIDE_RIM, rows + WIDE_RIM, dtype=jnp.int32)
    wide_flags = edge_flags(sides_row, wide_positions)
    flags = wide_flags[WIDE_RIM - RIM : WIDE_RIM + rows + RIM]

    g = pup_grad[0]
    g_top, g_bottom = rims(g, WIDE_RIM)
    dact = spread(widths, g, g_top, g_bottom, wide_flags)

    h1, qkv_groups = project_qkv(x, line(ln1_gain), line(ln1_bias), qkv_weight, line(qv_bias))
    if by_heads:
        qkv = lax.all_to_all(qkv_groups, "blk", 0, 0, tiled=True).reshape(length, 384)
        o_heads, lse = attention(starts, counts, qkv)
        o_groups = lax.all_to_all(o_heads.reshape(blks, rows, 128), "blk", 0, 0, tiled=True)
    else:
        queries = from_groups(qkv_groups, 0).reshape(rows, HEADS, HEAD)
        near = near_blocks(sides_row, from_groups(qkv_groups, 1), from_groups(qkv_groups, 2))
        attended, lse = near_attention(near, queries)
        o_groups = in_groups(attended)
    x1, h2, act, slope, block_low = mlp(
        o_groups, x, proj_weight, line(proj_bias), line(ln2_gain), line(ln2_bias),
        up_weight, line(up_bias), down_weight, line(down_bias),
    )
    top, bottom = rims(block_low, RIM)
    z, z_sums = conv(widths, block_low, top, bottom, flags, conv_weight)
    z_top, z_bottom = rims(z, RIM)
    z_sums = small_sum(z_sums[None], False, 1)
    mean = z_sums[0:1] / samples
    inv = lax.rsqrt(z_sums[1:2] / samples - mean * mean + batch_eps)
    pup_out, normed, dbn, bn_sums = batch(
        widths, z, z_top, z_bottom, dact, flags, mean, inv, line(bn_gain), line(bn_bias)
    )
    bn_sums = small_sum(bn_sums[None], False, 2)

    conv_weight_grad, dy = conv_grad(
        widths, dbn, normed, flags, inv * line(bn_gain), bn_sums[0:1] / samples, bn_sums[1:2] / samples,
        conv_weight, block_low, out_grad[0],
    )
    down_grad, up_grad, up_bias_grad, dx1, do_groups, proj_grad, mlp_sums = mlp_grad(
        dy, act, slope, down_weight, up_weight, x1, h2, line(ln2_gain), proj_weight, o_groups
    )
    if by_heads:
        do_heads = lax.all_to_all(do_groups, "blk", 0, 0, tiled=True).reshape(length, 128)
        dqkv = attention_grad(starts, counts, qkv, do_heads, o_heads, lse)
        dqkv_groups = lax.all_to_all(dqkv.reshape(blks, rows, 384), "blk", 0, 0, tiled=True)
    else:
        grads = near_attention_grad(near, queries, lse, attended, from_groups(do_groups, 0))
        dqkv_groups = in_groups(*grads)
    qkv_weight_grad, dqb, dvb, tokens_grad, qkv_sums = qkv_grad(
        dqkv_groups, qkv_weight, h1, dx1, x, line(ln1_gain)
    )

    piece = D // blks
    vectors = [qkv_sums[0], qkv_sums[1], mlp_sums[0], mlp_sums[1], mlp_sums[2], mlp_sums[3]]
    vectors += [jnp.concatenate([dqb[0], dvb[0]]), up_bias_grad[0]]
    stacked = jnp.concatenate([vector.reshape(blks, -1) for vector in vectors], axis=1)
    if blks == 8:
        def by_place(array, parts=1):
            return array.reshape(parts, 4, 2, -1, array.shape[-1])

        flat = jnp.pad(stacked, ((0, 0), (0, 16 * 128 - stacked.shape[1])))
        down_grad, up_grad, conv_weight_grad, proj_grad, qkv_weight_grad, summed = reduce_grads(
            [
                by_place(down_grad),
                by_place(up_grad),
                by_place(conv_weight_grad),
                by_place(proj_grad),
                by_place(qkv_weight_grad, 3),
                by_place(flat.reshape(8, 16, 128)),
            ],
            3,
        )
        down_grad, up_grad, conv_weight_grad, proj_grad = [
            grad[0].astype(f32) for grad in (down_grad, up_grad, conv_weight_grad, proj_grad)
        ]
        qkv_weight_grad = jnp.concatenate([qkv_weight_grad[i] for i in range(3)], axis=1).astype(f32)
        summed = summed.reshape(-1)
    else:

        def scattered(grad):
            part = lax.psum_scatter(grad, "blk", scatter_dimension=0, tiled=True)
            return lax.psum(part, "seq").astype(f32)

        down_grad, up_grad, proj_grad, conv_weight_grad = [
            scattered(grad) for grad in (down_grad, up_grad, proj_grad, conv_weight_grad)
        ]
        qkv_weight_grad = scattered(qkv_weight_grad.transpose(1, 0, 2).reshape(D, 3 * D))
        summed = small_sum(stacked[:, None, :], True, 4)[0]
    small = []
    at = 0
    for cut in [piece] * 6 + [2 * piece, 4 * piece]:
        small.append(summed[at : at + cut])
        at += cut
    ln1_g, ln1_b, proj_b, ln2_g, ln2_b, down_b, qv_b, up_b = small
    channel_piece = C // blks
    gain_slice = lax.dynamic_slice_in_dim(bn_sums[1], place * channel_piece, channel_piece)
    bias_slice = lax.dynamic_slice_in_dim(bn_sums[0], place * channel_piece, channel_piece)
    return (
        block_low[None],
        pup_out[None],
        tokens_grad[None],
        ln1_g,
        ln1_b,
        qkv_weight_grad,
        qv_b,
        proj_grad,
        proj_b,
        ln2_g,
        ln2_b,
        up_grad,
        up_b,
        down_grad,
        down_b,
        conv_weight_grad,
        gain_slice,
        bias_slice,
    )


def solution(mesh):
    replicated = P()
    packed = P("seq", "blk", None)
    placed = (packed, P("seq", None)) + (replicated,) * 15 + (packed, packed)
    rows, vector = P("blk", None), P("blk")
    return jax.shard_map(
        shards,
        mesh=mesh,
        in_specs=placed,
        out_specs=(
            packed, packed, packed, vector, vector, rows, vector, rows, vector, vector, vector, rows,
            vector, rows, vector, rows, vector, vector,
        ),
        check_vma=False,
    )
```

```python
import functools

import jax
import jax.numpy as jnp
from jax import lax
from jax.experimental import pallas as pl
from jax.experimental.pallas import tpu as pltpu
from jax.sharding import PartitionSpec as P

D = 1024
HEADS = 16
HEAD = 64
FF = 4096
C = 256
REACH = 4
UNIT = 16
BLOCK = UNIT * UNIT
IMAGE_BLOCKS = (1, 4, 9)
RIM = 64
WIDE_RIM = 128
LOG2E = 1.4426950408889634
MESH = pl.DeviceIdType.MESH

norm_eps = 1e-06
batch_eps = 1e-05
masked_score = -1e30
f32 = jnp.float32
bf16 = jnp.bfloat16

NT = (((1,), (1,)), ((), ()))
TN = (((0,), (0,)), ((), ()))


def dot(left, right):
    return jnp.dot(left, right, preferred_element_type=f32)


def dot_nt(left, right):
    return lax.dot_general(left, right, NT, preferred_element_type=f32)


def dot_tn(left, right):
    return lax.dot_general(left, right, TN, preferred_element_type=f32)


def whole(shape):
    zeros = (0,) * len(shape)
    return pl.BlockSpec(shape, lambda *_: zeros)


def params(megabytes, **more):
    return pltpu.CompilerParams(vmem_limit_bytes=megabytes << 20, **more)


def cost(flops, moved, transcendentals=0):
    return pl.CostEstimate(
        flops=int(flops), bytes_accessed=int(moved), transcendentals=int(transcendentals)
    )


def place_copies(blks, source, target, sends, receives):
    me = lax.axis_index("blk")
    copies = []
    for step in range(1, blks):
        to = lax.rem(me + step, blks)
        copies.append(
            pltpu.make_async_remote_copy(
                src_ref=source.at[to],
                dst_ref=target.at[me],
                send_sem=sends.at[step],
                recv_sem=receives.at[step],
                device_id={"blk": to},
                device_id_type=MESH,
            )
        )
    return copies


def exchange_start(blks, source, target, sends, receives, own_sem):
    me = lax.axis_index("blk")
    barrier = pltpu.get_barrier_semaphore()
    for step in range(1, blks):
        pl.semaphore_signal(
            barrier, inc=1, device_id={"blk": lax.rem(me + step, blks)}, device_id_type=MESH
        )
    pl.semaphore_wait(barrier, blks - 1)
    for copy in place_copies(blks, source, target, sends, receives):
        copy.start()
    pltpu.make_async_copy(source.at[me], target.at[me], own_sem).start()


def exchange_wait(blks, source, target, sends, receives, own_sem):
    me = lax.axis_index("blk")
    for copy in place_copies(blks, source, target, sends, receives):
        copy.wait()
    pltpu.make_async_copy(source.at[me], target.at[me], own_sem).wait()


def image_info(image_sides, positions):
    image_areas = image_sides * image_sides
    image_ends = jnp.cumsum(image_areas).astype(jnp.int32)
    image_starts = (image_ends - image_areas).astype(jnp.int32)
    segment = jnp.sum((image_ends[None, :] <= positions[:, None]).astype(jnp.int32), axis=1).astype(
        jnp.int32
    )
    picked = segment[:, None] == jnp.arange(image_sides.shape[0], dtype=jnp.int32)[None, :]
    image_width = jnp.sum(jnp.where(picked, image_sides[None, :], 0), axis=1).astype(jnp.int32)
    image_width = jnp.maximum(image_width, 1).astype(jnp.int32)
    image_begin = jnp.sum(jnp.where(picked, image_starts[None, :], 0), axis=1).astype(jnp.int32)
    offset = (positions - image_begin).astype(jnp.int32)
    row_index = (offset // image_width).astype(jnp.int32)
    col_index = (offset - row_index * image_width).astype(jnp.int32)
    return (segment, image_width, row_index, col_index, image_begin)


def edge_flags(image_sides, positions):
    _, width, row, col, _ = image_info(image_sides, positions)
    flags = jnp.stack([row > 0, row < width - 1, col > 0, col < width - 1], axis=1)
    return jnp.concatenate([flags, flags], axis=1).astype(f32)


def layer_stats(values):
    mean = jnp.mean(values, axis=-1, keepdims=True)
    centred = values - mean
    scale_inv = lax.rsqrt(jnp.mean(centred * centred, axis=-1, keepdims=True) + norm_eps)
    return centred * scale_inv, scale_inv


def layer_backward(grad_out, normed, scale_inv, gain):
    scaled = grad_out * gain
    inner = (
        scaled
        - jnp.mean(scaled, axis=-1, keepdims=True)
        - normed * jnp.mean(scaled * normed, axis=-1, keepdims=True)
    )
    return scale_inv * inner


def column_sums(values):
    return jnp.sum(values, axis=0, keepdims=True)


def gelu_parts(values):
    cumulative = 0.5 + 0.5 * lax.erf(values * 0.7071067811865476)
    weighted = values * (0.3989422804014327 * jnp.exp(values * values * -0.5))
    return cumulative, weighted


def qkv_kernel(x_ref, gain_ref, bias_ref, wq_ref, wk_ref, wv_ref, bq_ref, bv_ref, h_ref, out_ref):
    @pl.when(pl.program_id(0) == 0)
    def _():
        normed, _ = layer_stats(x_ref[...].astype(f32))
        h_ref[...] = (normed * gain_ref[...] + bias_ref[...]).astype(bf16)

    hidden = h_ref[...]
    query = ((dot(hidden, wq_ref[...]) + bq_ref[...]) * (HEAD**-0.5 * LOG2E)).astype(bf16)
    key = dot(hidden, wk_ref[...]).astype(bf16)
    value = (dot(hidden, wv_ref[...]) + bv_ref[...]).astype(bf16)
    for part in range(2):
        lanes = slice(128 * part, 128 * part + 128)
        out_ref[part, :, 0:128] = query[:, lanes]
        out_ref[part, :, 128:256] = key[:, lanes]
        out_ref[part, :, 256:384] = value[:, lanes]


def project_qkv(x, gain, bias, weight, qv_bias):
    rows = x.shape[0]
    groups = D // 128
    return pl.pallas_call(
        qkv_kernel,
        grid=(groups // 2,),
        in_specs=[
            whole((rows, D)),
            whole((1, D)),
            whole((1, D)),
            pl.BlockSpec((D, 256), lambda i: (0, i)),
            pl.BlockSpec((D, 256), lambda i: (0, 4 + i)),
            pl.BlockSpec((D, 256), lambda i: (0, 8 + i)),
            pl.BlockSpec((1, 256), lambda i: (0, i)),
            pl.BlockSpec((1, 256), lambda i: (0, 4 + i)),
        ],
        out_specs=[whole((rows, D)), pl.BlockSpec((2, rows, 384), lambda i: (i, 0, 0))],
        out_shape=[
            jax.ShapeDtypeStruct((rows, D), bf16),
            jax.ShapeDtypeStruct((groups, rows, 384), bf16),
        ],
        compiler_params=params(40),
        cost_estimate=cost(2 * rows * D * 3 * D, 12 << 20),
        name="norm_qkv",
    )(x, gain, bias, weight, weight, weight, qv_bias, qv_bias)


def attention_kernel(starts, counts, qkv, o_ref, lse_ref, value_t):
    step = pl.program_id(0)

    @pl.when(step == 0)
    def _():
        value_t[...] = qkv[:, 256:384].T

    own = pl.ds(pl.multiple_of(step * BLOCK, BLOCK), BLOCK)
    query = qkv[own, 0:128]
    lane = lax.broadcasted_iota(jnp.int32, (BLOCK, 128), 1)
    zero = jnp.zeros_like(query)
    queries = [jnp.where(lane < HEAD, query, zero), jnp.where(lane >= HEAD, query, zero)]
    first, count = starts[step], counts[step]
    for blocks in IMAGE_BLOCKS:

        @pl.when(count == blocks)
        def _(blocks=blocks):
            image = pl.ds(pl.multiple_of(first * BLOCK, BLOCK), blocks * BLOCK)
            keys = qkv[image, 128:256]
            scores = [dot_nt(keys, part) for part in queries]
            outs, logs = [], []
            for head in range(2):
                peak = jnp.max(scores[head], axis=0, keepdims=True)
                grown = jnp.exp2(scores[head] - peak)
                total = jnp.sum(grown, axis=0, keepdims=True)
                rows = slice(HEAD * head, HEAD * head + HEAD)
                outs.append(dot(value_t[rows, image], grown.astype(bf16)) * (1.0 / total))
                logs.append(peak + jnp.log2(total))
            o_ref[...] = jnp.concatenate(outs, axis=0).T.astype(bf16)
            lse_ref[...] = jnp.concatenate(logs + [jnp.zeros((6, BLOCK), f32)], axis=0)


def attention(starts, counts, qkv):
    length = qkv.shape[0]
    pairs = 100 * 2 * BLOCK * BLOCK
    return pl.pallas_call(
        attention_kernel,
        grid_spec=pltpu.PrefetchScalarGridSpec(
            num_scalar_prefetch=2,
            grid=(length // BLOCK,),
            in_specs=[whole((length, 384))],
            out_specs=[
                pl.BlockSpec((BLOCK, 128), lambda i, *_: (i, 0)),
                pl.BlockSpec((8, BLOCK), lambda i, *_: (0, i)),
            ],
            scratch_shapes=[pltpu.VMEM((128, length), bf16)],
        ),
        out_shape=[
            jax.ShapeDtypeStruct((length, 128), bf16),
            jax.ShapeDtypeStruct((8, length), f32),
        ],
        compiler_params=params(40),
        cost_estimate=cost(4 * HEAD * pairs, 5 << 20, pairs),
        name="attention",
    )(starts, counts, qkv)


def attention_grad_kernel(
    starts, counts, qkv, do_ref, o_ref, lse, out_ref, query_m, do_m, key_t, dq_t, delta
):
    step = pl.program_id(0)
    length = do_ref.shape[0]
    lane = lax.broadcasted_iota(jnp.int32, (BLOCK, 128), 1)
    low = lane < HEAD

    @pl.when(step == 0)
    def _():
        key_t[...] = qkv[:, 128:256].T
        dq_t[...] = jnp.zeros_like(dq_t)

        def prepare(i, _):
            rows = pl.ds(pl.multiple_of(i * BLOCK, BLOCK), BLOCK)
            grad = do_ref[rows, :]
            product = (grad.astype(f32) * o_ref[rows, :].astype(f32)).T
            delta[0:1, rows] = jnp.sum(product[:HEAD], axis=0, keepdims=True)
            delta[1:2, rows] = jnp.sum(product[HEAD:], axis=0, keepdims=True)
            query = qkv[rows, 0:128]
            zero = jnp.zeros_like(query)
            query_m[0, rows, :] = jnp.where(low, query, zero)
            query_m[1, rows, :] = jnp.where(low, zero, query)
            do_m[0, rows, :] = jnp.where(low, grad, zero)
            do_m[1, rows, :] = jnp.where(low, zero, grad)
            return 0

        lax.fori_loop(0, length // BLOCK, prepare, 0)

    own = pl.ds(pl.multiple_of(step * BLOCK, BLOCK), BLOCK)
    key = qkv[own, 128:256]
    value = qkv[own, 256:384]
    first, count = starts[step], counts[step]
    for blocks in IMAGE_BLOCKS:

        @pl.when(count == blocks)
        def _(blocks=blocks):
            image = pl.ds(pl.multiple_of(first * BLOCK, BLOCK), blocks * BLOCK)
            dk = dv = None
            for head in range(2):
                rows = slice(HEAD * head, HEAD * head + HEAD)
                query, grad = query_m[head, image, :], do_m[head, image, :]
                scores = dot_nt(key, query)
                value_grad = dot_nt(value, grad)
                weights = jnp.exp2(scores - lse[head : head + 1, image])
                score_grad = (weights * (value_grad - delta[head : head + 1, image])).astype(bf16)
                dv_part = dot(weights.astype(bf16), grad)
                dk_part = dot(score_grad, query)
                dv = dv_part if dv is None else dv + dv_part
                dk = dk_part if dk is None else dk + dk_part
                dq_t[rows, image] += dot(key_t[rows, own], score_grad)
            out_ref[own, 128:256] = (dk * (1.0 / LOG2E)).astype(bf16)
            out_ref[own, 256:384] = dv.astype(bf16)

    @pl.when(step == pl.num_programs(0) - 1)
    def _():
        def finish(i, _):
            rows = pl.ds(pl.multiple_of(i * BLOCK, BLOCK), BLOCK)
            out_ref[rows, 0:128] = dq_t[:, rows].T.astype(bf16) * jnp.asarray(HEAD**-0.5, bf16)
            return 0

        lax.fori_loop(0, length // BLOCK, finish, 0)


def attention_grad(starts, counts, qkv, do, o, lse):
    length = qkv.shape[0]
    pairs = 100 * 2 * BLOCK * BLOCK
    return pl.pallas_call(
        attention_grad_kernel,
        grid_spec=pltpu.PrefetchScalarGridSpec(
            num_scalar_prefetch=2,
            grid=(length // BLOCK,),
            in_specs=[
                whole((length, 384)),
                whole((length, 128)),
                whole((length, 128)),
                whole((8, length)),
            ],
            out_specs=whole((length, 384)),
            scratch_shapes=[
                pltpu.VMEM((2, length, 128), bf16),
                pltpu.VMEM((2, length, 128), bf16),
                pltpu.VMEM((128, length), bf16),
                pltpu.VMEM((128, length), f32),
                pltpu.VMEM((8, length), f32),
            ],
        ),
        out_shape=jax.ShapeDtypeStruct((length, 384), bf16),
        compiler_params=params(56),
        cost_estimate=cost(10 * HEAD * pairs, 12 << 20, pairs),
        name="attention_grad",
    )(starts, counts, qkv, do, o, lse)


FF_TILE = 512


def mlp_kernel(
    o_ref, x_ref, wp_ref, pb_ref, gain_ref, bias_ref, wu_ref, ub_ref, wd_ref, db_ref,
    x1_ref, h_ref, act_ref, slope_ref, out_ref, total,
):
    step = pl.program_id(0)

    @pl.when(step == 0)
    def _():
        attended = jnp.concatenate([o_ref[i] for i in range(o_ref.shape[0])], axis=1)
        x1 = x_ref[...].astype(f32) + dot(attended, wp_ref[...]) + pb_ref[...]
        x1_ref[...] = x1
        normed, _ = layer_stats(x1)
        h_ref[...] = (normed * gain_ref[...] + bias_ref[...]).astype(bf16)
        total[...] = x1 + db_ref[...]

    raised = dot(h_ref[...], wu_ref[...]) + ub_ref[...]
    cumulative, weighted = gelu_parts(raised)
    act = (raised * cumulative).astype(bf16)
    act_ref[...] = act
    slope_ref[...] = (cumulative + weighted).astype(bf16)
    total[...] += dot(act, wd_ref[...])

    @pl.when(step == pl.num_programs(0) - 1)
    def _():
        out_ref[...] = total[...].astype(bf16)


def mlp(o, x, wp, pb, gain, bias, wu, ub, wd, db):
    rows = x.shape[0]
    groups = o.shape[0]
    tile = FF_TILE
    return pl.pallas_call(
        mlp_kernel,
        grid=(FF // tile,),
        in_specs=[
            whole((groups, rows, 128)),
            whole((rows, D)),
            whole((D, D)),
            whole((1, D)),
            whole((1, D)),
            whole((1, D)),
            pl.BlockSpec((D, tile), lambda i: (0, i)),
            pl.BlockSpec((1, tile), lambda i: (0, i)),
            pl.BlockSpec((tile, D), lambda i: (i, 0)),
            whole((1, D)),
        ],
        out_specs=[
            whole((rows, D)),
            whole((rows, D)),
            pl.BlockSpec((rows, tile), lambda i: (0, i)),
            pl.BlockSpec((rows, tile), lambda i: (0, i)),
            whole((rows, D)),
        ],
        out_shape=[
            jax.ShapeDtypeStruct((rows, D), f32),
            jax.ShapeDtypeStruct((rows, D), bf16),
            jax.ShapeDtypeStruct((rows, FF), bf16),
            jax.ShapeDtypeStruct((rows, FF), bf16),
            jax.ShapeDtypeStruct((rows, D), bf16),
        ],
        scratch_shapes=[pltpu.VMEM((rows, D), f32)],
        compiler_params=params(56),
        cost_estimate=cost(2 * rows * D * (D + 2 * FF), 34 << 20, rows * FF),
        name="proj_norm_mlp",
    )(o, x, wp, pb, gain, bias, wu, ub, wd, db)


def mlp_grad_kernel(
    dy_ref, dm_ref, slope_ref, wd_ref, wu_ref, x1_ref, gain_ref, wp_ref,
    du_ref, dub_ref, dx1_ref, da_ref, do_ref, sums_ref, total,
):
    step = pl.program_id(0)

    @pl.when(step == 0)
    def _():
        total[...] = jnp.zeros_like(total)

    act_grad = dot_nt(dm_ref[...], wd_ref[...])
    raised_low = (act_grad * slope_ref[...].astype(f32)).astype(bf16)
    du_ref[...] = raised_low
    dub_ref[...] = column_sums(raised_low.astype(f32))
    total[...] += dot_nt(raised_low, wu_ref[...])

    @pl.when(step == pl.num_programs(0) - 1)
    def _():
        grad = total[...]
        normed, scale_inv = layer_stats(x1_ref[...])
        dx1 = dy_ref[...] + layer_backward(grad, normed, scale_inv, gain_ref[...])
        dx1_ref[...] = dx1
        low = dx1.astype(bf16)
        da_ref[...] = low
        sums_ref[0:1, :] = column_sums(low.astype(f32))
        sums_ref[1:2, :] = column_sums(grad * normed)
        sums_ref[2:3, :] = column_sums(grad)
        sums_ref[3:4, :] = column_sums(dm_ref[...].astype(f32))
        sums_ref[4:8, :] = jnp.zeros((4, D), f32)
        attended_grad = dot_nt(low, wp_ref[...]).astype(bf16)
        for i in range(do_ref.shape[0]):
            do_ref[i] = attended_grad[:, 128 * i : 128 * i + 128]


def mlp_grad(dy, dm, slope, wd, wu, x1, gain, wp):
    rows = dy.shape[0]
    groups = D // 128
    tile = FF_TILE
    return pl.pallas_call(
        mlp_grad_kernel,
        grid=(FF // tile,),
        in_specs=[
            whole((rows, D)),
            whole((rows, D)),
            pl.BlockSpec((rows, tile), lambda i: (0, i)),
            pl.BlockSpec((tile, D), lambda i: (i, 0)),
            pl.BlockSpec((D, tile), lambda i: (0, i)),
            whole((rows, D)),
            whole((1, D)),
            whole((D, D)),
        ],
        out_specs=[
            pl.BlockSpec((rows, tile), lambda i: (0, i)),
            pl.BlockSpec((1, tile), lambda i: (0, i)),
            whole((rows, D)),
            whole((rows, D)),
            whole((groups, rows, 128)),
            whole((8, D)),
        ],
        out_shape=[
            jax.ShapeDtypeStruct((rows, FF), bf16),
            jax.ShapeDtypeStruct((1, FF), f32),
            jax.ShapeDtypeStruct((rows, D), f32),
            jax.ShapeDtypeStruct((rows, D), bf16),
            jax.ShapeDtypeStruct((groups, rows, 128), bf16),
            jax.ShapeDtypeStruct((8, D), f32),
        ],
        scratch_shapes=[pltpu.VMEM((rows, D), f32)],
        compiler_params=params(56),
        cost_estimate=cost(2 * rows * D * (D + 2 * FF), 34 << 20),
        name="mlp_norm_proj_grad",
    )(dy, dm, slope, wd, wu, x1, gain, wp)


def down_weight_kernel(act_ref, dm_ref, dwd_ref):
    dwd_ref[...] = dot_tn(act_ref[...], dm_ref[...]).astype(bf16)


def down_weight_grad_of(act, dm):
    rows = dm.shape[0]
    tile = FF_TILE
    return pl.pallas_call(
        down_weight_kernel,
        grid=(FF // tile,),
        in_specs=[pl.BlockSpec((rows, tile), lambda i: (0, i)), whole((rows, D))],
        out_specs=pl.BlockSpec((tile, D), lambda i: (i, 0)),
        out_shape=jax.ShapeDtypeStruct((FF, D), bf16),
        compiler_params=params(32),
        cost_estimate=cost(2 * rows * D * FF, 13 << 20),
        name="down_weight_grad",
    )(act, dm)


def conv_weight_kernel(x_ref, taps_ref, dw_ref, x_t):
    @pl.when(pl.program_id(0) == 0)
    def _():
        x_t[...] = x_ref[...].T

    for tap in range(3):
        dw_ref[D * tap : D * tap + D, :] = dot(x_t[...], taps_ref[tap]).astype(bf16)


def conv_weight_grad_of(x, taps):
    rows = x.shape[0]
    return pl.pallas_call(
        conv_weight_kernel,
        grid=(3,),
        in_specs=[whole((rows, D)), pl.BlockSpec((3, rows, C), lambda i: (i, 0, 0))],
        out_specs=pl.BlockSpec((3 * D, C), lambda i: (i, 0)),
        out_shape=jax.ShapeDtypeStruct((9 * D, C), bf16),
        scratch_shapes=[pltpu.VMEM((D, rows), bf16)],
        compiler_params=params(32),
        cost_estimate=cost(2 * rows * D * 9 * C, 9 << 20),
        name="conv_weight_grad",
    )(x, taps)


def exchange_semaphores(blks):
    count = max(blks, 1)
    return [
        pltpu.SemaphoreType.DMA((count,)),
        pltpu.SemaphoreType.DMA((count,)),
        pltpu.SemaphoreType.DMA,
    ]


def exchange_params(blks, megabytes, collective_id):
    if blks:
        return params(megabytes, collective_id=collective_id, has_side_effects=True)
    return params(megabytes)


def late_weights_kernel(
    blks, h_ref, du_ref, o_ref, da_ref, source, dwu_ref, dwp_ref, target, h_t, *semaphores
):
    step = pl.program_id(0)

    @pl.when(step == 0)
    def _():
        if blks:
            exchange_start(blks, source, target, *semaphores)
        h_t[...] = h_ref[...].T
        attended = jnp.concatenate([o_ref[i] for i in range(o_ref.shape[0])], axis=1)
        dwp_ref[...] = dot_tn(attended, da_ref[...]).astype(bf16)

    dwu_ref[...] = dot(h_t[...], du_ref[...]).astype(bf16)

    if blks:

        @pl.when(step == pl.num_programs(0) - 1)
        def _():
            exchange_wait(blks, source, target, *semaphores)


def late_weights(h, du, o, da, sent, blks, collective_id):
    rows = h.shape[0]
    groups = D // 128
    tile = FF_TILE
    anywhere = pl.BlockSpec(memory_space=pl.ANY)
    return pl.pallas_call(
        functools.partial(late_weights_kernel, blks),
        grid=(FF // tile,),
        in_specs=[
            whole((rows, D)),
            pl.BlockSpec((rows, tile), lambda i: (0, i)),
            whole((groups, rows, 128)),
            whole((rows, D)),
            anywhere,
        ],
        out_specs=[pl.BlockSpec((D, tile), lambda i: (0, i)), whole((D, D)), anywhere],
        out_shape=[
            jax.ShapeDtypeStruct((D, FF), bf16),
            jax.ShapeDtypeStruct((D, D), bf16),
            jax.ShapeDtypeStruct(sent.shape, bf16),
        ],
        scratch_shapes=[pltpu.VMEM((D, rows), bf16)] + exchange_semaphores(blks),
        compiler_params=exchange_params(blks, 40, collective_id),
        cost_estimate=cost(2 * rows * D * (FF + D), 18 << 20),
        name="up_proj_weight_grads",
    )(h, du, o, da, sent)


def qkv_grad_kernel(
    g_ref, wq_ref, wk_ref, wv_ref, h_ref, dx1_ref, x_ref, gain_ref,
    dw_ref, dqb_ref, dvb_ref, dx_ref, sums_ref, h_t, total,
):
    step = pl.program_id(0)

    @pl.when(step == 0)
    def _():
        h_t[...] = h_ref[...].T
        total[...] = jnp.zeros_like(total)

    for part, w_ref in enumerate((wq_ref, wk_ref, wv_ref)):
        lanes = slice(128 * part, 128 * part + 128)
        grad = jnp.concatenate([g_ref[0, :, lanes], g_ref[1, :, lanes]], axis=1)
        total[...] += dot_nt(grad, w_ref[...])
        dw_ref[part] = dot(h_t[...], grad).astype(bf16)
        if part == 0:
            dqb_ref[...] = column_sums(grad.astype(f32))
        if part == 2:
            dvb_ref[...] = column_sums(grad.astype(f32))

    @pl.when(step == pl.num_programs(0) - 1)
    def _():
        grad = total[...]
        normed, scale_inv = layer_stats(x_ref[...].astype(f32))
        dx_ref[...] = dx1_ref[...] + layer_backward(grad, normed, scale_inv, gain_ref[...])
        sums_ref[0:1, :] = column_sums(grad * normed)
        sums_ref[1:2, :] = column_sums(grad)
        sums_ref[2:8, :] = jnp.zeros((6, D), f32)


def qkv_grad(g, weight, h, dx1, x, gain):
    rows = x.shape[0]
    groups = D // 128
    return pl.pallas_call(
        qkv_grad_kernel,
        grid=(groups // 2,),
        in_specs=[
            pl.BlockSpec((2, rows, 384), lambda i: (i, 0, 0)),
            pl.BlockSpec((D, 256), lambda i: (0, i)),
            pl.BlockSpec((D, 256), lambda i: (0, 4 + i)),
            pl.BlockSpec((D, 256), lambda i: (0, 8 + i)),
            whole((rows, D)),
            whole((rows, D)),
            whole((rows, D)),
            whole((1, D)),
        ],
        out_specs=[
            pl.BlockSpec((3, D, 256), lambda i: (0, 0, i)),
            pl.BlockSpec((1, 256), lambda i: (0, i)),
            pl.BlockSpec((1, 256), lambda i: (0, i)),
            whole((rows, D)),
            whole((8, D)),
        ],
        out_shape=[
            jax.ShapeDtypeStruct((3, D, D), bf16),
            jax.ShapeDtypeStruct((1, D), f32),
            jax.ShapeDtypeStruct((1, D), f32),
            jax.ShapeDtypeStruct((rows, D), f32),
            jax.ShapeDtypeStruct((8, D), f32),
        ],
        scratch_shapes=[pltpu.VMEM((D, rows), bf16), pltpu.VMEM((rows, D), f32)],
        compiler_params=params(48),
        cost_estimate=cost(4 * rows * D * 3 * D, 24 << 20),
        name="qkv_norm_grad",
    )(g, weight, weight, weight, h, dx1, x, gain)


def row_segments(rows, rim):
    count = rows // BLOCK
    pieces = []
    for block in range(count):
        first = block * BLOCK - (rim if block == 0 else 0)
        last = (block + 1) * BLOCK + (rim if block == count - 1 else 0)
        pieces.append((first, last - first, block))
    return pieces


def shifted_rows(start, shift, size):
    return pl.ds(pl.multiple_of(start + shift, UNIT), size)


def conv_kernel(widths, x_ref, top_ref, bottom_ref, flags, w_ref, z_ref, sums_ref, x_ext, left, right, centre):
    step = pl.program_id(0)
    rows = x_ref.shape[0]
    extent = rows + 2 * RIM

    @pl.when(step == 0)
    def _():
        x_ext[0:RIM, :] = top_ref[...]
        x_ext[RIM : RIM + rows, :] = x_ref[...]
        x_ext[RIM + rows :, :] = bottom_ref[...]
        left[...] = jnp.zeros_like(left)
        right[...] = jnp.zeros_like(right)

    source = x_ext[...]
    left[8 : 8 + extent, :] = dot(source, w_ref[0:D, :])
    right[8 : 8 + extent, :] = dot(source, w_ref[2 * D : 3 * D, :])
    centre[...] = (
        dot(source, w_ref[D : 2 * D, :])
        + flags[:, 2:3] * left[7 : 7 + extent, :]
        + flags[:, 3:4] * right[9 : 9 + extent, :]
    )
    for first, size, block in row_segments(rows, 0):
        own = slice(first, first + size)
        width = widths[block]
        for tap in range(3):

            @pl.when(step == tap)
            def _(tap=tap, first=first, size=size, own=own, width=width):
                found = centre[shifted_rows(RIM + first, (tap - 1) * width, size), :]
                if tap == 0:
                    z_ref[own, :] = flags[RIM + first : RIM + first + size, 0:1] * found
                elif tap == 1:
                    z_ref[own, :] += found
                else:
                    z_ref[own, :] += flags[RIM + first : RIM + first + size, 1:2] * found

    @pl.when(step == 2)
    def _():
        z = z_ref[...]
        sums_ref[0:1, :] = column_sums(z)
        sums_ref[1:2, :] = column_sums(z * z)
        sums_ref[2:8, :] = jnp.zeros((6, C), f32)


def conv(widths, x, top, bottom, flags, weight):
    rows = x.shape[0]
    extent = rows + 2 * RIM
    return pl.pallas_call(
        conv_kernel,
        grid_spec=pltpu.PrefetchScalarGridSpec(
            num_scalar_prefetch=1,
            grid=(3,),
            in_specs=[
                whole((rows, D)),
                whole((RIM, D)),
                whole((RIM, D)),
                whole((extent, 8)),
                pl.BlockSpec((3 * D, C), lambda i, *_: (i, 0)),
            ],
            out_specs=[whole((rows, C)), whole((8, C))],
            scratch_shapes=[
                pltpu.VMEM((extent, D), bf16),
                pltpu.VMEM((extent + 16, C), f32),
                pltpu.VMEM((extent + 16, C), f32),
                pltpu.VMEM((extent, C), f32),
            ],
        ),
        out_shape=[jax.ShapeDtypeStruct((rows, C), f32), jax.ShapeDtypeStruct((8, C), f32)],
        compiler_params=params(40),
        cost_estimate=cost(2 * extent * 9 * D * C, 8 << 20),
        name="conv",
    )(widths, x, top, bottom, flags, weight)


def spread_kernel(widths, g_ref, top_ref, bottom_ref, flags, out_ref, upper, lower, g_ext):
    rows = g_ref.shape[0]
    extent = rows + 2 * WIDE_RIM
    g_ext[0:WIDE_RIM, :] = top_ref[...].astype(f32)
    g_ext[WIDE_RIM : WIDE_RIM + rows, :] = g_ref[...].astype(f32)
    g_ext[WIDE_RIM + rows :, :] = bottom_ref[...].astype(f32)
    inner = slice(8, extent - 8)
    has_left, has_right = flags[inner, 2:3], flags[inner, 3:4]
    for i, target in enumerate((upper, lower)):
        near = g_ext[:, 2 * i * C : (2 * i + 1) * C]
        far = g_ext[:, (2 * i + 1) * C : (2 * i + 2) * C]
        target[0:8, :] = jnp.zeros((8, C), f32)
        target[extent - 8 :, :] = jnp.zeros((8, C), f32)
        target[inner, :] = (
            (1.0 - 0.25 * has_left) * near[inner, :]
            + (1.0 - 0.25 * has_right) * far[inner, :]
            + 0.25 * has_right * g_ext[9 : extent - 7, 2 * i * C : (2 * i + 1) * C]
            + 0.25 * has_left * g_ext[7 : extent - 9, (2 * i + 1) * C : (2 * i + 2) * C]
        )
    for first, size, block in row_segments(rows, RIM):
        width = widths[block]
        here = WIDE_RIM + first
        has_up, has_down = flags[here : here + size, 0:1], flags[here : here + size, 1:2]
        out_ref[RIM + first : RIM + first + size, :] = (
            (1.0 - 0.25 * has_up) * upper[here : here + size, :]
            + (1.0 - 0.25 * has_down) * lower[here : here + size, :]
            + 0.25 * has_down * upper[shifted_rows(here, width, size), :]
            + 0.25 * has_up * lower[shifted_rows(here, -width, size), :]
        )


def spread(widths, g, top, bottom, flags):
    rows = g.shape[0]
    extent = rows + 2 * WIDE_RIM
    return pl.pallas_call(
        spread_kernel,
        grid_spec=pltpu.PrefetchScalarGridSpec(
            num_scalar_prefetch=1,
            grid=(1,),
            in_specs=[
                whole((rows, D)),
                whole((WIDE_RIM, D)),
                whole((WIDE_RIM, D)),
                whole((extent, 8)),
            ],
            out_specs=whole((rows + 2 * RIM, C)),
            scratch_shapes=[
                pltpu.VMEM((extent, C), f32),
                pltpu.VMEM((extent, C), f32),
                pltpu.VMEM((extent, D), f32),
            ],
        ),
        out_shape=jax.ShapeDtypeStruct((rows + 2 * RIM, C), f32),
        compiler_params=params(40),
        cost_estimate=cost(20 * extent * D, 3 << 20),
        name="upsample_grad",
    )(widths, g, top, bottom, flags)


def batch_kernel(
    widths, z_ref, top_ref, bottom_ref, dact_ref, flags, mean_ref, inv_ref, gain_ref, bias_ref,
    up_ref, normed_ref, dbn_ref, sums_ref, act, mixed,
):
    rows = z_ref.shape[0]
    z = jnp.concatenate([top_ref[...], z_ref[...], bottom_ref[...]], axis=0)
    normed = (z - mean_ref[...]) * inv_ref[...]
    normed_ref[...] = normed
    pre = normed * gain_ref[...] + bias_ref[...]
    cumulative, weighted = gelu_parts(pre)
    act[...] = (pre * cumulative).astype(bf16).astype(f32)
    dbn = dact_ref[...] * (cumulative + weighted)
    dbn_ref[...] = dbn
    own = slice(RIM, RIM + rows)
    sums_ref[0:1, :] = column_sums(dbn[own, :])
    sums_ref[1:2, :] = column_sums(dbn[own, :] * normed[own, :])
    sums_ref[2:8, :] = jnp.zeros((6, C), f32)
    for first, size, block in row_segments(rows, 0):
        width = widths[block]
        here = RIM + first
        outer = slice(here - 8, here + size + 8)
        for i in range(2):
            has = flags[outer, i : i + 1]
            mixed[...] = (1.0 - 0.25 * has) * act[outer, :] + 0.25 * has * act[
                pl.ds(pl.multiple_of(here - 8 + (2 * i - 1) * width, 8), size + 16), :
            ]
            for j in range(2):
                has = flags[here : here + size, 2 + j : 3 + j]
                up_ref[first : first + size, (2 * i + j) * C : (2 * i + j + 1) * C] = (
                    (1.0 - 0.25 * has) * mixed[8 : 8 + size, :]
                    + 0.25 * has * mixed[7 + 2 * j : 7 + 2 * j + size, :]
                ).astype(bf16)


def batch(widths, z, top, bottom, dact, flags, mean, inv, gain, bias):
    rows = z.shape[0]
    extent = rows + 2 * RIM
    return pl.pallas_call(
        batch_kernel,
        grid_spec=pltpu.PrefetchScalarGridSpec(
            num_scalar_prefetch=1,
            grid=(1,),
            in_specs=[
                whole((rows, C)),
                whole((RIM, C)),
                whole((RIM, C)),
                whole((extent, C)),
                whole((extent, 8)),
                whole((1, C)),
                whole((1, C)),
                whole((1, C)),
                whole((1, C)),
            ],
            out_specs=[
                whole((rows, D)),
                whole((extent, C)),
                whole((extent, C)),
                whole((8, C)),
            ],
            scratch_shapes=[pltpu.VMEM((extent, C), f32), pltpu.VMEM((BLOCK + 16, C), f32)],
        ),
        out_shape=[
            jax.ShapeDtypeStruct((rows, D), bf16),
            jax.ShapeDtypeStruct((extent, C), f32),
            jax.ShapeDtypeStruct((extent, C), f32),
            jax.ShapeDtypeStruct((8, C), f32),
        ],
        compiler_params=params(40),
        cost_estimate=cost(60 * extent * C, 4 << 20),
        name="batch_norm",
    )(widths, z, top, bottom, dact, flags, mean, inv, gain, bias)


def conv_grad_kernel(
    widths, dbn_ref, normed_ref, flags, scale_ref, shift_ref, slope_ref, w_ref, og_ref,
    taps, dy_ref, dm_ref, moved,
):
    step = pl.program_id(0)
    rows = og_ref.shape[0]
    extent = rows + 2 * RIM

    @pl.when(step == 0)
    def _():
        dz = scale_ref[...] * (dbn_ref[...] - shift_ref[...] - normed_ref[...] * slope_ref[...])
        dz = dz.astype(bf16).astype(f32)
        dy_ref[...] = og_ref[...].astype(f32)
        moved[0, 0:8, :] = jnp.zeros((8, C), f32)
        moved[0, 8 + extent :, :] = jnp.zeros((8, C), f32)
        moved[0, 8 : 8 + extent, :] = dz
        moved[1, 8 : 8 + extent, :] = flags[:, 3:4] * moved[0, 9 : 9 + extent, :]
        moved[2, 8 : 8 + extent, :] = flags[:, 2:3] * moved[0, 7 : 7 + extent, :]
        for first, size, block in row_segments(rows, 0):
            width = widths[block]
            here = RIM + first
            for row in range(3):
                for col, slot in enumerate((1, 0, 2)):
                    found = moved[slot, pl.ds(pl.multiple_of(8 + here + (1 - row) * width, 8), size), :]
                    if row == 0:
                        found = flags[here : here + size, 1:2] * found
                    if row == 2:
                        found = flags[here : here + size, 0:1] * found
                    taps[3 * row + col, first : first + size, :] = found.astype(bf16)

    for part in range(3):
        dy_ref[...] += dot_nt(taps[3 * step + part], w_ref[D * part : D * part + D, :])

    @pl.when(step == pl.num_programs(0) - 1)
    def _():
        dm_ref[...] = dy_ref[...].astype(bf16)


def conv_grad(widths, dbn, normed, flags, scale, shift, slope, weight, out_grad):
    rows = out_grad.shape[0]
    extent = rows + 2 * RIM
    return pl.pallas_call(
        conv_grad_kernel,
        grid_spec=pltpu.PrefetchScalarGridSpec(
            num_scalar_prefetch=1,
            grid=(3,),
            in_specs=[
                whole((extent, C)),
                whole((extent, C)),
                whole((extent, 8)),
                whole((1, C)),
                whole((1, C)),
                whole((1, C)),
                pl.BlockSpec((3 * D, C), lambda i, *_: (i, 0)),
                whole((rows, D)),
            ],
            out_specs=[whole((9, rows, C)), whole((rows, D)), whole((rows, D))],
            scratch_shapes=[pltpu.VMEM((3, extent + 16, C), f32)],
        ),
        out_shape=[
            jax.ShapeDtypeStruct((9, rows, C), bf16),
            jax.ShapeDtypeStruct((rows, D), f32),
            jax.ShapeDtypeStruct((rows, D), bf16),
        ],
        compiler_params=params(48),
        cost_estimate=cost(2 * rows * 9 * D * C, 12 << 20),
        name="conv_grad",
    )(widths, dbn, normed, flags, scale, shift, slope, weight, out_grad)


def small_sum_kernel(scatter, blks, seqs, x_ref, out_ref, first, second, sends, receives, sends2, receives2):
    blk, seq = lax.axis_index("blk"), lax.axis_index("seq")
    barrier = pltpu.get_barrier_semaphore()
    for step in range(1, blks):
        pl.semaphore_signal(
            barrier, inc=1, device_id={"blk": lax.rem(blk + step, blks)}, device_id_type=MESH
        )
    for step in range(1, seqs):
        pl.semaphore_signal(
            barrier, inc=1, device_id={"seq": lax.rem(seq + step, seqs)}, device_id_type=MESH
        )
    pl.semaphore_wait(barrier, blks + seqs - 2)
    copies = []
    for step in range(1, blks):
        to = lax.rem(blk + step, blks)
        copy = pltpu.make_async_remote_copy(
            src_ref=x_ref.at[to] if scatter else x_ref.at[0],
            dst_ref=first.at[blk],
            send_sem=sends.at[step],
            recv_sem=receives.at[step],
            device_id={"blk": to},
            device_id_type=MESH,
        )
        copy.start()
        copies.append(copy)
    first[blk] = x_ref[blk] if scatter else x_ref[0]
    for copy in copies:
        copy.wait()
    total = first[0]
    for i in range(1, blks):
        total = total + first[i]
    second[seq] = total
    copies = []
    for step in range(1, seqs):
        copy = pltpu.make_async_remote_copy(
            src_ref=second.at[seq],
            dst_ref=second.at[seq],
            send_sem=sends2.at[step],
            recv_sem=receives2.at[step],
            device_id={"seq": lax.rem(seq + step, seqs)},
            device_id_type=MESH,
        )
        copy.start()
        copies.append(copy)
    for copy in copies:
        copy.wait()
    total = second[0]
    for i in range(1, seqs):
        total = total + second[i]
    out_ref[...] = total


def small_sum(x, scatter, collective_id):
    blks, seqs = lax.axis_size("blk"), lax.axis_size("seq")
    part = x.shape[1:]
    return pl.pallas_call(
        functools.partial(small_sum_kernel, scatter, blks, seqs),
        in_specs=[pl.BlockSpec(memory_space=pltpu.VMEM)],
        out_specs=pl.BlockSpec(memory_space=pltpu.VMEM),
        out_shape=jax.ShapeDtypeStruct(part, f32),
        scratch_shapes=[
            pltpu.VMEM((blks, *part), f32),
            pltpu.VMEM((seqs, *part), f32),
            pltpu.SemaphoreType.DMA((blks,)),
            pltpu.SemaphoreType.DMA((blks,)),
            pltpu.SemaphoreType.DMA((seqs,)),
            pltpu.SemaphoreType.DMA((seqs,)),
        ],
        compiler_params=params(16, collective_id=collective_id, has_side_effects=True),
        name="small_sum",
    )(x)


LAG = 2
PIECE_ROWS = 64


def reduce_kernel(seqs, units, *refs):
    count = 1 + max(unit[0] for unit in units)
    along = [ref.shape[1] == 1 for ref in refs[:count]]
    ins, outs = refs[:count], refs[count:2 * count]
    own, near, side, last, below, above = [refs[(2 + i) * count:(3 + i) * count] for i in range(6)]
    (load_sem, s1, r1, s2, r2, s3, r3, sb, rb, sa, ra, out_sem) = refs[8 * count:]
    blk, seq = lax.axis_index("blk"), lax.axis_index("seq")
    core, x, y = blk % 2, (blk // 2) % 2, blk // 4
    pair, over_x, over_y = (blk + 1 - 2 * core, blk + 2 - 4 * x, blk + 4 - 8 * y)
    root = 1
    barrier = pltpu.get_barrier_semaphore()
    for peer in (pair, over_x, over_y):
        pl.semaphore_signal(barrier, inc=1, device_id={"blk": peer}, device_id_type=MESH)
    @pl.when(seq > 0)
    def _():
        pl.semaphore_signal(barrier, inc=1, device_id={"seq": seq - 1}, device_id_type=MESH)
    @pl.when(seq < seqs - 1)
    def _():
        pl.semaphore_signal(barrier, inc=1, device_id={"seq": seq + 1}, device_id_type=MESH)
    ends = jnp.where(seq > 0, 1, 0) + jnp.where(seq < seqs - 1, 1, 0)
    pl.semaphore_wait(barrier, 3 + ends)

    def send(src, dst, ssem, rsem, peer):
        return pltpu.make_async_remote_copy(src_ref=src, dst_ref=dst, send_sem=ssem, recv_sem=rsem, device_id=peer, device_id_type=MESH)

    def load(u):
        a, part, rows, cols = units[u]
        if along[a]:
            return pltpu.make_async_copy(ins[a].at[part, 0, 0, rows, cols], own[a].at[part, 0, rows, cols], load_sem.at[u])
        return pltpu.make_async_copy(ins[a].at[part, :, core, rows, cols], own[a].at[part, :, rows, cols], load_sem.at[u])
    def first(u):
        a, part, rows, cols = units[u]
        return send(ins[a].at[part, :, 1 - core, rows, cols], near[a].at[part, :, rows, cols], s1.at[u], r1.at[u], {"blk": pair})
    def second(u):
        a, part, rows, cols = units[u]
        if u % 2 == 0:
            src = [own[a].at[part, pl.ds(1 - x + 2 * i, 1), rows, cols] for i in range(2)]
            peer = over_x
        else:
            src = [own[a].at[part, pl.ds(2 * (1 - y) + i, 1), rows, cols] for i in range(2)]
            peer = over_y
        return [send(src[i], side[a].at[part, pl.ds(i,1), rows, cols], s2.at[u, i], r2.at[u, i], {"blk": peer}) for i in range(2)]
    def third(u):
        a, part, rows, cols = units[u]
        if u % 2 == 0:
            src, peer = 2 * (1 - y) + x, over_y
        else:
            src, peer = 2 * y + 1 - x, over_x
        return send(own[a].at[part, src, rows, cols], last[a].at[part, rows, cols], s3.at[u], r3.at[u], {"blk": peer})
    mine = 2 * y + x
    def result(u):
        a, part, rows, cols = units[u]
        return own[a].at[part, 0 if along[a] else mine, rows, cols]
    def down(u):
        a, part, rows, cols = units[u]
        return send(result(u), above[a].at[part, rows, cols], sa.at[u], ra.at[u], {"seq": seq - 1})
    def up(u):
        a, part, rows, cols = units[u]
        return send(result(u), below[a].at[part, rows, cols], sb.at[u], rb.at[u], {"seq": seq + 1})
    def store(u):
        a, part, rows, cols = units[u]
        return pltpu.make_async_copy(result(u), outs[a].at[part, rows, cols], out_sem.at[u])

    def add_to(target, *sources):
        total = target[...].astype(f32)
        for source in sources:
            total = total + source[...].astype(f32)
        target[...] = total.astype(target.dtype)

    def stage_near(u):
        a, part, rows, cols = units[u]
        if along[a]:
            load(u).wait()
            return
        load(u).wait()
        first(u).wait_recv()
        for i in range(4):
            add_to(own[a].at[part, i, rows, cols], near[a].at[part, i, rows, cols])
        for copy in second(u): copy.start()
    def stage_side(u):
        a, part, rows, cols = units[u]
        if along[a]:
            return
        for i, copy in enumerate(second(u)):
            copy.wait_recv()
            keep = 2 * i + x if u % 2 == 0 else 2 * y + i
            add_to(own[a].at[part, keep, rows, cols], side[a].at[part, i, rows, cols])
        third(u).start()
    def stage_last(u):
        a, part, rows, cols = units[u]
        if not along[a]:
            third(u).wait_recv()
            add_to(result(u), last[a].at[part, rows, cols])
        @pl.when(seq < root)
        def _():
            up(u).start()
        @pl.when(seq == seqs - 1)
        def _():
            down(u).start()
    def stage_chain(u, place):
        a, part, rows, cols = units[u]
        @pl.when(seq == place)
        def _():
            down(u).wait_recv()
            add_to(result(u), above[a].at[part, rows, cols])
            down(u).start()
    def stage_root(u):
        a, part, rows, cols = units[u]
        @pl.when(seq == root)
        def _():
            up(u).wait_recv()
            down(u).wait_recv()
            add_to(result(u), below[a].at[part, rows, cols], above[a].at[part, rows, cols])
            up(u).start()
            down(u).start()
            store(u).start()
    def stage_spread(u, place):
        a, part, rows, cols = units[u]
        @pl.when(seq == place)
        def _():
            if place < root:
                down(u).wait_recv()
                up(u).wait_send()
                result(u)[...] = above[a].at[part, rows, cols][...]
            else:
                up(u).wait_recv()
                down(u).wait_send()
                result(u)[...] = below[a].at[part, rows, cols][...]
                if place < seqs - 1: up(u).start()
            store(u).start()

    stages = [(0, stage_near), (LAG, stage_side), (2 * LAG, stage_last)]
    at = 3 * LAG
    for place in range(seqs - 2, root, -1):
        stages.append((at, functools.partial(stage_chain, place=place))); at += LAG
    stages.append((at, stage_root)); at += LAG
    for place in range(root): stages.append((at, functools.partial(stage_spread, place=place)))
    for place in range(root + 1, seqs):
        stages.append((at, functools.partial(stage_spread, place=place))); at += LAG
    for u in range(len(units)):
        load(u).start()
        if not along[units[u][0]]:
            first(u).start()
    far = [u for u in range(len(units)) if not along[units[u][0]]]
    short = [u for u in range(len(units)) if along[units[u][0]]]
    for t in range(max(len(far), len(short)) + stages[-1][0]):
        for lag, stage in reversed(stages):
            if 0 <= t - lag < len(far):
                stage(far[t - lag])
        for lag, stage in reversed(stages[2:]):
            if stage is stage_last and t < len(short):
                stage_near(short[t])
            if 0 <= t - (lag - stages[2][0]) < len(short):
                stage(short[t - (lag - stages[2][0])])
    for u in range(len(units)):
        if not along[units[u][0]]:
            first(u).wait_send()
            for copy in second(u):
                copy.wait_send()
            third(u).wait_send()
        @pl.when(seq == root)
        def _():
            down(u).wait_send()
            up(u).wait_send()
        @pl.when((seq > root) & (seq < seqs - 1))
        def _():
            up(u).wait_send()
        store(u).wait()


def cuts(size, piece):
    return [slice(first, min(size, first + piece)) for first in range(0, size, piece)]


def reduce_grads(arrays, collective_id):
    shapes = [(array.shape[0],) + array.shape[3:] for array in arrays]
    units = []
    for index, (parts, rows, columns) in enumerate(shapes):
        piece = PIECE_ROWS if columns >= D else 3 * PIECE_ROWS
        for part in range(parts):
            for row in cuts(rows, piece):
                for column in cuts(columns, D):
                    units.append((index, part, row, column))
    count, total = len(arrays), len(units)
    scratch = []
    for lead in ((4,), (4,), (2,), (1,), (), ()):
        for shape, array in zip(shapes, arrays):
            places = array.shape[1] * array.shape[2]
            if places == 1 and lead:
                lead_here = (1,)
                shape_here = shape if lead == (4,) and len(scratch) < count else (1, 16, 128)
            else:
                lead_here, shape_here = (() if lead == (1,) else lead), shape
            scratch.append(pltpu.VMEM((shape_here[0],) + lead_here + shape_here[1:], array.dtype))
    for lanes in (1, 1, 1, 2, 2, 1, 1, 1, 1, 1, 1, 1):
        scratch.append(pltpu.SemaphoreType.DMA((total, 2) if lanes == 2 else (total,)))
    anywhere = pl.BlockSpec(memory_space=pl.ANY)
    return pl.pallas_call(
        functools.partial(reduce_kernel, lax.axis_size("seq"), units),
        in_specs=[anywhere] * count,
        out_specs=[anywhere] * count,
        out_shape=[
            jax.ShapeDtypeStruct(shape, array.dtype) for shape, array in zip(shapes, arrays)
        ],
        scratch_shapes=scratch,
        compiler_params=params(60, collective_id=collective_id, has_side_effects=True),
        name="reduce_grads",
    )(*arrays)


def widen_kernel(counts, *refs):
    matrices = len(refs) - len(counts) - 1 >> 1
    sources, vectors = refs[:matrices], refs[matrices]
    targets, pieces = refs[matrices + 1 : 2 * matrices + 1], refs[2 * matrices + 1 :]
    for source, target in zip(sources[:-1], targets[:-1]):
        target[...] = source[0].astype(f32)
    for part in range(3):
        targets[-1][:, D * part : D * part + D] = sources[-1][part].astype(f32)
    row = 0
    for count, piece in zip(counts, pieces):
        for i in range(count):
            piece[:, 128 * i : 128 * i + 128] = vectors[0, row : row + 1, :]
            row += 1


def widen(arrays, vectors, counts):
    steps = 4
    return pl.pallas_call(
        functools.partial(widen_kernel, counts),
        grid=(steps,),
        in_specs=[
            pl.BlockSpec((a.shape[0], a.shape[1] // steps, a.shape[2]), lambda i: (0, i, 0))
            for a in arrays
        ]
        + [whole(vectors.shape)],
        out_specs=[
            pl.BlockSpec((a.shape[1] // steps, a.shape[0] * a.shape[2]), lambda i: (i, 0))
            for a in arrays
        ]
        + [whole((1, 128 * count)) for count in counts],
        out_shape=[
            jax.ShapeDtypeStruct((a.shape[1], a.shape[0] * a.shape[2]), f32) for a in arrays
        ]
        + [jax.ShapeDtypeStruct((1, 128 * count), f32) for count in counts],
        compiler_params=params(62),
        name="widen",
    )(*arrays, vectors)


def shifted(value, axis, steps):
    count = lax.axis_size(axis)
    leading, last = (max(0, -steps), min(count, count - steps))
    return lax.ppermute(value, axis, [(source, source + steps) for source in range(leading, last)])


def near_blocks(sides_row, keys_own, values_own):
    rows = keys_own.shape[0]
    place, length = lax.axis_index("blk"), rows * lax.axis_size("blk")
    centre = jnp.arange(rows, dtype=jnp.int32)
    segment = image_info(sides_row, place * rows + centre)[0]
    found = []
    for offset in range(-REACH, REACH + 1):
        keys, values = (keys_own, values_own) if offset == 0 else shifted((keys_own, values_own), "blk", -offset)
        positions = (place + offset) * rows + centre
        inside = (positions >= 0) & (positions < length)
        allowed = (segment[:, None] == image_info(sides_row, positions)[0][None, :]) & inside[None, :]
        found.append((offset, keys.reshape(rows, HEADS, HEAD), values.reshape(rows, HEADS, HEAD), allowed))
    return found


def near_scores(queries, keys, allowed):
    scores = jnp.einsum("qhd,khd->hqk", queries, keys, preferred_element_type=f32)
    return jnp.where(allowed[None], scores, masked_score)


def near_attention(near, queries):
    rows = queries.shape[0]
    peak = jnp.full((HEADS, rows), masked_score, f32)
    total = jnp.zeros((HEADS, rows), f32)
    for _, keys, _, allowed in near:
        scores = near_scores(queries, keys, allowed)
        new_peak = jnp.maximum(peak, jnp.max(scores, axis=-1))
        grown = jnp.where(allowed[None], jnp.exp2(scores - new_peak[..., None]), 0.0)
        total = total * jnp.exp2(peak - new_peak) + jnp.sum(grown, axis=-1)
        peak = new_peak
    lse = peak + jnp.log2(total)
    out = jnp.zeros((rows, HEADS, HEAD), f32)
    for _, keys, values, allowed in near:
        scores = near_scores(queries, keys, allowed)
        weights = jnp.where(allowed[None], jnp.exp2(scores - lse[..., None]), 0.0).astype(bf16)
        out = out + jnp.einsum("hqk,khd->qhd", weights, values, preferred_element_type=f32)
    return out.reshape(rows, D).astype(bf16), lse


def near_attention_grad(near, queries, lse, out, grad):
    rows = queries.shape[0]
    grad_heads = grad.reshape(rows, HEADS, HEAD)
    delta = jnp.sum((grad.astype(f32) * out.astype(f32)).reshape(rows, HEADS, HEAD), axis=-1).T
    dq = jnp.zeros((rows, HEADS, HEAD), f32)
    dk = jnp.zeros((rows, HEADS, HEAD), f32)
    dv = jnp.zeros((rows, HEADS, HEAD), f32)
    for offset, keys, values, allowed in near:
        scores = near_scores(queries, keys, allowed)
        weights = jnp.where(allowed[None], jnp.exp2(scores - lse[..., None]), 0.0)
        value_grad = jnp.einsum("qhd,khd->hqk", grad_heads, values, preferred_element_type=f32)
        score_grad = (weights * (value_grad - delta[..., None])).astype(bf16)
        dq = dq + jnp.einsum("hqk,khd->qhd", score_grad, keys, preferred_element_type=f32)
        dk_part = jnp.einsum("hqk,qhd->khd", score_grad, queries, preferred_element_type=f32)
        dv_part = jnp.einsum(
            "hqk,qhd->khd", weights.astype(bf16), grad_heads, preferred_element_type=f32
        )
        if offset:
            dk_part, dv_part = shifted((dk_part.astype(bf16), dv_part.astype(bf16)), "blk", offset)
        dk = dk + dk_part.astype(f32)
        dv = dv + dv_part.astype(f32)
    dq = dq.reshape(rows, D).astype(bf16) * jnp.asarray(HEAD**-0.5, bf16)
    dk = (dk * (1.0 / LOG2E)).reshape(rows, D).astype(bf16)
    return dq, dk, dv.reshape(rows, D).astype(bf16)


def in_groups(*parts):
    rows = parts[0].shape[0]
    stacked = jnp.stack([part.reshape(rows, D // 128, 128) for part in parts], axis=2)
    return stacked.transpose(1, 0, 2, 3).reshape(D // 128, rows, 128 * len(parts))


def from_groups(groups, part):
    picked = groups[:, :, 128 * part : 128 * part + 128]
    return picked.transpose(1, 0, 2).reshape(groups.shape[1], D)


def rims(rows_own, width):
    count = lax.axis_size("blk")
    top = lax.ppermute(rows_own[-width:], "blk", [(i, i + 1) for i in range(count - 1)])
    bottom = lax.ppermute(rows_own[:width], "blk", [(i + 1, i) for i in range(count - 1)])
    return top, bottom


def line(vector):
    return vector.reshape(1, -1)


def shards(
    tokens,
    image_sides,
    ln1_gain,
    ln1_bias,
    qkv_weight,
    qv_bias,
    proj_weight,
    proj_bias,
    ln2_gain,
    ln2_bias,
    up_weight,
    up_bias,
    down_weight,
    down_bias,
    conv_weight,
    bn_gain,
    bn_bias,
    out_grad,
    pup_grad,
):
    x = tokens[0]
    sides_row = image_sides[0]
    rows = x.shape[0]
    blks, seqs = lax.axis_size("blk"), lax.axis_size("seq")
    place = lax.axis_index("blk")
    length = rows * blks
    samples = length * seqs
    by_heads = HEADS // 2 == blks

    block_starts = jnp.arange(length // BLOCK, dtype=jnp.int32) * BLOCK
    _, block_width, _, _, block_begin = image_info(sides_row, block_starts)
    starts = (block_begin // BLOCK).astype(jnp.int32)
    counts = (block_width * block_width // BLOCK).astype(jnp.int32)
    own_blocks = rows // BLOCK
    widths = lax.dynamic_slice_in_dim(block_width, place * own_blocks, own_blocks)
    wide_positions = place * rows + jnp.arange(-WIDE_RIM, rows + WIDE_RIM, dtype=jnp.int32)
    wide_flags = edge_flags(sides_row, wide_positions)
    flags = wide_flags[WIDE_RIM - RIM : WIDE_RIM + rows + RIM]

    g = pup_grad[0]
    g_top, g_bottom = rims(g, WIDE_RIM)
    dact = spread(widths, g, g_top, g_bottom, wide_flags)

    h1, qkv_groups = project_qkv(x, line(ln1_gain), line(ln1_bias), qkv_weight, line(qv_bias))
    if by_heads:
        qkv = lax.all_to_all(qkv_groups, "blk", 0, 0, tiled=True).reshape(length, 384)
        o_heads, lse = attention(starts, counts, qkv)
        o_groups = lax.all_to_all(o_heads.reshape(blks, rows, 128), "blk", 0, 0, tiled=True)
    else:
        queries = from_groups(qkv_groups, 0).reshape(rows, HEADS, HEAD)
        near = near_blocks(sides_row, from_groups(qkv_groups, 1), from_groups(qkv_groups, 2))
        attended, lse = near_attention(near, queries)
        o_groups = in_groups(attended)
    x1, h2, act, slope, block_low = mlp(
        o_groups, x, proj_weight, line(proj_bias), line(ln2_gain), line(ln2_bias),
        up_weight, line(up_bias), down_weight, line(down_bias),
    )
    top, bottom = rims(block_low, RIM)
    z, z_sums = conv(widths, block_low, top, bottom, flags, conv_weight)
    z_top, z_bottom = rims(z, RIM)
    z_sums = small_sum(z_sums[None], False, 1)
    mean = z_sums[0:1] / samples
    inv = lax.rsqrt(z_sums[1:2] / samples - mean * mean + batch_eps)
    pup_out, normed, dbn, bn_sums = batch(
        widths, z, z_top, z_bottom, dact, flags, mean, inv, line(bn_gain), line(bn_bias)
    )
    bn_sums = small_sum(bn_sums[None], False, 2)

    taps, dy, dm = conv_grad(
        widths, dbn, normed, flags, inv * line(bn_gain), bn_sums[0:1] / samples, bn_sums[1:2] / samples,
        conv_weight, out_grad[0],
    )
    down_grad = down_weight_grad_of(act, dm)
    conv_weight_grad = conv_weight_grad_of(block_low, taps)
    du, up_bias_grad, dx1, da, do_groups, mlp_sums = mlp_grad(
        dy, dm, slope, down_weight, up_weight, x1, line(ln2_gain), proj_weight
    )
    up_grad, proj_grad, do_moved = late_weights(
        h2, du, o_groups, da, do_groups, blks if by_heads else 0, 5
    )
    if by_heads:
        dqkv = attention_grad(starts, counts, qkv, do_moved.reshape(length, 128), o_heads, lse)
        dqkv_groups = lax.all_to_all(dqkv.reshape(blks, rows, 384), "blk", 0, 0, tiled=True)
    else:
        grads = near_attention_grad(near, queries, lse, attended, from_groups(do_groups, 0))
        dqkv_groups = in_groups(*grads)
    qkv_weight_grad, dqb, dvb, tokens_grad, qkv_sums = qkv_grad(
        dqkv_groups, qkv_weight, h1, dx1, x, line(ln1_gain)
    )

    piece = D // blks
    cuts_of = [piece] * 6 + [2 * piece, 4 * piece]
    vectors = [qkv_sums[0], qkv_sums[1], mlp_sums[0], mlp_sums[1], mlp_sums[2], mlp_sums[3]]
    vectors += [jnp.concatenate([dqb[0], dvb[0]]), up_bias_grad[0]]
    stacked = jnp.concatenate([vector.reshape(blks, -1) for vector in vectors], axis=1)
    if blks == 8:
        def by_place(array, parts=1):
            return array.reshape(parts, 4, 2, -1, array.shape[-1])

        flat = jnp.pad(stacked, ((0, 0), (0, 16 * 128 - stacked.shape[1])))
        down_grad, up_grad, conv_weight_grad, proj_grad, qkv_weight_grad, summed = reduce_grads(
            [
                by_place(down_grad),
                by_place(up_grad),
                by_place(conv_weight_grad),
                by_place(proj_grad),
                by_place(qkv_weight_grad, 3),
                by_place(flat.reshape(8, 16, 128)),
            ],
            3,
        )
        down_grad, up_grad, conv_weight_grad, proj_grad, qkv_weight_grad, *small = widen(
            [down_grad, up_grad, conv_weight_grad, proj_grad, qkv_weight_grad],
            summed,
            [cut // 128 for cut in cuts_of],
        )
        small = [vector[0] for vector in small]
    else:

        def scattered(grad):
            part = lax.psum_scatter(grad, "blk", scatter_dimension=0, tiled=True)
            return lax.psum(part, "seq").astype(f32)

        down_grad, up_grad, proj_grad, conv_weight_grad = [
            scattered(grad) for grad in (down_grad, up_grad, proj_grad, conv_weight_grad)
        ]
        qkv_weight_grad = scattered(qkv_weight_grad.transpose(1, 0, 2).reshape(D, 3 * D))
        summed = small_sum(stacked[:, None, :], True, 4)[0]
        ends = [sum(cuts_of[: i + 1]) for i in range(len(cuts_of))]
        small = [summed[end - cut : end] for cut, end in zip(cuts_of, ends)]
    ln1_g, ln1_b, proj_b, ln2_g, ln2_b, down_b, qv_b, up_b = small
    channel_piece = C // blks
    gain_slice = lax.dynamic_slice_in_dim(bn_sums[1], place * channel_piece, channel_piece)
    bias_slice = lax.dynamic_slice_in_dim(bn_sums[0], place * channel_piece, channel_piece)
    return (
        block_low[None],
        pup_out[None],
        tokens_grad[None],
        ln1_g,
        ln1_b,
        qkv_weight_grad,
        qv_b,
        proj_grad,
        proj_b,
        ln2_g,
        ln2_b,
        up_grad,
        up_b,
        down_grad,
        down_b,
        conv_weight_grad,
        gain_slice,
        bias_slice,
    )


def solution(mesh):
    replicated = P()
    packed = P("seq", "blk", None)
    placed = (packed, P("seq", None)) + (replicated,) * 15 + (packed, packed)
    rows, vector = P("blk", None), P("blk")
    return jax.shard_map(
        shards,
        mesh=mesh,
        in_specs=placed,
        out_specs=(
            packed, packed, packed, vector, vector, rows, vector, rows, vector, vector, vector, rows,
            vector, rows, vector, rows, vector, vector,
        ),
        check_vma=False,
    )
```

```python
import functools

import jax
import jax.numpy as jnp
from jax import lax
from jax.experimental import pallas as pl
from jax.experimental.pallas import tpu as pltpu
from jax.sharding import PartitionSpec as P

D = 1024
HEADS = 16
HEAD = 64
FF = 4096
C = 256
REACH = 4
UNIT = 16
BLOCK = UNIT * UNIT
IMAGE_BLOCKS = (1, 4, 9)
RIM = 64
WIDE_RIM = 128
LOG2E = 1.4426950408889634
MESH = pl.DeviceIdType.MESH

norm_eps = 1e-06
batch_eps = 1e-05
masked_score = -1e30
f32 = jnp.float32
bf16 = jnp.bfloat16

NT = (((1,), (1,)), ((), ()))
TN = (((0,), (0,)), ((), ()))


def dot(left, right):
    return jnp.dot(left, right, preferred_element_type=f32)


def dot_nt(left, right):
    return lax.dot_general(left, right, NT, preferred_element_type=f32)


def dot_tn(left, right):
    return lax.dot_general(left, right, TN, preferred_element_type=f32)


def whole(shape):
    zeros = (0,) * len(shape)
    return pl.BlockSpec(shape, lambda *_: zeros)


def params(megabytes, **more):
    return pltpu.CompilerParams(vmem_limit_bytes=megabytes << 20, **more)


def cost(flops, moved, transcendentals=0):
    return pl.CostEstimate(
        flops=int(flops), bytes_accessed=int(moved), transcendentals=int(transcendentals)
    )


def place_copies(blks, source, target, sends, receives):
    me = lax.axis_index("blk")
    copies = []
    for step in range(1, blks):
        to = lax.rem(me + step, blks)
        copies.append(
            pltpu.make_async_remote_copy(
                src_ref=source.at[to],
                dst_ref=target.at[me],
                send_sem=sends.at[step],
                recv_sem=receives.at[step],
                device_id={"blk": to},
                device_id_type=MESH,
            )
        )
    return copies


def greet(blks, seqs=0):
    me, seq = lax.axis_index("blk"), lax.axis_index("seq")
    barrier = pltpu.get_barrier_semaphore()
    for step in range(1, blks):
        pl.semaphore_signal(
            barrier, inc=1, device_id={"blk": lax.rem(me + step, blks)}, device_id_type=MESH
        )
    ends = 0
    if seqs:

        @pl.when(seq > 0)
        def _():
            pl.semaphore_signal(barrier, inc=1, device_id={"seq": seq - 1}, device_id_type=MESH)

        @pl.when(seq < seqs - 1)
        def _():
            pl.semaphore_signal(barrier, inc=1, device_id={"seq": seq + 1}, device_id_type=MESH)

        ends = jnp.where(seq > 0, 1, 0) + jnp.where(seq < seqs - 1, 1, 0)
    pl.semaphore_wait(barrier, blks - 1 + ends)


def exchange_start(blks, source, target, sends, receives, own_sem):
    me = lax.axis_index("blk")
    for copy in place_copies(blks, source, target, sends, receives):
        copy.start()
    pltpu.make_async_copy(source.at[me], target.at[me], own_sem).start()


def exchange_wait(blks, source, target, sends, receives, own_sem):
    me = lax.axis_index("blk")
    for copy in place_copies(blks, source, target, sends, receives):
        copy.wait()
    pltpu.make_async_copy(source.at[me], target.at[me], own_sem).wait()


def image_info(image_sides, positions):
    image_areas = image_sides * image_sides
    image_ends = jnp.cumsum(image_areas).astype(jnp.int32)
    image_starts = (image_ends - image_areas).astype(jnp.int32)
    segment = jnp.sum((image_ends[None, :] <= positions[:, None]).astype(jnp.int32), axis=1).astype(
        jnp.int32
    )
    picked = segment[:, None] == jnp.arange(image_sides.shape[0], dtype=jnp.int32)[None, :]
    image_width = jnp.sum(jnp.where(picked, image_sides[None, :], 0), axis=1).astype(jnp.int32)
    image_width = jnp.maximum(image_width, 1).astype(jnp.int32)
    image_begin = jnp.sum(jnp.where(picked, image_starts[None, :], 0), axis=1).astype(jnp.int32)
    offset = (positions - image_begin).astype(jnp.int32)
    row_index = (offset // image_width).astype(jnp.int32)
    col_index = (offset - row_index * image_width).astype(jnp.int32)
    return (segment, image_width, row_index, col_index, image_begin)


def edge_flags(image_sides, positions):
    _, width, row, col, _ = image_info(image_sides, positions)
    flags = jnp.stack([row > 0, row < width - 1, col > 0, col < width - 1], axis=1)
    return jnp.concatenate([flags, flags], axis=1).astype(f32)


def layer_stats(values):
    mean = jnp.mean(values, axis=-1, keepdims=True)
    centred = values - mean
    scale_inv = lax.rsqrt(jnp.mean(centred * centred, axis=-1, keepdims=True) + norm_eps)
    return centred * scale_inv, scale_inv


def layer_backward(grad_out, normed, scale_inv, gain):
    scaled = grad_out * gain
    inner = (
        scaled
        - jnp.mean(scaled, axis=-1, keepdims=True)
        - normed * jnp.mean(scaled * normed, axis=-1, keepdims=True)
    )
    return scale_inv * inner


def column_sums(values):
    return jnp.sum(values, axis=0, keepdims=True)


def gelu_parts(values):
    cumulative = 0.5 + 0.5 * lax.erf(values * 0.7071067811865476)
    weighted = values * (0.3989422804014327 * jnp.exp(values * values * -0.5))
    return cumulative, weighted


def qkv_kernel(x_ref, gain_ref, bias_ref, wq_ref, wk_ref, wv_ref, bq_ref, bv_ref, h_ref, out_ref):
    @pl.when(pl.program_id(0) == 0)
    def _():
        normed, _ = layer_stats(x_ref[...].astype(f32))
        h_ref[...] = (normed * gain_ref[...] + bias_ref[...]).astype(bf16)

    hidden = h_ref[...]
    query = ((dot(hidden, wq_ref[...]) + bq_ref[...]) * (HEAD**-0.5 * LOG2E)).astype(bf16)
    key = dot(hidden, wk_ref[...]).astype(bf16)
    value = (dot(hidden, wv_ref[...]) + bv_ref[...]).astype(bf16)
    for part in range(2):
        lanes = slice(128 * part, 128 * part + 128)
        out_ref[part, :, 0:128] = query[:, lanes]
        out_ref[part, :, 128:256] = key[:, lanes]
        out_ref[part, :, 256:384] = value[:, lanes]


def project_qkv(x, gain, bias, weight, qv_bias):
    rows = x.shape[0]
    groups = D // 128
    return pl.pallas_call(
        qkv_kernel,
        grid=(groups // 2,),
        in_specs=[
            whole((rows, D)),
            whole((1, D)),
            whole((1, D)),
            pl.BlockSpec((D, 256), lambda i: (0, i)),
            pl.BlockSpec((D, 256), lambda i: (0, 4 + i)),
            pl.BlockSpec((D, 256), lambda i: (0, 8 + i)),
            pl.BlockSpec((1, 256), lambda i: (0, i)),
            pl.BlockSpec((1, 256), lambda i: (0, 4 + i)),
        ],
        out_specs=[whole((rows, D)), pl.BlockSpec((2, rows, 384), lambda i: (i, 0, 0))],
        out_shape=[
            jax.ShapeDtypeStruct((rows, D), bf16),
            jax.ShapeDtypeStruct((groups, rows, 384), bf16),
        ],
        compiler_params=params(40),
        cost_estimate=cost(2 * rows * D * 3 * D, 12 << 20),
        name="norm_qkv",
    )(x, gain, bias, weight, weight, weight, qv_bias, qv_bias)


def attention_kernel(starts, counts, qkv, o_ref, lse_ref, value_t):
    step = pl.program_id(0)

    @pl.when(step == 0)
    def _():
        value_t[...] = qkv[:, 256:384].T

    own = pl.ds(pl.multiple_of(step * BLOCK, BLOCK), BLOCK)
    query = qkv[own, 0:128]
    lane = lax.broadcasted_iota(jnp.int32, (BLOCK, 128), 1)
    zero = jnp.zeros_like(query)
    queries = [jnp.where(lane < HEAD, query, zero), jnp.where(lane >= HEAD, query, zero)]
    first, count = starts[step], counts[step]
    for blocks in IMAGE_BLOCKS:

        @pl.when(count == blocks)
        def _(blocks=blocks):
            image = pl.ds(pl.multiple_of(first * BLOCK, BLOCK), blocks * BLOCK)
            keys = qkv[image, 128:256]
            scores = [dot_nt(keys, part) for part in queries]
            outs, logs = [], []
            for head in range(2):
                peak = jnp.max(scores[head], axis=0, keepdims=True)
                grown = jnp.exp2(scores[head] - peak)
                total = jnp.sum(grown, axis=0, keepdims=True)
                rows = slice(HEAD * head, HEAD * head + HEAD)
                outs.append(dot(value_t[rows, image], grown.astype(bf16)) * (1.0 / total))
                logs.append(peak + jnp.log2(total))
            o_ref[...] = jnp.concatenate(outs, axis=0).T.astype(bf16)
            lse_ref[...] = jnp.concatenate(logs + [jnp.zeros((6, BLOCK), f32)], axis=0)


def attention(starts, counts, qkv):
    length = qkv.shape[0]
    pairs = 100 * 2 * BLOCK * BLOCK
    return pl.pallas_call(
        attention_kernel,
        grid_spec=pltpu.PrefetchScalarGridSpec(
            num_scalar_prefetch=2,
            grid=(length // BLOCK,),
            in_specs=[whole((length, 384))],
            out_specs=[
                pl.BlockSpec((BLOCK, 128), lambda i, *_: (i, 0)),
                pl.BlockSpec((8, BLOCK), lambda i, *_: (0, i)),
            ],
            scratch_shapes=[pltpu.VMEM((128, length), bf16)],
        ),
        out_shape=[
            jax.ShapeDtypeStruct((length, 128), bf16),
            jax.ShapeDtypeStruct((8, length), f32),
        ],
        compiler_params=params(40),
        cost_estimate=cost(4 * HEAD * pairs, 5 << 20, pairs),
        name="attention",
    )(starts, counts, qkv)


def attention_grad_kernel(
    starts, counts, qkv, do_ref, o_ref, lse, out_ref, query_m, do_m, key_t, dq_t, delta
):
    step = pl.program_id(0)
    length = do_ref.shape[0]
    lane = lax.broadcasted_iota(jnp.int32, (BLOCK, 128), 1)
    low = lane < HEAD

    @pl.when(step == 0)
    def _():
        key_t[...] = qkv[:, 128:256].T
        dq_t[...] = jnp.zeros_like(dq_t)

        def prepare(i, _):
            rows = pl.ds(pl.multiple_of(i * BLOCK, BLOCK), BLOCK)
            grad = do_ref[rows, :]
            product = (grad.astype(f32) * o_ref[rows, :].astype(f32)).T
            delta[0:1, rows] = jnp.sum(product[:HEAD], axis=0, keepdims=True)
            delta[1:2, rows] = jnp.sum(product[HEAD:], axis=0, keepdims=True)
            query = qkv[rows, 0:128]
            zero = jnp.zeros_like(query)
            query_m[0, rows, :] = jnp.where(low, query, zero)
            query_m[1, rows, :] = jnp.where(low, zero, query)
            do_m[0, rows, :] = jnp.where(low, grad, zero)
            do_m[1, rows, :] = jnp.where(low, zero, grad)
            return 0

        lax.fori_loop(0, length // BLOCK, prepare, 0)

    own = pl.ds(pl.multiple_of(step * BLOCK, BLOCK), BLOCK)
    key = qkv[own, 128:256]
    value = qkv[own, 256:384]
    first, count = starts[step], counts[step]
    for blocks in IMAGE_BLOCKS:

        @pl.when(count == blocks)
        def _(blocks=blocks):
            image = pl.ds(pl.multiple_of(first * BLOCK, BLOCK), blocks * BLOCK)
            dk = dv = None
            for head in range(2):
                rows = slice(HEAD * head, HEAD * head + HEAD)
                query, grad = query_m[head, image, :], do_m[head, image, :]
                scores = dot_nt(key, query)
                value_grad = dot_nt(value, grad)
                weights = jnp.exp2(scores - lse[head : head + 1, image])
                score_grad = (weights * (value_grad - delta[head : head + 1, image])).astype(bf16)
                dv_part = dot(weights.astype(bf16), grad)
                dk_part = dot(score_grad, query)
                dv = dv_part if dv is None else dv + dv_part
                dk = dk_part if dk is None else dk + dk_part
                dq_t[rows, image] += dot(key_t[rows, own], score_grad)
            out_ref[own, 128:256] = (dk * (1.0 / LOG2E)).astype(bf16)
            out_ref[own, 256:384] = dv.astype(bf16)

    @pl.when(step == pl.num_programs(0) - 1)
    def _():
        def finish(i, _):
            rows = pl.ds(pl.multiple_of(i * BLOCK, BLOCK), BLOCK)
            out_ref[rows, 0:128] = dq_t[:, rows].T.astype(bf16) * jnp.asarray(HEAD**-0.5, bf16)
            return 0

        lax.fori_loop(0, length // BLOCK, finish, 0)


def attention_grad(starts, counts, qkv, do, o, lse):
    length = qkv.shape[0]
    pairs = 100 * 2 * BLOCK * BLOCK
    return pl.pallas_call(
        attention_grad_kernel,
        grid_spec=pltpu.PrefetchScalarGridSpec(
            num_scalar_prefetch=2,
            grid=(length // BLOCK,),
            in_specs=[
                whole((length, 384)),
                whole((length, 128)),
                whole((length, 128)),
                whole((8, length)),
            ],
            out_specs=whole((length, 384)),
            scratch_shapes=[
                pltpu.VMEM((2, length, 128), bf16),
                pltpu.VMEM((2, length, 128), bf16),
                pltpu.VMEM((128, length), bf16),
                pltpu.VMEM((128, length), f32),
                pltpu.VMEM((8, length), f32),
            ],
        ),
        out_shape=jax.ShapeDtypeStruct((length, 384), bf16),
        compiler_params=params(56),
        cost_estimate=cost(10 * HEAD * pairs, 12 << 20, pairs),
        name="attention_grad",
    )(starts, counts, qkv, do, o, lse)


FF_TILE = 512


def mlp_kernel(
    o_ref, x_ref, wp_ref, pb_ref, gain_ref, bias_ref, wu_ref, ub_ref, wd_ref, db_ref,
    x1_ref, h_ref, act_ref, slope_ref, out_ref, total,
):
    step = pl.program_id(0)

    @pl.when(step == 0)
    def _():
        attended = jnp.concatenate([o_ref[i] for i in range(o_ref.shape[0])], axis=1)
        x1 = x_ref[...].astype(f32) + dot(attended, wp_ref[...]) + pb_ref[...]
        x1_ref[...] = x1
        normed, _ = layer_stats(x1)
        h_ref[...] = (normed * gain_ref[...] + bias_ref[...]).astype(bf16)
        total[...] = x1 + db_ref[...]

    raised = dot(h_ref[...], wu_ref[...]) + ub_ref[...]
    cumulative, weighted = gelu_parts(raised)
    act = (raised * cumulative).astype(bf16)
    act_ref[...] = act
    slope_ref[...] = (cumulative + weighted).astype(bf16)
    total[...] += dot(act, wd_ref[...])

    @pl.when(step == pl.num_programs(0) - 1)
    def _():
        out_ref[...] = total[...].astype(bf16)


def mlp(o, x, wp, pb, gain, bias, wu, ub, wd, db):
    rows = x.shape[0]
    groups = o.shape[0]
    tile = FF_TILE
    return pl.pallas_call(
        mlp_kernel,
        grid=(FF // tile,),
        in_specs=[
            whole((groups, rows, 128)),
            whole((rows, D)),
            whole((D, D)),
            whole((1, D)),
            whole((1, D)),
            whole((1, D)),
            pl.BlockSpec((D, tile), lambda i: (0, i)),
            pl.BlockSpec((1, tile), lambda i: (0, i)),
            pl.BlockSpec((tile, D), lambda i: (i, 0)),
            whole((1, D)),
        ],
        out_specs=[
            whole((rows, D)),
            whole((rows, D)),
            pl.BlockSpec((rows, tile), lambda i: (0, i)),
            pl.BlockSpec((rows, tile), lambda i: (0, i)),
            whole((rows, D)),
        ],
        out_shape=[
            jax.ShapeDtypeStruct((rows, D), f32),
            jax.ShapeDtypeStruct((rows, D), bf16),
            jax.ShapeDtypeStruct((rows, FF), bf16),
            jax.ShapeDtypeStruct((rows, FF), bf16),
            jax.ShapeDtypeStruct((rows, D), bf16),
        ],
        scratch_shapes=[pltpu.VMEM((rows, D), f32)],
        compiler_params=params(56),
        cost_estimate=cost(2 * rows * D * (D + 2 * FF), 34 << 20, rows * FF),
        name="proj_norm_mlp",
    )(o, x, wp, pb, gain, bias, wu, ub, wd, db)


def mlp_grad_kernel(
    dy_ref, dm_ref, slope_ref, wd_ref, wu_ref, x1_ref, gain_ref, wp_ref,
    du_ref, dub_ref, dx1_ref, da_ref, do_ref, sums_ref, total,
):
    step = pl.program_id(0)

    @pl.when(step == 0)
    def _():
        total[...] = jnp.zeros_like(total)

    act_grad = dot_nt(dm_ref[...], wd_ref[...])
    raised_low = (act_grad * slope_ref[...].astype(f32)).astype(bf16)
    du_ref[...] = raised_low
    dub_ref[...] = column_sums(raised_low.astype(f32))
    total[...] += dot_nt(raised_low, wu_ref[...])

    @pl.when(step == pl.num_programs(0) - 1)
    def _():
        grad = total[...]
        normed, scale_inv = layer_stats(x1_ref[...])
        dx1 = dy_ref[...] + layer_backward(grad, normed, scale_inv, gain_ref[...])
        dx1_ref[...] = dx1
        low = dx1.astype(bf16)
        da_ref[...] = low
        sums_ref[0:1, :] = column_sums(low.astype(f32))
        sums_ref[1:2, :] = column_sums(grad * normed)
        sums_ref[2:3, :] = column_sums(grad)
        sums_ref[3:4, :] = column_sums(dm_ref[...].astype(f32))
        sums_ref[4:8, :] = jnp.zeros((4, D), f32)
        attended_grad = dot_nt(low, wp_ref[...]).astype(bf16)
        for i in range(do_ref.shape[0]):
            do_ref[i] = attended_grad[:, 128 * i : 128 * i + 128]


def mlp_grad(dy, dm, slope, wd, wu, x1, gain, wp):
    rows = dy.shape[0]
    groups = D // 128
    tile = FF_TILE
    return pl.pallas_call(
        mlp_grad_kernel,
        grid=(FF // tile,),
        in_specs=[
            whole((rows, D)),
            whole((rows, D)),
            pl.BlockSpec((rows, tile), lambda i: (0, i)),
            pl.BlockSpec((tile, D), lambda i: (i, 0)),
            pl.BlockSpec((D, tile), lambda i: (0, i)),
            whole((rows, D)),
            whole((1, D)),
            whole((D, D)),
        ],
        out_specs=[
            pl.BlockSpec((rows, tile), lambda i: (0, i)),
            pl.BlockSpec((1, tile), lambda i: (0, i)),
            whole((rows, D)),
            whole((rows, D)),
            whole((groups, rows, 128)),
            whole((8, D)),
        ],
        out_shape=[
            jax.ShapeDtypeStruct((rows, FF), bf16),
            jax.ShapeDtypeStruct((1, FF), f32),
            jax.ShapeDtypeStruct((rows, D), f32),
            jax.ShapeDtypeStruct((rows, D), bf16),
            jax.ShapeDtypeStruct((groups, rows, 128), bf16),
            jax.ShapeDtypeStruct((8, D), f32),
        ],
        scratch_shapes=[pltpu.VMEM((rows, D), f32)],
        compiler_params=params(56),
        cost_estimate=cost(2 * rows * D * (D + 2 * FF), 34 << 20),
        name="mlp_norm_proj_grad",
    )(dy, dm, slope, wd, wu, x1, gain, wp)


def down_weight_kernel(act_ref, dm_ref, dwd_ref):
    dwd_ref[...] = dot_tn(act_ref[...], dm_ref[...]).astype(bf16)


def down_weight_grad_of(act, dm):
    rows = dm.shape[0]
    tile = FF_TILE
    return pl.pallas_call(
        down_weight_kernel,
        grid=(FF // tile,),
        in_specs=[pl.BlockSpec((rows, tile), lambda i: (0, i)), whole((rows, D))],
        out_specs=pl.BlockSpec((tile, D), lambda i: (i, 0)),
        out_shape=jax.ShapeDtypeStruct((FF, D), bf16),
        compiler_params=params(32),
        cost_estimate=cost(2 * rows * D * FF, 13 << 20),
        name="down_weight_grad",
    )(act, dm)


def conv_weight_kernel(x_ref, taps_ref, dw_ref, x_t):
    @pl.when(pl.program_id(0) == 0)
    def _():
        x_t[...] = x_ref[...].T

    for tap in range(3):
        dw_ref[D * tap : D * tap + D, :] = dot(x_t[...], taps_ref[tap]).astype(bf16)


def conv_weight_grad_of(x, taps):
    rows = x.shape[0]
    return pl.pallas_call(
        conv_weight_kernel,
        grid=(3,),
        in_specs=[whole((rows, D)), pl.BlockSpec((3, rows, C), lambda i: (i, 0, 0))],
        out_specs=pl.BlockSpec((3 * D, C), lambda i: (i, 0)),
        out_shape=jax.ShapeDtypeStruct((9 * D, C), bf16),
        scratch_shapes=[pltpu.VMEM((D, rows), bf16)],
        compiler_params=params(32),
        cost_estimate=cost(2 * rows * D * 9 * C, 9 << 20),
        name="conv_weight_grad",
    )(x, taps)


def exchange_semaphores(blks):
    count = max(blks, 1)
    return [
        pltpu.SemaphoreType.DMA((count,)),
        pltpu.SemaphoreType.DMA((count,)),
        pltpu.SemaphoreType.DMA,
    ]


def exchange_params(blks, megabytes, collective_id):
    if blks:
        return params(megabytes, collective_id=collective_id, has_side_effects=True)
    return params(megabytes)


def late_weights_kernel(h_ref, du_ref, o_ref, da_ref, dwu_ref, dwp_ref, h_t):
    @pl.when(pl.program_id(0) == 0)
    def _():
        h_t[...] = h_ref[...].T
        attended = jnp.concatenate([o_ref[i] for i in range(o_ref.shape[0])], axis=1)
        dwp_ref[...] = dot_tn(attended, da_ref[...]).astype(bf16)

    dwu_ref[...] = dot(h_t[...], du_ref[...]).astype(bf16)


def late_weights(h, du, o, da):
    rows = h.shape[0]
    groups = D // 128
    tile = FF_TILE
    return pl.pallas_call(
        late_weights_kernel,
        grid=(FF // tile,),
        in_specs=[
            whole((rows, D)),
            pl.BlockSpec((rows, tile), lambda i: (0, i)),
            whole((groups, rows, 128)),
            whole((rows, D)),
        ],
        out_specs=[pl.BlockSpec((D, tile), lambda i: (0, i)), whole((D, D))],
        out_shape=[jax.ShapeDtypeStruct((D, FF), bf16), jax.ShapeDtypeStruct((D, D), bf16)],
        scratch_shapes=[pltpu.VMEM((D, rows), bf16)],
        compiler_params=params(40),
        cost_estimate=cost(2 * rows * D * (FF + D), 18 << 20),
        name="up_proj_weight_grads",
    )(h, du, o, da)


def weights_kernel(
    blks, act_ref, dm_ref, h_ref, du_ref, x_ref, taps_ref, o_ref, da_ref, sent,
    dw_ref, dwp_ref, moved, down_keep, down_send, up_keep, up_send,
    down, up, down_near, up_near, h_t, x_t, ex_send, ex_recv, ex_own, ds, dr, us, ur, do_sem, uo_sem,
):
    step = pl.program_id(0)
    steps = FF // FF_TILE
    blk = lax.axis_index("blk")
    core, x, y = blk % 2, (blk // 2) % 2, blk // 4
    exchange = (blks, sent, moved, ex_send, ex_recv, ex_own)

    def to_pair(source, target, sent_sem, received):
        return pltpu.make_async_remote_copy(
            src_ref=source, dst_ref=target, send_sem=sent_sem, recv_sem=received,
            device_id={"blk": blk + 1 - 2 * core}, device_id_type=MESH,
        )

    def down_copy(i):
        return to_pair(down.at[i, 1 - core], down_near.at[i], ds.at[i], dr.at[i])

    def up_columns(t):
        return pl.ds(pl.multiple_of(t * FF_TILE, FF_TILE), FF_TILE)

    def up_copy(t):
        return to_pair(up.at[:, 1 - core, :, up_columns(t)], up_near.at[:, :, up_columns(t)], us.at[t], ur.at[t])

    def down_out(i, keep):
        return pltpu.make_async_copy(
            down.at[i, core], (down_keep if keep else down_send).at[i // 2], do_sem.at[i]
        )

    def up_out(t, i, keep):
        return pltpu.make_async_copy(
            up.at[i, core, :, up_columns(t)],
            (up_keep if keep else up_send).at[i % 2, :, up_columns(t)],
            uo_sem.at[t, i],
        )

    def add_down(i):
        down_copy(i).wait_recv()
        down[i, core] = (down[i, core].astype(f32) + down_near[i].astype(f32)).astype(bf16)
        for keep in (True, False):

            @pl.when((i % 2 == x) == keep)
            def _(keep=keep):
                down_out(i, keep).start()

    def add_up(t):
        up_copy(t).wait_recv()
        columns = up_columns(t)
        for i in range(4):
            up[i, core, :, columns] = (
                up[i, core, :, columns].astype(f32) + up_near[i, :, columns].astype(f32)
            ).astype(bf16)
            for keep in (True, False):

                @pl.when((i // 2 == y) == keep)
                def _(i=i, keep=keep):
                    up_out(t, i, keep).start()

    @pl.when(step == 0)
    def _():
        greet(blks)
        exchange_start(*exchange)
        h_t[...] = h_ref[...].T
        x_t[...] = x_ref[...].T

    down[step // 2, step % 2] = dot_tn(act_ref[...], dm_ref[...]).astype(bf16)

    @pl.when(step % 2 != core)
    def _():
        down_copy(step // 2).start()

    up[:, :, :, up_columns(step)] = (
        dot(h_t[...], du_ref[...]).astype(bf16).reshape(4, 2, D // 8, FF_TILE)
    )
    up_copy(step).start()

    @pl.when(step < 3)
    def _():
        for tap in range(3):
            dw_ref[D * tap : D * tap + D, :] = dot(x_t[...], taps_ref[tap]).astype(bf16)

    @pl.when(step == 3)
    def _():
        attended = jnp.concatenate([o_ref[i] for i in range(o_ref.shape[0])], axis=1)
        dwp_ref[...] = dot_tn(attended, da_ref[...]).astype(bf16)

    @pl.when(step >= 1)
    def _():
        add_up(step - 1)

    @pl.when((step >= 2) & (step % 2 == 0))
    def _():
        add_down(step // 2 - 1)

    @pl.when(step == steps - 1)
    def _():
        add_up(steps - 1)
        add_down(3)
        exchange_wait(*exchange)
        for t in range(steps):
            up_copy(t).wait_send()
            for i in range(4):
                up_out(t, i, True).wait()
        for i in range(4):
            down_copy(i).wait_send()
            down_out(i, True).wait()


def weights(act, dm, h, du, x, taps, o, da, sent, blks, collective_id):
    rows = h.shape[0]
    groups = D // 128
    tile = FF_TILE
    steps = FF // tile
    anywhere = pl.BlockSpec(memory_space=pl.ANY)
    third = lambda i: jnp.minimum(i, 2)
    dma = pltpu.SemaphoreType.DMA
    half_down, half_up = (2, FF // 8, D), (2, D // 8, FF)
    return pl.pallas_call(
        functools.partial(weights_kernel, blks),
        grid=(steps,),
        in_specs=[
            pl.BlockSpec((rows, tile), lambda i: (0, i)),
            whole((rows, D)),
            whole((rows, D)),
            pl.BlockSpec((rows, tile), lambda i: (0, i)),
            whole((rows, D)),
            pl.BlockSpec((3, rows, C), lambda i: (third(i), 0, 0)),
            whole((groups, rows, 128)),
            whole((rows, D)),
            anywhere,
        ],
        out_specs=[pl.BlockSpec((3 * D, C), lambda i: (third(i), 0)), whole((D, D))]
        + [anywhere] * 5,
        out_shape=[
            jax.ShapeDtypeStruct(shape, bf16)
            for shape in ((9 * D, C), (D, D), sent.shape, half_down, half_down, half_up, half_up)
        ],
        scratch_shapes=[
            pltpu.VMEM((4, 2, FF // 8, D), bf16),
            pltpu.VMEM((4, 2, D // 8, FF), bf16),
            pltpu.VMEM((4, FF // 8, D), bf16),
            pltpu.VMEM((4, D // 8, FF), bf16),
            pltpu.VMEM((D, rows), bf16),
            pltpu.VMEM((D, rows), bf16),
        ]
        + exchange_semaphores(blks)
        + [dma((4,)), dma((4,)), dma((steps,)), dma((steps,)), dma((4,)), dma((steps, 4))],
        compiler_params=exchange_params(blks, 62, collective_id),
        cost_estimate=cost(2 * rows * D * (2 * FF + D + 9 * C), 50 << 20),
        name="weight_grads",
    )(act, dm, h, du, x, taps, o, da, sent)


def qkv_grad_kernel(
    g_ref, wq_ref, wk_ref, wv_ref, h_ref, dx1_ref, x_ref, gain_ref,
    dw_ref, dqb_ref, dvb_ref, dx_ref, sums_ref, h_t, total,
):
    step = pl.program_id(0)

    @pl.when(step == 0)
    def _():
        h_t[...] = h_ref[...].T
        total[...] = jnp.zeros_like(total)

    for part, w_ref in enumerate((wq_ref, wk_ref, wv_ref)):
        lanes = slice(128 * part, 128 * part + 128)
        grad = jnp.concatenate([g_ref[0, :, lanes], g_ref[1, :, lanes]], axis=1)
        total[...] += dot_nt(grad, w_ref[...])
        dw_ref[part] = dot(h_t[...], grad).astype(bf16)
        if part == 0:
            dqb_ref[...] = column_sums(grad.astype(f32))
        if part == 2:
            dvb_ref[...] = column_sums(grad.astype(f32))

    @pl.when(step == pl.num_programs(0) - 1)
    def _():
        grad = total[...]
        normed, scale_inv = layer_stats(x_ref[...].astype(f32))
        dx_ref[...] = dx1_ref[...] + layer_backward(grad, normed, scale_inv, gain_ref[...])
        sums_ref[0:1, :] = column_sums(grad * normed)
        sums_ref[1:2, :] = column_sums(grad)
        sums_ref[2:8, :] = jnp.zeros((6, D), f32)


def qkv_grad(g, weight, h, dx1, x, gain):
    rows = x.shape[0]
    groups = D // 128
    return pl.pallas_call(
        qkv_grad_kernel,
        grid=(groups // 2,),
        in_specs=[
            pl.BlockSpec((2, rows, 384), lambda i: (i, 0, 0)),
            pl.BlockSpec((D, 256), lambda i: (0, i)),
            pl.BlockSpec((D, 256), lambda i: (0, 4 + i)),
            pl.BlockSpec((D, 256), lambda i: (0, 8 + i)),
            whole((rows, D)),
            whole((rows, D)),
            whole((rows, D)),
            whole((1, D)),
        ],
        out_specs=[
            pl.BlockSpec((3, D, 256), lambda i: (0, 0, i)),
            pl.BlockSpec((1, 256), lambda i: (0, i)),
            pl.BlockSpec((1, 256), lambda i: (0, i)),
            whole((rows, D)),
            whole((8, D)),
        ],
        out_shape=[
            jax.ShapeDtypeStruct((3, D, D), bf16),
            jax.ShapeDtypeStruct((1, D), f32),
            jax.ShapeDtypeStruct((1, D), f32),
            jax.ShapeDtypeStruct((rows, D), f32),
            jax.ShapeDtypeStruct((8, D), f32),
        ],
        scratch_shapes=[pltpu.VMEM((D, rows), bf16), pltpu.VMEM((rows, D), f32)],
        compiler_params=params(48),
        cost_estimate=cost(4 * rows * D * 3 * D, 24 << 20),
        name="qkv_norm_grad",
    )(g, weight, weight, weight, h, dx1, x, gain)


def row_segments(rows, rim):
    count = rows // BLOCK
    pieces = []
    for block in range(count):
        first = block * BLOCK - (rim if block == 0 else 0)
        last = (block + 1) * BLOCK + (rim if block == count - 1 else 0)
        pieces.append((first, last - first, block))
    return pieces


def shifted_rows(start, shift, size):
    return pl.ds(pl.multiple_of(start + shift, UNIT), size)


def conv_kernel(widths, x_ref, top_ref, bottom_ref, flags, w_ref, z_ref, sums_ref, x_ext, left, right, centre):
    step = pl.program_id(0)
    rows = x_ref.shape[0]
    extent = rows + 2 * RIM

    @pl.when(step == 0)
    def _():
        x_ext[0:RIM, :] = top_ref[...]
        x_ext[RIM : RIM + rows, :] = x_ref[...]
        x_ext[RIM + rows :, :] = bottom_ref[...]
        left[...] = jnp.zeros_like(left)
        right[...] = jnp.zeros_like(right)

    source = x_ext[...]
    left[8 : 8 + extent, :] = dot(source, w_ref[0:D, :])
    right[8 : 8 + extent, :] = dot(source, w_ref[2 * D : 3 * D, :])
    centre[...] = (
        dot(source, w_ref[D : 2 * D, :])
        + flags[:, 2:3] * left[7 : 7 + extent, :]
        + flags[:, 3:4] * right[9 : 9 + extent, :]
    )
    for first, size, block in row_segments(rows, 0):
        own = slice(first, first + size)
        width = widths[block]
        for tap in range(3):

            @pl.when(step == tap)
            def _(tap=tap, first=first, size=size, own=own, width=width):
                found = centre[shifted_rows(RIM + first, (tap - 1) * width, size), :]
                if tap == 0:
                    z_ref[own, :] = flags[RIM + first : RIM + first + size, 0:1] * found
                elif tap == 1:
                    z_ref[own, :] += found
                else:
                    z_ref[own, :] += flags[RIM + first : RIM + first + size, 1:2] * found

    @pl.when(step == 2)
    def _():
        z = z_ref[...]
        sums_ref[0:1, :] = column_sums(z)
        sums_ref[1:2, :] = column_sums(z * z)
        sums_ref[2:8, :] = jnp.zeros((6, C), f32)


def conv(widths, x, top, bottom, flags, weight):
    rows = x.shape[0]
    extent = rows + 2 * RIM
    return pl.pallas_call(
        conv_kernel,
        grid_spec=pltpu.PrefetchScalarGridSpec(
            num_scalar_prefetch=1,
            grid=(3,),
            in_specs=[
                whole((rows, D)),
                whole((RIM, D)),
                whole((RIM, D)),
                whole((extent, 8)),
                pl.BlockSpec((3 * D, C), lambda i, *_: (i, 0)),
            ],
            out_specs=[whole((rows, C)), whole((8, C))],
            scratch_shapes=[
                pltpu.VMEM((extent, D), bf16),
                pltpu.VMEM((extent + 16, C), f32),
                pltpu.VMEM((extent + 16, C), f32),
                pltpu.VMEM((extent, C), f32),
            ],
        ),
        out_shape=[jax.ShapeDtypeStruct((rows, C), f32), jax.ShapeDtypeStruct((8, C), f32)],
        compiler_params=params(40),
        cost_estimate=cost(2 * extent * 9 * D * C, 8 << 20),
        name="conv",
    )(widths, x, top, bottom, flags, weight)


def spread_kernel(widths, g_ref, top_ref, bottom_ref, flags, out_ref, upper, lower, g_ext):
    rows = g_ref.shape[0]
    extent = rows + 2 * WIDE_RIM
    g_ext[0:WIDE_RIM, :] = top_ref[...].astype(f32)
    g_ext[WIDE_RIM : WIDE_RIM + rows, :] = g_ref[...].astype(f32)
    g_ext[WIDE_RIM + rows :, :] = bottom_ref[...].astype(f32)
    inner = slice(8, extent - 8)
    has_left, has_right = flags[inner, 2:3], flags[inner, 3:4]
    for i, target in enumerate((upper, lower)):
        near = g_ext[:, 2 * i * C : (2 * i + 1) * C]
        far = g_ext[:, (2 * i + 1) * C : (2 * i + 2) * C]
        target[0:8, :] = jnp.zeros((8, C), f32)
        target[extent - 8 :, :] = jnp.zeros((8, C), f32)
        target[inner, :] = (
            (1.0 - 0.25 * has_left) * near[inner, :]
            + (1.0 - 0.25 * has_right) * far[inner, :]
            + 0.25 * has_right * g_ext[9 : extent - 7, 2 * i * C : (2 * i + 1) * C]
            + 0.25 * has_left * g_ext[7 : extent - 9, (2 * i + 1) * C : (2 * i + 2) * C]
        )
    for first, size, block in row_segments(rows, RIM):
        width = widths[block]
        here = WIDE_RIM + first
        has_up, has_down = flags[here : here + size, 0:1], flags[here : here + size, 1:2]
        out_ref[RIM + first : RIM + first + size, :] = (
            (1.0 - 0.25 * has_up) * upper[here : here + size, :]
            + (1.0 - 0.25 * has_down) * lower[here : here + size, :]
            + 0.25 * has_down * upper[shifted_rows(here, width, size), :]
            + 0.25 * has_up * lower[shifted_rows(here, -width, size), :]
        )


def spread(widths, g, top, bottom, flags):
    rows = g.shape[0]
    extent = rows + 2 * WIDE_RIM
    return pl.pallas_call(
        spread_kernel,
        grid_spec=pltpu.PrefetchScalarGridSpec(
            num_scalar_prefetch=1,
            grid=(1,),
            in_specs=[
                whole((rows, D)),
                whole((WIDE_RIM, D)),
                whole((WIDE_RIM, D)),
                whole((extent, 8)),
            ],
            out_specs=whole((rows + 2 * RIM, C)),
            scratch_shapes=[
                pltpu.VMEM((extent, C), f32),
                pltpu.VMEM((extent, C), f32),
                pltpu.VMEM((extent, D), f32),
            ],
        ),
        out_shape=jax.ShapeDtypeStruct((rows + 2 * RIM, C), f32),
        compiler_params=params(40),
        cost_estimate=cost(20 * extent * D, 3 << 20),
        name="upsample_grad",
    )(widths, g, top, bottom, flags)


def batch_kernel(
    widths, z_ref, top_ref, bottom_ref, dact_ref, flags, mean_ref, inv_ref, gain_ref, bias_ref,
    up_ref, normed_ref, dbn_ref, sums_ref, act, mixed,
):
    rows = z_ref.shape[0]
    z = jnp.concatenate([top_ref[...], z_ref[...], bottom_ref[...]], axis=0)
    normed = (z - mean_ref[...]) * inv_ref[...]
    normed_ref[...] = normed
    pre = normed * gain_ref[...] + bias_ref[...]
    cumulative, weighted = gelu_parts(pre)
    act[...] = (pre * cumulative).astype(bf16).astype(f32)
    dbn = dact_ref[...] * (cumulative + weighted)
    dbn_ref[...] = dbn
    own = slice(RIM, RIM + rows)
    sums_ref[0:1, :] = column_sums(dbn[own, :])
    sums_ref[1:2, :] = column_sums(dbn[own, :] * normed[own, :])
    sums_ref[2:8, :] = jnp.zeros((6, C), f32)
    for first, size, block in row_segments(rows, 0):
        width = widths[block]
        here = RIM + first
        outer = slice(here - 8, here + size + 8)
        for i in range(2):
            has = flags[outer, i : i + 1]
            mixed[...] = (1.0 - 0.25 * has) * act[outer, :] + 0.25 * has * act[
                pl.ds(pl.multiple_of(here - 8 + (2 * i - 1) * width, 8), size + 16), :
            ]
            for j in range(2):
                has = flags[here : here + size, 2 + j : 3 + j]
                up_ref[first : first + size, (2 * i + j) * C : (2 * i + j + 1) * C] = (
                    (1.0 - 0.25 * has) * mixed[8 : 8 + size, :]
                    + 0.25 * has * mixed[7 + 2 * j : 7 + 2 * j + size, :]
                ).astype(bf16)


def batch(widths, z, top, bottom, dact, flags, mean, inv, gain, bias):
    rows = z.shape[0]
    extent = rows + 2 * RIM
    return pl.pallas_call(
        batch_kernel,
        grid_spec=pltpu.PrefetchScalarGridSpec(
            num_scalar_prefetch=1,
            grid=(1,),
            in_specs=[
                whole((rows, C)),
                whole((RIM, C)),
                whole((RIM, C)),
                whole((extent, C)),
                whole((extent, 8)),
                whole((1, C)),
                whole((1, C)),
                whole((1, C)),
                whole((1, C)),
            ],
            out_specs=[
                whole((rows, D)),
                whole((extent, C)),
                whole((extent, C)),
                whole((8, C)),
            ],
            scratch_shapes=[pltpu.VMEM((extent, C), f32), pltpu.VMEM((BLOCK + 16, C), f32)],
        ),
        out_shape=[
            jax.ShapeDtypeStruct((rows, D), bf16),
            jax.ShapeDtypeStruct((extent, C), f32),
            jax.ShapeDtypeStruct((extent, C), f32),
            jax.ShapeDtypeStruct((8, C), f32),
        ],
        compiler_params=params(40),
        cost_estimate=cost(60 * extent * C, 4 << 20),
        name="batch_norm",
    )(widths, z, top, bottom, dact, flags, mean, inv, gain, bias)


def conv_grad_kernel(
    widths, dbn_ref, normed_ref, flags, scale_ref, shift_ref, slope_ref, w_ref, og_ref,
    taps, dy_ref, dm_ref, moved,
):
    step = pl.program_id(0)
    rows = og_ref.shape[0]
    extent = rows + 2 * RIM

    @pl.when(step == 0)
    def _():
        dz = scale_ref[...] * (dbn_ref[...] - shift_ref[...] - normed_ref[...] * slope_ref[...])
        dz = dz.astype(bf16).astype(f32)
        dy_ref[...] = og_ref[...].astype(f32)
        moved[0, 0:8, :] = jnp.zeros((8, C), f32)
        moved[0, 8 + extent :, :] = jnp.zeros((8, C), f32)
        moved[0, 8 : 8 + extent, :] = dz
        moved[1, 8 : 8 + extent, :] = flags[:, 3:4] * moved[0, 9 : 9 + extent, :]
        moved[2, 8 : 8 + extent, :] = flags[:, 2:3] * moved[0, 7 : 7 + extent, :]
        for first, size, block in row_segments(rows, 0):
            width = widths[block]
            here = RIM + first
            for row in range(3):
                for col, slot in enumerate((1, 0, 2)):
                    found = moved[slot, pl.ds(pl.multiple_of(8 + here + (1 - row) * width, 8), size), :]
                    if row == 0:
                        found = flags[here : here + size, 1:2] * found
                    if row == 2:
                        found = flags[here : here + size, 0:1] * found
                    taps[3 * row + col, first : first + size, :] = found.astype(bf16)

    for part in range(3):
        dy_ref[...] += dot_nt(taps[3 * step + part], w_ref[D * part : D * part + D, :])

    @pl.when(step == pl.num_programs(0) - 1)
    def _():
        dm_ref[...] = dy_ref[...].astype(bf16)


def conv_grad(widths, dbn, normed, flags, scale, shift, slope, weight, out_grad):
    rows = out_grad.shape[0]
    extent = rows + 2 * RIM
    return pl.pallas_call(
        conv_grad_kernel,
        grid_spec=pltpu.PrefetchScalarGridSpec(
            num_scalar_prefetch=1,
            grid=(3,),
            in_specs=[
                whole((extent, C)),
                whole((extent, C)),
                whole((extent, 8)),
                whole((1, C)),
                whole((1, C)),
                whole((1, C)),
                pl.BlockSpec((3 * D, C), lambda i, *_: (i, 0)),
                whole((rows, D)),
            ],
            out_specs=[whole((9, rows, C)), whole((rows, D)), whole((rows, D))],
            scratch_shapes=[pltpu.VMEM((3, extent + 16, C), f32)],
        ),
        out_shape=[
            jax.ShapeDtypeStruct((9, rows, C), bf16),
            jax.ShapeDtypeStruct((rows, D), f32),
            jax.ShapeDtypeStruct((rows, D), bf16),
        ],
        compiler_params=params(48),
        cost_estimate=cost(2 * rows * 9 * D * C, 12 << 20),
        name="conv_grad",
    )(widths, dbn, normed, flags, scale, shift, slope, weight, out_grad)


def small_sum_kernel(scatter, blks, seqs, x_ref, out_ref, first, second, sends, receives, sends2, receives2):
    blk, seq = lax.axis_index("blk"), lax.axis_index("seq")
    barrier = pltpu.get_barrier_semaphore()
    for step in range(1, blks):
        pl.semaphore_signal(
            barrier, inc=1, device_id={"blk": lax.rem(blk + step, blks)}, device_id_type=MESH
        )
    for step in range(1, seqs):
        pl.semaphore_signal(
            barrier, inc=1, device_id={"seq": lax.rem(seq + step, seqs)}, device_id_type=MESH
        )
    pl.semaphore_wait(barrier, blks + seqs - 2)
    copies = []
    for step in range(1, blks):
        to = lax.rem(blk + step, blks)
        copy = pltpu.make_async_remote_copy(
            src_ref=x_ref.at[to] if scatter else x_ref.at[0],
            dst_ref=first.at[blk],
            send_sem=sends.at[step],
            recv_sem=receives.at[step],
            device_id={"blk": to},
            device_id_type=MESH,
        )
        copy.start()
        copies.append(copy)
    first[blk] = x_ref[blk] if scatter else x_ref[0]
    for copy in copies:
        copy.wait()
    total = first[0]
    for i in range(1, blks):
        total = total + first[i]
    second[seq] = total
    copies = []
    for step in range(1, seqs):
        copy = pltpu.make_async_remote_copy(
            src_ref=second.at[seq],
            dst_ref=second.at[seq],
            send_sem=sends2.at[step],
            recv_sem=receives2.at[step],
            device_id={"seq": lax.rem(seq + step, seqs)},
            device_id_type=MESH,
        )
        copy.start()
        copies.append(copy)
    for copy in copies:
        copy.wait()
    total = second[0]
    for i in range(1, seqs):
        total = total + second[i]
    out_ref[...] = total


def small_sum(x, scatter, collective_id):
    blks, seqs = lax.axis_size("blk"), lax.axis_size("seq")
    part = x.shape[1:]
    return pl.pallas_call(
        functools.partial(small_sum_kernel, scatter, blks, seqs),
        in_specs=[pl.BlockSpec(memory_space=pltpu.VMEM)],
        out_specs=pl.BlockSpec(memory_space=pltpu.VMEM),
        out_shape=jax.ShapeDtypeStruct(part, f32),
        scratch_shapes=[
            pltpu.VMEM((blks, *part), f32),
            pltpu.VMEM((seqs, *part), f32),
            pltpu.SemaphoreType.DMA((blks,)),
            pltpu.SemaphoreType.DMA((blks,)),
            pltpu.SemaphoreType.DMA((seqs,)),
            pltpu.SemaphoreType.DMA((seqs,)),
        ],
        compiler_params=params(16, collective_id=collective_id, has_side_effects=True),
        name="small_sum",
    )(x)


LAG = 2
PIECE_ROWS = 64
SLOTS = 3
ROOT = 1


def cuts(size, piece):
    return [slice(first, min(size, first + piece)) for first in range(0, size, piece)]


def pieces_of(index, shape):
    parts, rows, columns = shape
    piece = PIECE_ROWS if columns >= D else 3 * PIECE_ROWS
    return [
        (index, part, row, column)
        for part in range(parts)
        for row in cuts(rows, piece)
        for column in cuts(columns, D)
    ]


class Reducer:
    @staticmethod
    def scratch(shapes, dtypes, staged, halves, units):
        places = []
        for lead in ((4,), (2,), (), (), ()):
            places += [
                pltpu.VMEM(
                    (shape[0],) + ((2,) if lead and index in halves else lead) + shape[1:], dtype
                )
                for index, (shape, dtype) in enumerate(zip(shapes, dtypes))
            ]
        for index in range(len(shapes)):
            _, _, rows, columns = next(unit for unit in units if unit[0] == index)
            size = (rows.stop - rows.start, columns.stop - columns.start)
            size = (SLOTS, 4) + size if index in staged else (1, 1, 16, 128)
            places.append(pltpu.VMEM(size, dtypes[index]))
        total = len(units)
        semaphores = [pltpu.SemaphoreType.DMA((total, 2))] * 2
        semaphores += [pltpu.SemaphoreType.DMA((total,))] * 10
        return places + semaphores

    def __init__(self, seqs, units, staged, halves, ins, outs, refs):
        count = len(ins)
        self.seqs, self.units, self.staged, self.ins, self.outs = seqs, units, staged, ins, outs
        self.halves = halves
        self.sums, self.side, self.last, self.below, self.above, self.slots = [
            refs[i * count : (i + 1) * count] for i in range(6)
        ]
        (self.s2, self.r2, self.load_sem, self.s1, self.r1, self.s3, self.r3, self.sb, self.rb,
         self.sa, self.ra, self.out_sem) = refs[6 * count :]
        blk, self.seq = lax.axis_index("blk"), lax.axis_index("seq")
        self.core, self.x, self.y = blk % 2, (blk // 2) % 2, blk // 4
        self.pair = {"blk": blk + 1 - 2 * self.core}
        self.over_x = {"blk": blk + 2 - 4 * self.x}
        self.over_y = {"blk": blk + 4 - 8 * self.y}
        self.order = {}
        for u, unit in enumerate(units):
            self.order.setdefault(unit[0], []).append(u)

    def send(self, source, target, sent, received, peer):
        return pltpu.make_async_remote_copy(
            src_ref=source, dst_ref=target, send_sem=sent, recv_sem=received,
            device_id=peer, device_id_type=MESH,
        )

    def own(self, u):
        index, part, rows, columns = self.units[u]
        if index in self.staged:
            return self.slots[index].at[self.order[index].index(u) % SLOTS]
        return self.ins[index].at[part, :, self.core, rows, columns]

    def load(self, u):
        index, part, rows, columns = self.units[u]
        return pltpu.make_async_copy(
            self.ins[index].at[part, :, self.core, rows, columns], self.own(u), self.load_sem.at[u]
        )

    def load_half(self, u):
        index, part, rows, columns = self.units[u]
        kept, arrived = self.ins[index]
        return [
            pltpu.make_async_copy(
                kept.at[:, rows, columns], self.sums[index].at[part, :, rows, columns], self.load_sem.at[u]
            ),
            pltpu.make_async_copy(
                arrived.at[:, rows, columns], self.side[index].at[part, :, rows, columns], self.r1.at[u]
            ),
        ]

    def over_x_first(self, u):
        index = self.units[u][0]
        if index in self.halves:
            return self.halves[index] == 0
        return [v for v, unit in enumerate(self.units) if unit[0] not in self.halves].index(u) % 2 == 0

    def first(self, u):
        index, part, rows, columns = self.units[u]
        return self.send(
            self.ins[index].at[part, :, 1 - self.core, rows, columns],
            self.sums[index].at[part, :, rows, columns],
            self.s1.at[u], self.r1.at[u], self.pair,
        )

    def second(self, u):
        index, part, rows, columns = self.units[u]
        copies = []
        for i in range(2):
            x_first = self.over_x_first(u)
            place = 1 - self.x + 2 * i if x_first else 2 * (1 - self.y) + i
            copies.append(
                self.send(
                    self.sums[index].at[part, place, rows, columns],
                    self.side[index].at[part, i, rows, columns],
                    self.s2.at[u, i], self.r2.at[u, i], self.over_x if x_first else self.over_y,
                )
            )
        return copies

    def third(self, u):
        index, part, rows, columns = self.units[u]
        x_first = self.over_x_first(u)
        if index in self.halves:
            place = 1 - self.y if x_first else 1 - self.x
        else:
            place = 2 * (1 - self.y) + self.x if x_first else 2 * self.y + 1 - self.x
        return self.send(
            self.sums[index].at[part, place, rows, columns],
            self.last[index].at[part, rows, columns],
            self.s3.at[u], self.r3.at[u], self.over_y if x_first else self.over_x,
        )

    def result(self, u):
        index, part, rows, columns = self.units[u]
        if index in self.halves:
            return self.sums[index].at[part, self.y if self.over_x_first(u) else self.x, rows, columns]
        return self.sums[index].at[part, 2 * self.y + self.x, rows, columns]

    def down(self, u):
        index, part, rows, columns = self.units[u]
        return self.send(
            self.result(u), self.above[index].at[part, rows, columns],
            self.sa.at[u], self.ra.at[u], {"seq": self.seq - 1},
        )

    def up(self, u):
        index, part, rows, columns = self.units[u]
        return self.send(
            self.result(u), self.below[index].at[part, rows, columns],
            self.sb.at[u], self.rb.at[u], {"seq": self.seq + 1},
        )

    def store(self, u):
        index, part, rows, columns = self.units[u]
        return pltpu.make_async_copy(
            self.result(u), self.outs[index].at[part, rows, columns], self.out_sem.at[u]
        )

    def add_to(self, target, *sources):
        total = target[...].astype(f32)
        for source in sources:
            total = total + source[...].astype(f32)
        target[...] = total.astype(target.dtype)

    def enter(self, u):
        if self.units[u][0] in self.halves:
            for copy in self.load_half(u):
                copy.start()
            return
        self.first(u).start()
        index = self.units[u][0]
        if index in self.staged and self.order[index].index(u) < SLOTS:
            self.load(u).start()

    def stage_near(self, u):
        index, part, rows, columns = self.units[u]
        if index in self.halves:
            return
        if index in self.staged:
            self.load(u).wait()
        self.first(u).wait_recv()
        own = self.own(u)
        for i in range(4):
            self.add_to(self.sums[index].at[part, i, rows, columns], own.at[i])
        if index in self.staged:
            later = self.order[index].index(u) + SLOTS
            if later < len(self.order[index]):
                self.load(self.order[index][later]).start()
        for copy in self.second(u):
            copy.start()

    def stage_side(self, u):
        index, part, rows, columns = self.units[u]
        if index in self.halves:
            for copy in self.load_half(u):
                copy.wait()
            for i in range(2):
                self.add_to(
                    self.sums[index].at[part, i, rows, columns],
                    self.side[index].at[part, i, rows, columns],
                )
            self.third(u).start()
            return
        for i, copy in enumerate(self.second(u)):
            copy.wait_recv()
            keep = 2 * i + self.x if self.over_x_first(u) else 2 * self.y + i
            self.add_to(
                self.sums[index].at[part, keep, rows, columns],
                self.side[index].at[part, i, rows, columns],
            )
        self.third(u).start()

    def stage_last(self, u):
        index, part, rows, columns = self.units[u]
        self.third(u).wait_recv()
        self.add_to(self.result(u), self.last[index].at[part, rows, columns])

        @pl.when(self.seq < ROOT)
        def _():
            self.up(u).start()

        @pl.when(self.seq == self.seqs - 1)
        def _():
            self.down(u).start()

    def stage_chain(self, u, place):
        index, part, rows, columns = self.units[u]

        @pl.when(self.seq == place)
        def _():
            self.down(u).wait_recv()
            self.add_to(self.result(u), self.above[index].at[part, rows, columns])
            self.down(u).start()

    def stage_root(self, u):
        index, part, rows, columns = self.units[u]

        @pl.when(self.seq == ROOT)
        def _():
            self.up(u).wait_recv()
            self.down(u).wait_recv()
            self.add_to(
                self.result(u),
                self.below[index].at[part, rows, columns],
                self.above[index].at[part, rows, columns],
            )
            self.up(u).start()
            self.down(u).start()
            self.store(u).start()

    def stage_spread(self, u, place):
        index, part, rows, columns = self.units[u]

        @pl.when(self.seq == place)
        def _():
            if place < ROOT:
                self.down(u).wait_recv()
                self.up(u).wait_send()
                self.result(u)[...] = self.above[index].at[part, rows, columns][...]
            else:
                self.up(u).wait_recv()
                self.down(u).wait_send()
                self.result(u)[...] = self.below[index].at[part, rows, columns][...]
                if place < self.seqs - 1:
                    self.up(u).start()
            self.store(u).start()

    def stages(self):
        found = [(0, self.stage_near), (LAG, self.stage_side), (2 * LAG, self.stage_last)]
        at = 3 * LAG
        for place in range(self.seqs - 2, ROOT, -1):
            found.append((at, functools.partial(self.stage_chain, place=place)))
            at += LAG
        found.append((at, self.stage_root))
        at += LAG
        for place in range(ROOT):
            found.append((at, functools.partial(self.stage_spread, place=place)))
        for place in range(ROOT + 1, self.seqs):
            found.append((at, functools.partial(self.stage_spread, place=place)))
            at += LAG
        return found

    def steps(self):
        return len(self.units) + self.stages()[-1][0]

    def step(self, t):
        for lag, stage in self.stages():
            if 0 <= t - lag < len(self.units):
                stage(t - lag)

    def finish(self):
        for u in range(len(self.units)):
            if self.units[u][0] not in self.halves:
                self.first(u).wait_send()
                for copy in self.second(u):
                    copy.wait_send()
            self.third(u).wait_send()

            @pl.when(self.seq == ROOT)
            def _(u=u):
                self.down(u).wait_send()
                self.up(u).wait_send()

            @pl.when((self.seq > ROOT) & (self.seq < self.seqs - 1))
            def _(u=u):
                self.up(u).wait_send()

            self.store(u).wait()


STAGED = (2, 3)
HALVES = {0: 0, 1: 1}

AHEAD = 10


def tail_kernel(
    blks, seqs, units, sent, w_ref, h_ref, dx1_ref, x_ref, gain_ref, sums_ref, dub_ref,
    down_in, down_side, up_in, up_side, conv_in, proj_in, dx_ref,
    down_out, up_out, conv_out, proj_out, qkv_out, vec_out,
    moved, dw, vectors, h_t, w_slots, ex_send, ex_recv, ex_own, w_sem, *refs
):
    reducer = Reducer(
        seqs, units, STAGED, HALVES,
        ((down_in, down_side), (up_in, up_side), conv_in, proj_in, dw, vectors),
        (down_out, up_out, conv_out, proj_out, qkv_out, vec_out), refs,
    )
    early = [u for u, unit in enumerate(units) if unit[0] < 4]
    exchange = (blks, sent, moved, ex_send, ex_recv, ex_own)
    slots = w_slots.shape[0]

    def weight(k):
        part, i = divmod(k, 4)
        first = D * part + 256 * i
        return pltpu.make_async_copy(
            w_ref.at[:, first : first + 256], w_slots.at[k % slots], w_sem.at[k]
        )

    def put(vector, row, index):
        for place in range(8):
            vectors[0, place // 2, place % 2, row : row + 1, :] = vector[:, 128 * index(place) : 128 * index(place) + 128]

    def chunk(k):
        part, i = divmod(k, 4)
        lanes = slice(128 * part, 128 * part + 128)
        weight(k).wait()
        grad = jnp.concatenate([moved[2 * i, :, lanes], moved[2 * i + 1, :, lanes]], axis=1)
        dx_ref[...] += dot_nt(grad, w_slots[k % slots])
        dw[part, :, :, :, 256 * i : 256 * i + 256] = (
            dot(h_t[...], grad).astype(bf16).reshape(4, 2, 128, 256)
        )
        if k + slots < 12:
            weight(k + slots).start()
        if part != 1:
            bias = column_sums(grad.astype(f32))
            place = i + (4 if part else 0)
            for half in range(2):
                vectors[0, place // 2, place % 2, 6 + half : 7 + half, :] = bias[:, 128 * half : 128 * half + 128]
        if i == 3:
            for u, unit in enumerate(units):
                if unit[0] == 4 and unit[1] == part:
                    reducer.enter(u)

    def norm():
        grad = dx_ref[...]
        normed, scale_inv = layer_stats(x_ref[...].astype(f32))
        dx_ref[...] = dx1_ref[...] + layer_backward(grad, normed, scale_inv, gain_ref[...])
        put(column_sums(grad * normed), 0, lambda place: place)
        put(column_sums(grad), 1, lambda place: place)
        for row in range(4):
            put(sums_ref[row : row + 1, :], 2 + row, lambda place: place)
            put(dub_ref[...], 8 + row, lambda place, row=row: 4 * place + row)
        for place in range(8):
            vectors[0, place // 2, place % 2, 12:16, :] = jnp.zeros((4, 128), f32)
        for u, unit in enumerate(units):
            if unit[0] == 5:
                reducer.enter(u)

    greet(blks, seqs)
    exchange_start(*exchange)
    for u in early:
        reducer.enter(u)
    for k in range(slots):
        weight(k).start()
    h_t[...] = h_ref[...].T
    dx_ref[...] = jnp.zeros_like(dx_ref)
    at = 0
    while at < AHEAD:
        reducer.step(at)
        at += 1
    exchange_wait(*exchange)
    for k in range(12):
        chunk(k)
        if k % 2:
            reducer.step(at)
            at += 1
    norm()
    while at < reducer.steps():
        reducer.step(at)
        at += 1
    reducer.finish()


def tail(sent, weight, h, dx1, x, gain, sums, dub, arrays, collective_id):
    blks, seqs = lax.axis_size("blk"), lax.axis_size("seq")
    rows = x.shape[0]
    shapes = [(1, FF // 8, D), (1, D // 8, FF), (1, 9 * D // 8, C), (1, D // 8, D), (3, D // 8, D), (1, 16, 128)]
    dtypes = [bf16] * 5 + [f32]
    found = [pieces_of(index, shape) for index, shape in enumerate(shapes)]
    light = [unit for pair in zip(found[0], found[1]) for unit in pair]
    heavy = found[2] + found[3]
    units = [unit for pair in zip(heavy, light) for unit in pair]
    units += [unit for pair in zip(found[4], light[len(heavy) :]) for unit in pair] + found[5]
    units += light[len(heavy) + len(found[4]) :]
    anywhere = pl.BlockSpec(memory_space=pl.ANY)
    vmem = pl.BlockSpec(memory_space=pltpu.VMEM)
    return pl.pallas_call(
        functools.partial(tail_kernel, blks, seqs, units),
        in_specs=[anywhere, anywhere] + [vmem] * 6 + [anywhere] * 6,
        out_specs=[vmem] + [anywhere] * 6,
        out_shape=[jax.ShapeDtypeStruct((rows, D), f32)]
        + [
            jax.ShapeDtypeStruct(shape, dtype) for shape, dtype in zip(shapes, dtypes)
        ],
        scratch_shapes=[
            pltpu.VMEM(sent.shape, bf16),
            pltpu.VMEM((3, 4, 2, D // 8, D), bf16),
            pltpu.VMEM((1, 4, 2, 16, 128), f32),
            pltpu.VMEM((D, rows), bf16),
            pltpu.VMEM((3, D, 256), bf16),
            pltpu.SemaphoreType.DMA((blks,)),
            pltpu.SemaphoreType.DMA((blks,)),
            pltpu.SemaphoreType.DMA,
            pltpu.SemaphoreType.DMA((12,)),
        ]
        + Reducer.scratch(shapes, dtypes, STAGED, HALVES, units),
        compiler_params=params(63, collective_id=collective_id, has_side_effects=True),
        name="qkv_grad_and_sums",
    )(sent, weight, h, dx1, x, gain, sums, dub, *arrays)


def widen_kernel(counts, *refs):
    matrices = len(refs) - len(counts) - 1 >> 1
    sources, vectors = refs[:matrices], refs[matrices]
    targets, pieces = refs[matrices + 1 : 2 * matrices + 1], refs[2 * matrices + 1 :]
    for source, target in zip(sources[:-1], targets[:-1]):
        target[...] = source[0].astype(f32)
    for part in range(3):
        targets[-1][:, D * part : D * part + D] = sources[-1][part].astype(f32)
    row = 0
    for count, piece in zip(counts, pieces):
        for i in range(count):
            piece[:, 128 * i : 128 * i + 128] = vectors[0, row : row + 1, :]
            row += 1


def widen(arrays, vectors, counts):
    steps = 4
    return pl.pallas_call(
        functools.partial(widen_kernel, counts),
        grid=(steps,),
        in_specs=[
            pl.BlockSpec((a.shape[0], a.shape[1] // steps, a.shape[2]), lambda i: (0, i, 0))
            for a in arrays
        ]
        + [whole(vectors.shape)],
        out_specs=[
            pl.BlockSpec((a.shape[1] // steps, a.shape[0] * a.shape[2]), lambda i: (i, 0))
            for a in arrays
        ]
        + [whole((1, 128 * count)) for count in counts],
        out_shape=[
            jax.ShapeDtypeStruct((a.shape[1], a.shape[0] * a.shape[2]), f32) for a in arrays
        ]
        + [jax.ShapeDtypeStruct((1, 128 * count), f32) for count in counts],
        compiler_params=params(62),
        name="widen",
    )(*arrays, vectors)


def shifted(value, axis, steps):
    count = lax.axis_size(axis)
    leading, last = (max(0, -steps), min(count, count - steps))
    return lax.ppermute(value, axis, [(source, source + steps) for source in range(leading, last)])


def near_blocks(sides_row, keys_own, values_own):
    rows = keys_own.shape[0]
    place, length = lax.axis_index("blk"), rows * lax.axis_size("blk")
    centre = jnp.arange(rows, dtype=jnp.int32)
    segment = image_info(sides_row, place * rows + centre)[0]
    found = []
    for offset in range(-REACH, REACH + 1):
        keys, values = (keys_own, values_own) if offset == 0 else shifted((keys_own, values_own), "blk", -offset)
        positions = (place + offset) * rows + centre
        inside = (positions >= 0) & (positions < length)
        allowed = (segment[:, None] == image_info(sides_row, positions)[0][None, :]) & inside[None, :]
        found.append((offset, keys.reshape(rows, HEADS, HEAD), values.reshape(rows, HEADS, HEAD), allowed))
    return found


def near_scores(queries, keys, allowed):
    scores = jnp.einsum("qhd,khd->hqk", queries, keys, preferred_element_type=f32)
    return jnp.where(allowed[None], scores, masked_score)


def near_attention(near, queries):
    rows = queries.shape[0]
    peak = jnp.full((HEADS, rows), masked_score, f32)
    total = jnp.zeros((HEADS, rows), f32)
    for _, keys, _, allowed in near:
        scores = near_scores(queries, keys, allowed)
        new_peak = jnp.maximum(peak, jnp.max(scores, axis=-1))
        grown = jnp.where(allowed[None], jnp.exp2(scores - new_peak[..., None]), 0.0)
        total = total * jnp.exp2(peak - new_peak) + jnp.sum(grown, axis=-1)
        peak = new_peak
    lse = peak + jnp.log2(total)
    out = jnp.zeros((rows, HEADS, HEAD), f32)
    for _, keys, values, allowed in near:
        scores = near_scores(queries, keys, allowed)
        weights = jnp.where(allowed[None], jnp.exp2(scores - lse[..., None]), 0.0).astype(bf16)
        out = out + jnp.einsum("hqk,khd->qhd", weights, values, preferred_element_type=f32)
    return out.reshape(rows, D).astype(bf16), lse


def near_attention_grad(near, queries, lse, out, grad):
    rows = queries.shape[0]
    grad_heads = grad.reshape(rows, HEADS, HEAD)
    delta = jnp.sum((grad.astype(f32) * out.astype(f32)).reshape(rows, HEADS, HEAD), axis=-1).T
    dq = jnp.zeros((rows, HEADS, HEAD), f32)
    dk = jnp.zeros((rows, HEADS, HEAD), f32)
    dv = jnp.zeros((rows, HEADS, HEAD), f32)
    for offset, keys, values, allowed in near:
        scores = near_scores(queries, keys, allowed)
        weights = jnp.where(allowed[None], jnp.exp2(scores - lse[..., None]), 0.0)
        value_grad = jnp.einsum("qhd,khd->hqk", grad_heads, values, preferred_element_type=f32)
        score_grad = (weights * (value_grad - delta[..., None])).astype(bf16)
        dq = dq + jnp.einsum("hqk,khd->qhd", score_grad, keys, preferred_element_type=f32)
        dk_part = jnp.einsum("hqk,qhd->khd", score_grad, queries, preferred_element_type=f32)
        dv_part = jnp.einsum(
            "hqk,qhd->khd", weights.astype(bf16), grad_heads, preferred_element_type=f32
        )
        if offset:
            dk_part, dv_part = shifted((dk_part.astype(bf16), dv_part.astype(bf16)), "blk", offset)
        dk = dk + dk_part.astype(f32)
        dv = dv + dv_part.astype(f32)
    dq = dq.reshape(rows, D).astype(bf16) * jnp.asarray(HEAD**-0.5, bf16)
    dk = (dk * (1.0 / LOG2E)).reshape(rows, D).astype(bf16)
    return dq, dk, dv.reshape(rows, D).astype(bf16)


def in_groups(*parts):
    rows = parts[0].shape[0]
    stacked = jnp.stack([part.reshape(rows, D // 128, 128) for part in parts], axis=2)
    return stacked.transpose(1, 0, 2, 3).reshape(D // 128, rows, 128 * len(parts))


def from_groups(groups, part):
    picked = groups[:, :, 128 * part : 128 * part + 128]
    return picked.transpose(1, 0, 2).reshape(groups.shape[1], D)


def rims(rows_own, width):
    count = lax.axis_size("blk")
    top = lax.ppermute(rows_own[-width:], "blk", [(i, i + 1) for i in range(count - 1)])
    bottom = lax.ppermute(rows_own[:width], "blk", [(i + 1, i) for i in range(count - 1)])
    return top, bottom


def line(vector):
    return vector.reshape(1, -1)


def shards(
    tokens,
    image_sides,
    ln1_gain,
    ln1_bias,
    qkv_weight,
    qv_bias,
    proj_weight,
    proj_bias,
    ln2_gain,
    ln2_bias,
    up_weight,
    up_bias,
    down_weight,
    down_bias,
    conv_weight,
    bn_gain,
    bn_bias,
    out_grad,
    pup_grad,
):
    x = tokens[0]
    sides_row = image_sides[0]
    rows = x.shape[0]
    blks, seqs = lax.axis_size("blk"), lax.axis_size("seq")
    place = lax.axis_index("blk")
    length = rows * blks
    samples = length * seqs
    by_heads = blks == 8 and HEADS // 2 == blks

    block_starts = jnp.arange(length // BLOCK, dtype=jnp.int32) * BLOCK
    _, block_width, _, _, block_begin = image_info(sides_row, block_starts)
    starts = (block_begin // BLOCK).astype(jnp.int32)
    counts = (block_width * block_width // BLOCK).astype(jnp.int32)
    own_blocks = rows // BLOCK
    widths = lax.dynamic_slice_in_dim(block_width, place * own_blocks, own_blocks)
    wide_positions = place * rows + jnp.arange(-WIDE_RIM, rows + WIDE_RIM, dtype=jnp.int32)
    wide_flags = edge_flags(sides_row, wide_positions)
    flags = wide_flags[WIDE_RIM - RIM : WIDE_RIM + rows + RIM]

    g = pup_grad[0]
    g_top, g_bottom = rims(g, WIDE_RIM)
    dact = spread(widths, g, g_top, g_bottom, wide_flags)

    h1, qkv_groups = project_qkv(x, line(ln1_gain), line(ln1_bias), qkv_weight, line(qv_bias))
    if by_heads:
        qkv = lax.all_to_all(qkv_groups, "blk", 0, 0, tiled=True).reshape(length, 384)
        o_heads, lse = attention(starts, counts, qkv)
        o_groups = lax.all_to_all(o_heads.reshape(blks, rows, 128), "blk", 0, 0, tiled=True)
    else:
        queries = from_groups(qkv_groups, 0).reshape(rows, HEADS, HEAD)
        near = near_blocks(sides_row, from_groups(qkv_groups, 1), from_groups(qkv_groups, 2))
        attended, lse = near_attention(near, queries)
        o_groups = in_groups(attended)
    x1, h2, act, slope, block_low = mlp(
        o_groups, x, proj_weight, line(proj_bias), line(ln2_gain), line(ln2_bias),
        up_weight, line(up_bias), down_weight, line(down_bias),
    )
    top, bottom = rims(block_low, RIM)
    z, z_sums = conv(widths, block_low, top, bottom, flags, conv_weight)
    z_top, z_bottom = rims(z, RIM)
    z_sums = small_sum(z_sums[None], False, 1)
    mean = z_sums[0:1] / samples
    inv = lax.rsqrt(z_sums[1:2] / samples - mean * mean + batch_eps)
    pup_out, normed, dbn, bn_sums = batch(
        widths, z, z_top, z_bottom, dact, flags, mean, inv, line(bn_gain), line(bn_bias)
    )
    bn_sums = small_sum(bn_sums[None], False, 2)

    taps, dy, dm = conv_grad(
        widths, dbn, normed, flags, inv * line(bn_gain), bn_sums[0:1] / samples, bn_sums[1:2] / samples,
        conv_weight, out_grad[0],
    )
    du, up_bias_grad, dx1, da, do_groups, mlp_sums = mlp_grad(
        dy, dm, slope, down_weight, up_weight, x1, line(ln2_gain), proj_weight
    )
    if by_heads:
        conv_weight_grad, proj_grad, do_moved, down_keep, down_send, up_keep, up_send = weights(
            act, dm, h2, du, block_low, taps, o_groups, da, do_groups, blks, 5
        )
        down_side = lax.ppermute(down_send, "blk", [(i, i ^ 2) for i in range(blks)])
        up_side = lax.ppermute(up_send, "blk", [(i, i ^ 4) for i in range(blks)])
        dqkv = attention_grad(starts, counts, qkv, do_moved.reshape(length, 128), o_heads, lse)
        dqkv_groups = dqkv.reshape(blks, rows, 384)
    else:
        down_grad = down_weight_grad_of(act, dm)
        conv_weight_grad = conv_weight_grad_of(block_low, taps)
        up_grad, proj_grad = late_weights(h2, du, o_groups, da)
        grads = near_attention_grad(near, queries, lse, attended, from_groups(do_groups, 0))
        dqkv_groups = in_groups(*grads)

    piece = D // blks
    cuts_of = [piece] * 6 + [2 * piece, 4 * piece]
    if by_heads:
        tokens_grad, *summed = tail(
            dqkv_groups, qkv_weight, h1, dx1, x, line(ln1_gain), mlp_sums, up_bias_grad,
            [
                down_keep, down_side, up_keep, up_side,
                conv_weight_grad.reshape(1, 4, 2, -1, C), proj_grad.reshape(1, 4, 2, -1, D),
            ],
            3,
        )
        tokens_grad, down_grad, up_grad, conv_weight_grad, proj_grad, qkv_weight_grad, *small = widen(
            [tokens_grad[None]] + summed[:5], summed[5], [cut // 128 for cut in cuts_of]
        )
        small = [vector[0] for vector in small]
    else:
        qkv_weight_grad, dqb, dvb, tokens_grad, qkv_sums = qkv_grad(
            dqkv_groups, qkv_weight, h1, dx1, x, line(ln1_gain)
        )

        def scattered(grad):
            part = lax.psum_scatter(grad, "blk", scatter_dimension=0, tiled=True)
            return lax.psum(part, "seq").astype(f32)

        down_grad, up_grad, proj_grad, conv_weight_grad = [
            scattered(grad) for grad in (down_grad, up_grad, proj_grad, conv_weight_grad)
        ]
        qkv_weight_grad = scattered(qkv_weight_grad.transpose(1, 0, 2).reshape(D, 3 * D))
        vectors = [qkv_sums[0], qkv_sums[1], mlp_sums[0], mlp_sums[1], mlp_sums[2], mlp_sums[3]]
        vectors += [jnp.concatenate([dqb[0], dvb[0]]), up_bias_grad[0]]
        stacked = jnp.concatenate([vector.reshape(blks, -1) for vector in vectors], axis=1)
        summed = small_sum(stacked[:, None, :], True, 4)[0]
        ends = [sum(cuts_of[: i + 1]) for i in range(len(cuts_of))]
        small = [summed[end - cut : end] for cut, end in zip(cuts_of, ends)]
    ln1_g, ln1_b, proj_b, ln2_g, ln2_b, down_b, qv_b, up_b = small
    channel_piece = C // blks
    gain_slice = lax.dynamic_slice_in_dim(bn_sums[1], place * channel_piece, channel_piece)
    bias_slice = lax.dynamic_slice_in_dim(bn_sums[0], place * channel_piece, channel_piece)
    return (
        block_low[None],
        pup_out[None],
        tokens_grad[None],
        ln1_g,
        ln1_b,
        qkv_weight_grad,
        qv_b,
        proj_grad,
        proj_b,
        ln2_g,
        ln2_b,
        up_grad,
        up_b,
        down_grad,
        down_b,
        conv_weight_grad,
        gain_slice,
        bias_slice,
    )


def solution(mesh):
    replicated = P()
    packed = P("seq", "blk", None)
    placed = (packed, P("seq", None)) + (replicated,) * 15 + (packed, packed)
    rows, vector = P("blk", None), P("blk")
    return jax.shard_map(
        shards,
        mesh=mesh,
        in_specs=placed,
        out_specs=(
            packed, packed, packed, vector, vector, rows, vector, rows, vector, vector, vector, rows,
            vector, rows, vector, rows, vector, vector,
        ),
        check_vma=False,
    )
```

```python
import functools

import jax
import jax.numpy as jnp
from jax import lax
from jax.experimental import pallas as pl
from jax.experimental.pallas import tpu as pltpu
from jax.sharding import PartitionSpec as P

D = 1024
HEADS = 16
HEAD = 64
FF = 4096
C = 256
REACH = 4
UNIT = 16
BLOCK = UNIT * UNIT
IMAGE_BLOCKS = (1, 4, 9)
RIM = 64
WIDE_RIM = 128
LOG2E = 1.4426950408889634
MESH = pl.DeviceIdType.MESH

norm_eps = 1e-06
batch_eps = 1e-05
masked_score = -1e30
f32 = jnp.float32
bf16 = jnp.bfloat16

NT = (((1,), (1,)), ((), ()))
TN = (((0,), (0,)), ((), ()))


def dot(left, right):
    return jnp.dot(left, right, preferred_element_type=f32)


def dot_nt(left, right):
    return lax.dot_general(left, right, NT, preferred_element_type=f32)


def dot_tn(left, right):
    return lax.dot_general(left, right, TN, preferred_element_type=f32)


def whole(shape):
    zeros = (0,) * len(shape)
    return pl.BlockSpec(shape, lambda *_: zeros)


def params(megabytes, **more):
    return pltpu.CompilerParams(vmem_limit_bytes=megabytes << 20, **more)


def cost(flops, moved, transcendentals=0):
    return pl.CostEstimate(
        flops=int(flops), bytes_accessed=int(moved), transcendentals=int(transcendentals)
    )


def place_copies(blks, source, target, sends, receives):
    me = lax.axis_index("blk")
    copies = []
    for step in range(1, blks):
        to = lax.rem(me + step, blks)
        copies.append(
            pltpu.make_async_remote_copy(
                src_ref=source.at[to],
                dst_ref=target.at[me],
                send_sem=sends.at[step],
                recv_sem=receives.at[step],
                device_id={"blk": to},
                device_id_type=MESH,
            )
        )
    return copies


def greet(blks, seqs=0):
    me, seq = lax.axis_index("blk"), lax.axis_index("seq")
    barrier = pltpu.get_barrier_semaphore()
    for step in range(1, blks):
        pl.semaphore_signal(
            barrier, inc=1, device_id={"blk": lax.rem(me + step, blks)}, device_id_type=MESH
        )
    ends = 0
    if seqs:

        @pl.when(seq > 0)
        def _():
            pl.semaphore_signal(barrier, inc=1, device_id={"seq": seq - 1}, device_id_type=MESH)

        @pl.when(seq < seqs - 1)
        def _():
            pl.semaphore_signal(barrier, inc=1, device_id={"seq": seq + 1}, device_id_type=MESH)

        ends = jnp.where(seq > 0, 1, 0) + jnp.where(seq < seqs - 1, 1, 0)
    pl.semaphore_wait(barrier, blks - 1 + ends)


def exchange_start(blks, source, target, sends, receives, own_sem):
    me = lax.axis_index("blk")
    for copy in place_copies(blks, source, target, sends, receives):
        copy.start()
    pltpu.make_async_copy(source.at[me], target.at[me], own_sem).start()


def exchange_wait(blks, source, target, sends, receives, own_sem):
    me = lax.axis_index("blk")
    for copy in place_copies(blks, source, target, sends, receives):
        copy.wait()
    pltpu.make_async_copy(source.at[me], target.at[me], own_sem).wait()


class Rims:
    def __init__(self, blks, rows_own, top, bottom, landing, semaphores):
        me = lax.axis_index("blk")
        width, last = top.shape[0], rows_own.shape[0]
        self.after, self.before = me < blks - 1, me > 0
        self.top, self.bottom, self.landing = top, bottom, landing
        self.downward = pltpu.make_async_remote_copy(
            src_ref=rows_own.at[last - width : last], dst_ref=landing.at[0],
            send_sem=semaphores.at[0], recv_sem=semaphores.at[1],
            device_id={"blk": me + 1}, device_id_type=MESH,
        )
        self.upward = pltpu.make_async_remote_copy(
            src_ref=rows_own.at[0:width], dst_ref=landing.at[1],
            send_sem=semaphores.at[2], recv_sem=semaphores.at[3],
            device_id={"blk": me - 1}, device_id_type=MESH,
        )

    def start(self):
        @pl.when(self.after)
        def _():
            self.downward.start()

        @pl.when(self.before)
        def _():
            self.upward.start()

        @pl.when(jnp.logical_not(self.after))
        def _():
            self.bottom[...] = jnp.zeros_like(self.bottom)

        @pl.when(jnp.logical_not(self.before))
        def _():
            self.top[...] = jnp.zeros_like(self.top)

    def wait(self):
        @pl.when(self.after)
        def _():
            self.downward.wait_send()
            self.upward.wait_recv()
            self.bottom[...] = self.landing[1]

        @pl.when(self.before)
        def _():
            self.upward.wait_send()
            self.downward.wait_recv()
            self.top[...] = self.landing[0]


def exchange_kernel(blks, source, target, *semaphores):
    greet(blks)
    exchange_start(blks, source, target, *semaphores)
    exchange_wait(blks, source, target, *semaphores)


def exchange(groups, collective_id):
    blks = lax.axis_size("blk")
    anywhere = pl.BlockSpec(memory_space=pl.ANY)
    return pl.pallas_call(
        functools.partial(exchange_kernel, blks),
        in_specs=[anywhere],
        out_specs=anywhere,
        out_shape=jax.ShapeDtypeStruct(groups.shape, groups.dtype),
        scratch_shapes=exchange_semaphores(blks),
        compiler_params=params(16, collective_id=collective_id, has_side_effects=True),
        name="exchange",
    )(groups)


def image_info(image_sides, positions):
    image_areas = image_sides * image_sides
    image_ends = jnp.cumsum(image_areas).astype(jnp.int32)
    image_starts = (image_ends - image_areas).astype(jnp.int32)
    segment = jnp.sum((image_ends[None, :] <= positions[:, None]).astype(jnp.int32), axis=1).astype(
        jnp.int32
    )
    picked = segment[:, None] == jnp.arange(image_sides.shape[0], dtype=jnp.int32)[None, :]
    image_width = jnp.sum(jnp.where(picked, image_sides[None, :], 0), axis=1).astype(jnp.int32)
    image_width = jnp.maximum(image_width, 1).astype(jnp.int32)
    image_begin = jnp.sum(jnp.where(picked, image_starts[None, :], 0), axis=1).astype(jnp.int32)
    offset = (positions - image_begin).astype(jnp.int32)
    row_index = (offset // image_width).astype(jnp.int32)
    col_index = (offset - row_index * image_width).astype(jnp.int32)
    return (segment, image_width, row_index, col_index, image_begin)


def edge_flags(image_sides, positions):
    _, width, row, col, _ = image_info(image_sides, positions)
    flags = jnp.stack([row > 0, row < width - 1, col > 0, col < width - 1], axis=1)
    return jnp.concatenate([flags, flags], axis=1).astype(f32)


def layer_stats(values):
    mean = jnp.mean(values, axis=-1, keepdims=True)
    centred = values - mean
    scale_inv = lax.rsqrt(jnp.mean(centred * centred, axis=-1, keepdims=True) + norm_eps)
    return centred * scale_inv, scale_inv


def layer_backward(grad_out, normed, scale_inv, gain):
    scaled = grad_out * gain
    inner = (
        scaled
        - jnp.mean(scaled, axis=-1, keepdims=True)
        - normed * jnp.mean(scaled * normed, axis=-1, keepdims=True)
    )
    return scale_inv * inner


def column_sums(values):
    return jnp.sum(values, axis=0, keepdims=True)


def gelu_parts(values):
    cumulative = 0.5 + 0.5 * lax.erf(values * 0.7071067811865476)
    weighted = values * (0.3989422804014327 * jnp.exp(values * values * -0.5))
    return cumulative, weighted


def qkv_kernel(x_ref, gain_ref, bias_ref, wq_ref, wk_ref, wv_ref, bq_ref, bv_ref, h_ref, out_ref):
    @pl.when(pl.program_id(0) == 0)
    def _():
        normed, _ = layer_stats(x_ref[...].astype(f32))
        h_ref[...] = (normed * gain_ref[...] + bias_ref[...]).astype(bf16)

    hidden = h_ref[...]
    query = ((dot(hidden, wq_ref[...]) + bq_ref[...]) * (HEAD**-0.5 * LOG2E)).astype(bf16)
    key = dot(hidden, wk_ref[...]).astype(bf16)
    value = (dot(hidden, wv_ref[...]) + bv_ref[...]).astype(bf16)
    for part in range(2):
        lanes = slice(128 * part, 128 * part + 128)
        out_ref[part, :, 0:128] = query[:, lanes]
        out_ref[part, :, 128:256] = key[:, lanes]
        out_ref[part, :, 256:384] = value[:, lanes]


def project_qkv(x, gain, bias, weight, qv_bias):
    rows = x.shape[0]
    groups = D // 128
    return pl.pallas_call(
        qkv_kernel,
        grid=(groups // 2,),
        in_specs=[
            whole((rows, D)),
            whole((1, D)),
            whole((1, D)),
            pl.BlockSpec((D, 256), lambda i: (0, i)),
            pl.BlockSpec((D, 256), lambda i: (0, 4 + i)),
            pl.BlockSpec((D, 256), lambda i: (0, 8 + i)),
            pl.BlockSpec((1, 256), lambda i: (0, i)),
            pl.BlockSpec((1, 256), lambda i: (0, 4 + i)),
        ],
        out_specs=[whole((rows, D)), pl.BlockSpec((2, rows, 384), lambda i: (i, 0, 0))],
        out_shape=[
            jax.ShapeDtypeStruct((rows, D), bf16),
            jax.ShapeDtypeStruct((groups, rows, 384), bf16),
        ],
        compiler_params=params(40),
        cost_estimate=cost(2 * rows * D * 3 * D, 12 << 20),
        name="norm_qkv",
    )(x, gain, bias, weight, weight, weight, qv_bias, qv_bias)


def qkv_exchange_kernel(
    blks, x_ref, gain_ref, bias_ref, bq_ref, bv_ref, w_ref, g_ref,
    h_ref, top, bottom, moved, groups, w_all, landing, w_sem, sends, receives, own_sem, rim_sem,
):
    me = lax.axis_index("blk")
    chips = blks // 2
    chip, core = me // 2, me % 2
    order = [lax.rem(chip + 1 + i, chips) for i in range(chips)]

    def weight(i, part):
        columns = pl.ds(pl.multiple_of(D * part + 256 * order[i], 256), 256)
        return pltpu.make_async_copy(w_ref.at[:, columns], w_all.at[i, part], w_sem.at[i, part])

    def to(place):
        return pltpu.make_async_remote_copy(
            src_ref=groups.at[place], dst_ref=moved.at[me],
            send_sem=sends.at[place], recv_sem=receives.at[me],
            device_id={"blk": place}, device_id_type=MESH,
        )

    def own():
        return pltpu.make_async_copy(groups.at[me], moved.at[me], own_sem)

    for i in range(chips):
        for part in range(3):
            weight(i, part).start()
    greet(blks)
    rims = Rims(blks, g_ref, top, bottom, landing, rim_sem)
    rims.start()
    normed, _ = layer_stats(x_ref[...].astype(f32))
    h_ref[...] = (normed * gain_ref[...] + bias_ref[...]).astype(bf16)
    for i in range(chips):
        for part in range(3):
            weight(i, part).wait()
        columns = pl.ds(pl.multiple_of(256 * order[i], 256), 256)
        hidden = h_ref[...]
        query = ((dot(hidden, w_all[i, 0]) + bq_ref[:, columns]) * (HEAD**-0.5 * LOG2E)).astype(bf16)
        key = dot(hidden, w_all[i, 1]).astype(bf16)
        value = (dot(hidden, w_all[i, 2]) + bv_ref[:, columns]).astype(bf16)
        for half in range(2):
            lanes = slice(128 * half, 128 * half + 128)
            place = 2 * order[i] + half
            groups[place, :, 0:128] = query[:, lanes]
            groups[place, :, 128:256] = key[:, lanes]
            groups[place, :, 256:384] = value[:, lanes]
        if i < chips - 1:
            to(2 * order[i]).start()
            to(2 * order[i] + 1).start()
    to(2 * chip + 1 - core).start()
    own().start()
    for step in range(1, blks):
        other = lax.rem(me + step, blks)
        to(other).wait_send()
        pltpu.make_async_remote_copy(
            src_ref=groups.at[other], dst_ref=moved.at[other],
            send_sem=sends.at[other], recv_sem=receives.at[other],
            device_id={"blk": other}, device_id_type=MESH,
        ).wait_recv()
    own().wait()
    rims.wait()


def project_qkv_exchanged(x, gain, bias, weight, qv_bias, g, collective_id):
    rows = x.shape[0]
    blks = lax.axis_size("blk")
    anywhere = pl.BlockSpec(memory_space=pl.ANY)
    vmem = pl.BlockSpec(memory_space=pltpu.VMEM)
    dma = pltpu.SemaphoreType.DMA
    return pl.pallas_call(
        functools.partial(qkv_exchange_kernel, blks),
        in_specs=[vmem] * 5 + [anywhere, anywhere],
        out_specs=[vmem, vmem, vmem, anywhere],
        out_shape=[
            jax.ShapeDtypeStruct((rows, D), bf16),
            jax.ShapeDtypeStruct((WIDE_RIM, D), bf16),
            jax.ShapeDtypeStruct((WIDE_RIM, D), bf16),
            jax.ShapeDtypeStruct((blks, rows, 384), bf16),
        ],
        scratch_shapes=[
            pltpu.VMEM((blks, rows, 384), bf16),
            pltpu.VMEM((blks // 2, 3, D, 256), bf16),
            pltpu.VMEM((2, WIDE_RIM, D), bf16),
            dma((blks // 2, 3)),
            dma((blks,)),
            dma((blks,)),
            dma,
            dma((4,)),
        ],
        compiler_params=params(60, collective_id=collective_id, has_side_effects=True),
        name="norm_qkv",
    )(x, gain, bias, qv_bias[:, :D], qv_bias[:, D:], weight, g)


def attention_kernel(starts, counts, qkv, o_ref, lse_ref, value_t):
    step = pl.program_id(0)

    @pl.when(step == 0)
    def _():
        value_t[...] = qkv[:, 256:384].T

    own = pl.ds(pl.multiple_of(step * BLOCK, BLOCK), BLOCK)
    query = qkv[own, 0:128]
    lane = lax.broadcasted_iota(jnp.int32, (BLOCK, 128), 1)
    zero = jnp.zeros_like(query)
    queries = [jnp.where(lane < HEAD, query, zero), jnp.where(lane >= HEAD, query, zero)]
    first, count = starts[step], counts[step]
    for blocks in IMAGE_BLOCKS:

        @pl.when(count == blocks)
        def _(blocks=blocks):
            image = pl.ds(pl.multiple_of(first * BLOCK, BLOCK), blocks * BLOCK)
            keys = qkv[image, 128:256]
            scores = [dot_nt(keys, part) for part in queries]
            outs, logs = [], []
            for head in range(2):
                peak = jnp.max(scores[head], axis=0, keepdims=True)
                grown = jnp.exp2(scores[head] - peak)
                total = jnp.sum(grown, axis=0, keepdims=True)
                rows = slice(HEAD * head, HEAD * head + HEAD)
                outs.append(dot(value_t[rows, image], grown.astype(bf16)) * (1.0 / total))
                logs.append(peak + jnp.log2(total))
            o_ref[...] = jnp.concatenate(outs, axis=0).T.astype(bf16)
            lse_ref[...] = jnp.concatenate(logs + [jnp.zeros((6, BLOCK), f32)], axis=0)


def attention(starts, counts, qkv):
    length = qkv.shape[0]
    pairs = 100 * 2 * BLOCK * BLOCK
    return pl.pallas_call(
        attention_kernel,
        grid_spec=pltpu.PrefetchScalarGridSpec(
            num_scalar_prefetch=2,
            grid=(length // BLOCK,),
            in_specs=[whole((length, 384))],
            out_specs=[
                pl.BlockSpec((BLOCK, 128), lambda i, *_: (i, 0)),
                pl.BlockSpec((8, BLOCK), lambda i, *_: (0, i)),
            ],
            scratch_shapes=[pltpu.VMEM((128, length), bf16)],
        ),
        out_shape=[
            jax.ShapeDtypeStruct((length, 128), bf16),
            jax.ShapeDtypeStruct((8, length), f32),
        ],
        compiler_params=params(40),
        cost_estimate=cost(4 * HEAD * pairs, 5 << 20, pairs),
        name="attention",
    )(starts, counts, qkv)


def attention_grad_kernel(
    starts, counts, qkv, do_ref, o_ref, lse, out_ref, query_m, do_m, key_t, dq_t, delta
):
    step = pl.program_id(0)
    length = do_ref.shape[0]
    lane = lax.broadcasted_iota(jnp.int32, (BLOCK, 128), 1)
    low = lane < HEAD

    @pl.when(step == 0)
    def _():
        key_t[...] = qkv[:, 128:256].T
        dq_t[...] = jnp.zeros_like(dq_t)

        def prepare(i, _):
            rows = pl.ds(pl.multiple_of(i * BLOCK, BLOCK), BLOCK)
            grad = do_ref[rows, :]
            product = (grad.astype(f32) * o_ref[rows, :].astype(f32)).T
            delta[0:1, rows] = jnp.sum(product[:HEAD], axis=0, keepdims=True)
            delta[1:2, rows] = jnp.sum(product[HEAD:], axis=0, keepdims=True)
            query = qkv[rows, 0:128]
            zero = jnp.zeros_like(query)
            query_m[0, rows, :] = jnp.where(low, query, zero)
            query_m[1, rows, :] = jnp.where(low, zero, query)
            do_m[0, rows, :] = jnp.where(low, grad, zero)
            do_m[1, rows, :] = jnp.where(low, zero, grad)
            return 0

        lax.fori_loop(0, length // BLOCK, prepare, 0)

    own = pl.ds(pl.multiple_of(step * BLOCK, BLOCK), BLOCK)
    key = qkv[own, 128:256]
    value = qkv[own, 256:384]
    first, count = starts[step], counts[step]
    for blocks in IMAGE_BLOCKS:

        @pl.when(count == blocks)
        def _(blocks=blocks):
            image = pl.ds(pl.multiple_of(first * BLOCK, BLOCK), blocks * BLOCK)
            dk = dv = None
            for head in range(2):
                rows = slice(HEAD * head, HEAD * head + HEAD)
                query, grad = query_m[head, image, :], do_m[head, image, :]
                scores = dot_nt(key, query)
                value_grad = dot_nt(value, grad)
                weights = jnp.exp2(scores - lse[head : head + 1, image])
                score_grad = (weights * (value_grad - delta[head : head + 1, image])).astype(bf16)
                dv_part = dot(weights.astype(bf16), grad)
                dk_part = dot(score_grad, query)
                dv = dv_part if dv is None else dv + dv_part
                dk = dk_part if dk is None else dk + dk_part
                dq_t[rows, image] += dot(key_t[rows, own], score_grad)
            out_ref[own, 128:256] = (dk * (1.0 / LOG2E)).astype(bf16)
            out_ref[own, 256:384] = dv.astype(bf16)

    @pl.when(step == pl.num_programs(0) - 1)
    def _():
        def finish(i, _):
            rows = pl.ds(pl.multiple_of(i * BLOCK, BLOCK), BLOCK)
            out_ref[rows, 0:128] = dq_t[:, rows].T.astype(bf16) * jnp.asarray(HEAD**-0.5, bf16)
            return 0

        lax.fori_loop(0, length // BLOCK, finish, 0)


def attention_grad(starts, counts, qkv, do, o, lse):
    length = qkv.shape[0]
    pairs = 100 * 2 * BLOCK * BLOCK
    return pl.pallas_call(
        attention_grad_kernel,
        grid_spec=pltpu.PrefetchScalarGridSpec(
            num_scalar_prefetch=2,
            grid=(length // BLOCK,),
            in_specs=[
                whole((length, 384)),
                whole((length, 128)),
                whole((length, 128)),
                whole((8, length)),
            ],
            out_specs=whole((length, 384)),
            scratch_shapes=[
                pltpu.VMEM((2, length, 128), bf16),
                pltpu.VMEM((2, length, 128), bf16),
                pltpu.VMEM((128, length), bf16),
                pltpu.VMEM((128, length), f32),
                pltpu.VMEM((8, length), f32),
            ],
        ),
        out_shape=jax.ShapeDtypeStruct((length, 384), bf16),
        compiler_params=params(56),
        cost_estimate=cost(10 * HEAD * pairs, 12 << 20, pairs),
        name="attention_grad",
    )(starts, counts, qkv, do, o, lse)


FF_TILE = 512


def mlp_kernel(
    blks, o_ref, x_ref, wp_ref, pb_ref, gain_ref, bias_ref, wu_ref, ub_ref, wd_ref, db_ref,
    x1_ref, h_ref, act_ref, slope_ref, out_ref, top, bottom, total, landing, rim_sem,
):
    step = pl.program_id(0)

    @pl.when(step == 0)
    def _():
        greet(blks)
        attended = jnp.concatenate([o_ref[i] for i in range(o_ref.shape[0])], axis=1)
        x1 = x_ref[...].astype(f32) + dot(attended, wp_ref[...]) + pb_ref[...]
        x1_ref[...] = x1
        normed, _ = layer_stats(x1)
        h_ref[...] = (normed * gain_ref[...] + bias_ref[...]).astype(bf16)
        total[...] = x1 + db_ref[...]

    raised = dot(h_ref[...], wu_ref[...]) + ub_ref[...]
    cumulative, weighted = gelu_parts(raised)
    act = (raised * cumulative).astype(bf16)
    act_ref[...] = act
    slope_ref[...] = (cumulative + weighted).astype(bf16)
    total[...] += dot(act, wd_ref[...])

    @pl.when(step == pl.num_programs(0) - 1)
    def _():
        out_ref[...] = total[...].astype(bf16)
        rims = Rims(blks, out_ref, top, bottom, landing, rim_sem)
        rims.start()
        rims.wait()


def mlp(o, x, wp, pb, gain, bias, wu, ub, wd, db, collective_id):
    rows = x.shape[0]
    groups = o.shape[0]
    tile = 2 * FF_TILE
    return pl.pallas_call(
        functools.partial(mlp_kernel, lax.axis_size("blk")),
        grid=(FF // tile,),
        in_specs=[
            whole((groups, rows, 128)),
            whole((rows, D)),
            whole((D, D)),
            whole((1, D)),
            whole((1, D)),
            whole((1, D)),
            pl.BlockSpec((D, tile), lambda i: (0, i)),
            pl.BlockSpec((1, tile), lambda i: (0, i)),
            pl.BlockSpec((tile, D), lambda i: (i, 0)),
            whole((1, D)),
        ],
        out_specs=[
            whole((rows, D)),
            whole((rows, D)),
            pl.BlockSpec((rows, tile), lambda i: (0, i)),
            pl.BlockSpec((rows, tile), lambda i: (0, i)),
            whole((rows, D)),
            whole((RIM, D)),
            whole((RIM, D)),
        ],
        out_shape=[
            jax.ShapeDtypeStruct((rows, D), f32),
            jax.ShapeDtypeStruct((rows, D), bf16),
            jax.ShapeDtypeStruct((rows, FF), bf16),
            jax.ShapeDtypeStruct((rows, FF), bf16),
            jax.ShapeDtypeStruct((rows, D), bf16),
            jax.ShapeDtypeStruct((RIM, D), bf16),
            jax.ShapeDtypeStruct((RIM, D), bf16),
        ],
        scratch_shapes=[
            pltpu.VMEM((rows, D), f32),
            pltpu.VMEM((2, RIM, D), bf16),
            pltpu.SemaphoreType.DMA((4,)),
        ],
        compiler_params=params(56, collective_id=collective_id, has_side_effects=True),
        cost_estimate=cost(2 * rows * D * (D + 2 * FF), 34 << 20, rows * FF),
        name="proj_norm_mlp",
    )(o, x, wp, pb, gain, bias, wu, ub, wd, db)


def mlp_grad_kernel(
    dy_ref, dm_ref, slope_ref, wd_ref, wu_ref, x1_ref, gain_ref, wp_ref,
    du_ref, dub_ref, dx1_ref, da_ref, do_ref, sums_ref, total,
):
    step = pl.program_id(0)

    @pl.when(step == 0)
    def _():
        total[...] = jnp.zeros_like(total)

    act_grad = dot_nt(dm_ref[...], wd_ref[...])
    raised_low = (act_grad * slope_ref[...].astype(f32)).astype(bf16)
    du_ref[...] = raised_low
    dub_ref[...] = column_sums(raised_low.astype(f32))
    total[...] += dot_nt(raised_low, wu_ref[...])

    @pl.when(step == pl.num_programs(0) - 1)
    def _():
        grad = total[...]
        normed, scale_inv = layer_stats(x1_ref[...])
        dx1 = dy_ref[...] + layer_backward(grad, normed, scale_inv, gain_ref[...])
        dx1_ref[...] = dx1
        low = dx1.astype(bf16)
        da_ref[...] = low
        sums_ref[0:1, :] = column_sums(low.astype(f32))
        sums_ref[1:2, :] = column_sums(grad * normed)
        sums_ref[2:3, :] = column_sums(grad)
        sums_ref[3:4, :] = column_sums(dm_ref[...].astype(f32))
        sums_ref[4:8, :] = jnp.zeros((4, D), f32)
        attended_grad = dot_nt(low, wp_ref[...]).astype(bf16)
        for i in range(do_ref.shape[0]):
            do_ref[i] = attended_grad[:, 128 * i : 128 * i + 128]


def mlp_grad(dy, dm, slope, wd, wu, x1, gain, wp):
    rows = dy.shape[0]
    groups = D // 128
    tile = 2 * FF_TILE
    return pl.pallas_call(
        mlp_grad_kernel,
        grid=(FF // tile,),
        in_specs=[
            whole((rows, D)),
            whole((rows, D)),
            pl.BlockSpec((rows, tile), lambda i: (0, i)),
            pl.BlockSpec((tile, D), lambda i: (i, 0)),
            pl.BlockSpec((D, tile), lambda i: (0, i)),
            whole((rows, D)),
            whole((1, D)),
            whole((D, D)),
        ],
        out_specs=[
            pl.BlockSpec((rows, tile), lambda i: (0, i)),
            pl.BlockSpec((1, tile), lambda i: (0, i)),
            whole((rows, D)),
            whole((rows, D)),
            whole((groups, rows, 128)),
            whole((8, D)),
        ],
        out_shape=[
            jax.ShapeDtypeStruct((rows, FF), bf16),
            jax.ShapeDtypeStruct((1, FF), f32),
            jax.ShapeDtypeStruct((rows, D), f32),
            jax.ShapeDtypeStruct((rows, D), bf16),
            jax.ShapeDtypeStruct((groups, rows, 128), bf16),
            jax.ShapeDtypeStruct((8, D), f32),
        ],
        scratch_shapes=[pltpu.VMEM((rows, D), f32)],
        compiler_params=params(56),
        cost_estimate=cost(2 * rows * D * (D + 2 * FF), 34 << 20),
        name="mlp_norm_proj_grad",
    )(dy, dm, slope, wd, wu, x1, gain, wp)


def down_weight_kernel(act_ref, dm_ref, dwd_ref):
    dwd_ref[...] = dot_tn(act_ref[...], dm_ref[...]).astype(bf16)


def down_weight_grad_of(act, dm):
    rows = dm.shape[0]
    tile = FF_TILE
    return pl.pallas_call(
        down_weight_kernel,
        grid=(FF // tile,),
        in_specs=[pl.BlockSpec((rows, tile), lambda i: (0, i)), whole((rows, D))],
        out_specs=pl.BlockSpec((tile, D), lambda i: (i, 0)),
        out_shape=jax.ShapeDtypeStruct((FF, D), bf16),
        compiler_params=params(32),
        cost_estimate=cost(2 * rows * D * FF, 13 << 20),
        name="down_weight_grad",
    )(act, dm)


def conv_weight_kernel(x_ref, taps_ref, dw_ref, x_t):
    @pl.when(pl.program_id(0) == 0)
    def _():
        x_t[...] = x_ref[...].T

    for tap in range(3):
        dw_ref[D * tap : D * tap + D, :] = dot(x_t[...], taps_ref[tap]).astype(bf16)


def conv_weight_grad_of(x, taps):
    rows = x.shape[0]
    return pl.pallas_call(
        conv_weight_kernel,
        grid=(3,),
        in_specs=[whole((rows, D)), pl.BlockSpec((3, rows, C), lambda i: (i, 0, 0))],
        out_specs=pl.BlockSpec((3 * D, C), lambda i: (i, 0)),
        out_shape=jax.ShapeDtypeStruct((9 * D, C), bf16),
        scratch_shapes=[pltpu.VMEM((D, rows), bf16)],
        compiler_params=params(32),
        cost_estimate=cost(2 * rows * D * 9 * C, 9 << 20),
        name="conv_weight_grad",
    )(x, taps)


def exchange_semaphores(blks):
    count = max(blks, 1)
    return [
        pltpu.SemaphoreType.DMA((count,)),
        pltpu.SemaphoreType.DMA((count,)),
        pltpu.SemaphoreType.DMA,
    ]


def exchange_params(blks, megabytes, collective_id):
    if blks:
        return params(megabytes, collective_id=collective_id, has_side_effects=True)
    return params(megabytes)


def late_weights_kernel(h_ref, du_ref, o_ref, da_ref, dwu_ref, dwp_ref, h_t):
    @pl.when(pl.program_id(0) == 0)
    def _():
        h_t[...] = h_ref[...].T
        attended = jnp.concatenate([o_ref[i] for i in range(o_ref.shape[0])], axis=1)
        dwp_ref[...] = dot_tn(attended, da_ref[...]).astype(bf16)

    dwu_ref[...] = dot(h_t[...], du_ref[...]).astype(bf16)


def late_weights(h, du, o, da):
    rows = h.shape[0]
    groups = D // 128
    tile = FF_TILE
    return pl.pallas_call(
        late_weights_kernel,
        grid=(FF // tile,),
        in_specs=[
            whole((rows, D)),
            pl.BlockSpec((rows, tile), lambda i: (0, i)),
            whole((groups, rows, 128)),
            whole((rows, D)),
        ],
        out_specs=[pl.BlockSpec((D, tile), lambda i: (0, i)), whole((D, D))],
        out_shape=[jax.ShapeDtypeStruct((D, FF), bf16), jax.ShapeDtypeStruct((D, D), bf16)],
        scratch_shapes=[pltpu.VMEM((D, rows), bf16)],
        compiler_params=params(40),
        cost_estimate=cost(2 * rows * D * (FF + D), 18 << 20),
        name="up_proj_weight_grads",
    )(h, du, o, da)


def weights_kernel(
    blks, act_ref, dm_ref, h_ref, du_ref, x_ref, taps_ref, o_ref, da_ref, sent,
    dw_ref, dwp_ref, moved, down_keep, down_send, up_keep, up_send,
    down, up, down_near, up_near, h_t, x_t, ex_send, ex_recv, ex_own, ds, dr, us, ur, do_sem, uo_sem,
):
    step = pl.program_id(0)
    steps = FF // FF_TILE
    blk = lax.axis_index("blk")
    core, x, y = blk % 2, (blk // 2) % 2, blk // 4
    exchange = (blks, sent, moved, ex_send, ex_recv, ex_own)

    def to_pair(source, target, sent_sem, received):
        return pltpu.make_async_remote_copy(
            src_ref=source, dst_ref=target, send_sem=sent_sem, recv_sem=received,
            device_id={"blk": blk + 1 - 2 * core}, device_id_type=MESH,
        )

    def down_copy(i):
        return to_pair(down.at[i, 1 - core], down_near.at[i], ds.at[i], dr.at[i])

    def up_columns(t):
        return pl.ds(pl.multiple_of(t * FF_TILE, FF_TILE), FF_TILE)

    def up_copy(t):
        return to_pair(up.at[:, 1 - core, :, up_columns(t)], up_near.at[:, :, up_columns(t)], us.at[t], ur.at[t])

    def down_out(i, keep):
        return pltpu.make_async_copy(
            down.at[i, core], (down_keep if keep else down_send).at[i // 2], do_sem.at[i]
        )

    def up_out(t, i, keep):
        return pltpu.make_async_copy(
            up.at[i, core, :, up_columns(t)],
            (up_keep if keep else up_send).at[i % 2, :, up_columns(t)],
            uo_sem.at[t, i],
        )

    def add_down(i):
        down_copy(i).wait_recv()
        down[i, core] = (down[i, core].astype(f32) + down_near[i].astype(f32)).astype(bf16)
        for keep in (True, False):

            @pl.when((i % 2 == x) == keep)
            def _(keep=keep):
                down_out(i, keep).start()

    def add_up(t):
        up_copy(t).wait_recv()
        columns = up_columns(t)
        for i in range(4):
            up[i, core, :, columns] = (
                up[i, core, :, columns].astype(f32) + up_near[i, :, columns].astype(f32)
            ).astype(bf16)
            for keep in (True, False):

                @pl.when((i // 2 == y) == keep)
                def _(i=i, keep=keep):
                    up_out(t, i, keep).start()

    @pl.when(step == 0)
    def _():
        greet(blks)
        exchange_start(*exchange)
        h_t[...] = h_ref[...].T
        x_t[...] = x_ref[...].T

    down[step // 2, step % 2] = dot_tn(act_ref[...], dm_ref[...]).astype(bf16)

    @pl.when(step % 2 != core)
    def _():
        down_copy(step // 2).start()

    up[:, :, :, up_columns(step)] = (
        dot(h_t[...], du_ref[...]).astype(bf16).reshape(4, 2, D // 8, FF_TILE)
    )
    up_copy(step).start()

    @pl.when(step < 3)
    def _():
        for tap in range(3):
            dw_ref[D * tap : D * tap + D, :] = dot(x_t[...], taps_ref[tap]).astype(bf16)

    @pl.when(step == 3)
    def _():
        attended = jnp.concatenate([o_ref[i] for i in range(o_ref.shape[0])], axis=1)
        dwp_ref[...] = dot_tn(attended, da_ref[...]).astype(bf16)

    @pl.when(step >= 1)
    def _():
        add_up(step - 1)

    @pl.when((step >= 2) & (step % 2 == 0))
    def _():
        add_down(step // 2 - 1)

    @pl.when(step == steps - 1)
    def _():
        add_up(steps - 1)
        add_down(3)
        exchange_wait(*exchange)
        for t in range(steps):
            up_copy(t).wait_send()
            for i in range(4):
                up_out(t, i, True).wait()
        for i in range(4):
            down_copy(i).wait_send()
            down_out(i, True).wait()


def weights(act, dm, h, du, x, taps, o, da, sent, blks, collective_id):
    rows = h.shape[0]
    groups = D // 128
    tile = FF_TILE
    steps = FF // tile
    anywhere = pl.BlockSpec(memory_space=pl.ANY)
    third = lambda i: jnp.minimum(i, 2)
    dma = pltpu.SemaphoreType.DMA
    half_down, half_up = (2, FF // 8, D), (2, D // 8, FF)
    return pl.pallas_call(
        functools.partial(weights_kernel, blks),
        grid=(steps,),
        in_specs=[
            pl.BlockSpec((rows, tile), lambda i: (0, i)),
            whole((rows, D)),
            whole((rows, D)),
            pl.BlockSpec((rows, tile), lambda i: (0, i)),
            whole((rows, D)),
            pl.BlockSpec((3, rows, C), lambda i: (third(i), 0, 0)),
            whole((groups, rows, 128)),
            whole((rows, D)),
            anywhere,
        ],
        out_specs=[pl.BlockSpec((3 * D, C), lambda i: (third(i), 0)), whole((D, D))]
        + [anywhere] * 5,
        out_shape=[
            jax.ShapeDtypeStruct(shape, bf16)
            for shape in ((9 * D, C), (D, D), sent.shape, half_down, half_down, half_up, half_up)
        ],
        scratch_shapes=[
            pltpu.VMEM((4, 2, FF // 8, D), bf16),
            pltpu.VMEM((4, 2, D // 8, FF), bf16),
            pltpu.VMEM((4, FF // 8, D), bf16),
            pltpu.VMEM((4, D // 8, FF), bf16),
            pltpu.VMEM((D, rows), bf16),
            pltpu.VMEM((D, rows), bf16),
        ]
        + exchange_semaphores(blks)
        + [dma((4,)), dma((4,)), dma((steps,)), dma((steps,)), dma((4,)), dma((steps, 4))],
        compiler_params=exchange_params(blks, 62, collective_id),
        cost_estimate=cost(2 * rows * D * (2 * FF + D + 9 * C), 50 << 20),
        name="weight_grads",
    )(act, dm, h, du, x, taps, o, da, sent)


def qkv_grad_kernel(
    g_ref, wq_ref, wk_ref, wv_ref, h_ref, dx1_ref, x_ref, gain_ref,
    dw_ref, dqb_ref, dvb_ref, dx_ref, sums_ref, h_t, total,
):
    step = pl.program_id(0)

    @pl.when(step == 0)
    def _():
        h_t[...] = h_ref[...].T
        total[...] = jnp.zeros_like(total)

    for part, w_ref in enumerate((wq_ref, wk_ref, wv_ref)):
        lanes = slice(128 * part, 128 * part + 128)
        grad = jnp.concatenate([g_ref[0, :, lanes], g_ref[1, :, lanes]], axis=1)
        total[...] += dot_nt(grad, w_ref[...])
        dw_ref[part] = dot(h_t[...], grad).astype(bf16)
        if part == 0:
            dqb_ref[...] = column_sums(grad.astype(f32))
        if part == 2:
            dvb_ref[...] = column_sums(grad.astype(f32))

    @pl.when(step == pl.num_programs(0) - 1)
    def _():
        grad = total[...]
        normed, scale_inv = layer_stats(x_ref[...].astype(f32))
        dx_ref[...] = dx1_ref[...] + layer_backward(grad, normed, scale_inv, gain_ref[...])
        sums_ref[0:1, :] = column_sums(grad * normed)
        sums_ref[1:2, :] = column_sums(grad)
        sums_ref[2:8, :] = jnp.zeros((6, D), f32)


def qkv_grad(g, weight, h, dx1, x, gain):
    rows = x.shape[0]
    groups = D // 128
    return pl.pallas_call(
        qkv_grad_kernel,
        grid=(groups // 2,),
        in_specs=[
            pl.BlockSpec((2, rows, 384), lambda i: (i, 0, 0)),
            pl.BlockSpec((D, 256), lambda i: (0, i)),
            pl.BlockSpec((D, 256), lambda i: (0, 4 + i)),
            pl.BlockSpec((D, 256), lambda i: (0, 8 + i)),
            whole((rows, D)),
            whole((rows, D)),
            whole((rows, D)),
            whole((1, D)),
        ],
        out_specs=[
            pl.BlockSpec((3, D, 256), lambda i: (0, 0, i)),
            pl.BlockSpec((1, 256), lambda i: (0, i)),
            pl.BlockSpec((1, 256), lambda i: (0, i)),
            whole((rows, D)),
            whole((8, D)),
        ],
        out_shape=[
            jax.ShapeDtypeStruct((3, D, D), bf16),
            jax.ShapeDtypeStruct((1, D), f32),
            jax.ShapeDtypeStruct((1, D), f32),
            jax.ShapeDtypeStruct((rows, D), f32),
            jax.ShapeDtypeStruct((8, D), f32),
        ],
        scratch_shapes=[pltpu.VMEM((D, rows), bf16), pltpu.VMEM((rows, D), f32)],
        compiler_params=params(48),
        cost_estimate=cost(4 * rows * D * 3 * D, 24 << 20),
        name="qkv_norm_grad",
    )(g, weight, weight, weight, h, dx1, x, gain)


def row_segments(rows, rim):
    count = rows // BLOCK
    pieces = []
    for block in range(count):
        first = block * BLOCK - (rim if block == 0 else 0)
        last = (block + 1) * BLOCK + (rim if block == count - 1 else 0)
        pieces.append((first, last - first, block))
    return pieces


def shifted_rows(start, shift, size):
    return pl.ds(pl.multiple_of(start + shift, UNIT), size)


def conv_kernel(widths, x_ref, top_ref, bottom_ref, flags, w_ref, z_ref, sums_ref, x_ext, left, right, centre):
    step = pl.program_id(0)
    rows = x_ref.shape[0]
    extent = rows + 2 * RIM

    @pl.when(step == 0)
    def _():
        x_ext[0:RIM, :] = top_ref[...]
        x_ext[RIM : RIM + rows, :] = x_ref[...]
        x_ext[RIM + rows :, :] = bottom_ref[...]
        left[...] = jnp.zeros_like(left)
        right[...] = jnp.zeros_like(right)

    source = x_ext[...]
    left[8 : 8 + extent, :] = dot(source, w_ref[0:D, :])
    right[8 : 8 + extent, :] = dot(source, w_ref[2 * D : 3 * D, :])
    centre[...] = (
        dot(source, w_ref[D : 2 * D, :])
        + flags[:, 2:3] * left[7 : 7 + extent, :]
        + flags[:, 3:4] * right[9 : 9 + extent, :]
    )
    for first, size, block in row_segments(rows, 0):
        own = slice(first, first + size)
        width = widths[block]
        for tap in range(3):

            @pl.when(step == tap)
            def _(tap=tap, first=first, size=size, own=own, width=width):
                found = centre[shifted_rows(RIM + first, (tap - 1) * width, size), :]
                if tap == 0:
                    z_ref[own, :] = flags[RIM + first : RIM + first + size, 0:1] * found
                elif tap == 1:
                    z_ref[own, :] += found
                else:
                    z_ref[own, :] += flags[RIM + first : RIM + first + size, 1:2] * found

    @pl.when(step == 2)
    def _():
        z = z_ref[...]
        sums_ref[0:1, :] = column_sums(z)
        sums_ref[1:2, :] = column_sums(z * z)
        sums_ref[2:8, :] = jnp.zeros((6, C), f32)


def conv(widths, x, top, bottom, flags, weight):
    rows = x.shape[0]
    extent = rows + 2 * RIM
    return pl.pallas_call(
        conv_kernel,
        grid_spec=pltpu.PrefetchScalarGridSpec(
            num_scalar_prefetch=1,
            grid=(3,),
            in_specs=[
                whole((rows, D)),
                whole((RIM, D)),
                whole((RIM, D)),
                whole((extent, 8)),
                pl.BlockSpec((3 * D, C), lambda i, *_: (i, 0)),
            ],
            out_specs=[whole((rows, C)), whole((8, C))],
            scratch_shapes=[
                pltpu.VMEM((extent, D), bf16),
                pltpu.VMEM((extent + 16, C), f32),
                pltpu.VMEM((extent + 16, C), f32),
                pltpu.VMEM((extent, C), f32),
            ],
        ),
        out_shape=[jax.ShapeDtypeStruct((rows, C), f32), jax.ShapeDtypeStruct((8, C), f32)],
        compiler_params=params(40),
        cost_estimate=cost(2 * extent * 9 * D * C, 8 << 20),
        name="conv",
    )(widths, x, top, bottom, flags, weight)


def spread_kernel(widths, g_ref, top_ref, bottom_ref, flags, out_ref, upper, lower, g_ext):
    rows = g_ref.shape[0]
    extent = rows + 2 * WIDE_RIM
    g_ext[0:WIDE_RIM, :] = top_ref[...].astype(f32)
    g_ext[WIDE_RIM : WIDE_RIM + rows, :] = g_ref[...].astype(f32)
    g_ext[WIDE_RIM + rows :, :] = bottom_ref[...].astype(f32)
    inner = slice(8, extent - 8)
    has_left, has_right = flags[inner, 2:3], flags[inner, 3:4]
    for i, target in enumerate((upper, lower)):
        near = g_ext[:, 2 * i * C : (2 * i + 1) * C]
        far = g_ext[:, (2 * i + 1) * C : (2 * i + 2) * C]
        target[0:8, :] = jnp.zeros((8, C), f32)
        target[extent - 8 :, :] = jnp.zeros((8, C), f32)
        target[inner, :] = (
            (1.0 - 0.25 * has_left) * near[inner, :]
            + (1.0 - 0.25 * has_right) * far[inner, :]
            + 0.25 * has_right * g_ext[9 : extent - 7, 2 * i * C : (2 * i + 1) * C]
            + 0.25 * has_left * g_ext[7 : extent - 9, (2 * i + 1) * C : (2 * i + 2) * C]
        )
    for first, size, block in row_segments(rows, RIM):
        width = widths[block]
        here = WIDE_RIM + first
        has_up, has_down = flags[here : here + size, 0:1], flags[here : here + size, 1:2]
        out_ref[RIM + first : RIM + first + size, :] = (
            (1.0 - 0.25 * has_up) * upper[here : here + size, :]
            + (1.0 - 0.25 * has_down) * lower[here : here + size, :]
            + 0.25 * has_down * upper[shifted_rows(here, width, size), :]
            + 0.25 * has_up * lower[shifted_rows(here, -width, size), :]
        )


def spread(widths, g, top, bottom, flags):
    rows = g.shape[0]
    extent = rows + 2 * WIDE_RIM
    return pl.pallas_call(
        spread_kernel,
        grid_spec=pltpu.PrefetchScalarGridSpec(
            num_scalar_prefetch=1,
            grid=(1,),
            in_specs=[
                whole((rows, D)),
                whole((WIDE_RIM, D)),
                whole((WIDE_RIM, D)),
                whole((extent, 8)),
            ],
            out_specs=whole((rows + 2 * RIM, C)),
            scratch_shapes=[
                pltpu.VMEM((extent, C), f32),
                pltpu.VMEM((extent, C), f32),
                pltpu.VMEM((extent, D), f32),
            ],
        ),
        out_shape=jax.ShapeDtypeStruct((rows + 2 * RIM, C), f32),
        compiler_params=params(40),
        cost_estimate=cost(20 * extent * D, 3 << 20),
        name="upsample_grad",
    )(widths, g, top, bottom, flags)


def batch_kernel(
    widths, z_ref, top_ref, bottom_ref, dact_ref, flags, mean_ref, inv_ref, gain_ref, bias_ref,
    up_ref, normed_ref, dbn_ref, sums_ref, act, mixed,
):
    rows = z_ref.shape[0]
    z = jnp.concatenate([top_ref[...], z_ref[...], bottom_ref[...]], axis=0)
    normed = (z - mean_ref[...]) * inv_ref[...]
    normed_ref[...] = normed
    pre = normed * gain_ref[...] + bias_ref[...]
    cumulative, weighted = gelu_parts(pre)
    act[...] = (pre * cumulative).astype(bf16).astype(f32)
    dbn = dact_ref[...] * (cumulative + weighted)
    dbn_ref[...] = dbn
    own = slice(RIM, RIM + rows)
    sums_ref[0:1, :] = column_sums(dbn[own, :])
    sums_ref[1:2, :] = column_sums(dbn[own, :] * normed[own, :])
    sums_ref[2:8, :] = jnp.zeros((6, C), f32)
    for first, size, block in row_segments(rows, 0):
        width = widths[block]
        here = RIM + first
        outer = slice(here - 8, here + size + 8)
        for i in range(2):
            has = flags[outer, i : i + 1]
            mixed[...] = (1.0 - 0.25 * has) * act[outer, :] + 0.25 * has * act[
                pl.ds(pl.multiple_of(here - 8 + (2 * i - 1) * width, 8), size + 16), :
            ]
            for j in range(2):
                has = flags[here : here + size, 2 + j : 3 + j]
                up_ref[first : first + size, (2 * i + j) * C : (2 * i + j + 1) * C] = (
                    (1.0 - 0.25 * has) * mixed[8 : 8 + size, :]
                    + 0.25 * has * mixed[7 + 2 * j : 7 + 2 * j + size, :]
                ).astype(bf16)


def batch(widths, z, top, bottom, dact, flags, mean, inv, gain, bias):
    rows = z.shape[0]
    extent = rows + 2 * RIM
    return pl.pallas_call(
        batch_kernel,
        grid_spec=pltpu.PrefetchScalarGridSpec(
            num_scalar_prefetch=1,
            grid=(1,),
            in_specs=[
                whole((rows, C)),
                whole((RIM, C)),
                whole((RIM, C)),
                whole((extent, C)),
                whole((extent, 8)),
                whole((1, C)),
                whole((1, C)),
                whole((1, C)),
                whole((1, C)),
            ],
            out_specs=[
                whole((rows, D)),
                whole((extent, C)),
                whole((extent, C)),
                whole((8, C)),
            ],
            scratch_shapes=[pltpu.VMEM((extent, C), f32), pltpu.VMEM((BLOCK + 16, C), f32)],
        ),
        out_shape=[
            jax.ShapeDtypeStruct((rows, D), bf16),
            jax.ShapeDtypeStruct((extent, C), f32),
            jax.ShapeDtypeStruct((extent, C), f32),
            jax.ShapeDtypeStruct((8, C), f32),
        ],
        compiler_params=params(40),
        cost_estimate=cost(60 * extent * C, 4 << 20),
        name="batch_norm",
    )(widths, z, top, bottom, dact, flags, mean, inv, gain, bias)


def conv_grad_kernel(
    widths, dbn_ref, normed_ref, flags, scale_ref, shift_ref, slope_ref, w_ref, og_ref,
    taps, dy_ref, dm_ref, moved,
):
    step = pl.program_id(0)
    rows = og_ref.shape[0]
    extent = rows + 2 * RIM

    @pl.when(step == 0)
    def _():
        dz = scale_ref[...] * (dbn_ref[...] - shift_ref[...] - normed_ref[...] * slope_ref[...])
        dz = dz.astype(bf16).astype(f32)
        dy_ref[...] = og_ref[...].astype(f32)
        moved[0, 0:8, :] = jnp.zeros((8, C), f32)
        moved[0, 8 + extent :, :] = jnp.zeros((8, C), f32)
        moved[0, 8 : 8 + extent, :] = dz
        moved[1, 8 : 8 + extent, :] = flags[:, 3:4] * moved[0, 9 : 9 + extent, :]
        moved[2, 8 : 8 + extent, :] = flags[:, 2:3] * moved[0, 7 : 7 + extent, :]
        for first, size, block in row_segments(rows, 0):
            width = widths[block]
            here = RIM + first
            for row in range(3):
                for col, slot in enumerate((1, 0, 2)):
                    found = moved[slot, pl.ds(pl.multiple_of(8 + here + (1 - row) * width, 8), size), :]
                    if row == 0:
                        found = flags[here : here + size, 1:2] * found
                    if row == 2:
                        found = flags[here : here + size, 0:1] * found
                    taps[3 * row + col, first : first + size, :] = found.astype(bf16)

    for part in range(3):
        dy_ref[...] += dot_nt(taps[3 * step + part], w_ref[D * part : D * part + D, :])

    @pl.when(step == pl.num_programs(0) - 1)
    def _():
        dm_ref[...] = dy_ref[...].astype(bf16)


def conv_grad(widths, dbn, normed, flags, scale, shift, slope, weight, out_grad):
    rows = out_grad.shape[0]
    extent = rows + 2 * RIM
    return pl.pallas_call(
        conv_grad_kernel,
        grid_spec=pltpu.PrefetchScalarGridSpec(
            num_scalar_prefetch=1,
            grid=(3,),
            in_specs=[
                whole((extent, C)),
                whole((extent, C)),
                whole((extent, 8)),
                whole((1, C)),
                whole((1, C)),
                whole((1, C)),
                pl.BlockSpec((3 * D, C), lambda i, *_: (i, 0)),
                whole((rows, D)),
            ],
            out_specs=[whole((9, rows, C)), whole((rows, D)), whole((rows, D))],
            scratch_shapes=[pltpu.VMEM((3, extent + 16, C), f32)],
        ),
        out_shape=[
            jax.ShapeDtypeStruct((9, rows, C), bf16),
            jax.ShapeDtypeStruct((rows, D), f32),
            jax.ShapeDtypeStruct((rows, D), bf16),
        ],
        compiler_params=params(48),
        cost_estimate=cost(2 * rows * 9 * D * C, 12 << 20),
        name="conv_grad",
    )(widths, dbn, normed, flags, scale, shift, slope, weight, out_grad)


def small_sum_kernel(scatter, blks, seqs, rimmed, x_ref, *refs):
    blk, seq = lax.axis_index("blk"), lax.axis_index("seq")
    if rimmed:
        z_ref, out_ref, top, bottom, *refs = refs
    else:
        out_ref, *refs = refs
    first, second, sends, receives, sends2, receives2 = refs[:6]
    barrier = pltpu.get_barrier_semaphore()
    for step in range(1, blks):
        pl.semaphore_signal(
            barrier, inc=1, device_id={"blk": lax.rem(blk + step, blks)}, device_id_type=MESH
        )
    for step in range(1, seqs):
        pl.semaphore_signal(
            barrier, inc=1, device_id={"seq": lax.rem(seq + step, seqs)}, device_id_type=MESH
        )
    pl.semaphore_wait(barrier, blks + seqs - 2)
    copies = []
    for step in range(1, blks):
        to = lax.rem(blk + step, blks)
        copy = pltpu.make_async_remote_copy(
            src_ref=x_ref.at[to] if scatter else x_ref.at[0],
            dst_ref=first.at[blk],
            send_sem=sends.at[step],
            recv_sem=receives.at[step],
            device_id={"blk": to},
            device_id_type=MESH,
        )
        copy.start()
        copies.append(copy)
    if rimmed:
        rims = Rims(blks, z_ref, top, bottom, *refs[6:])
        rims.start()
    first[blk] = x_ref[blk] if scatter else x_ref[0]
    for copy in copies:
        copy.wait()
    total = first[0]
    for i in range(1, blks):
        total = total + first[i]
    second[seq] = total
    copies = []
    for step in range(1, seqs):
        copy = pltpu.make_async_remote_copy(
            src_ref=second.at[seq],
            dst_ref=second.at[seq],
            send_sem=sends2.at[step],
            recv_sem=receives2.at[step],
            device_id={"seq": lax.rem(seq + step, seqs)},
            device_id_type=MESH,
        )
        copy.start()
        copies.append(copy)
    for copy in copies:
        copy.wait()
    total = second[0]
    for i in range(1, seqs):
        total = total + second[i]
    out_ref[...] = total
    if rimmed:
        rims.wait()


def small_sum(x, scatter, collective_id, rimmed=None):
    blks, seqs = lax.axis_size("blk"), lax.axis_size("seq")
    part = x.shape[1:]
    vmem = pl.BlockSpec(memory_space=pltpu.VMEM)
    given, found, extra = [x], [jax.ShapeDtypeStruct(part, f32)], []
    if rimmed is not None:
        given.append(rimmed)
        found += [jax.ShapeDtypeStruct((RIM, rimmed.shape[1]), f32)] * 2
        extra.append(pltpu.VMEM((2, RIM, rimmed.shape[1]), f32))
        extra.append(pltpu.SemaphoreType.DMA((4,)))
    found = pl.pallas_call(
        functools.partial(small_sum_kernel, scatter, blks, seqs, rimmed is not None),
        in_specs=[vmem] * len(given),
        out_specs=[vmem] * len(found),
        out_shape=found,
        scratch_shapes=[
            pltpu.VMEM((blks, *part), f32),
            pltpu.VMEM((seqs, *part), f32),
            pltpu.SemaphoreType.DMA((blks,)),
            pltpu.SemaphoreType.DMA((blks,)),
            pltpu.SemaphoreType.DMA((seqs,)),
            pltpu.SemaphoreType.DMA((seqs,)),
        ]
        + extra,
        compiler_params=params(16, collective_id=collective_id, has_side_effects=True),
        name="small_sum",
    )(*given)
    return found if rimmed is not None else found[0]


LAG = 2
PIECE_ROWS = 64
SLOTS = 3
ROOT = 1


def cuts(size, piece):
    return [slice(first, min(size, first + piece)) for first in range(0, size, piece)]


def pieces_of(index, shape):
    parts, rows, columns = shape
    piece = PIECE_ROWS if columns >= D else 3 * PIECE_ROWS
    return [
        (index, part, row, column)
        for part in range(parts)
        for row in cuts(rows, piece)
        for column in cuts(columns, D)
    ]


class Reducer:
    @staticmethod
    def scratch(shapes, dtypes, staged, halves, units):
        places = []
        for lead in ((4,), (2,), (), (), ()):
            places += [
                pltpu.VMEM(
                    (shape[0],) + ((2,) if lead and index in halves else lead) + shape[1:], dtype
                )
                for index, (shape, dtype) in enumerate(zip(shapes, dtypes))
            ]
        for index in range(len(shapes)):
            _, _, rows, columns = next(unit for unit in units if unit[0] == index)
            size = (rows.stop - rows.start, columns.stop - columns.start)
            size = (SLOTS, 4) + size if index in staged else (1, 1, 16, 128)
            places.append(pltpu.VMEM(size, dtypes[index]))
        total = len(units)
        semaphores = [pltpu.SemaphoreType.DMA((total, 2))] * 2
        semaphores += [pltpu.SemaphoreType.DMA((total,))] * 10
        return places + semaphores

    def __init__(self, seqs, units, staged, halves, ins, outs, refs):
        count = len(ins)
        self.seqs, self.units, self.staged, self.ins, self.outs = seqs, units, staged, ins, outs
        self.halves = halves
        self.sums, self.side, self.last, self.below, self.above, self.slots = [
            refs[i * count : (i + 1) * count] for i in range(6)
        ]
        (self.s2, self.r2, self.load_sem, self.s1, self.r1, self.s3, self.r3, self.sb, self.rb,
         self.sa, self.ra, self.out_sem) = refs[6 * count :]
        blk, self.seq = lax.axis_index("blk"), lax.axis_index("seq")
        self.core, self.x, self.y = blk % 2, (blk // 2) % 2, blk // 4
        self.pair = {"blk": blk + 1 - 2 * self.core}
        self.over_x = {"blk": blk + 2 - 4 * self.x}
        self.over_y = {"blk": blk + 4 - 8 * self.y}
        self.order = {}
        for u, unit in enumerate(units):
            self.order.setdefault(unit[0], []).append(u)

    def send(self, source, target, sent, received, peer):
        return pltpu.make_async_remote_copy(
            src_ref=source, dst_ref=target, send_sem=sent, recv_sem=received,
            device_id=peer, device_id_type=MESH,
        )

    def own(self, u):
        index, part, rows, columns = self.units[u]
        if index in self.staged:
            return self.slots[index].at[self.order[index].index(u) % SLOTS]
        return self.ins[index].at[part, :, self.core, rows, columns]

    def load(self, u):
        index, part, rows, columns = self.units[u]
        return pltpu.make_async_copy(
            self.ins[index].at[part, :, self.core, rows, columns], self.own(u), self.load_sem.at[u]
        )

    def load_half(self, u):
        index, part, rows, columns = self.units[u]
        kept, arrived = self.ins[index]
        return [
            pltpu.make_async_copy(
                kept.at[:, rows, columns], self.sums[index].at[part, :, rows, columns], self.load_sem.at[u]
            ),
            pltpu.make_async_copy(
                arrived.at[:, rows, columns], self.side[index].at[part, :, rows, columns], self.r1.at[u]
            ),
        ]

    def over_x_first(self, u):
        index = self.units[u][0]
        if index in self.halves:
            return self.halves[index] == 0
        return [v for v, unit in enumerate(self.units) if unit[0] not in self.halves].index(u) % 2 == 0

    def first(self, u):
        index, part, rows, columns = self.units[u]
        return self.send(
            self.ins[index].at[part, :, 1 - self.core, rows, columns],
            self.sums[index].at[part, :, rows, columns],
            self.s1.at[u], self.r1.at[u], self.pair,
        )

    def second(self, u):
        index, part, rows, columns = self.units[u]
        copies = []
        for i in range(2):
            x_first = self.over_x_first(u)
            place = 1 - self.x + 2 * i if x_first else 2 * (1 - self.y) + i
            copies.append(
                self.send(
                    self.sums[index].at[part, place, rows, columns],
                    self.side[index].at[part, i, rows, columns],
                    self.s2.at[u, i], self.r2.at[u, i], self.over_x if x_first else self.over_y,
                )
            )
        return copies

    def third(self, u):
        index, part, rows, columns = self.units[u]
        x_first = self.over_x_first(u)
        if index in self.halves:
            place = 1 - self.y if x_first else 1 - self.x
        else:
            place = 2 * (1 - self.y) + self.x if x_first else 2 * self.y + 1 - self.x
        return self.send(
            self.sums[index].at[part, place, rows, columns],
            self.last[index].at[part, rows, columns],
            self.s3.at[u], self.r3.at[u], self.over_y if x_first else self.over_x,
        )

    def result(self, u):
        index, part, rows, columns = self.units[u]
        if index in self.halves:
            return self.sums[index].at[part, self.y if self.over_x_first(u) else self.x, rows, columns]
        return self.sums[index].at[part, 2 * self.y + self.x, rows, columns]

    def down(self, u):
        index, part, rows, columns = self.units[u]
        return self.send(
            self.result(u), self.above[index].at[part, rows, columns],
            self.sa.at[u], self.ra.at[u], {"seq": self.seq - 1},
        )

    def up(self, u):
        index, part, rows, columns = self.units[u]
        return self.send(
            self.result(u), self.below[index].at[part, rows, columns],
            self.sb.at[u], self.rb.at[u], {"seq": self.seq + 1},
        )

    def store(self, u):
        index, part, rows, columns = self.units[u]
        return pltpu.make_async_copy(
            self.result(u), self.outs[index].at[part, rows, columns], self.out_sem.at[u]
        )

    def add_to(self, target, *sources):
        total = target[...].astype(f32)
        for source in sources:
            total = total + source[...].astype(f32)
        target[...] = total.astype(target.dtype)

    def enter(self, u):
        if self.units[u][0] in self.halves:
            for copy in self.load_half(u):
                copy.start()
            return
        self.first(u).start()
        index = self.units[u][0]
        if index in self.staged and self.order[index].index(u) < SLOTS:
            self.load(u).start()

    def stage_near(self, u):
        index, part, rows, columns = self.units[u]
        if index in self.halves:
            return
        if index in self.staged:
            self.load(u).wait()
        self.first(u).wait_recv()
        own = self.own(u)
        for i in range(4):
            self.add_to(self.sums[index].at[part, i, rows, columns], own.at[i])
        if index in self.staged:
            later = self.order[index].index(u) + SLOTS
            if later < len(self.order[index]):
                self.load(self.order[index][later]).start()
        for copy in self.second(u):
            copy.start()

    def stage_side(self, u):
        index, part, rows, columns = self.units[u]
        if index in self.halves:
            for copy in self.load_half(u):
                copy.wait()
            for i in range(2):
                self.add_to(
                    self.sums[index].at[part, i, rows, columns],
                    self.side[index].at[part, i, rows, columns],
                )
            self.third(u).start()
            return
        for i, copy in enumerate(self.second(u)):
            copy.wait_recv()
            keep = 2 * i + self.x if self.over_x_first(u) else 2 * self.y + i
            self.add_to(
                self.sums[index].at[part, keep, rows, columns],
                self.side[index].at[part, i, rows, columns],
            )
        self.third(u).start()

    def stage_last(self, u):
        index, part, rows, columns = self.units[u]
        self.third(u).wait_recv()
        self.add_to(self.result(u), self.last[index].at[part, rows, columns])

        @pl.when(self.seq < ROOT)
        def _():
            self.up(u).start()

        @pl.when(self.seq == self.seqs - 1)
        def _():
            self.down(u).start()

    def stage_chain(self, u, place):
        index, part, rows, columns = self.units[u]

        @pl.when(self.seq == place)
        def _():
            self.down(u).wait_recv()
            self.add_to(self.result(u), self.above[index].at[part, rows, columns])
            self.down(u).start()

    def stage_root(self, u):
        index, part, rows, columns = self.units[u]

        @pl.when(self.seq == ROOT)
        def _():
            self.up(u).wait_recv()
            self.down(u).wait_recv()
            self.add_to(
                self.result(u),
                self.below[index].at[part, rows, columns],
                self.above[index].at[part, rows, columns],
            )
            self.up(u).start()
            self.down(u).start()
            self.store(u).start()

    def stage_spread(self, u, place):
        index, part, rows, columns = self.units[u]

        @pl.when(self.seq == place)
        def _():
            if place < ROOT:
                self.down(u).wait_recv()
                self.up(u).wait_send()
                self.result(u)[...] = self.above[index].at[part, rows, columns][...]
            else:
                self.up(u).wait_recv()
                self.down(u).wait_send()
                self.result(u)[...] = self.below[index].at[part, rows, columns][...]
                if place < self.seqs - 1:
                    self.up(u).start()
            self.store(u).start()

    def stages(self):
        found = [(0, self.stage_near), (LAG, self.stage_side), (2 * LAG, self.stage_last)]
        at = 3 * LAG
        for place in range(self.seqs - 2, ROOT, -1):
            found.append((at, functools.partial(self.stage_chain, place=place)))
            at += LAG
        found.append((at, self.stage_root))
        at += LAG
        for place in range(ROOT):
            found.append((at, functools.partial(self.stage_spread, place=place)))
        for place in range(ROOT + 1, self.seqs):
            found.append((at, functools.partial(self.stage_spread, place=place)))
            at += LAG
        return found

    def steps(self):
        return len(self.units) + self.stages()[-1][0]

    def step(self, t):
        for lag, stage in self.stages():
            if 0 <= t - lag < len(self.units):
                stage(t - lag)

    def finish(self):
        for u in range(len(self.units)):
            if self.units[u][0] not in self.halves:
                self.first(u).wait_send()
                for copy in self.second(u):
                    copy.wait_send()
            self.third(u).wait_send()

            @pl.when(self.seq == ROOT)
            def _(u=u):
                self.down(u).wait_send()
                self.up(u).wait_send()

            @pl.when((self.seq > ROOT) & (self.seq < self.seqs - 1))
            def _(u=u):
                self.up(u).wait_send()

            self.store(u).wait()


STAGED = (2, 3)
HALVES = {0: 0, 1: 1}

AHEAD = 10


def tail_kernel(
    blks, seqs, units, sent, w_ref, h_ref, dx1_ref, x_ref, gain_ref, sums_ref, dub_ref,
    down_in, down_side, up_in, up_side, conv_in, proj_in, dx_ref,
    down_out, up_out, conv_out, proj_out, qkv_out, vec_out,
    moved, dw, vectors, h_t, w_slots, ex_send, ex_recv, ex_own, w_sem, *refs
):
    reducer = Reducer(
        seqs, units, STAGED, HALVES,
        ((down_in, down_side), (up_in, up_side), conv_in, proj_in, dw, vectors),
        (down_out, up_out, conv_out, proj_out, qkv_out, vec_out), refs,
    )
    early = [u for u, unit in enumerate(units) if unit[0] < 4]
    exchange = (blks, sent, moved, ex_send, ex_recv, ex_own)
    slots = w_slots.shape[0]

    def weight(k):
        part, i = divmod(k, 4)
        first = D * part + 256 * i
        return pltpu.make_async_copy(
            w_ref.at[:, first : first + 256], w_slots.at[k % slots], w_sem.at[k]
        )

    def put(vector, row, index):
        for place in range(8):
            vectors[0, place // 2, place % 2, row : row + 1, :] = vector[:, 128 * index(place) : 128 * index(place) + 128]

    def chunk(k):
        part, i = divmod(k, 4)
        lanes = slice(128 * part, 128 * part + 128)
        weight(k).wait()
        grad = jnp.concatenate([moved[2 * i, :, lanes], moved[2 * i + 1, :, lanes]], axis=1)
        dx_ref[...] += dot_nt(grad, w_slots[k % slots])
        dw[part, :, :, :, 256 * i : 256 * i + 256] = (
            dot(h_t[...], grad).astype(bf16).reshape(4, 2, 128, 256)
        )
        if k + slots < 12:
            weight(k + slots).start()
        if part != 1:
            bias = column_sums(grad.astype(f32))
            place = i + (4 if part else 0)
            for half in range(2):
                vectors[0, place // 2, place % 2, 6 + half : 7 + half, :] = bias[:, 128 * half : 128 * half + 128]
        if i == 3:
            for u, unit in enumerate(units):
                if unit[0] == 4 and unit[1] == part:
                    reducer.enter(u)

    def norm():
        grad = dx_ref[...]
        normed, scale_inv = layer_stats(x_ref[...].astype(f32))
        dx_ref[...] = dx1_ref[...] + layer_backward(grad, normed, scale_inv, gain_ref[...])
        put(column_sums(grad * normed), 0, lambda place: place)
        put(column_sums(grad), 1, lambda place: place)
        for row in range(4):
            put(sums_ref[row : row + 1, :], 2 + row, lambda place: place)
            put(dub_ref[...], 8 + row, lambda place, row=row: 4 * place + row)
        for place in range(8):
            vectors[0, place // 2, place % 2, 12:16, :] = jnp.zeros((4, 128), f32)
        for u, unit in enumerate(units):
            if unit[0] == 5:
                reducer.enter(u)

    greet(blks, seqs)
    exchange_start(*exchange)
    for u in early:
        reducer.enter(u)
    for k in range(slots):
        weight(k).start()
    h_t[...] = h_ref[...].T
    dx_ref[...] = jnp.zeros_like(dx_ref)
    at = 0
    while at < AHEAD:
        reducer.step(at)
        at += 1
    exchange_wait(*exchange)
    for k in range(12):
        chunk(k)
        if k % 2:
            reducer.step(at)
            at += 1
    norm()
    while at < reducer.steps():
        reducer.step(at)
        at += 1
    reducer.finish()


def tail(sent, weight, h, dx1, x, gain, sums, dub, arrays, collective_id):
    blks, seqs = lax.axis_size("blk"), lax.axis_size("seq")
    rows = x.shape[0]
    shapes = [(1, FF // 8, D), (1, D // 8, FF), (1, 9 * D // 8, C), (1, D // 8, D), (3, D // 8, D), (1, 16, 128)]
    dtypes = [bf16] * 5 + [f32]
    found = [pieces_of(index, shape) for index, shape in enumerate(shapes)]
    light = [unit for pair in zip(found[0], found[1]) for unit in pair]
    heavy = found[2] + found[3]
    units = [unit for pair in zip(heavy, light) for unit in pair]
    units += [unit for pair in zip(found[4], light[len(heavy) :]) for unit in pair] + found[5]
    units += light[len(heavy) + len(found[4]) :]
    anywhere = pl.BlockSpec(memory_space=pl.ANY)
    vmem = pl.BlockSpec(memory_space=pltpu.VMEM)
    return pl.pallas_call(
        functools.partial(tail_kernel, blks, seqs, units),
        in_specs=[anywhere, anywhere] + [vmem] * 6 + [anywhere] * 6,
        out_specs=[vmem] + [anywhere] * 6,
        out_shape=[jax.ShapeDtypeStruct((rows, D), f32)]
        + [
            jax.ShapeDtypeStruct(shape, dtype) for shape, dtype in zip(shapes, dtypes)
        ],
        scratch_shapes=[
            pltpu.VMEM(sent.shape, bf16),
            pltpu.VMEM((3, 4, 2, D // 8, D), bf16),
            pltpu.VMEM((1, 4, 2, 16, 128), f32),
            pltpu.VMEM((D, rows), bf16),
            pltpu.VMEM((3, D, 256), bf16),
            pltpu.SemaphoreType.DMA((blks,)),
            pltpu.SemaphoreType.DMA((blks,)),
            pltpu.SemaphoreType.DMA,
            pltpu.SemaphoreType.DMA((12,)),
        ]
        + Reducer.scratch(shapes, dtypes, STAGED, HALVES, units),
        compiler_params=params(63, collective_id=collective_id, has_side_effects=True),
        name="qkv_grad_and_sums",
    )(sent, weight, h, dx1, x, gain, sums, dub, *arrays)


def widen_kernel(counts, *refs):
    matrices = len(refs) - len(counts) - 1 >> 1
    sources, vectors = refs[:matrices], refs[matrices]
    targets, pieces = refs[matrices + 1 : 2 * matrices + 1], refs[2 * matrices + 1 :]
    for source, target in zip(sources[:-1], targets[:-1]):
        target[...] = source[0].astype(f32)
    for part in range(3):
        targets[-1][:, D * part : D * part + D] = sources[-1][part].astype(f32)
    row = 0
    for count, piece in zip(counts, pieces):
        for i in range(count):
            piece[:, 128 * i : 128 * i + 128] = vectors[0, row : row + 1, :]
            row += 1


def widen(arrays, vectors, counts):
    steps = 4
    return pl.pallas_call(
        functools.partial(widen_kernel, counts),
        grid=(steps,),
        in_specs=[
            pl.BlockSpec((a.shape[0], a.shape[1] // steps, a.shape[2]), lambda i: (0, i, 0))
            for a in arrays
        ]
        + [whole(vectors.shape)],
        out_specs=[
            pl.BlockSpec((a.shape[1] // steps, a.shape[0] * a.shape[2]), lambda i: (i, 0))
            for a in arrays
        ]
        + [whole((1, 128 * count)) for count in counts],
        out_shape=[
            jax.ShapeDtypeStruct((a.shape[1], a.shape[0] * a.shape[2]), f32) for a in arrays
        ]
        + [jax.ShapeDtypeStruct((1, 128 * count), f32) for count in counts],
        compiler_params=params(62),
        name="widen",
    )(*arrays, vectors)


def shifted(value, axis, steps):
    count = lax.axis_size(axis)
    leading, last = (max(0, -steps), min(count, count - steps))
    return lax.ppermute(value, axis, [(source, source + steps) for source in range(leading, last)])


def near_blocks(sides_row, keys_own, values_own):
    rows = keys_own.shape[0]
    place, length = lax.axis_index("blk"), rows * lax.axis_size("blk")
    centre = jnp.arange(rows, dtype=jnp.int32)
    segment = image_info(sides_row, place * rows + centre)[0]
    found = []
    for offset in range(-REACH, REACH + 1):
        keys, values = (keys_own, values_own) if offset == 0 else shifted((keys_own, values_own), "blk", -offset)
        positions = (place + offset) * rows + centre
        inside = (positions >= 0) & (positions < length)
        allowed = (segment[:, None] == image_info(sides_row, positions)[0][None, :]) & inside[None, :]
        found.append((offset, keys.reshape(rows, HEADS, HEAD), values.reshape(rows, HEADS, HEAD), allowed))
    return found


def near_scores(queries, keys, allowed):
    scores = jnp.einsum("qhd,khd->hqk", queries, keys, preferred_element_type=f32)
    return jnp.where(allowed[None], scores, masked_score)


def near_attention(near, queries):
    rows = queries.shape[0]
    peak = jnp.full((HEADS, rows), masked_score, f32)
    total = jnp.zeros((HEADS, rows), f32)
    for _, keys, _, allowed in near:
        scores = near_scores(queries, keys, allowed)
        new_peak = jnp.maximum(peak, jnp.max(scores, axis=-1))
        grown = jnp.where(allowed[None], jnp.exp2(scores - new_peak[..., None]), 0.0)
        total = total * jnp.exp2(peak - new_peak) + jnp.sum(grown, axis=-1)
        peak = new_peak
    lse = peak + jnp.log2(total)
    out = jnp.zeros((rows, HEADS, HEAD), f32)
    for _, keys, values, allowed in near:
        scores = near_scores(queries, keys, allowed)
        weights = jnp.where(allowed[None], jnp.exp2(scores - lse[..., None]), 0.0).astype(bf16)
        out = out + jnp.einsum("hqk,khd->qhd", weights, values, preferred_element_type=f32)
    return out.reshape(rows, D).astype(bf16), lse


def near_attention_grad(near, queries, lse, out, grad):
    rows = queries.shape[0]
    grad_heads = grad.reshape(rows, HEADS, HEAD)
    delta = jnp.sum((grad.astype(f32) * out.astype(f32)).reshape(rows, HEADS, HEAD), axis=-1).T
    dq = jnp.zeros((rows, HEADS, HEAD), f32)
    dk = jnp.zeros((rows, HEADS, HEAD), f32)
    dv = jnp.zeros((rows, HEADS, HEAD), f32)
    for offset, keys, values, allowed in near:
        scores = near_scores(queries, keys, allowed)
        weights = jnp.where(allowed[None], jnp.exp2(scores - lse[..., None]), 0.0)
        value_grad = jnp.einsum("qhd,khd->hqk", grad_heads, values, preferred_element_type=f32)
        score_grad = (weights * (value_grad - delta[..., None])).astype(bf16)
        dq = dq + jnp.einsum("hqk,khd->qhd", score_grad, keys, preferred_element_type=f32)
        dk_part = jnp.einsum("hqk,qhd->khd", score_grad, queries, preferred_element_type=f32)
        dv_part = jnp.einsum(
            "hqk,qhd->khd", weights.astype(bf16), grad_heads, preferred_element_type=f32
        )
        if offset:
            dk_part, dv_part = shifted((dk_part.astype(bf16), dv_part.astype(bf16)), "blk", offset)
        dk = dk + dk_part.astype(f32)
        dv = dv + dv_part.astype(f32)
    dq = dq.reshape(rows, D).astype(bf16) * jnp.asarray(HEAD**-0.5, bf16)
    dk = (dk * (1.0 / LOG2E)).reshape(rows, D).astype(bf16)
    return dq, dk, dv.reshape(rows, D).astype(bf16)


def in_groups(*parts):
    rows = parts[0].shape[0]
    stacked = jnp.stack([part.reshape(rows, D // 128, 128) for part in parts], axis=2)
    return stacked.transpose(1, 0, 2, 3).reshape(D // 128, rows, 128 * len(parts))


def from_groups(groups, part):
    picked = groups[:, :, 128 * part : 128 * part + 128]
    return picked.transpose(1, 0, 2).reshape(groups.shape[1], D)


def rims(rows_own, width):
    count = lax.axis_size("blk")
    top = lax.ppermute(rows_own[-width:], "blk", [(i, i + 1) for i in range(count - 1)])
    bottom = lax.ppermute(rows_own[:width], "blk", [(i + 1, i) for i in range(count - 1)])
    return top, bottom


def line(vector):
    return vector.reshape(1, -1)


def shards(
    tokens,
    image_sides,
    ln1_gain,
    ln1_bias,
    qkv_weight,
    qv_bias,
    proj_weight,
    proj_bias,
    ln2_gain,
    ln2_bias,
    up_weight,
    up_bias,
    down_weight,
    down_bias,
    conv_weight,
    bn_gain,
    bn_bias,
    out_grad,
    pup_grad,
):
    x = tokens[0]
    sides_row = image_sides[0]
    rows = x.shape[0]
    blks, seqs = lax.axis_size("blk"), lax.axis_size("seq")
    place = lax.axis_index("blk")
    length = rows * blks
    samples = length * seqs
    by_heads = blks == 8 and HEADS // 2 == blks

    block_starts = jnp.arange(length // BLOCK, dtype=jnp.int32) * BLOCK
    _, block_width, _, _, block_begin = image_info(sides_row, block_starts)
    starts = (block_begin // BLOCK).astype(jnp.int32)
    counts = (block_width * block_width // BLOCK).astype(jnp.int32)
    own_blocks = rows // BLOCK
    widths = lax.dynamic_slice_in_dim(block_width, place * own_blocks, own_blocks)
    wide_positions = place * rows + jnp.arange(-WIDE_RIM, rows + WIDE_RIM, dtype=jnp.int32)
    wide_flags = edge_flags(sides_row, wide_positions)
    flags = wide_flags[WIDE_RIM - RIM : WIDE_RIM + rows + RIM]

    g = pup_grad[0]
    if by_heads:
        h1, g_top, g_bottom, qkv = project_qkv_exchanged(
            x, line(ln1_gain), line(ln1_bias), qkv_weight, line(qv_bias), g, 6
        )
        qkv = qkv.reshape(length, 384)
        o_heads, lse = attention(starts, counts, qkv)
        o_groups = exchange(o_heads.reshape(blks, rows, 128), 7)
    else:
        g_top, g_bottom = rims(g, WIDE_RIM)
        h1, qkv_groups = project_qkv(x, line(ln1_gain), line(ln1_bias), qkv_weight, line(qv_bias))
        queries = from_groups(qkv_groups, 0).reshape(rows, HEADS, HEAD)
        near = near_blocks(sides_row, from_groups(qkv_groups, 1), from_groups(qkv_groups, 2))
        attended, lse = near_attention(near, queries)
        o_groups = in_groups(attended)
    dact = spread(widths, g, g_top, g_bottom, wide_flags)
    x1, h2, act, slope, block_low, top, bottom = mlp(
        o_groups, x, proj_weight, line(proj_bias), line(ln2_gain), line(ln2_bias),
        up_weight, line(up_bias), down_weight, line(down_bias), 8,
    )
    z, z_sums = conv(widths, block_low, top, bottom, flags, conv_weight)
    z_sums, z_top, z_bottom = small_sum(z_sums[None], False, 1, z)
    mean = z_sums[0:1] / samples
    inv = lax.rsqrt(z_sums[1:2] / samples - mean * mean + batch_eps)
    pup_out, normed, dbn, bn_sums = batch(
        widths, z, z_top, z_bottom, dact, flags, mean, inv, line(bn_gain), line(bn_bias)
    )
    bn_sums = small_sum(bn_sums[None], False, 2)

    taps, dy, dm = conv_grad(
        widths, dbn, normed, flags, inv * line(bn_gain), bn_sums[0:1] / samples, bn_sums[1:2] / samples,
        conv_weight, out_grad[0],
    )
    du, up_bias_grad, dx1, da, do_groups, mlp_sums = mlp_grad(
        dy, dm, slope, down_weight, up_weight, x1, line(ln2_gain), proj_weight
    )
    if by_heads:
        conv_weight_grad, proj_grad, do_moved, down_keep, down_send, up_keep, up_send = weights(
            act, dm, h2, du, block_low, taps, o_groups, da, do_groups, blks, 5
        )
        down_side = lax.ppermute(down_send, "blk", [(i, i ^ 2) for i in range(blks)])
        up_side = lax.ppermute(up_send, "blk", [(i, i ^ 4) for i in range(blks)])
        dqkv = attention_grad(starts, counts, qkv, do_moved.reshape(length, 128), o_heads, lse)
        dqkv_groups = dqkv.reshape(blks, rows, 384)
    else:
        down_grad = down_weight_grad_of(act, dm)
        conv_weight_grad = conv_weight_grad_of(block_low, taps)
        up_grad, proj_grad = late_weights(h2, du, o_groups, da)
        grads = near_attention_grad(near, queries, lse, attended, from_groups(do_groups, 0))
        dqkv_groups = in_groups(*grads)

    piece = D // blks
    cuts_of = [piece] * 6 + [2 * piece, 4 * piece]
    if by_heads:
        tokens_grad, *summed = tail(
            dqkv_groups, qkv_weight, h1, dx1, x, line(ln1_gain), mlp_sums, up_bias_grad,
            [
                down_keep, down_side, up_keep, up_side,
                conv_weight_grad.reshape(1, 4, 2, -1, C), proj_grad.reshape(1, 4, 2, -1, D),
            ],
            3,
        )
        tokens_grad, down_grad, up_grad, conv_weight_grad, proj_grad, qkv_weight_grad, *small = widen(
            [tokens_grad[None]] + summed[:5], summed[5], [cut // 128 for cut in cuts_of]
        )
        small = [vector[0] for vector in small]
    else:
        qkv_weight_grad, dqb, dvb, tokens_grad, qkv_sums = qkv_grad(
            dqkv_groups, qkv_weight, h1, dx1, x, line(ln1_gain)
        )

        def scattered(grad):
            part = lax.psum_scatter(grad, "blk", scatter_dimension=0, tiled=True)
            return lax.psum(part, "seq").astype(f32)

        down_grad, up_grad, proj_grad, conv_weight_grad = [
            scattered(grad) for grad in (down_grad, up_grad, proj_grad, conv_weight_grad)
        ]
        qkv_weight_grad = scattered(qkv_weight_grad.transpose(1, 0, 2).reshape(D, 3 * D))
        vectors = [qkv_sums[0], qkv_sums[1], mlp_sums[0], mlp_sums[1], mlp_sums[2], mlp_sums[3]]
        vectors += [jnp.concatenate([dqb[0], dvb[0]]), up_bias_grad[0]]
        stacked = jnp.concatenate([vector.reshape(blks, -1) for vector in vectors], axis=1)
        summed = small_sum(stacked[:, None, :], True, 4)[0]
        ends = [sum(cuts_of[: i + 1]) for i in range(len(cuts_of))]
        small = [summed[end - cut : end] for cut, end in zip(cuts_of, ends)]
    ln1_g, ln1_b, proj_b, ln2_g, ln2_b, down_b, qv_b, up_b = small
    channel_piece = C // blks
    gain_slice = lax.dynamic_slice_in_dim(bn_sums[1], place * channel_piece, channel_piece)
    bias_slice = lax.dynamic_slice_in_dim(bn_sums[0], place * channel_piece, channel_piece)
    return (
        block_low[None],
        pup_out[None],
        tokens_grad[None],
        ln1_g,
        ln1_b,
        qkv_weight_grad,
        qv_b,
        proj_grad,
        proj_b,
        ln2_g,
        ln2_b,
        up_grad,
        up_b,
        down_grad,
        down_b,
        conv_weight_grad,
        gain_slice,
        bias_slice,
    )


def solution(mesh):
    replicated = P()
    packed = P("seq", "blk", None)
    placed = (packed, P("seq", None)) + (replicated,) * 15 + (packed, packed)
    rows, vector = P("blk", None), P("blk")
    return jax.shard_map(
        shards,
        mesh=mesh,
        in_specs=placed,
        out_specs=(
            packed, packed, packed, vector, vector, rows, vector, rows, vector, vector, vector, rows,
            vector, rows, vector, rows, vector, vector,
        ),
        check_vma=False,
    )
```

```python
import functools

import jax
import jax.numpy as jnp
from jax import lax
from jax.experimental import pallas as pl
from jax.experimental.pallas import tpu as pltpu
from jax.sharding import PartitionSpec as P

D = 1024
HEADS = 16
HEAD = 64
FF = 4096
C = 256
REACH = 4
UNIT = 16
BLOCK = UNIT * UNIT
IMAGE_BLOCKS = (1, 4, 9)
RIM = 64
WIDE_RIM = 128
LOG2E = 1.4426950408889634
LOOK = 4
MESH = pl.DeviceIdType.MESH

norm_eps = 1e-06
batch_eps = 1e-05
masked_score = -1e30
f32 = jnp.float32
bf16 = jnp.bfloat16

NT = (((1,), (1,)), ((), ()))
TN = (((0,), (0,)), ((), ()))


def dot(left, right):
    return jnp.dot(left, right, preferred_element_type=f32)


def dot_nt(left, right):
    return lax.dot_general(left, right, NT, preferred_element_type=f32)


def dot_tn(left, right):
    return lax.dot_general(left, right, TN, preferred_element_type=f32)


def whole(shape):
    zeros = (0,) * len(shape)
    return pl.BlockSpec(shape, lambda *_: zeros)


def params(megabytes, **more):
    return pltpu.CompilerParams(vmem_limit_bytes=megabytes << 20, **more)


def cost(flops, moved, transcendentals=0):
    return pl.CostEstimate(
        flops=int(flops), bytes_accessed=int(moved), transcendentals=int(transcendentals)
    )


def place_copies(blks, source, target, sends, receives):
    me = lax.axis_index("blk")
    copies = []
    for step in range(1, blks):
        to = lax.rem(me + step, blks)
        copies.append(
            pltpu.make_async_remote_copy(
                src_ref=source.at[to],
                dst_ref=target.at[me],
                send_sem=sends.at[step],
                recv_sem=receives.at[step],
                device_id={"blk": to},
                device_id_type=MESH,
            )
        )
    return copies


def greet_signal(blks, seqs=0):
    me, seq = lax.axis_index("blk"), lax.axis_index("seq")
    barrier = pltpu.get_barrier_semaphore()
    for step in range(1, blks):
        pl.semaphore_signal(
            barrier, inc=1, device_id={"blk": lax.rem(me + step, blks)}, device_id_type=MESH
        )
    if seqs:

        @pl.when(seq > 0)
        def _():
            pl.semaphore_signal(barrier, inc=1, device_id={"seq": seq - 1}, device_id_type=MESH)

        @pl.when(seq < seqs - 1)
        def _():
            pl.semaphore_signal(barrier, inc=1, device_id={"seq": seq + 1}, device_id_type=MESH)


def greet_wait(blks, seqs=0):
    seq = lax.axis_index("seq")
    ends = 0
    if seqs:
        ends = jnp.where(seq > 0, 1, 0) + jnp.where(seq < seqs - 1, 1, 0)
    pl.semaphore_wait(pltpu.get_barrier_semaphore(), blks - 1 + ends)


def greet(blks, seqs=0):
    greet_signal(blks, seqs)
    greet_wait(blks, seqs)


def exchange_start(blks, source, target, sends, receives, own_sem):
    me = lax.axis_index("blk")
    for copy in place_copies(blks, source, target, sends, receives):
        copy.start()
    pltpu.make_async_copy(source.at[me], target.at[me], own_sem).start()


def exchange_wait(blks, source, target, sends, receives, own_sem):
    me = lax.axis_index("blk")
    for copy in place_copies(blks, source, target, sends, receives):
        copy.wait()
    pltpu.make_async_copy(source.at[me], target.at[me], own_sem).wait()


class Rims:
    def __init__(self, blks, rows_own, top, bottom, landing, semaphores):
        me = lax.axis_index("blk")
        width, last = top.shape[0], rows_own.shape[0]
        self.after, self.before = me < blks - 1, me > 0
        self.top, self.bottom, self.landing = top, bottom, landing
        self.downward = pltpu.make_async_remote_copy(
            src_ref=rows_own.at[last - width : last], dst_ref=landing.at[0],
            send_sem=semaphores.at[0], recv_sem=semaphores.at[1],
            device_id={"blk": me + 1}, device_id_type=MESH,
        )
        self.upward = pltpu.make_async_remote_copy(
            src_ref=rows_own.at[0:width], dst_ref=landing.at[1],
            send_sem=semaphores.at[2], recv_sem=semaphores.at[3],
            device_id={"blk": me - 1}, device_id_type=MESH,
        )

    def start(self):
        @pl.when(self.after)
        def _():
            self.downward.start()

        @pl.when(self.before)
        def _():
            self.upward.start()

        @pl.when(jnp.logical_not(self.after))
        def _():
            self.bottom[...] = jnp.zeros_like(self.bottom)

        @pl.when(jnp.logical_not(self.before))
        def _():
            self.top[...] = jnp.zeros_like(self.top)

    def wait(self):
        @pl.when(self.after)
        def _():
            self.downward.wait_send()
            self.upward.wait_recv()
            self.bottom[...] = self.landing[1]

        @pl.when(self.before)
        def _():
            self.upward.wait_send()
            self.downward.wait_recv()
            self.top[...] = self.landing[0]


def exchange_kernel(blks, source, target, *semaphores):
    greet(blks)
    exchange_start(blks, source, target, *semaphores)
    exchange_wait(blks, source, target, *semaphores)


def exchange(groups, collective_id):
    blks = lax.axis_size("blk")
    anywhere = pl.BlockSpec(memory_space=pl.ANY)
    return pl.pallas_call(
        functools.partial(exchange_kernel, blks),
        in_specs=[anywhere],
        out_specs=anywhere,
        out_shape=jax.ShapeDtypeStruct(groups.shape, groups.dtype),
        scratch_shapes=exchange_semaphores(blks),
        compiler_params=params(16, collective_id=collective_id, has_side_effects=True),
        name="exchange",
    )(groups)


def image_info(image_sides, positions):
    image_areas = image_sides * image_sides
    image_ends = jnp.cumsum(image_areas).astype(jnp.int32)
    image_starts = (image_ends - image_areas).astype(jnp.int32)
    segment = jnp.sum((image_ends[None, :] <= positions[:, None]).astype(jnp.int32), axis=1).astype(
        jnp.int32
    )
    picked = segment[:, None] == jnp.arange(image_sides.shape[0], dtype=jnp.int32)[None, :]
    image_width = jnp.sum(jnp.where(picked, image_sides[None, :], 0), axis=1).astype(jnp.int32)
    image_width = jnp.maximum(image_width, 1).astype(jnp.int32)
    image_begin = jnp.sum(jnp.where(picked, image_starts[None, :], 0), axis=1).astype(jnp.int32)
    offset = (positions - image_begin).astype(jnp.int32)
    row_index = (offset // image_width).astype(jnp.int32)
    col_index = (offset - row_index * image_width).astype(jnp.int32)
    return (segment, image_width, row_index, col_index, image_begin)


def edge_flags(image_sides, positions):
    _, width, row, col, _ = image_info(image_sides, positions)
    flags = jnp.stack([row > 0, row < width - 1, col > 0, col < width - 1], axis=1)
    return jnp.concatenate([flags, flags], axis=1).astype(f32)


def layer_stats(values):
    mean = jnp.mean(values, axis=-1, keepdims=True)
    centred = values - mean
    scale_inv = lax.rsqrt(jnp.mean(centred * centred, axis=-1, keepdims=True) + norm_eps)
    return centred * scale_inv, scale_inv


def layer_backward(grad_out, normed, scale_inv, gain):
    scaled = grad_out * gain
    inner = (
        scaled
        - jnp.mean(scaled, axis=-1, keepdims=True)
        - normed * jnp.mean(scaled * normed, axis=-1, keepdims=True)
    )
    return scale_inv * inner


def column_sums(values):
    return jnp.sum(values, axis=0, keepdims=True)


def gelu_parts(values):
    cumulative = 0.5 + 0.5 * lax.erf(values * 0.7071067811865476)
    weighted = values * (0.3989422804014327 * jnp.exp(values * values * -0.5))
    return cumulative, weighted


def qkv_kernel(x_ref, gain_ref, bias_ref, wq_ref, wk_ref, wv_ref, bq_ref, bv_ref, h_ref, out_ref):
    @pl.when(pl.program_id(0) == 0)
    def _():
        normed, _ = layer_stats(x_ref[...].astype(f32))
        h_ref[...] = (normed * gain_ref[...] + bias_ref[...]).astype(bf16)

    hidden = h_ref[...]
    query = ((dot(hidden, wq_ref[...]) + bq_ref[...]) * (HEAD**-0.5 * LOG2E)).astype(bf16)
    key = dot(hidden, wk_ref[...]).astype(bf16)
    value = (dot(hidden, wv_ref[...]) + bv_ref[...]).astype(bf16)
    for part in range(2):
        lanes = slice(128 * part, 128 * part + 128)
        out_ref[part, :, 0:128] = query[:, lanes]
        out_ref[part, :, 128:256] = key[:, lanes]
        out_ref[part, :, 256:384] = value[:, lanes]


def project_qkv(x, gain, bias, weight, qv_bias):
    rows = x.shape[0]
    groups = D // 128
    return pl.pallas_call(
        qkv_kernel,
        grid=(groups // 2,),
        in_specs=[
            whole((rows, D)),
            whole((1, D)),
            whole((1, D)),
            pl.BlockSpec((D, 256), lambda i: (0, i)),
            pl.BlockSpec((D, 256), lambda i: (0, 4 + i)),
            pl.BlockSpec((D, 256), lambda i: (0, 8 + i)),
            pl.BlockSpec((1, 256), lambda i: (0, i)),
            pl.BlockSpec((1, 256), lambda i: (0, 4 + i)),
        ],
        out_specs=[whole((rows, D)), pl.BlockSpec((2, rows, 384), lambda i: (i, 0, 0))],
        out_shape=[
            jax.ShapeDtypeStruct((rows, D), bf16),
            jax.ShapeDtypeStruct((groups, rows, 384), bf16),
        ],
        compiler_params=params(40),
        cost_estimate=cost(2 * rows * D * 3 * D, 12 << 20),
        name="norm_qkv",
    )(x, gain, bias, weight, weight, weight, qv_bias, qv_bias)


def qkv_exchange_kernel(
    blks, x_ref, gain_ref, bias_ref, qv_ref, w_ref, g_ref,
    h_ref, top, bottom, moved, groups, w_all, landing, w_sem, sends, receives, own_sem, rim_sem,
):
    me = lax.axis_index("blk")
    chips = blks // 2
    chip, core = me // 2, me % 2
    order = [lax.rem(chip + 1 + i, chips) for i in range(chips)]

    def weight(i, part):
        columns = pl.ds(pl.multiple_of(D * part + 256 * order[i], 256), 256)
        return pltpu.make_async_copy(w_ref.at[:, columns], w_all.at[i, part], w_sem.at[i, part])

    def to(place):
        return pltpu.make_async_remote_copy(
            src_ref=groups.at[place], dst_ref=moved.at[me],
            send_sem=sends.at[place], recv_sem=receives.at[me],
            device_id={"blk": place}, device_id_type=MESH,
        )

    def own():
        return pltpu.make_async_copy(groups.at[me], moved.at[me], own_sem)

    for i in range(chips):
        for part in range(3):
            weight(i, part).start()
    greet_signal(blks)
    rims = Rims(blks, g_ref, top, bottom, landing, rim_sem)
    normed, _ = layer_stats(x_ref[...].astype(f32))
    h_ref[...] = (normed * gain_ref[...] + bias_ref[...]).astype(bf16)
    for i in range(chips):
        for part in range(3):
            weight(i, part).wait()
        columns = pl.ds(pl.multiple_of(256 * order[i], 256), 256)
        hidden = h_ref[...]
        query = ((dot(hidden, w_all[i, 0]) + qv_ref[:, columns]) * (HEAD**-0.5 * LOG2E)).astype(bf16)
        key = dot(hidden, w_all[i, 1]).astype(bf16)
        columns = pl.ds(pl.multiple_of(D + 256 * order[i], 256), 256)
        value = (dot(hidden, w_all[i, 2]) + qv_ref[:, columns]).astype(bf16)
        for half in range(2):
            lanes = slice(128 * half, 128 * half + 128)
            place = 2 * order[i] + half
            groups[place, :, 0:128] = query[:, lanes]
            groups[place, :, 128:256] = key[:, lanes]
            groups[place, :, 256:384] = value[:, lanes]
        if i == 0:
            greet_wait(blks)
        if i < chips - 1:
            to(2 * order[i]).start()
            to(2 * order[i] + 1).start()
    to(2 * chip + 1 - core).start()
    own().start()
    rims.start()
    for step in range(1, blks):
        other = lax.rem(me + step, blks)
        to(other).wait_send()
        pltpu.make_async_remote_copy(
            src_ref=groups.at[other], dst_ref=moved.at[other],
            send_sem=sends.at[other], recv_sem=receives.at[other],
            device_id={"blk": other}, device_id_type=MESH,
        ).wait_recv()
    own().wait()
    rims.wait()


def project_qkv_exchanged(x, gain, bias, weight, qv_bias, g, collective_id):
    rows = x.shape[0]
    blks = lax.axis_size("blk")
    anywhere = pl.BlockSpec(memory_space=pl.ANY)
    vmem = pl.BlockSpec(memory_space=pltpu.VMEM)
    dma = pltpu.SemaphoreType.DMA
    return pl.pallas_call(
        functools.partial(qkv_exchange_kernel, blks),
        in_specs=[vmem] * 4 + [anywhere, anywhere],
        out_specs=[vmem, vmem, vmem, anywhere],
        out_shape=[
            jax.ShapeDtypeStruct((rows, D), bf16),
            jax.ShapeDtypeStruct((WIDE_RIM, D), bf16),
            jax.ShapeDtypeStruct((WIDE_RIM, D), bf16),
            jax.ShapeDtypeStruct((blks, rows, 384), bf16),
        ],
        scratch_shapes=[
            pltpu.VMEM((blks, rows, 384), bf16),
            pltpu.VMEM((blks // 2, 3, D, 256), bf16),
            pltpu.VMEM((2, WIDE_RIM, D), bf16),
            dma((blks // 2, 3)),
            dma((blks,)),
            dma((blks,)),
            dma,
            dma((4,)),
        ],
        compiler_params=params(60, collective_id=collective_id, has_side_effects=True),
        name="norm_qkv",
    )(x, gain, bias, qv_bias, weight, g)


def attention_kernel(starts, counts, qkv, o_ref, lse_ref, value_t):
    step = pl.program_id(0)

    @pl.when(step == 0)
    def _():
        value_t[...] = qkv[:, 256:384].T

    own = pl.ds(pl.multiple_of(step * BLOCK, BLOCK), BLOCK)
    query = qkv[own, 0:128]
    lane = lax.broadcasted_iota(jnp.int32, (BLOCK, 128), 1)
    zero = jnp.zeros_like(query)
    queries = [jnp.where(lane < HEAD, query, zero), jnp.where(lane >= HEAD, query, zero)]
    first, count = starts[step], counts[step]
    for blocks in IMAGE_BLOCKS:

        @pl.when(count == blocks)
        def _(blocks=blocks):
            items = [(head, block) for block in range(blocks) for head in range(2)]

            def rows_of(block):
                return pl.ds(pl.multiple_of((first + block) * BLOCK, BLOCK), BLOCK)

            def scores_of(item):
                return dot_nt(qkv[rows_of(item[1]), 128:256], queries[item[0]])

            scores = [scores_of(item) for item in items[:LOOK]]
            state = {}
            for i, (head, block) in enumerate(items):
                if i + LOOK < len(items):
                    scores.append(scores_of(items[i + LOOK]))
                peak = jnp.max(scores[i], axis=0, keepdims=True)
                if block:
                    old_peak, old_total, old_out = state[head]
                    peak = jnp.maximum(old_peak, peak)
                    shrink = jnp.exp2(old_peak - peak)
                grown = jnp.exp2(scores[i] - peak)
                total = jnp.sum(grown, axis=0, keepdims=True)
                rows = slice(HEAD * head, HEAD * head + HEAD)
                out = dot(value_t[rows, rows_of(block)], grown.astype(bf16))
                if block:
                    total = old_total * shrink + total
                    out = old_out * shrink + out
                state[head] = (peak, total, out)
            outs = [state[head][2] * (1.0 / state[head][1]) for head in range(2)]
            logs = [state[head][0] + jnp.log2(state[head][1]) for head in range(2)]
            o_ref[...] = jnp.concatenate(outs, axis=0).T.astype(bf16)
            lse_ref[...] = jnp.concatenate(logs + [jnp.zeros((6, BLOCK), f32)], axis=0)


def attention(starts, counts, qkv):
    length = qkv.shape[0]
    pairs = 100 * 2 * BLOCK * BLOCK
    return pl.pallas_call(
        attention_kernel,
        grid_spec=pltpu.PrefetchScalarGridSpec(
            num_scalar_prefetch=2,
            grid=(length // BLOCK,),
            in_specs=[whole((length, 384))],
            out_specs=[
                pl.BlockSpec((BLOCK, 128), lambda i, *_: (i, 0)),
                pl.BlockSpec((8, BLOCK), lambda i, *_: (0, i)),
            ],
            scratch_shapes=[pltpu.VMEM((128, length), bf16)],
        ),
        out_shape=[
            jax.ShapeDtypeStruct((length, 128), bf16),
            jax.ShapeDtypeStruct((8, length), f32),
        ],
        compiler_params=params(40),
        cost_estimate=cost(4 * HEAD * pairs, 5 << 20, pairs),
        name="attention",
    )(starts, counts, qkv)


def attention_grad_kernel(
    starts, counts, qkv, do_ref, o_ref, lse, out_ref, query_m, do_m, key_t, dq_t, delta
):
    step = pl.program_id(0)
    length = do_ref.shape[0]
    lane = lax.broadcasted_iota(jnp.int32, (BLOCK, 128), 1)
    low = lane < HEAD

    @pl.when(step == 0)
    def _():
        key_t[...] = qkv[:, 128:256].T
        dq_t[...] = jnp.zeros_like(dq_t)

        def prepare(i, _):
            rows = pl.ds(pl.multiple_of(i * BLOCK, BLOCK), BLOCK)
            grad = do_ref[rows, :]
            product = (grad.astype(f32) * o_ref[rows, :].astype(f32)).T
            delta[0:1, rows] = jnp.sum(product[:HEAD], axis=0, keepdims=True)
            delta[1:2, rows] = jnp.sum(product[HEAD:], axis=0, keepdims=True)
            query = qkv[rows, 0:128]
            zero = jnp.zeros_like(query)
            query_m[0, rows, :] = jnp.where(low, query, zero)
            query_m[1, rows, :] = jnp.where(low, zero, query)
            do_m[0, rows, :] = jnp.where(low, grad, zero)
            do_m[1, rows, :] = jnp.where(low, zero, grad)
            return 0

        lax.fori_loop(0, length // BLOCK, prepare, 0)

    own = pl.ds(pl.multiple_of(step * BLOCK, BLOCK), BLOCK)
    key = qkv[own, 128:256]
    value = qkv[own, 256:384]
    first, count = starts[step], counts[step]
    for blocks in IMAGE_BLOCKS:

        @pl.when(count == blocks)
        def _(blocks=blocks):
            image = pl.ds(pl.multiple_of(first * BLOCK, BLOCK), blocks * BLOCK)
            dk = dv = None
            for head in range(2):
                rows = slice(HEAD * head, HEAD * head + HEAD)
                query, grad = query_m[head, image, :], do_m[head, image, :]
                scores = dot_nt(key, query)
                value_grad = dot_nt(value, grad)
                weights = jnp.exp2(scores - lse[head : head + 1, image])
                score_grad = (weights * (value_grad - delta[head : head + 1, image])).astype(bf16)
                dv_part = dot(weights.astype(bf16), grad)
                dk_part = dot(score_grad, query)
                dv = dv_part if dv is None else dv + dv_part
                dk = dk_part if dk is None else dk + dk_part
                dq_t[rows, image] += dot(key_t[rows, own], score_grad)
            out_ref[own, 128:256] = (dk * (1.0 / LOG2E)).astype(bf16)
            out_ref[own, 256:384] = dv.astype(bf16)

    @pl.when(step == pl.num_programs(0) - 1)
    def _():
        def finish(i, _):
            rows = pl.ds(pl.multiple_of(i * BLOCK, BLOCK), BLOCK)
            out_ref[rows, 0:128] = dq_t[:, rows].T.astype(bf16) * jnp.asarray(HEAD**-0.5, bf16)
            return 0

        lax.fori_loop(0, length // BLOCK, finish, 0)


def attention_grad(starts, counts, qkv, do, o, lse):
    length = qkv.shape[0]
    pairs = 100 * 2 * BLOCK * BLOCK
    return pl.pallas_call(
        attention_grad_kernel,
        grid_spec=pltpu.PrefetchScalarGridSpec(
            num_scalar_prefetch=2,
            grid=(length // BLOCK,),
            in_specs=[
                whole((length, 384)),
                whole((length, 128)),
                whole((length, 128)),
                whole((8, length)),
            ],
            out_specs=whole((length, 384)),
            scratch_shapes=[
                pltpu.VMEM((2, length, 128), bf16),
                pltpu.VMEM((2, length, 128), bf16),
                pltpu.VMEM((128, length), bf16),
                pltpu.VMEM((128, length), f32),
                pltpu.VMEM((8, length), f32),
            ],
        ),
        out_shape=jax.ShapeDtypeStruct((length, 384), bf16),
        compiler_params=params(46),
        cost_estimate=cost(10 * HEAD * pairs, 12 << 20, pairs),
        name="attention_grad",
    )(starts, counts, qkv, do, o, lse)


FF_TILE = 512


def mlp_kernel(
    blks, o_ref, x_ref, wp_ref, pb_ref, gain_ref, bias_ref, wu_ref, ub_ref, wd_ref, db_ref,
    x1_ref, h_ref, act_ref, slope_ref, out_ref, top, bottom, total, landing, rim_sem,
):
    step = pl.program_id(0)

    @pl.when(step == 0)
    def _():
        greet_signal(blks)
        attended = jnp.concatenate([o_ref[i] for i in range(o_ref.shape[0])], axis=1)
        x1 = x_ref[...].astype(f32) + dot(attended, wp_ref[...]) + pb_ref[...]
        x1_ref[...] = x1
        normed, _ = layer_stats(x1)
        h_ref[...] = (normed * gain_ref[...] + bias_ref[...]).astype(bf16)
        total[...] = x1 + db_ref[...]

    raised = dot(h_ref[...], wu_ref[...]) + ub_ref[...]
    cumulative, weighted = gelu_parts(raised)
    act = (raised * cumulative).astype(bf16)
    act_ref[...] = act
    slope_ref[...] = (cumulative + weighted).astype(bf16)
    total[...] += dot(act, wd_ref[...])

    @pl.when(step == pl.num_programs(0) - 1)
    def _():
        out_ref[...] = total[...].astype(bf16)
        greet_wait(blks)
        rims = Rims(blks, out_ref, top, bottom, landing, rim_sem)
        rims.start()
        rims.wait()


def mlp(o, x, wp, pb, gain, bias, wu, ub, wd, db, collective_id):
    rows = x.shape[0]
    groups = o.shape[0]
    tile = 2 * FF_TILE
    return pl.pallas_call(
        functools.partial(mlp_kernel, lax.axis_size("blk")),
        grid=(FF // tile,),
        in_specs=[
            whole((groups, rows, 128)),
            whole((rows, D)),
            whole((D, D)),
            whole((1, D)),
            whole((1, D)),
            whole((1, D)),
            pl.BlockSpec((D, tile), lambda i: (0, i)),
            pl.BlockSpec((1, tile), lambda i: (0, i)),
            pl.BlockSpec((tile, D), lambda i: (i, 0)),
            whole((1, D)),
        ],
        out_specs=[
            whole((rows, D)),
            whole((rows, D)),
            pl.BlockSpec((rows, tile), lambda i: (0, i)),
            pl.BlockSpec((rows, tile), lambda i: (0, i)),
            whole((rows, D)),
            whole((RIM, D)),
            whole((RIM, D)),
        ],
        out_shape=[
            jax.ShapeDtypeStruct((rows, D), f32),
            jax.ShapeDtypeStruct((rows, D), bf16),
            jax.ShapeDtypeStruct((rows, FF), bf16),
            jax.ShapeDtypeStruct((rows, FF), bf16),
            jax.ShapeDtypeStruct((rows, D), bf16),
            jax.ShapeDtypeStruct((RIM, D), bf16),
            jax.ShapeDtypeStruct((RIM, D), bf16),
        ],
        scratch_shapes=[
            pltpu.VMEM((rows, D), f32),
            pltpu.VMEM((2, RIM, D), bf16),
            pltpu.SemaphoreType.DMA((4,)),
        ],
        compiler_params=params(46, collective_id=collective_id, has_side_effects=True),
        cost_estimate=cost(2 * rows * D * (D + 2 * FF), 34 << 20, rows * FF),
        name="proj_norm_mlp",
    )(o, x, wp, pb, gain, bias, wu, ub, wd, db)


def mlp_grad_kernel(
    dy_ref, dm_ref, slope_ref, wd_ref, wu_ref, x1_ref, gain_ref, wp_ref,
    du_ref, dub_ref, dx1_ref, da_ref, do_ref, sums_ref, total,
):
    step = pl.program_id(0)

    @pl.when(step == 0)
    def _():
        total[...] = jnp.zeros_like(total)

    act_grad = dot_nt(dm_ref[...], wd_ref[...])
    raised_low = (act_grad * slope_ref[...].astype(f32)).astype(bf16)
    du_ref[...] = raised_low
    dub_ref[...] = column_sums(raised_low.astype(f32))
    total[...] += dot_nt(raised_low, wu_ref[...])

    @pl.when(step == pl.num_programs(0) - 1)
    def _():
        grad = total[...]
        normed, scale_inv = layer_stats(x1_ref[...])
        dx1 = dy_ref[...] + layer_backward(grad, normed, scale_inv, gain_ref[...])
        dx1_ref[...] = dx1
        low = dx1.astype(bf16)
        da_ref[...] = low
        sums_ref[0:1, :] = column_sums(low.astype(f32))
        sums_ref[1:2, :] = column_sums(grad * normed)
        sums_ref[2:3, :] = column_sums(grad)
        sums_ref[3:4, :] = column_sums(dm_ref[...].astype(f32))
        sums_ref[4:8, :] = jnp.zeros((4, D), f32)
        attended_grad = dot_nt(low, wp_ref[...]).astype(bf16)
        for i in range(do_ref.shape[0]):
            do_ref[i] = attended_grad[:, 128 * i : 128 * i + 128]


def mlp_grad(dy, dm, slope, wd, wu, x1, gain, wp):
    rows = dy.shape[0]
    groups = D // 128
    tile = 2 * FF_TILE
    return pl.pallas_call(
        mlp_grad_kernel,
        grid=(FF // tile,),
        in_specs=[
            whole((rows, D)),
            whole((rows, D)),
            pl.BlockSpec((rows, tile), lambda i: (0, i)),
            pl.BlockSpec((tile, D), lambda i: (i, 0)),
            pl.BlockSpec((D, tile), lambda i: (0, i)),
            whole((rows, D)),
            whole((1, D)),
            whole((D, D)),
        ],
        out_specs=[
            pl.BlockSpec((rows, tile), lambda i: (0, i)),
            pl.BlockSpec((1, tile), lambda i: (0, i)),
            whole((rows, D)),
            whole((rows, D)),
            whole((groups, rows, 128)),
            whole((8, D)),
        ],
        out_shape=[
            jax.ShapeDtypeStruct((rows, FF), bf16),
            jax.ShapeDtypeStruct((1, FF), f32),
            jax.ShapeDtypeStruct((rows, D), f32),
            jax.ShapeDtypeStruct((rows, D), bf16),
            jax.ShapeDtypeStruct((groups, rows, 128), bf16),
            jax.ShapeDtypeStruct((8, D), f32),
        ],
        scratch_shapes=[pltpu.VMEM((rows, D), f32)],
        compiler_params=params(46),
        cost_estimate=cost(2 * rows * D * (D + 2 * FF), 34 << 20),
        name="mlp_norm_proj_grad",
    )(dy, dm, slope, wd, wu, x1, gain, wp)


def down_weight_kernel(act_ref, dm_ref, dwd_ref):
    dwd_ref[...] = dot_tn(act_ref[...], dm_ref[...]).astype(bf16)


def down_weight_grad_of(act, dm):
    rows = dm.shape[0]
    tile = FF_TILE
    return pl.pallas_call(
        down_weight_kernel,
        grid=(FF // tile,),
        in_specs=[pl.BlockSpec((rows, tile), lambda i: (0, i)), whole((rows, D))],
        out_specs=pl.BlockSpec((tile, D), lambda i: (i, 0)),
        out_shape=jax.ShapeDtypeStruct((FF, D), bf16),
        compiler_params=params(32),
        cost_estimate=cost(2 * rows * D * FF, 13 << 20),
        name="down_weight_grad",
    )(act, dm)


def conv_weight_kernel(x_ref, taps_ref, dw_ref, x_t):
    @pl.when(pl.program_id(0) == 0)
    def _():
        x_t[...] = x_ref[...].T

    for tap in range(3):
        dw_ref[D * tap : D * tap + D, :] = dot(x_t[...], taps_ref[tap]).astype(bf16)


def conv_weight_grad_of(x, taps):
    rows = x.shape[0]
    return pl.pallas_call(
        conv_weight_kernel,
        grid=(3,),
        in_specs=[whole((rows, D)), pl.BlockSpec((3, rows, C), lambda i: (i, 0, 0))],
        out_specs=pl.BlockSpec((3 * D, C), lambda i: (i, 0)),
        out_shape=jax.ShapeDtypeStruct((9 * D, C), bf16),
        scratch_shapes=[pltpu.VMEM((D, rows), bf16)],
        compiler_params=params(32),
        cost_estimate=cost(2 * rows * D * 9 * C, 9 << 20),
        name="conv_weight_grad",
    )(x, taps)


def exchange_semaphores(blks):
    count = max(blks, 1)
    return [
        pltpu.SemaphoreType.DMA((count,)),
        pltpu.SemaphoreType.DMA((count,)),
        pltpu.SemaphoreType.DMA,
    ]


def exchange_params(blks, megabytes, collective_id):
    if blks:
        return params(megabytes, collective_id=collective_id, has_side_effects=True)
    return params(megabytes)


def late_weights_kernel(h_ref, du_ref, o_ref, da_ref, dwu_ref, dwp_ref, h_t):
    @pl.when(pl.program_id(0) == 0)
    def _():
        h_t[...] = h_ref[...].T
        attended = jnp.concatenate([o_ref[i] for i in range(o_ref.shape[0])], axis=1)
        dwp_ref[...] = dot_tn(attended, da_ref[...]).astype(bf16)

    dwu_ref[...] = dot(h_t[...], du_ref[...]).astype(bf16)


def late_weights(h, du, o, da):
    rows = h.shape[0]
    groups = D // 128
    tile = FF_TILE
    return pl.pallas_call(
        late_weights_kernel,
        grid=(FF // tile,),
        in_specs=[
            whole((rows, D)),
            pl.BlockSpec((rows, tile), lambda i: (0, i)),
            whole((groups, rows, 128)),
            whole((rows, D)),
        ],
        out_specs=[pl.BlockSpec((D, tile), lambda i: (0, i)), whole((D, D))],
        out_shape=[jax.ShapeDtypeStruct((D, FF), bf16), jax.ShapeDtypeStruct((D, D), bf16)],
        scratch_shapes=[pltpu.VMEM((D, rows), bf16)],
        compiler_params=params(40),
        cost_estimate=cost(2 * rows * D * (FF + D), 18 << 20),
        name="up_proj_weight_grads",
    )(h, du, o, da)


def weights_kernel(
    blks, act_ref, dm_ref, h_ref, du_ref, x_ref, taps_ref, o_ref, da_ref, sent,
    dw_ref, dwp_ref, moved, down_keep, down_send, up_keep, up_send,
    down, up, down_near, up_near, h_t, x_t, ex_send, ex_recv, ex_own, ds, dr, us, ur, do_sem, uo_sem,
):
    step = pl.program_id(0)
    steps = FF // FF_TILE
    blk = lax.axis_index("blk")
    core, x, y = blk % 2, (blk // 2) % 2, blk // 4
    exchange = (blks, sent, moved, ex_send, ex_recv, ex_own)

    def to_pair(source, target, sent_sem, received):
        return pltpu.make_async_remote_copy(
            src_ref=source, dst_ref=target, send_sem=sent_sem, recv_sem=received,
            device_id={"blk": blk + 1 - 2 * core}, device_id_type=MESH,
        )

    def down_copy(i):
        return to_pair(down.at[i, 1 - core], down_near.at[i + 1], ds.at[i], dr.at[i])

    def up_columns(t):
        return pl.ds(pl.multiple_of(t * FF_TILE, FF_TILE), FF_TILE)

    def up_copy(t):
        return to_pair(up.at[:, 1 - core, :, up_columns(t)], up_near.at[t + 1], us.at[t], ur.at[t])

    def down_out(i, keep):
        return pltpu.make_async_copy(
            down.at[i, core], (down_keep if keep else down_send).at[i // 2], do_sem.at[i]
        )

    def up_out(t, i, keep):
        return pltpu.make_async_copy(
            up.at[i, core, :, up_columns(t)],
            (up_keep if keep else up_send).at[i % 2, :, up_columns(t)],
            uo_sem.at[t, i],
        )

    def add_down(i, slot, half):
        rows = pl.ds(pl.multiple_of(half * (FF // 16), FF // 16), FF // 16)
        down[i, core, rows] = (
            down[i, core, rows].astype(f32) + down_near[slot, rows].astype(f32)
        ).astype(bf16)

    def out_down(i):
        for keep in (True, False):

            @pl.when((i % 2 == x) == keep)
            def _(keep=keep):
                down_out(i, keep).start()

    def add_up(t, slot):
        columns = up_columns(t)
        for i in range(4):
            up[i, core, :, columns] = (
                up[i, core, :, columns].astype(f32) + up_near[slot, i].astype(f32)
            ).astype(bf16)

    def out_up(t):
        for i in range(4):
            for keep in (True, False):

                @pl.when((i // 2 == y) == keep)
                def _(i=i, keep=keep):
                    up_out(t, i, keep).start()

    @pl.when(step == 0)
    def _():
        greet_signal(blks)
        h_t[...] = h_ref[...].T
        x_t[...] = x_ref[...].T
        greet_wait(blks)
        exchange_start(*exchange)

    piece = (step + 1) // 2 - 2

    @pl.when(step >= 2)
    def _():
        up_copy(step - 2).wait_recv()

    @pl.when((step >= 3) & (step % 2 == 1))
    def _():
        down_copy(piece).wait_recv()

    add_up(lax.rem(step + steps - 2, steps), jnp.maximum(step - 1, 0))
    add_down(lax.rem(piece + 4, 4), jnp.maximum(piece + 1, 0), (step + 1) % 2)
    down[step // 2, step % 2] = dot_tn(act_ref[...], dm_ref[...]).astype(bf16)
    up[:, :, :, up_columns(step)] = (
        dot(h_t[...], du_ref[...]).astype(bf16).reshape(4, 2, D // 8, FF_TILE)
    )

    @pl.when(step % 2 != core)
    def _():
        down_copy(step // 2).start()

    up_copy(step).start()

    @pl.when(step >= 2)
    def _():
        out_up(step - 2)

    @pl.when((step >= 4) & (step % 2 == 0))
    def _():
        out_down(piece)

    @pl.when(step < 3)
    def _():
        for tap in range(3):
            dw_ref[D * tap : D * tap + D, :] = dot(x_t[...], taps_ref[tap]).astype(bf16)

    @pl.when(step == 3)
    def _():
        attended = jnp.concatenate([o_ref[i] for i in range(o_ref.shape[0])], axis=1)
        dwp_ref[...] = dot_tn(attended, da_ref[...]).astype(bf16)

    @pl.when(step == steps - 1)
    def _():
        add_down(2, 3, 1)
        out_down(2)
        for t in (steps - 2, steps - 1):
            up_copy(t).wait_recv()
            add_up(t, t + 1)
            out_up(t)
        down_copy(3).wait_recv()
        for half in range(2):
            add_down(3, 4, half)
        out_down(3)
        exchange_wait(*exchange)
        for t in range(steps):
            up_copy(t).wait_send()
            for i in range(4):
                up_out(t, i, True).wait()
        for i in range(4):
            down_copy(i).wait_send()
            down_out(i, True).wait()


def weights(act, dm, h, du, x, taps, o, da, sent, blks, collective_id):
    rows = h.shape[0]
    groups = D // 128
    tile = FF_TILE
    steps = FF // tile
    anywhere = pl.BlockSpec(memory_space=pl.ANY)
    third = lambda i: jnp.minimum(i, 2)
    dma = pltpu.SemaphoreType.DMA
    half_down, half_up = (2, FF // 8, D), (2, D // 8, FF)
    return pl.pallas_call(
        functools.partial(weights_kernel, blks),
        grid=(steps,),
        in_specs=[
            pl.BlockSpec((rows, tile), lambda i: (0, i)),
            whole((rows, D)),
            whole((rows, D)),
            pl.BlockSpec((rows, tile), lambda i: (0, i)),
            whole((rows, D)),
            pl.BlockSpec((3, rows, C), lambda i: (third(i), 0, 0)),
            whole((groups, rows, 128)),
            whole((rows, D)),
            anywhere,
        ],
        out_specs=[pl.BlockSpec((3 * D, C), lambda i: (third(i), 0)), whole((D, D))]
        + [anywhere] * 5,
        out_shape=[
            jax.ShapeDtypeStruct(shape, bf16)
            for shape in ((9 * D, C), (D, D), sent.shape, half_down, half_down, half_up, half_up)
        ],
        scratch_shapes=[
            pltpu.VMEM((4, 2, FF // 8, D), bf16),
            pltpu.VMEM((4, 2, D // 8, FF), bf16),
            pltpu.VMEM((5, FF // 8, D), bf16),
            pltpu.VMEM((steps + 1, 4, D // 8, FF_TILE), bf16),
            pltpu.VMEM((D, rows), bf16),
            pltpu.VMEM((D, rows), bf16),
        ]
        + exchange_semaphores(blks)
        + [dma((4,)), dma((4,)), dma((steps,)), dma((steps,)), dma((4,)), dma((steps, 4))],
        compiler_params=exchange_params(blks, 62, collective_id),
        cost_estimate=cost(2 * rows * D * (2 * FF + D + 9 * C), 50 << 20),
        name="weight_grads",
    )(act, dm, h, du, x, taps, o, da, sent)


def qkv_grad_kernel(
    g_ref, wq_ref, wk_ref, wv_ref, h_ref, dx1_ref, x_ref, gain_ref,
    dw_ref, dqb_ref, dvb_ref, dx_ref, sums_ref, h_t, total,
):
    step = pl.program_id(0)

    @pl.when(step == 0)
    def _():
        h_t[...] = h_ref[...].T
        total[...] = jnp.zeros_like(total)

    for part, w_ref in enumerate((wq_ref, wk_ref, wv_ref)):
        lanes = slice(128 * part, 128 * part + 128)
        grad = jnp.concatenate([g_ref[0, :, lanes], g_ref[1, :, lanes]], axis=1)
        total[...] += dot_nt(grad, w_ref[...])
        dw_ref[part] = dot(h_t[...], grad).astype(bf16)
        if part == 0:
            dqb_ref[...] = column_sums(grad.astype(f32))
        if part == 2:
            dvb_ref[...] = column_sums(grad.astype(f32))

    @pl.when(step == pl.num_programs(0) - 1)
    def _():
        grad = total[...]
        normed, scale_inv = layer_stats(x_ref[...].astype(f32))
        dx_ref[...] = dx1_ref[...] + layer_backward(grad, normed, scale_inv, gain_ref[...])
        sums_ref[0:1, :] = column_sums(grad * normed)
        sums_ref[1:2, :] = column_sums(grad)
        sums_ref[2:8, :] = jnp.zeros((6, D), f32)


def qkv_grad(g, weight, h, dx1, x, gain):
    rows = x.shape[0]
    groups = D // 128
    return pl.pallas_call(
        qkv_grad_kernel,
        grid=(groups // 2,),
        in_specs=[
            pl.BlockSpec((2, rows, 384), lambda i: (i, 0, 0)),
            pl.BlockSpec((D, 256), lambda i: (0, i)),
            pl.BlockSpec((D, 256), lambda i: (0, 4 + i)),
            pl.BlockSpec((D, 256), lambda i: (0, 8 + i)),
            whole((rows, D)),
            whole((rows, D)),
            whole((rows, D)),
            whole((1, D)),
        ],
        out_specs=[
            pl.BlockSpec((3, D, 256), lambda i: (0, 0, i)),
            pl.BlockSpec((1, 256), lambda i: (0, i)),
            pl.BlockSpec((1, 256), lambda i: (0, i)),
            whole((rows, D)),
            whole((8, D)),
        ],
        out_shape=[
            jax.ShapeDtypeStruct((3, D, D), bf16),
            jax.ShapeDtypeStruct((1, D), f32),
            jax.ShapeDtypeStruct((1, D), f32),
            jax.ShapeDtypeStruct((rows, D), f32),
            jax.ShapeDtypeStruct((8, D), f32),
        ],
        scratch_shapes=[pltpu.VMEM((D, rows), bf16), pltpu.VMEM((rows, D), f32)],
        compiler_params=params(48),
        cost_estimate=cost(4 * rows * D * 3 * D, 24 << 20),
        name="qkv_norm_grad",
    )(g, weight, weight, weight, h, dx1, x, gain)


def row_segments(rows, rim):
    count = rows // BLOCK
    pieces = []
    for block in range(count):
        first = block * BLOCK - (rim if block == 0 else 0)
        last = (block + 1) * BLOCK + (rim if block == count - 1 else 0)
        pieces.append((first, last - first, block))
    return pieces


def shifted_rows(start, shift, size):
    return pl.ds(pl.multiple_of(start + shift, UNIT), size)


def conv_kernel(widths, x_ref, top_ref, bottom_ref, flags, w_ref, z_ref, sums_ref, x_ext, left, right, centre):
    step = pl.program_id(0)
    rows = x_ref.shape[0]
    extent = rows + 2 * RIM

    @pl.when(step == 0)
    def _():
        x_ext[0:RIM, :] = top_ref[...]
        x_ext[RIM : RIM + rows, :] = x_ref[...]
        x_ext[RIM + rows :, :] = bottom_ref[...]
        left[...] = jnp.zeros_like(left)
        right[...] = jnp.zeros_like(right)

    source = x_ext[...]
    left[8 : 8 + extent, :] = dot(source, w_ref[0:D, :])
    right[8 : 8 + extent, :] = dot(source, w_ref[2 * D : 3 * D, :])
    centre[...] = (
        dot(source, w_ref[D : 2 * D, :])
        + flags[:, 2:3] * left[7 : 7 + extent, :]
        + flags[:, 3:4] * right[9 : 9 + extent, :]
    )
    for first, size, block in row_segments(rows, 0):
        own = slice(first, first + size)
        width = widths[block]
        for tap in range(3):

            @pl.when(step == tap)
            def _(tap=tap, first=first, size=size, own=own, width=width):
                found = centre[shifted_rows(RIM + first, (tap - 1) * width, size), :]
                if tap == 0:
                    z_ref[own, :] = flags[RIM + first : RIM + first + size, 0:1] * found
                elif tap == 1:
                    z_ref[own, :] += found
                else:
                    z_ref[own, :] += flags[RIM + first : RIM + first + size, 1:2] * found

    @pl.when(step == 2)
    def _():
        z = z_ref[...]
        sums_ref[0:1, :] = column_sums(z)
        sums_ref[1:2, :] = column_sums(z * z)
        sums_ref[2:8, :] = jnp.zeros((6, C), f32)


def conv(widths, x, top, bottom, flags, weight):
    rows = x.shape[0]
    extent = rows + 2 * RIM
    return pl.pallas_call(
        conv_kernel,
        grid_spec=pltpu.PrefetchScalarGridSpec(
            num_scalar_prefetch=1,
            grid=(3,),
            in_specs=[
                whole((rows, D)),
                whole((RIM, D)),
                whole((RIM, D)),
                whole((extent, 8)),
                pl.BlockSpec((3 * D, C), lambda i, *_: (i, 0)),
            ],
            out_specs=[whole((rows, C)), whole((8, C))],
            scratch_shapes=[
                pltpu.VMEM((extent, D), bf16),
                pltpu.VMEM((extent + 16, C), f32),
                pltpu.VMEM((extent + 16, C), f32),
                pltpu.VMEM((extent, C), f32),
            ],
        ),
        out_shape=[jax.ShapeDtypeStruct((rows, C), f32), jax.ShapeDtypeStruct((8, C), f32)],
        compiler_params=params(26),
        cost_estimate=cost(2 * extent * 9 * D * C, 8 << 20),
        name="conv",
    )(widths, x, top, bottom, flags, weight)


def spread_kernel(widths, g_ref, top_ref, bottom_ref, flags, out_ref, upper, lower, g_ext):
    rows = g_ref.shape[0]
    extent = rows + 2 * WIDE_RIM
    g_ext[0:WIDE_RIM, :] = top_ref[...].astype(f32)
    g_ext[WIDE_RIM : WIDE_RIM + rows, :] = g_ref[...].astype(f32)
    g_ext[WIDE_RIM + rows :, :] = bottom_ref[...].astype(f32)
    inner = slice(8, extent - 8)
    has_left, has_right = flags[inner, 2:3], flags[inner, 3:4]
    for i, target in enumerate((upper, lower)):
        near = g_ext[:, 2 * i * C : (2 * i + 1) * C]
        far = g_ext[:, (2 * i + 1) * C : (2 * i + 2) * C]
        target[0:8, :] = jnp.zeros((8, C), f32)
        target[extent - 8 :, :] = jnp.zeros((8, C), f32)
        target[inner, :] = (
            (1.0 - 0.25 * has_left) * near[inner, :]
            + (1.0 - 0.25 * has_right) * far[inner, :]
            + 0.25 * has_right * g_ext[9 : extent - 7, 2 * i * C : (2 * i + 1) * C]
            + 0.25 * has_left * g_ext[7 : extent - 9, (2 * i + 1) * C : (2 * i + 2) * C]
        )
    for first, size, block in row_segments(rows, RIM):
        width = widths[block]
        here = WIDE_RIM + first
        has_up, has_down = flags[here : here + size, 0:1], flags[here : here + size, 1:2]
        out_ref[RIM + first : RIM + first + size, :] = (
            (1.0 - 0.25 * has_up) * upper[here : here + size, :]
            + (1.0 - 0.25 * has_down) * lower[here : here + size, :]
            + 0.25 * has_down * upper[shifted_rows(here, width, size), :]
            + 0.25 * has_up * lower[shifted_rows(here, -width, size), :]
        )


def spread(widths, g, top, bottom, flags):
    rows = g.shape[0]
    extent = rows + 2 * WIDE_RIM
    return pl.pallas_call(
        spread_kernel,
        grid_spec=pltpu.PrefetchScalarGridSpec(
            num_scalar_prefetch=1,
            grid=(1,),
            in_specs=[
                whole((rows, D)),
                whole((WIDE_RIM, D)),
                whole((WIDE_RIM, D)),
                whole((extent, 8)),
            ],
            out_specs=whole((rows + 2 * RIM, C)),
            scratch_shapes=[
                pltpu.VMEM((extent, C), f32),
                pltpu.VMEM((extent, C), f32),
                pltpu.VMEM((extent, D), f32),
            ],
        ),
        out_shape=jax.ShapeDtypeStruct((rows + 2 * RIM, C), f32),
        compiler_params=params(24),
        cost_estimate=cost(20 * extent * D, 3 << 20),
        name="upsample_grad",
    )(widths, g, top, bottom, flags)


def batch_kernel(
    widths, z_ref, top_ref, bottom_ref, dact_ref, flags, mean_ref, inv_ref, gain_ref, bias_ref,
    up_ref, normed_ref, dbn_ref, sums_ref, act, mixed,
):
    rows = z_ref.shape[0]
    z = jnp.concatenate([top_ref[...], z_ref[...], bottom_ref[...]], axis=0)
    normed = (z - mean_ref[...]) * inv_ref[...]
    normed_ref[...] = normed
    pre = normed * gain_ref[...] + bias_ref[...]
    cumulative, weighted = gelu_parts(pre)
    act[...] = (pre * cumulative).astype(bf16).astype(f32)
    dbn = dact_ref[...] * (cumulative + weighted)
    dbn_ref[...] = dbn
    own = slice(RIM, RIM + rows)
    sums_ref[0:1, :] = column_sums(dbn[own, :])
    sums_ref[1:2, :] = column_sums(dbn[own, :] * normed[own, :])
    sums_ref[2:8, :] = jnp.zeros((6, C), f32)
    for first, size, block in row_segments(rows, 0):
        width = widths[block]
        here = RIM + first
        outer = slice(here - 8, here + size + 8)
        for i in range(2):
            has = flags[outer, i : i + 1]
            mixed[...] = (1.0 - 0.25 * has) * act[outer, :] + 0.25 * has * act[
                pl.ds(pl.multiple_of(here - 8 + (2 * i - 1) * width, 8), size + 16), :
            ]
            for j in range(2):
                has = flags[here : here + size, 2 + j : 3 + j]
                up_ref[first : first + size, (2 * i + j) * C : (2 * i + j + 1) * C] = (
                    (1.0 - 0.25 * has) * mixed[8 : 8 + size, :]
                    + 0.25 * has * mixed[7 + 2 * j : 7 + 2 * j + size, :]
                ).astype(bf16)


def batch(widths, z, top, bottom, dact, flags, mean, inv, gain, bias):
    rows = z.shape[0]
    extent = rows + 2 * RIM
    return pl.pallas_call(
        batch_kernel,
        grid_spec=pltpu.PrefetchScalarGridSpec(
            num_scalar_prefetch=1,
            grid=(1,),
            in_specs=[
                whole((rows, C)),
                whole((RIM, C)),
                whole((RIM, C)),
                whole((extent, C)),
                whole((extent, 8)),
                whole((1, C)),
                whole((1, C)),
                whole((1, C)),
                whole((1, C)),
            ],
            out_specs=[
                whole((rows, D)),
                whole((extent, C)),
                whole((extent, C)),
                whole((8, C)),
            ],
            scratch_shapes=[pltpu.VMEM((extent, C), f32), pltpu.VMEM((BLOCK + 16, C), f32)],
        ),
        out_shape=[
            jax.ShapeDtypeStruct((rows, D), bf16),
            jax.ShapeDtypeStruct((extent, C), f32),
            jax.ShapeDtypeStruct((extent, C), f32),
            jax.ShapeDtypeStruct((8, C), f32),
        ],
        compiler_params=params(24),
        cost_estimate=cost(60 * extent * C, 4 << 20),
        name="batch_norm",
    )(widths, z, top, bottom, dact, flags, mean, inv, gain, bias)


def conv_grad_kernel(
    widths, dbn_ref, normed_ref, flags, scale_ref, shift_ref, slope_ref, w_ref, og_ref,
    taps, dy_ref, dm_ref, moved,
):
    step = pl.program_id(0)
    rows = og_ref.shape[0]
    extent = rows + 2 * RIM

    @pl.when(step == 0)
    def _():
        dz = scale_ref[...] * (dbn_ref[...] - shift_ref[...] - normed_ref[...] * slope_ref[...])
        dz = dz.astype(bf16).astype(f32)
        dy_ref[...] = og_ref[...].astype(f32)
        moved[0, 0:8, :] = jnp.zeros((8, C), f32)
        moved[0, 8 + extent :, :] = jnp.zeros((8, C), f32)
        moved[0, 8 : 8 + extent, :] = dz
        moved[1, 8 : 8 + extent, :] = flags[:, 3:4] * moved[0, 9 : 9 + extent, :]
        moved[2, 8 : 8 + extent, :] = flags[:, 2:3] * moved[0, 7 : 7 + extent, :]
        for first, size, block in row_segments(rows, 0):
            width = widths[block]
            here = RIM + first
            for row in range(3):
                for col, slot in enumerate((1, 0, 2)):
                    found = moved[slot, pl.ds(pl.multiple_of(8 + here + (1 - row) * width, 8), size), :]
                    if row == 0:
                        found = flags[here : here + size, 1:2] * found
                    if row == 2:
                        found = flags[here : here + size, 0:1] * found
                    taps[3 * row + col, first : first + size, :] = found.astype(bf16)

    for part in range(3):
        dy_ref[...] += dot_nt(taps[3 * step + part], w_ref[D * part : D * part + D, :])

    @pl.when(step == pl.num_programs(0) - 1)
    def _():
        dm_ref[...] = dy_ref[...].astype(bf16)


def conv_grad(widths, dbn, normed, flags, scale, shift, slope, weight, out_grad):
    rows = out_grad.shape[0]
    extent = rows + 2 * RIM
    return pl.pallas_call(
        conv_grad_kernel,
        grid_spec=pltpu.PrefetchScalarGridSpec(
            num_scalar_prefetch=1,
            grid=(3,),
            in_specs=[
                whole((extent, C)),
                whole((extent, C)),
                whole((extent, 8)),
                whole((1, C)),
                whole((1, C)),
                whole((1, C)),
                pl.BlockSpec((3 * D, C), lambda i, *_: (i, 0)),
                whole((rows, D)),
            ],
            out_specs=[whole((9, rows, C)), whole((rows, D)), whole((rows, D))],
            scratch_shapes=[pltpu.VMEM((3, extent + 16, C), f32)],
        ),
        out_shape=[
            jax.ShapeDtypeStruct((9, rows, C), bf16),
            jax.ShapeDtypeStruct((rows, D), f32),
            jax.ShapeDtypeStruct((rows, D), bf16),
        ],
        compiler_params=params(32),
        cost_estimate=cost(2 * rows * 9 * D * C, 12 << 20),
        name="conv_grad",
    )(widths, dbn, normed, flags, scale, shift, slope, weight, out_grad)


def small_sum_kernel(scatter, blks, seqs, rimmed, x_ref, *refs):
    blk, seq = lax.axis_index("blk"), lax.axis_index("seq")
    if rimmed:
        z_ref, out_ref, top, bottom, *refs = refs
    else:
        out_ref, *refs = refs
    first, second, sends, receives, sends2, receives2 = refs[:6]
    barrier = pltpu.get_barrier_semaphore()
    for step in range(1, blks):
        pl.semaphore_signal(
            barrier, inc=1, device_id={"blk": lax.rem(blk + step, blks)}, device_id_type=MESH
        )
    for step in range(1, seqs):
        pl.semaphore_signal(
            barrier, inc=1, device_id={"seq": lax.rem(seq + step, seqs)}, device_id_type=MESH
        )
    pl.semaphore_wait(barrier, blks + seqs - 2)
    copies = []
    for step in range(1, blks):
        to = lax.rem(blk + step, blks)
        copy = pltpu.make_async_remote_copy(
            src_ref=x_ref.at[to] if scatter else x_ref.at[0],
            dst_ref=first.at[blk],
            send_sem=sends.at[step],
            recv_sem=receives.at[step],
            device_id={"blk": to},
            device_id_type=MESH,
        )
        copy.start()
        copies.append(copy)
    if rimmed:
        rims = Rims(blks, z_ref, top, bottom, *refs[6:])
        rims.start()
    first[blk] = x_ref[blk] if scatter else x_ref[0]
    for copy in copies:
        copy.wait()
    total = first[0]
    for i in range(1, blks):
        total = total + first[i]
    second[seq] = total
    copies = []
    for step in range(1, seqs):
        copy = pltpu.make_async_remote_copy(
            src_ref=second.at[seq],
            dst_ref=second.at[seq],
            send_sem=sends2.at[step],
            recv_sem=receives2.at[step],
            device_id={"seq": lax.rem(seq + step, seqs)},
            device_id_type=MESH,
        )
        copy.start()
        copies.append(copy)
    for copy in copies:
        copy.wait()
    total = second[0]
    for i in range(1, seqs):
        total = total + second[i]
    out_ref[...] = total
    if rimmed:
        rims.wait()


def small_sum(x, scatter, collective_id, rimmed=None):
    blks, seqs = lax.axis_size("blk"), lax.axis_size("seq")
    part = x.shape[1:]
    vmem = pl.BlockSpec(memory_space=pltpu.VMEM)
    given, found, extra = [x], [jax.ShapeDtypeStruct(part, f32)], []
    if rimmed is not None:
        given.append(rimmed)
        found += [jax.ShapeDtypeStruct((RIM, rimmed.shape[1]), f32)] * 2
        extra.append(pltpu.VMEM((2, RIM, rimmed.shape[1]), f32))
        extra.append(pltpu.SemaphoreType.DMA((4,)))
    found = pl.pallas_call(
        functools.partial(small_sum_kernel, scatter, blks, seqs, rimmed is not None),
        in_specs=[vmem] * len(given),
        out_specs=[vmem] * len(found),
        out_shape=found,
        scratch_shapes=[
            pltpu.VMEM((blks, *part), f32),
            pltpu.VMEM((seqs, *part), f32),
            pltpu.SemaphoreType.DMA((blks,)),
            pltpu.SemaphoreType.DMA((blks,)),
            pltpu.SemaphoreType.DMA((seqs,)),
            pltpu.SemaphoreType.DMA((seqs,)),
        ]
        + extra,
        compiler_params=params(16, collective_id=collective_id, has_side_effects=True),
        name="small_sum",
    )(*given)
    return found if rimmed is not None else found[0]


LAG = 2
PIECE_ROWS = 64
SLOTS = 3
ROOT = 1


def cuts(size, piece):
    return [slice(first, min(size, first + piece)) for first in range(0, size, piece)]


def pieces_of(index, shape):
    parts, rows, columns = shape
    piece = PIECE_ROWS if columns >= D else 3 * PIECE_ROWS
    return [
        (index, part, row, column)
        for part in range(parts)
        for row in cuts(rows, piece)
        for column in cuts(columns, D)
    ]


class Reducer:
    @staticmethod
    def scratch(shapes, dtypes, staged, halves, units):
        places = []
        for lead in ((4,), (2,), (), (), ()):
            places += [
                pltpu.VMEM(
                    (shape[0],) + ((2,) if lead and index in halves else lead) + shape[1:], dtype
                )
                for index, (shape, dtype) in enumerate(zip(shapes, dtypes))
            ]
        for index in range(len(shapes)):
            _, _, rows, columns = next(unit for unit in units if unit[0] == index)
            size = (rows.stop - rows.start, columns.stop - columns.start)
            size = (SLOTS, 4) + size if index in staged else (1, 1, 16, 128)
            places.append(pltpu.VMEM(size, dtypes[index]))
        total = len(units)
        semaphores = [pltpu.SemaphoreType.DMA((total, 2))] * 2
        semaphores += [pltpu.SemaphoreType.DMA((total,))] * 10
        return places + semaphores

    def __init__(self, seqs, units, staged, halves, ins, outs, refs):
        count = len(ins)
        self.seqs, self.units, self.staged, self.ins, self.outs = seqs, units, staged, ins, outs
        self.halves = halves
        self.sums, self.side, self.last, self.below, self.above, self.slots = [
            refs[i * count : (i + 1) * count] for i in range(6)
        ]
        (self.s2, self.r2, self.load_sem, self.s1, self.r1, self.s3, self.r3, self.sb, self.rb,
         self.sa, self.ra, self.out_sem) = refs[6 * count :]
        blk, self.seq = lax.axis_index("blk"), lax.axis_index("seq")
        self.core, self.x, self.y = blk % 2, (blk // 2) % 2, blk // 4
        self.pair = {"blk": blk + 1 - 2 * self.core}
        self.over_x = {"blk": blk + 2 - 4 * self.x}
        self.over_y = {"blk": blk + 4 - 8 * self.y}
        self.order = {}
        for u, unit in enumerate(units):
            self.order.setdefault(unit[0], []).append(u)

    def send(self, source, target, sent, received, peer):
        return pltpu.make_async_remote_copy(
            src_ref=source, dst_ref=target, send_sem=sent, recv_sem=received,
            device_id=peer, device_id_type=MESH,
        )

    def own(self, u):
        index, part, rows, columns = self.units[u]
        if index in self.staged:
            return self.slots[index].at[self.order[index].index(u) % SLOTS]
        return self.ins[index].at[part, :, self.core, rows, columns]

    def load(self, u):
        index, part, rows, columns = self.units[u]
        return pltpu.make_async_copy(
            self.ins[index].at[part, :, self.core, rows, columns], self.own(u), self.load_sem.at[u]
        )

    def load_half(self, u):
        index, part, rows, columns = self.units[u]
        kept, arrived = self.ins[index]
        return [
            pltpu.make_async_copy(
                kept.at[:, rows, columns], self.sums[index].at[part, :, rows, columns], self.load_sem.at[u]
            ),
            pltpu.make_async_copy(
                arrived.at[:, rows, columns], self.side[index].at[part, :, rows, columns], self.r1.at[u]
            ),
        ]

    def over_x_first(self, u):
        index = self.units[u][0]
        if index in self.halves:
            return self.halves[index] == 0
        return [v for v, unit in enumerate(self.units) if unit[0] not in self.halves].index(u) % 2 == 0

    def first(self, u):
        index, part, rows, columns = self.units[u]
        return self.send(
            self.ins[index].at[part, :, 1 - self.core, rows, columns],
            self.sums[index].at[part, :, rows, columns],
            self.s1.at[u], self.r1.at[u], self.pair,
        )

    def second(self, u):
        index, part, rows, columns = self.units[u]
        copies = []
        for i in range(2):
            x_first = self.over_x_first(u)
            place = 1 - self.x + 2 * i if x_first else 2 * (1 - self.y) + i
            copies.append(
                self.send(
                    self.sums[index].at[part, place, rows, columns],
                    self.side[index].at[part, i, rows, columns],
                    self.s2.at[u, i], self.r2.at[u, i], self.over_x if x_first else self.over_y,
                )
            )
        return copies

    def third(self, u):
        index, part, rows, columns = self.units[u]
        x_first = self.over_x_first(u)
        if index in self.halves:
            place = 1 - self.y if x_first else 1 - self.x
        else:
            place = 2 * (1 - self.y) + self.x if x_first else 2 * self.y + 1 - self.x
        return self.send(
            self.sums[index].at[part, place, rows, columns],
            self.last[index].at[part, rows, columns],
            self.s3.at[u], self.r3.at[u], self.over_y if x_first else self.over_x,
        )

    def result(self, u):
        index, part, rows, columns = self.units[u]
        if index in self.halves:
            return self.sums[index].at[part, self.y if self.over_x_first(u) else self.x, rows, columns]
        return self.sums[index].at[part, 2 * self.y + self.x, rows, columns]

    def down(self, u):
        index, part, rows, columns = self.units[u]
        return self.send(
            self.result(u), self.above[index].at[part, rows, columns],
            self.sa.at[u], self.ra.at[u], {"seq": self.seq - 1},
        )

    def up(self, u):
        index, part, rows, columns = self.units[u]
        return self.send(
            self.result(u), self.below[index].at[part, rows, columns],
            self.sb.at[u], self.rb.at[u], {"seq": self.seq + 1},
        )

    def store(self, u):
        index, part, rows, columns = self.units[u]
        return pltpu.make_async_copy(
            self.result(u), self.outs[index].at[part, rows, columns], self.out_sem.at[u]
        )

    def add_to(self, target, *sources):
        total = target[...].astype(f32)
        for source in sources:
            total = total + source[...].astype(f32)
        target[...] = total.astype(target.dtype)

    def enter(self, u):
        if self.units[u][0] in self.halves:
            for copy in self.load_half(u):
                copy.start()
            return
        self.first(u).start()
        index = self.units[u][0]
        if index in self.staged and self.order[index].index(u) < SLOTS:
            self.load(u).start()

    def stage_near(self, u):
        index, part, rows, columns = self.units[u]
        if index in self.halves:
            return
        if index in self.staged:
            self.load(u).wait()
        self.first(u).wait_recv()
        own = self.own(u)
        for i in range(4):
            self.add_to(self.sums[index].at[part, i, rows, columns], own.at[i])
        if index in self.staged:
            later = self.order[index].index(u) + SLOTS
            if later < len(self.order[index]):
                self.load(self.order[index][later]).start()
        for copy in self.second(u):
            copy.start()

    def stage_side(self, u):
        index, part, rows, columns = self.units[u]
        if index in self.halves:
            for copy in self.load_half(u):
                copy.wait()
            for i in range(2):
                self.add_to(
                    self.sums[index].at[part, i, rows, columns],
                    self.side[index].at[part, i, rows, columns],
                )
            self.third(u).start()
            return
        for i, copy in enumerate(self.second(u)):
            copy.wait_recv()
            keep = 2 * i + self.x if self.over_x_first(u) else 2 * self.y + i
            self.add_to(
                self.sums[index].at[part, keep, rows, columns],
                self.side[index].at[part, i, rows, columns],
            )
        self.third(u).start()

    def stage_last(self, u):
        index, part, rows, columns = self.units[u]
        self.third(u).wait_recv()
        self.add_to(self.result(u), self.last[index].at[part, rows, columns])

        @pl.when(self.seq < ROOT)
        def _():
            self.up(u).start()

        @pl.when(self.seq == self.seqs - 1)
        def _():
            self.down(u).start()

    def stage_chain(self, u, place):
        index, part, rows, columns = self.units[u]

        @pl.when(self.seq == place)
        def _():
            self.down(u).wait_recv()
            self.add_to(self.result(u), self.above[index].at[part, rows, columns])
            self.down(u).start()

    def stage_root(self, u):
        index, part, rows, columns = self.units[u]

        @pl.when(self.seq == ROOT)
        def _():
            self.up(u).wait_recv()
            self.down(u).wait_recv()
            self.add_to(
                self.result(u),
                self.below[index].at[part, rows, columns],
                self.above[index].at[part, rows, columns],
            )
            self.up(u).start()
            self.down(u).start()
            self.store(u).start()

    def stage_spread(self, u, place):
        index, part, rows, columns = self.units[u]

        @pl.when(self.seq == place)
        def _():
            if place < ROOT:
                self.down(u).wait_recv()
                self.up(u).wait_send()
                self.result(u)[...] = self.above[index].at[part, rows, columns][...]
            else:
                self.up(u).wait_recv()
                self.down(u).wait_send()
                self.result(u)[...] = self.below[index].at[part, rows, columns][...]
                if place < self.seqs - 1:
                    self.up(u).start()
            self.store(u).start()

    def stages(self):
        found = [(0, self.stage_near), (LAG, self.stage_side), (2 * LAG, self.stage_last)]
        at = 3 * LAG
        for place in range(self.seqs - 2, ROOT, -1):
            found.append((at, functools.partial(self.stage_chain, place=place)))
            at += LAG
        found.append((at, self.stage_root))
        at += LAG
        for place in range(ROOT):
            found.append((at, functools.partial(self.stage_spread, place=place)))
        for place in range(ROOT + 1, self.seqs):
            found.append((at, functools.partial(self.stage_spread, place=place)))
            at += LAG
        return found

    def steps(self):
        return len(self.units) + self.stages()[-1][0]

    def step(self, t):
        for lag, stage in self.stages():
            if 0 <= t - lag < len(self.units):
                stage(t - lag)

    def finish(self):
        for u in range(len(self.units)):
            if self.units[u][0] not in self.halves:
                self.first(u).wait_send()
                for copy in self.second(u):
                    copy.wait_send()
            self.third(u).wait_send()

            @pl.when(self.seq == ROOT)
            def _(u=u):
                self.down(u).wait_send()
                self.up(u).wait_send()

            @pl.when((self.seq > ROOT) & (self.seq < self.seqs - 1))
            def _(u=u):
                self.up(u).wait_send()

            self.store(u).wait()


STAGED = (2, 3)
HALVES = {0: 0, 1: 1}

AHEAD = 10


def tail_kernel(
    blks, seqs, units, sent, w_ref, h_in, dx1_in, x_in, gain_ref, sums_ref, dub_ref,
    down_in, down_side, up_in, up_side, conv_in, proj_in, dx_out,
    down_out, up_out, conv_out, proj_out, qkv_out, vec_out,
    moved, dw, vectors, h_ref, dx1_ref, x_ref, dx_ref, h_t, w_slots, in_sem, ex_send, ex_recv, ex_own, w_sem, *refs
):
    reducer = Reducer(
        seqs, units, STAGED, HALVES,
        ((down_in, down_side), (up_in, up_side), conv_in, proj_in, dw, vectors),
        (down_out, up_out, conv_out, proj_out, qkv_out, vec_out), refs,
    )
    early = [u for u, unit in enumerate(units) if unit[0] < 4]
    given = [
        pltpu.make_async_copy(source, target, in_sem.at[i])
        for i, (source, target) in enumerate(((h_in, h_ref), (dx1_in, dx1_ref), (x_in, x_ref)))
    ]
    dx_copy = pltpu.make_async_copy(dx_ref, dx_out, in_sem.at[3])
    exchange = (blks, sent, moved, ex_send, ex_recv, ex_own)
    slots = w_slots.shape[0]

    def weight(k):
        part, i = divmod(k, 4)
        first = D * part + 256 * i
        return pltpu.make_async_copy(
            w_ref.at[:, first : first + 256], w_slots.at[k % slots], w_sem.at[k]
        )

    def put(vector, row, index):
        for place in range(8):
            vectors[0, place // 2, place % 2, row : row + 1, :] = vector[:, 128 * index(place) : 128 * index(place) + 128]

    def chunk(k):
        part, i = divmod(k, 4)
        lanes = slice(128 * part, 128 * part + 128)
        weight(k).wait()
        grad = jnp.concatenate([moved[2 * i, :, lanes], moved[2 * i + 1, :, lanes]], axis=1)
        dx_ref[...] += dot_nt(grad, w_slots[k % slots])
        dw[part, :, :, :, 256 * i : 256 * i + 256] = (
            dot(h_t[...], grad).astype(bf16).reshape(4, 2, 128, 256)
        )
        if k + slots < 12:
            weight(k + slots).start()
        if part != 1:
            bias = column_sums(grad.astype(f32))
            place = i + (4 if part else 0)
            for half in range(2):
                vectors[0, place // 2, place % 2, 6 + half : 7 + half, :] = bias[:, 128 * half : 128 * half + 128]
        if i == 3:
            for u, unit in enumerate(units):
                if unit[0] == 4 and unit[1] == part:
                    reducer.enter(u)

    def norm():
        given[1].wait()
        given[2].wait()
        grad = dx_ref[...]
        normed, scale_inv = layer_stats(x_ref[...].astype(f32))
        dx_ref[...] = dx1_ref[...] + layer_backward(grad, normed, scale_inv, gain_ref[...])
        dx_copy.start()
        put(column_sums(grad * normed), 0, lambda place: place)
        put(column_sums(grad), 1, lambda place: place)
        for row in range(4):
            put(sums_ref[row : row + 1, :], 2 + row, lambda place: place)
            put(dub_ref[...], 8 + row, lambda place, row=row: 4 * place + row)
        for place in range(8):
            vectors[0, place // 2, place % 2, 12:16, :] = jnp.zeros((4, 128), f32)
        for u, unit in enumerate(units):
            if unit[0] == 5:
                reducer.enter(u)

    for copy in given:
        copy.start()
    greet(blks, seqs)
    exchange_start(*exchange)
    for u in early:
        reducer.enter(u)
    for k in range(slots):
        weight(k).start()
    given[0].wait()
    h_t[...] = h_ref[...].T
    dx_ref[...] = jnp.zeros_like(dx_ref)
    at = 0
    while at < AHEAD:
        reducer.step(at)
        at += 1
    exchange_wait(*exchange)
    for k in range(12):
        chunk(k)
        if k % 2:
            reducer.step(at)
            at += 1
    norm()
    while at < reducer.steps():
        reducer.step(at)
        at += 1
    reducer.finish()
    dx_copy.wait()


def tail(sent, weight, h, dx1, x, gain, sums, dub, arrays, collective_id):
    blks, seqs = lax.axis_size("blk"), lax.axis_size("seq")
    rows = x.shape[0]
    shapes = [(1, FF // 8, D), (1, D // 8, FF), (1, 9 * D // 8, C), (1, D // 8, D), (3, D // 8, D), (1, 16, 128)]
    dtypes = [bf16] * 5 + [f32]
    found = [pieces_of(index, shape) for index, shape in enumerate(shapes)]
    light = [unit for pair in zip(found[0], found[1]) for unit in pair]
    heavy = found[2] + found[3] + found[4]
    units = []
    for i, unit in enumerate(heavy):
        units += [unit] + light[i * len(light) // len(heavy) : (i + 1) * len(light) // len(heavy)]
    units += found[5]
    anywhere = pl.BlockSpec(memory_space=pl.ANY)
    vmem = pl.BlockSpec(memory_space=pltpu.VMEM)
    return pl.pallas_call(
        functools.partial(tail_kernel, blks, seqs, units),
        in_specs=[anywhere] * 5 + [vmem] * 3 + [anywhere] * 6,
        out_specs=[anywhere] * 7,
        out_shape=[jax.ShapeDtypeStruct((rows, D), f32)]
        + [
            jax.ShapeDtypeStruct(shape, dtype) for shape, dtype in zip(shapes, dtypes)
        ],
        scratch_shapes=[
            pltpu.VMEM(sent.shape, bf16),
            pltpu.VMEM((3, 4, 2, D // 8, D), bf16),
            pltpu.VMEM((1, 4, 2, 16, 128), f32),
            pltpu.VMEM((rows, D), bf16),
            pltpu.VMEM((rows, D), f32),
            pltpu.VMEM((rows, D), bf16),
            pltpu.VMEM((rows, D), f32),
            pltpu.VMEM((D, rows), bf16),
            pltpu.VMEM((3, D, 256), bf16),
            pltpu.SemaphoreType.DMA((4,)),
            pltpu.SemaphoreType.DMA((blks,)),
            pltpu.SemaphoreType.DMA((blks,)),
            pltpu.SemaphoreType.DMA,
            pltpu.SemaphoreType.DMA((12,)),
        ]
        + Reducer.scratch(shapes, dtypes, STAGED, HALVES, units),
        compiler_params=params(63, collective_id=collective_id, has_side_effects=True),
        name="qkv_grad_and_sums",
    )(sent, weight, h, dx1, x, gain, sums, dub, *arrays)


def widen_kernel(counts, *refs):
    matrices = len(refs) - len(counts) - 1 >> 1
    sources, vectors = refs[:matrices], refs[matrices]
    targets, pieces = refs[matrices + 1 : 2 * matrices + 1], refs[2 * matrices + 1 :]
    for source, target in zip(sources[:-1], targets[:-1]):
        target[...] = source[0].astype(f32)
    for part in range(3):
        targets[-1][:, D * part : D * part + D] = sources[-1][part].astype(f32)
    row = 0
    for count, piece in zip(counts, pieces):
        for i in range(count):
            piece[:, 128 * i : 128 * i + 128] = vectors[0, row : row + 1, :]
            row += 1


def widen(arrays, vectors, counts):
    steps = 4
    return pl.pallas_call(
        functools.partial(widen_kernel, counts),
        grid=(steps,),
        in_specs=[
            pl.BlockSpec((a.shape[0], a.shape[1] // steps, a.shape[2]), lambda i: (0, i, 0))
            for a in arrays
        ]
        + [whole(vectors.shape)],
        out_specs=[
            pl.BlockSpec((a.shape[1] // steps, a.shape[0] * a.shape[2]), lambda i: (i, 0))
            for a in arrays
        ]
        + [whole((1, 128 * count)) for count in counts],
        out_shape=[
            jax.ShapeDtypeStruct((a.shape[1], a.shape[0] * a.shape[2]), f32) for a in arrays
        ]
        + [jax.ShapeDtypeStruct((1, 128 * count), f32) for count in counts],
        compiler_params=params(62),
        name="widen",
    )(*arrays, vectors)


def shifted(value, axis, steps):
    count = lax.axis_size(axis)
    leading, last = (max(0, -steps), min(count, count - steps))
    return lax.ppermute(value, axis, [(source, source + steps) for source in range(leading, last)])


def near_blocks(sides_row, keys_own, values_own):
    rows = keys_own.shape[0]
    place, length = lax.axis_index("blk"), rows * lax.axis_size("blk")
    centre = jnp.arange(rows, dtype=jnp.int32)
    segment = image_info(sides_row, place * rows + centre)[0]
    found = []
    for offset in range(-REACH, REACH + 1):
        keys, values = (keys_own, values_own) if offset == 0 else shifted((keys_own, values_own), "blk", -offset)
        positions = (place + offset) * rows + centre
        inside = (positions >= 0) & (positions < length)
        allowed = (segment[:, None] == image_info(sides_row, positions)[0][None, :]) & inside[None, :]
        found.append((offset, keys.reshape(rows, HEADS, HEAD), values.reshape(rows, HEADS, HEAD), allowed))
    return found


def near_scores(queries, keys, allowed):
    scores = jnp.einsum("qhd,khd->hqk", queries, keys, preferred_element_type=f32)
    return jnp.where(allowed[None], scores, masked_score)


def near_attention(near, queries):
    rows = queries.shape[0]
    peak = jnp.full((HEADS, rows), masked_score, f32)
    total = jnp.zeros((HEADS, rows), f32)
    for _, keys, _, allowed in near:
        scores = near_scores(queries, keys, allowed)
        new_peak = jnp.maximum(peak, jnp.max(scores, axis=-1))
        grown = jnp.where(allowed[None], jnp.exp2(scores - new_peak[..., None]), 0.0)
        total = total * jnp.exp2(peak - new_peak) + jnp.sum(grown, axis=-1)
        peak = new_peak
    lse = peak + jnp.log2(total)
    out = jnp.zeros((rows, HEADS, HEAD), f32)
    for _, keys, values, allowed in near:
        scores = near_scores(queries, keys, allowed)
        weights = jnp.where(allowed[None], jnp.exp2(scores - lse[..., None]), 0.0).astype(bf16)
        out = out + jnp.einsum("hqk,khd->qhd", weights, values, preferred_element_type=f32)
    return out.reshape(rows, D).astype(bf16), lse


def near_attention_grad(near, queries, lse, out, grad):
    rows = queries.shape[0]
    grad_heads = grad.reshape(rows, HEADS, HEAD)
    delta = jnp.sum((grad.astype(f32) * out.astype(f32)).reshape(rows, HEADS, HEAD), axis=-1).T
    dq = jnp.zeros((rows, HEADS, HEAD), f32)
    dk = jnp.zeros((rows, HEADS, HEAD), f32)
    dv = jnp.zeros((rows, HEADS, HEAD), f32)
    for offset, keys, values, allowed in near:
        scores = near_scores(queries, keys, allowed)
        weights = jnp.where(allowed[None], jnp.exp2(scores - lse[..., None]), 0.0)
        value_grad = jnp.einsum("qhd,khd->hqk", grad_heads, values, preferred_element_type=f32)
        score_grad = (weights * (value_grad - delta[..., None])).astype(bf16)
        dq = dq + jnp.einsum("hqk,khd->qhd", score_grad, keys, preferred_element_type=f32)
        dk_part = jnp.einsum("hqk,qhd->khd", score_grad, queries, preferred_element_type=f32)
        dv_part = jnp.einsum(
            "hqk,qhd->khd", weights.astype(bf16), grad_heads, preferred_element_type=f32
        )
        if offset:
            dk_part, dv_part = shifted((dk_part.astype(bf16), dv_part.astype(bf16)), "blk", offset)
        dk = dk + dk_part.astype(f32)
        dv = dv + dv_part.astype(f32)
    dq = dq.reshape(rows, D).astype(bf16) * jnp.asarray(HEAD**-0.5, bf16)
    dk = (dk * (1.0 / LOG2E)).reshape(rows, D).astype(bf16)
    return dq, dk, dv.reshape(rows, D).astype(bf16)


def in_groups(*parts):
    rows = parts[0].shape[0]
    stacked = jnp.stack([part.reshape(rows, D // 128, 128) for part in parts], axis=2)
    return stacked.transpose(1, 0, 2, 3).reshape(D // 128, rows, 128 * len(parts))


def from_groups(groups, part):
    picked = groups[:, :, 128 * part : 128 * part + 128]
    return picked.transpose(1, 0, 2).reshape(groups.shape[1], D)


def rims(rows_own, width):
    count = lax.axis_size("blk")
    top = lax.ppermute(rows_own[-width:], "blk", [(i, i + 1) for i in range(count - 1)])
    bottom = lax.ppermute(rows_own[:width], "blk", [(i + 1, i) for i in range(count - 1)])
    return top, bottom


def line(vector):
    return vector.reshape(1, -1)


def shards(
    tokens,
    image_sides,
    ln1_gain,
    ln1_bias,
    qkv_weight,
    qv_bias,
    proj_weight,
    proj_bias,
    ln2_gain,
    ln2_bias,
    up_weight,
    up_bias,
    down_weight,
    down_bias,
    conv_weight,
    bn_gain,
    bn_bias,
    out_grad,
    pup_grad,
):
    x = tokens[0]
    sides_row = image_sides[0]
    rows = x.shape[0]
    blks, seqs = lax.axis_size("blk"), lax.axis_size("seq")
    place = lax.axis_index("blk")
    length = rows * blks
    samples = length * seqs
    by_heads = blks == 8 and HEADS // 2 == blks

    block_starts = jnp.arange(length // BLOCK, dtype=jnp.int32) * BLOCK
    _, block_width, _, _, block_begin = image_info(sides_row, block_starts)
    starts = (block_begin // BLOCK).astype(jnp.int32)
    counts = (block_width * block_width // BLOCK).astype(jnp.int32)
    own_blocks = rows // BLOCK
    widths = lax.dynamic_slice_in_dim(block_width, place * own_blocks, own_blocks)
    wide_positions = place * rows + jnp.arange(-WIDE_RIM, rows + WIDE_RIM, dtype=jnp.int32)
    wide_flags = edge_flags(sides_row, wide_positions)
    flags = wide_flags[WIDE_RIM - RIM : WIDE_RIM + rows + RIM]

    g = pup_grad[0]
    if by_heads:
        h1, g_top, g_bottom, qkv = project_qkv_exchanged(
            x, line(ln1_gain), line(ln1_bias), qkv_weight, line(qv_bias), g, 6
        )
        qkv = qkv.reshape(length, 384)
        o_heads, lse = attention(starts, counts, qkv)
        o_groups = exchange(o_heads.reshape(blks, rows, 128), 7)
    else:
        g_top, g_bottom = rims(g, WIDE_RIM)
        h1, qkv_groups = project_qkv(x, line(ln1_gain), line(ln1_bias), qkv_weight, line(qv_bias))
        queries = from_groups(qkv_groups, 0).reshape(rows, HEADS, HEAD)
        near = near_blocks(sides_row, from_groups(qkv_groups, 1), from_groups(qkv_groups, 2))
        attended, lse = near_attention(near, queries)
        o_groups = in_groups(attended)
    dact = spread(widths, g, g_top, g_bottom, wide_flags)
    x1, h2, act, slope, block_low, top, bottom = mlp(
        o_groups, x, proj_weight, line(proj_bias), line(ln2_gain), line(ln2_bias),
        up_weight, line(up_bias), down_weight, line(down_bias), 8,
    )
    z, z_sums = conv(widths, block_low, top, bottom, flags, conv_weight)
    z_sums, z_top, z_bottom = small_sum(z_sums[None], False, 1, z)
    mean = z_sums[0:1] / samples
    inv = lax.rsqrt(z_sums[1:2] / samples - mean * mean + batch_eps)
    pup_out, normed, dbn, bn_sums = batch(
        widths, z, z_top, z_bottom, dact, flags, mean, inv, line(bn_gain), line(bn_bias)
    )
    bn_sums = small_sum(bn_sums[None], False, 2)

    taps, dy, dm = conv_grad(
        widths, dbn, normed, flags, inv * line(bn_gain), bn_sums[0:1] / samples, bn_sums[1:2] / samples,
        conv_weight, out_grad[0],
    )
    du, up_bias_grad, dx1, da, do_groups, mlp_sums = mlp_grad(
        dy, dm, slope, down_weight, up_weight, x1, line(ln2_gain), proj_weight
    )
    if by_heads:
        conv_weight_grad, proj_grad, do_moved, down_keep, down_send, up_keep, up_send = weights(
            act, dm, h2, du, block_low, taps, o_groups, da, do_groups, blks, 5
        )
        down_side = lax.ppermute(down_send, "blk", [(i, i ^ 2) for i in range(blks)])
        up_side = lax.ppermute(up_send, "blk", [(i, i ^ 4) for i in range(blks)])
        dqkv = attention_grad(starts, counts, qkv, do_moved.reshape(length, 128), o_heads, lse)
        dqkv_groups = dqkv.reshape(blks, rows, 384)
    else:
        down_grad = down_weight_grad_of(act, dm)
        conv_weight_grad = conv_weight_grad_of(block_low, taps)
        up_grad, proj_grad = late_weights(h2, du, o_groups, da)
        grads = near_attention_grad(near, queries, lse, attended, from_groups(do_groups, 0))
        dqkv_groups = in_groups(*grads)

    piece = D // blks
    cuts_of = [piece] * 6 + [2 * piece, 4 * piece]
    if by_heads:
        tokens_grad, *summed = tail(
            dqkv_groups, qkv_weight, h1, dx1, x, line(ln1_gain), mlp_sums, up_bias_grad,
            [
                down_keep, down_side, up_keep, up_side,
                conv_weight_grad.reshape(1, 4, 2, -1, C), proj_grad.reshape(1, 4, 2, -1, D),
            ],
            3,
        )
        tokens_grad, down_grad, up_grad, conv_weight_grad, proj_grad, qkv_weight_grad, *small = widen(
            [tokens_grad[None]] + summed[:5], summed[5], [cut // 128 for cut in cuts_of]
        )
        small = [vector[0] for vector in small]
    else:
        qkv_weight_grad, dqb, dvb, tokens_grad, qkv_sums = qkv_grad(
            dqkv_groups, qkv_weight, h1, dx1, x, line(ln1_gain)
        )

        def scattered(grad):
            part = lax.psum_scatter(grad, "blk", scatter_dimension=0, tiled=True)
            return lax.psum(part, "seq").astype(f32)

        down_grad, up_grad, proj_grad, conv_weight_grad = [
            scattered(grad) for grad in (down_grad, up_grad, proj_grad, conv_weight_grad)
        ]
        qkv_weight_grad = scattered(qkv_weight_grad.transpose(1, 0, 2).reshape(D, 3 * D))
        vectors = [qkv_sums[0], qkv_sums[1], mlp_sums[0], mlp_sums[1], mlp_sums[2], mlp_sums[3]]
        vectors += [jnp.concatenate([dqb[0], dvb[0]]), up_bias_grad[0]]
        stacked = jnp.concatenate([vector.reshape(blks, -1) for vector in vectors], axis=1)
        summed = small_sum(stacked[:, None, :], True, 4)[0]
        ends = [sum(cuts_of[: i + 1]) for i in range(len(cuts_of))]
        small = [summed[end - cut : end] for cut, end in zip(cuts_of, ends)]
    ln1_g, ln1_b, proj_b, ln2_g, ln2_b, down_b, qv_b, up_b = small
    channel_piece = C // blks
    gain_slice = lax.dynamic_slice_in_dim(bn_sums[1], place * channel_piece, channel_piece)
    bias_slice = lax.dynamic_slice_in_dim(bn_sums[0], place * channel_piece, channel_piece)
    return (
        block_low[None],
        pup_out[None],
        tokens_grad[None],
        ln1_g,
        ln1_b,
        qkv_weight_grad,
        qv_b,
        proj_grad,
        proj_b,
        ln2_g,
        ln2_b,
        up_grad,
        up_b,
        down_grad,
        down_b,
        conv_weight_grad,
        gain_slice,
        bias_slice,
    )


def solution(mesh):
    replicated = P()
    packed = P("seq", "blk", None)
    placed = (packed, P("seq", None)) + (replicated,) * 15 + (packed, packed)
    rows, vector = P("blk", None), P("blk")
    return jax.shard_map(
        shards,
        mesh=mesh,
        in_specs=placed,
        out_specs=(
            packed, packed, packed, vector, vector, rows, vector, rows, vector, vector, vector, rows,
            vector, rows, vector, rows, vector, vector,
        ),
        check_vma=False,
    )
```

```python
import functools

import jax
import jax.numpy as jnp
from jax import lax
from jax.experimental import pallas as pl
from jax.experimental.pallas import tpu as pltpu
from jax.sharding import PartitionSpec as P

D = 1024
HEADS = 16
HEAD = 64
FF = 4096
C = 256
REACH = 4
UNIT = 16
BLOCK = UNIT * UNIT
IMAGE_BLOCKS = (1, 4, 9)
RIM = 64
WIDE_RIM = 128
LOG2E = 1.4426950408889634
LOOK = 4
MESH = pl.DeviceIdType.MESH

norm_eps = 1e-06
batch_eps = 1e-05
masked_score = -1e30
f32 = jnp.float32
bf16 = jnp.bfloat16

NT = (((1,), (1,)), ((), ()))
TN = (((0,), (0,)), ((), ()))


def dot(left, right):
    return jnp.dot(left, right, preferred_element_type=f32)


def dot_nt(left, right):
    return lax.dot_general(left, right, NT, preferred_element_type=f32)


def dot_tn(left, right):
    return lax.dot_general(left, right, TN, preferred_element_type=f32)


def whole(shape):
    zeros = (0,) * len(shape)
    return pl.BlockSpec(shape, lambda *_: zeros)


def params(megabytes, **more):
    return pltpu.CompilerParams(vmem_limit_bytes=megabytes << 20, **more)


def cost(flops, moved, transcendentals=0):
    return pl.CostEstimate(
        flops=int(flops), bytes_accessed=int(moved), transcendentals=int(transcendentals)
    )


def place_copies(blks, source, target, sends, receives):
    me = lax.axis_index("blk")
    copies = []
    for step in range(1, blks):
        to = lax.rem(me + step, blks)
        copies.append(
            pltpu.make_async_remote_copy(
                src_ref=source.at[to],
                dst_ref=target.at[me],
                send_sem=sends.at[step],
                recv_sem=receives.at[step],
                device_id={"blk": to},
                device_id_type=MESH,
            )
        )
    return copies


def greet_signal(blks, seqs=0):
    me, seq = lax.axis_index("blk"), lax.axis_index("seq")
    barrier = pltpu.get_barrier_semaphore()
    for step in range(1, blks):
        pl.semaphore_signal(
            barrier, inc=1, device_id={"blk": lax.rem(me + step, blks)}, device_id_type=MESH
        )
    if seqs:

        @pl.when(seq > 0)
        def _():
            pl.semaphore_signal(barrier, inc=1, device_id={"seq": seq - 1}, device_id_type=MESH)

        @pl.when(seq < seqs - 1)
        def _():
            pl.semaphore_signal(barrier, inc=1, device_id={"seq": seq + 1}, device_id_type=MESH)


def greet_wait(blks, seqs=0):
    seq = lax.axis_index("seq")
    ends = 0
    if seqs:
        ends = jnp.where(seq > 0, 1, 0) + jnp.where(seq < seqs - 1, 1, 0)
    pl.semaphore_wait(pltpu.get_barrier_semaphore(), blks - 1 + ends)


def greet(blks, seqs=0):
    greet_signal(blks, seqs)
    greet_wait(blks, seqs)


def exchange_start(blks, source, target, sends, receives, own_sem):
    me = lax.axis_index("blk")
    for copy in place_copies(blks, source, target, sends, receives):
        copy.start()
    pltpu.make_async_copy(source.at[me], target.at[me], own_sem).start()


def exchange_wait(blks, source, target, sends, receives, own_sem):
    me = lax.axis_index("blk")
    for copy in place_copies(blks, source, target, sends, receives):
        copy.wait()
    pltpu.make_async_copy(source.at[me], target.at[me], own_sem).wait()


class Rims:
    def __init__(self, blks, rows_own, top, bottom, landing, semaphores):
        me = lax.axis_index("blk")
        width, last = top.shape[0], rows_own.shape[0]
        self.after, self.before = me < blks - 1, me > 0
        self.top, self.bottom, self.landing = top, bottom, landing
        self.downward = pltpu.make_async_remote_copy(
            src_ref=rows_own.at[last - width : last], dst_ref=landing.at[0],
            send_sem=semaphores.at[0], recv_sem=semaphores.at[1],
            device_id={"blk": me + 1}, device_id_type=MESH,
        )
        self.upward = pltpu.make_async_remote_copy(
            src_ref=rows_own.at[0:width], dst_ref=landing.at[1],
            send_sem=semaphores.at[2], recv_sem=semaphores.at[3],
            device_id={"blk": me - 1}, device_id_type=MESH,
        )

    def start(self):
        @pl.when(self.after)
        def _():
            self.downward.start()

        @pl.when(self.before)
        def _():
            self.upward.start()

        @pl.when(jnp.logical_not(self.after))
        def _():
            self.bottom[...] = jnp.zeros_like(self.bottom)

        @pl.when(jnp.logical_not(self.before))
        def _():
            self.top[...] = jnp.zeros_like(self.top)

    def wait(self):
        @pl.when(self.after)
        def _():
            self.downward.wait_send()
            self.upward.wait_recv()
            self.bottom[...] = self.landing[1]

        @pl.when(self.before)
        def _():
            self.upward.wait_send()
            self.downward.wait_recv()
            self.top[...] = self.landing[0]


def exchange_kernel(blks, source, target, *semaphores):
    greet(blks)
    exchange_start(blks, source, target, *semaphores)
    exchange_wait(blks, source, target, *semaphores)


def exchange(groups, collective_id):
    blks = lax.axis_size("blk")
    anywhere = pl.BlockSpec(memory_space=pl.ANY)
    return pl.pallas_call(
        functools.partial(exchange_kernel, blks),
        in_specs=[anywhere],
        out_specs=anywhere,
        out_shape=jax.ShapeDtypeStruct(groups.shape, groups.dtype),
        scratch_shapes=exchange_semaphores(blks),
        compiler_params=params(62, collective_id=collective_id, has_side_effects=True),
        name="exchange",
    )(groups)


def image_info(image_sides, positions):
    image_areas = image_sides * image_sides
    image_ends = jnp.cumsum(image_areas).astype(jnp.int32)
    image_starts = (image_ends - image_areas).astype(jnp.int32)
    segment = jnp.sum((image_ends[None, :] <= positions[:, None]).astype(jnp.int32), axis=1).astype(
        jnp.int32
    )
    picked = segment[:, None] == jnp.arange(image_sides.shape[0], dtype=jnp.int32)[None, :]
    image_width = jnp.sum(jnp.where(picked, image_sides[None, :], 0), axis=1).astype(jnp.int32)
    image_width = jnp.maximum(image_width, 1).astype(jnp.int32)
    image_begin = jnp.sum(jnp.where(picked, image_starts[None, :], 0), axis=1).astype(jnp.int32)
    offset = (positions - image_begin).astype(jnp.int32)
    row_index = (offset // image_width).astype(jnp.int32)
    col_index = (offset - row_index * image_width).astype(jnp.int32)
    return (segment, image_width, row_index, col_index, image_begin)


def edge_flags(image_sides, positions):
    _, width, row, col, _ = image_info(image_sides, positions)
    flags = jnp.stack([row > 0, row < width - 1, col > 0, col < width - 1], axis=1)
    return jnp.concatenate([flags, flags], axis=1).astype(f32)


def layer_stats(values):
    mean = jnp.mean(values, axis=-1, keepdims=True)
    centred = values - mean
    scale_inv = lax.rsqrt(jnp.mean(centred * centred, axis=-1, keepdims=True) + norm_eps)
    return centred * scale_inv, scale_inv


def layer_backward(grad_out, normed, scale_inv, gain):
    scaled = grad_out * gain
    inner = (
        scaled
        - jnp.mean(scaled, axis=-1, keepdims=True)
        - normed * jnp.mean(scaled * normed, axis=-1, keepdims=True)
    )
    return scale_inv * inner


def column_sums(values):
    return jnp.sum(values, axis=0, keepdims=True)


def gelu_parts(values):
    cumulative = 0.5 + 0.5 * lax.erf(values * 0.7071067811865476)
    weighted = values * (0.3989422804014327 * jnp.exp(values * values * -0.5))
    return cumulative, weighted


def qkv_kernel(x_ref, gain_ref, bias_ref, wq_ref, wk_ref, wv_ref, bq_ref, bv_ref, h_ref, out_ref):
    @pl.when(pl.program_id(0) == 0)
    def _():
        normed, _ = layer_stats(x_ref[...].astype(f32))
        h_ref[...] = (normed * gain_ref[...] + bias_ref[...]).astype(bf16)

    hidden = h_ref[...]
    query = ((dot(hidden, wq_ref[...]) + bq_ref[...]) * (HEAD**-0.5 * LOG2E)).astype(bf16)
    key = dot(hidden, wk_ref[...]).astype(bf16)
    value = (dot(hidden, wv_ref[...]) + bv_ref[...]).astype(bf16)
    for part in range(2):
        lanes = slice(128 * part, 128 * part + 128)
        out_ref[part, :, 0:128] = query[:, lanes]
        out_ref[part, :, 128:256] = key[:, lanes]
        out_ref[part, :, 256:384] = value[:, lanes]


def project_qkv(x, gain, bias, weight, qv_bias):
    rows = x.shape[0]
    groups = D // 128
    return pl.pallas_call(
        qkv_kernel,
        grid=(groups // 2,),
        in_specs=[
            whole((rows, D)),
            whole((1, D)),
            whole((1, D)),
            pl.BlockSpec((D, 256), lambda i: (0, i)),
            pl.BlockSpec((D, 256), lambda i: (0, 4 + i)),
            pl.BlockSpec((D, 256), lambda i: (0, 8 + i)),
            pl.BlockSpec((1, 256), lambda i: (0, i)),
            pl.BlockSpec((1, 256), lambda i: (0, 4 + i)),
        ],
        out_specs=[whole((rows, D)), pl.BlockSpec((2, rows, 384), lambda i: (i, 0, 0))],
        out_shape=[
            jax.ShapeDtypeStruct((rows, D), bf16),
            jax.ShapeDtypeStruct((groups, rows, 384), bf16),
        ],
        compiler_params=params(40),
        cost_estimate=cost(2 * rows * D * 3 * D, 12 << 20),
        name="norm_qkv",
    )(x, gain, bias, weight, weight, weight, qv_bias, qv_bias)


def qkv_exchange_kernel(
    blks, x_ref, gain_ref, bias_ref, qv_ref, w_ref, g_ref,
    h_ref, top, bottom, moved, groups, w_all, landing, w_sem, sends, receives, own_sem, rim_sem,
):
    me = lax.axis_index("blk")
    chips = blks // 2
    chip, core = me // 2, me % 2
    order = [lax.rem(chip + 1 + i, chips) for i in range(chips)]

    def weight(i, part):
        columns = pl.ds(pl.multiple_of(D * part + 256 * order[i], 256), 256)
        return pltpu.make_async_copy(w_ref.at[:, columns], w_all.at[i, part], w_sem.at[i, part])

    def to(place):
        return pltpu.make_async_remote_copy(
            src_ref=groups.at[place], dst_ref=moved.at[me],
            send_sem=sends.at[place], recv_sem=receives.at[me],
            device_id={"blk": place}, device_id_type=MESH,
        )

    def own():
        return pltpu.make_async_copy(groups.at[me], moved.at[me], own_sem)

    for i in range(chips):
        for part in range(3):
            weight(i, part).start()
    greet_signal(blks)
    rims = Rims(blks, g_ref, top, bottom, landing, rim_sem)
    normed, _ = layer_stats(x_ref[...].astype(f32))
    h_ref[...] = (normed * gain_ref[...] + bias_ref[...]).astype(bf16)
    for i in range(chips):
        for part in range(3):
            weight(i, part).wait()
        columns = pl.ds(pl.multiple_of(256 * order[i], 256), 256)
        hidden = h_ref[...]
        query = ((dot(hidden, w_all[i, 0]) + qv_ref[:, columns]) * (HEAD**-0.5 * LOG2E)).astype(bf16)
        key = dot(hidden, w_all[i, 1]).astype(bf16)
        columns = pl.ds(pl.multiple_of(D + 256 * order[i], 256), 256)
        value = (dot(hidden, w_all[i, 2]) + qv_ref[:, columns]).astype(bf16)
        for half in range(2):
            lanes = slice(128 * half, 128 * half + 128)
            place = 2 * order[i] + half
            groups[place, :, 0:128] = query[:, lanes]
            groups[place, :, 128:256] = key[:, lanes]
            groups[place, :, 256:384] = value[:, lanes]
        if i == 0:
            greet_wait(blks)
        if i < chips - 1:
            to(2 * order[i]).start()
            to(2 * order[i] + 1).start()
    to(2 * chip + 1 - core).start()
    own().start()
    rims.start()
    for step in range(1, blks):
        other = lax.rem(me + step, blks)
        to(other).wait_send()
        pltpu.make_async_remote_copy(
            src_ref=groups.at[other], dst_ref=moved.at[other],
            send_sem=sends.at[other], recv_sem=receives.at[other],
            device_id={"blk": other}, device_id_type=MESH,
        ).wait_recv()
    own().wait()
    rims.wait()


def project_qkv_exchanged(x, gain, bias, weight, qv_bias, g, collective_id):
    rows = x.shape[0]
    blks = lax.axis_size("blk")
    anywhere = pl.BlockSpec(memory_space=pl.ANY)
    vmem = pl.BlockSpec(memory_space=pltpu.VMEM)
    dma = pltpu.SemaphoreType.DMA
    return pl.pallas_call(
        functools.partial(qkv_exchange_kernel, blks),
        in_specs=[vmem] * 4 + [anywhere, anywhere],
        out_specs=[vmem, vmem, vmem, anywhere],
        out_shape=[
            jax.ShapeDtypeStruct((rows, D), bf16),
            jax.ShapeDtypeStruct((WIDE_RIM, D), bf16),
            jax.ShapeDtypeStruct((WIDE_RIM, D), bf16),
            jax.ShapeDtypeStruct((blks, rows, 384), bf16),
        ],
        scratch_shapes=[
            pltpu.VMEM((blks, rows, 384), bf16),
            pltpu.VMEM((blks // 2, 3, D, 256), bf16),
            pltpu.VMEM((2, WIDE_RIM, D), bf16),
            dma((blks // 2, 3)),
            dma((blks,)),
            dma((blks,)),
            dma,
            dma((4,)),
        ],
        compiler_params=params(60, collective_id=collective_id, has_side_effects=True),
        name="norm_qkv",
    )(x, gain, bias, qv_bias, weight, g)


def attention_kernel(starts, counts, qkv, o_ref, lse_ref, value_t):
    step = pl.program_id(0)

    @pl.when(step == 0)
    def _():
        value_t[...] = qkv[:, 256:384].T

    own = pl.ds(pl.multiple_of(step * BLOCK, BLOCK), BLOCK)
    query = qkv[own, 0:128]
    lane = lax.broadcasted_iota(jnp.int32, (BLOCK, 128), 1)
    zero = jnp.zeros_like(query)
    queries = [jnp.where(lane < HEAD, query, zero), jnp.where(lane >= HEAD, query, zero)]
    first, count = starts[step], counts[step]
    for blocks in IMAGE_BLOCKS:

        @pl.when(count == blocks)
        def _(blocks=blocks):
            items = [(head, block) for block in range(blocks) for head in range(2)]

            def rows_of(block):
                return pl.ds(pl.multiple_of((first + block) * BLOCK, BLOCK), BLOCK)

            def scores_of(item):
                return dot_nt(qkv[rows_of(item[1]), 128:256], queries[item[0]])

            scores = [scores_of(item) for item in items[:LOOK]]
            state = {}
            for i, (head, block) in enumerate(items):
                if i + LOOK < len(items):
                    scores.append(scores_of(items[i + LOOK]))
                peak = jnp.max(scores[i], axis=0, keepdims=True)
                if block:
                    old_peak, old_total, old_out = state[head]
                    peak = jnp.maximum(old_peak, peak)
                    shrink = jnp.exp2(old_peak - peak)
                grown = jnp.exp2(scores[i] - peak)
                total = jnp.sum(grown, axis=0, keepdims=True)
                rows = slice(HEAD * head, HEAD * head + HEAD)
                out = dot(value_t[rows, rows_of(block)], grown.astype(bf16))
                if block:
                    total = old_total * shrink + total
                    out = old_out * shrink + out
                state[head] = (peak, total, out)
            outs = [state[head][2] * (1.0 / state[head][1]) for head in range(2)]
            logs = [state[head][0] + jnp.log2(state[head][1]) for head in range(2)]
            o_ref[...] = jnp.concatenate(outs, axis=0).T.astype(bf16)
            lse_ref[...] = jnp.concatenate(logs + [jnp.zeros((6, BLOCK), f32)], axis=0)


def attention(starts, counts, qkv):
    length = qkv.shape[0]
    pairs = 100 * 2 * BLOCK * BLOCK
    return pl.pallas_call(
        attention_kernel,
        grid_spec=pltpu.PrefetchScalarGridSpec(
            num_scalar_prefetch=2,
            grid=(length // BLOCK,),
            in_specs=[whole((length, 384))],
            out_specs=[
                pl.BlockSpec((BLOCK, 128), lambda i, *_: (i, 0)),
                pl.BlockSpec((8, BLOCK), lambda i, *_: (0, i)),
            ],
            scratch_shapes=[pltpu.VMEM((128, length), bf16)],
        ),
        out_shape=[
            jax.ShapeDtypeStruct((length, 128), bf16),
            jax.ShapeDtypeStruct((8, length), f32),
        ],
        compiler_params=params(40),
        cost_estimate=cost(4 * HEAD * pairs, 5 << 20, pairs),
        name="attention",
    )(starts, counts, qkv)


def attention_grad_kernel(
    starts, counts, qkv, do_ref, o_ref, lse, out_ref, query_m, do_m, key_t, dq_t, delta
):
    step = pl.program_id(0)
    length = do_ref.shape[0]
    lane = lax.broadcasted_iota(jnp.int32, (BLOCK, 128), 1)
    low = lane < HEAD

    @pl.when(step == 0)
    def _():
        key_t[...] = qkv[:, 128:256].T
        dq_t[...] = jnp.zeros_like(dq_t)

        def prepare(i, _):
            rows = pl.ds(pl.multiple_of(i * BLOCK, BLOCK), BLOCK)
            grad = do_ref[rows, :]
            product = (grad.astype(f32) * o_ref[rows, :].astype(f32)).T
            delta[0:1, rows] = jnp.sum(product[:HEAD], axis=0, keepdims=True)
            delta[1:2, rows] = jnp.sum(product[HEAD:], axis=0, keepdims=True)
            query = qkv[rows, 0:128]
            zero = jnp.zeros_like(query)
            query_m[0, rows, :] = jnp.where(low, query, zero)
            query_m[1, rows, :] = jnp.where(low, zero, query)
            do_m[0, rows, :] = jnp.where(low, grad, zero)
            do_m[1, rows, :] = jnp.where(low, zero, grad)
            return 0

        lax.fori_loop(0, length // BLOCK, prepare, 0)

    own = pl.ds(pl.multiple_of(step * BLOCK, BLOCK), BLOCK)
    key = qkv[own, 128:256]
    value = qkv[own, 256:384]
    first, count = starts[step], counts[step]
    for blocks in IMAGE_BLOCKS:

        @pl.when(count == blocks)
        def _(blocks=blocks):
            image = pl.ds(pl.multiple_of(first * BLOCK, BLOCK), blocks * BLOCK)
            dk = dv = None
            for head in range(2):
                rows = slice(HEAD * head, HEAD * head + HEAD)
                query, grad = query_m[head, image, :], do_m[head, image, :]
                scores = dot_nt(key, query)
                value_grad = dot_nt(value, grad)
                weights = jnp.exp2(scores - lse[head : head + 1, image])
                score_grad = (weights * (value_grad - delta[head : head + 1, image])).astype(bf16)
                dv_part = dot(weights.astype(bf16), grad)
                dk_part = dot(score_grad, query)
                dv = dv_part if dv is None else dv + dv_part
                dk = dk_part if dk is None else dk + dk_part
                dq_t[rows, image] += dot(key_t[rows, own], score_grad)
            out_ref[own, 128:256] = (dk * (1.0 / LOG2E)).astype(bf16)
            out_ref[own, 256:384] = dv.astype(bf16)

    @pl.when(step == pl.num_programs(0) - 1)
    def _():
        def finish(i, _):
            rows = pl.ds(pl.multiple_of(i * BLOCK, BLOCK), BLOCK)
            out_ref[rows, 0:128] = dq_t[:, rows].T.astype(bf16) * jnp.asarray(HEAD**-0.5, bf16)
            return 0

        lax.fori_loop(0, length // BLOCK, finish, 0)


def attention_grad(starts, counts, qkv, do, o, lse):
    length = qkv.shape[0]
    pairs = 100 * 2 * BLOCK * BLOCK
    return pl.pallas_call(
        attention_grad_kernel,
        grid_spec=pltpu.PrefetchScalarGridSpec(
            num_scalar_prefetch=2,
            grid=(length // BLOCK,),
            in_specs=[
                whole((length, 384)),
                whole((length, 128)),
                whole((length, 128)),
                whole((8, length)),
            ],
            out_specs=whole((length, 384)),
            scratch_shapes=[
                pltpu.VMEM((2, length, 128), bf16),
                pltpu.VMEM((2, length, 128), bf16),
                pltpu.VMEM((128, length), bf16),
                pltpu.VMEM((128, length), f32),
                pltpu.VMEM((8, length), f32),
            ],
        ),
        out_shape=jax.ShapeDtypeStruct((length, 384), bf16),
        compiler_params=params(46),
        cost_estimate=cost(10 * HEAD * pairs, 12 << 20, pairs),
        name="attention_grad",
    )(starts, counts, qkv, do, o, lse)


FF_TILE = 512


def mlp_kernel(
    blks, o_ref, x_ref, wp_ref, pb_ref, gain_ref, bias_ref, wu_ref, ub_ref, wd_ref, db_ref,
    x1_ref, h_ref, act_ref, slope_ref, out_ref, top, bottom, total, landing, rim_sem,
):
    step = pl.program_id(0)

    @pl.when(step == 0)
    def _():
        greet_signal(blks)
        attended = jnp.concatenate([o_ref[i] for i in range(o_ref.shape[0])], axis=1)
        x1 = x_ref[...].astype(f32) + dot(attended, wp_ref[...]) + pb_ref[...]
        x1_ref[...] = x1
        normed, _ = layer_stats(x1)
        h_ref[...] = (normed * gain_ref[...] + bias_ref[...]).astype(bf16)
        total[...] = x1 + db_ref[...]

    raised = dot(h_ref[...], wu_ref[...]) + ub_ref[...]
    cumulative, weighted = gelu_parts(raised)
    act = (raised * cumulative).astype(bf16)
    act_ref[...] = act
    slope_ref[...] = (cumulative + weighted).astype(bf16)
    total[...] += dot(act, wd_ref[...])

    @pl.when(step == pl.num_programs(0) - 1)
    def _():
        out_ref[...] = total[...].astype(bf16)
        greet_wait(blks)
        rims = Rims(blks, out_ref, top, bottom, landing, rim_sem)
        rims.start()
        rims.wait()


def mlp(o, x, wp, pb, gain, bias, wu, ub, wd, db, collective_id):
    rows = x.shape[0]
    groups = o.shape[0]
    tile = 2 * FF_TILE
    return pl.pallas_call(
        functools.partial(mlp_kernel, lax.axis_size("blk")),
        grid=(FF // tile,),
        in_specs=[
            whole((groups, rows, 128)),
            whole((rows, D)),
            whole((D, D)),
            whole((1, D)),
            whole((1, D)),
            whole((1, D)),
            pl.BlockSpec((D, tile), lambda i: (0, i)),
            pl.BlockSpec((1, tile), lambda i: (0, i)),
            pl.BlockSpec((tile, D), lambda i: (i, 0)),
            whole((1, D)),
        ],
        out_specs=[
            whole((rows, D)),
            whole((rows, D)),
            pl.BlockSpec((rows, tile), lambda i: (0, i)),
            pl.BlockSpec((rows, tile), lambda i: (0, i)),
            whole((rows, D)),
            whole((RIM, D)),
            whole((RIM, D)),
        ],
        out_shape=[
            jax.ShapeDtypeStruct((rows, D), f32),
            jax.ShapeDtypeStruct((rows, D), bf16),
            jax.ShapeDtypeStruct((rows, FF), bf16),
            jax.ShapeDtypeStruct((rows, FF), bf16),
            jax.ShapeDtypeStruct((rows, D), bf16),
            jax.ShapeDtypeStruct((RIM, D), bf16),
            jax.ShapeDtypeStruct((RIM, D), bf16),
        ],
        scratch_shapes=[
            pltpu.VMEM((rows, D), f32),
            pltpu.VMEM((2, RIM, D), bf16),
            pltpu.SemaphoreType.DMA((4,)),
        ],
        compiler_params=params(46, collective_id=collective_id, has_side_effects=True),
        cost_estimate=cost(2 * rows * D * (D + 2 * FF), 34 << 20, rows * FF),
        name="proj_norm_mlp",
    )(o, x, wp, pb, gain, bias, wu, ub, wd, db)


def mlp_grad_kernel(
    dy_ref, dm_ref, slope_ref, wd_ref, wu_ref, x1_ref, gain_ref, wp_ref,
    du_ref, dub_ref, dx1_ref, da_ref, do_ref, sums_ref, total,
):
    step = pl.program_id(0)

    @pl.when(step == 0)
    def _():
        total[...] = jnp.zeros_like(total)

    act_grad = dot_nt(dm_ref[...], wd_ref[...])
    raised_low = (act_grad * slope_ref[...].astype(f32)).astype(bf16)
    du_ref[...] = raised_low
    dub_ref[...] = column_sums(raised_low.astype(f32))
    total[...] += dot_nt(raised_low, wu_ref[...])

    @pl.when(step == pl.num_programs(0) - 1)
    def _():
        grad = total[...]
        normed, scale_inv = layer_stats(x1_ref[...])
        dx1 = dy_ref[...] + layer_backward(grad, normed, scale_inv, gain_ref[...])
        dx1_ref[...] = dx1
        low = dx1.astype(bf16)
        da_ref[...] = low
        sums_ref[0:1, :] = column_sums(low.astype(f32))
        sums_ref[1:2, :] = column_sums(grad * normed)
        sums_ref[2:3, :] = column_sums(grad)
        sums_ref[3:4, :] = column_sums(dm_ref[...].astype(f32))
        sums_ref[4:8, :] = jnp.zeros((4, D), f32)
        attended_grad = dot_nt(low, wp_ref[...]).astype(bf16)
        for i in range(do_ref.shape[0]):
            do_ref[i] = attended_grad[:, 128 * i : 128 * i + 128]


def mlp_grad(dy, dm, slope, wd, wu, x1, gain, wp):
    rows = dy.shape[0]
    groups = D // 128
    tile = 2 * FF_TILE
    return pl.pallas_call(
        mlp_grad_kernel,
        grid=(FF // tile,),
        in_specs=[
            whole((rows, D)),
            whole((rows, D)),
            pl.BlockSpec((rows, tile), lambda i: (0, i)),
            pl.BlockSpec((tile, D), lambda i: (i, 0)),
            pl.BlockSpec((D, tile), lambda i: (0, i)),
            whole((rows, D)),
            whole((1, D)),
            whole((D, D)),
        ],
        out_specs=[
            pl.BlockSpec((rows, tile), lambda i: (0, i)),
            pl.BlockSpec((1, tile), lambda i: (0, i)),
            whole((rows, D)),
            whole((rows, D)),
            whole((groups, rows, 128)),
            whole((8, D)),
        ],
        out_shape=[
            jax.ShapeDtypeStruct((rows, FF), bf16),
            jax.ShapeDtypeStruct((1, FF), f32),
            jax.ShapeDtypeStruct((rows, D), f32),
            jax.ShapeDtypeStruct((rows, D), bf16),
            jax.ShapeDtypeStruct((groups, rows, 128), bf16),
            jax.ShapeDtypeStruct((8, D), f32),
        ],
        scratch_shapes=[pltpu.VMEM((rows, D), f32)],
        compiler_params=params(56),
        cost_estimate=cost(2 * rows * D * (D + 2 * FF), 34 << 20),
        name="mlp_norm_proj_grad",
    )(dy, dm, slope, wd, wu, x1, gain, wp)


def down_weight_kernel(act_ref, dm_ref, dwd_ref):
    dwd_ref[...] = dot_tn(act_ref[...], dm_ref[...]).astype(bf16)


def down_weight_grad_of(act, dm):
    rows = dm.shape[0]
    tile = FF_TILE
    return pl.pallas_call(
        down_weight_kernel,
        grid=(FF // tile,),
        in_specs=[pl.BlockSpec((rows, tile), lambda i: (0, i)), whole((rows, D))],
        out_specs=pl.BlockSpec((tile, D), lambda i: (i, 0)),
        out_shape=jax.ShapeDtypeStruct((FF, D), bf16),
        compiler_params=params(32),
        cost_estimate=cost(2 * rows * D * FF, 13 << 20),
        name="down_weight_grad",
    )(act, dm)


def conv_weight_kernel(x_ref, taps_ref, dw_ref, x_t):
    @pl.when(pl.program_id(0) == 0)
    def _():
        x_t[...] = x_ref[...].T

    for tap in range(3):
        dw_ref[D * tap : D * tap + D, :] = dot(x_t[...], taps_ref[tap]).astype(bf16)


def conv_weight_grad_of(x, taps):
    rows = x.shape[0]
    return pl.pallas_call(
        conv_weight_kernel,
        grid=(3,),
        in_specs=[whole((rows, D)), pl.BlockSpec((3, rows, C), lambda i: (i, 0, 0))],
        out_specs=pl.BlockSpec((3 * D, C), lambda i: (i, 0)),
        out_shape=jax.ShapeDtypeStruct((9 * D, C), bf16),
        scratch_shapes=[pltpu.VMEM((D, rows), bf16)],
        compiler_params=params(32),
        cost_estimate=cost(2 * rows * D * 9 * C, 9 << 20),
        name="conv_weight_grad",
    )(x, taps)


def exchange_semaphores(blks):
    count = max(blks, 1)
    return [
        pltpu.SemaphoreType.DMA((count,)),
        pltpu.SemaphoreType.DMA((count,)),
        pltpu.SemaphoreType.DMA,
    ]


def exchange_params(blks, megabytes, collective_id):
    if blks:
        return params(megabytes, collective_id=collective_id, has_side_effects=True)
    return params(megabytes)


def late_weights_kernel(h_ref, du_ref, o_ref, da_ref, dwu_ref, dwp_ref, h_t):
    @pl.when(pl.program_id(0) == 0)
    def _():
        h_t[...] = h_ref[...].T
        attended = jnp.concatenate([o_ref[i] for i in range(o_ref.shape[0])], axis=1)
        dwp_ref[...] = dot_tn(attended, da_ref[...]).astype(bf16)

    dwu_ref[...] = dot(h_t[...], du_ref[...]).astype(bf16)


def late_weights(h, du, o, da):
    rows = h.shape[0]
    groups = D // 128
    tile = FF_TILE
    return pl.pallas_call(
        late_weights_kernel,
        grid=(FF // tile,),
        in_specs=[
            whole((rows, D)),
            pl.BlockSpec((rows, tile), lambda i: (0, i)),
            whole((groups, rows, 128)),
            whole((rows, D)),
        ],
        out_specs=[pl.BlockSpec((D, tile), lambda i: (0, i)), whole((D, D))],
        out_shape=[jax.ShapeDtypeStruct((D, FF), bf16), jax.ShapeDtypeStruct((D, D), bf16)],
        scratch_shapes=[pltpu.VMEM((D, rows), bf16)],
        compiler_params=params(40),
        cost_estimate=cost(2 * rows * D * (FF + D), 18 << 20),
        name="up_proj_weight_grads",
    )(h, du, o, da)


def weights_kernel(
    blks, act_ref, dm_ref, h_ref, du_ref, x_ref, taps_ref, o_ref, da_ref, sent,
    dw_ref, dwp_ref, moved, down_keep, down_send, up_keep, up_send,
    down, up, down_near, up_near, h_t, x_t, ex_send, ex_recv, ex_own, ds, dr, us, ur, do_sem, uo_sem,
):
    step = pl.program_id(0)
    steps = FF // FF_TILE
    blk = lax.axis_index("blk")
    core, x, y = blk % 2, (blk // 2) % 2, blk // 4
    exchange = (blks, sent, moved, ex_send, ex_recv, ex_own)

    def to_pair(source, target, sent_sem, received):
        return pltpu.make_async_remote_copy(
            src_ref=source, dst_ref=target, send_sem=sent_sem, recv_sem=received,
            device_id={"blk": blk + 1 - 2 * core}, device_id_type=MESH,
        )

    def down_copy(i):
        return to_pair(down.at[i, 1 - core], down_near.at[i + 1], ds.at[i], dr.at[i])

    def up_columns(t):
        return pl.ds(pl.multiple_of(t * FF_TILE, FF_TILE), FF_TILE)

    def up_copy(t):
        return to_pair(up.at[:, 1 - core, :, up_columns(t)], up_near.at[t + 1], us.at[t], ur.at[t])

    def down_out(i, keep):
        return pltpu.make_async_copy(
            down.at[i, core], (down_keep if keep else down_send).at[i // 2], do_sem.at[i]
        )

    def up_out(t, i, keep):
        return pltpu.make_async_copy(
            up.at[i, core, :, up_columns(t)],
            (up_keep if keep else up_send).at[i % 2, :, up_columns(t)],
            uo_sem.at[t, i],
        )

    def add_down(i, slot, half):
        rows = pl.ds(pl.multiple_of(half * (FF // 16), FF // 16), FF // 16)
        down[i, core, rows] = (
            down[i, core, rows].astype(f32) + down_near[slot, rows].astype(f32)
        ).astype(bf16)

    def out_down(i):
        for keep in (True, False):

            @pl.when((i % 2 == x) == keep)
            def _(keep=keep):
                down_out(i, keep).start()

    def add_up(t, slot):
        columns = up_columns(t)
        for i in range(4):
            up[i, core, :, columns] = (
                up[i, core, :, columns].astype(f32) + up_near[slot, i].astype(f32)
            ).astype(bf16)

    def out_up(t):
        for i in range(4):
            for keep in (True, False):

                @pl.when((i // 2 == y) == keep)
                def _(i=i, keep=keep):
                    up_out(t, i, keep).start()

    @pl.when(step == 0)
    def _():
        greet_signal(blks)
        h_t[...] = h_ref[...].T
        x_t[...] = x_ref[...].T
        greet_wait(blks)
        exchange_start(*exchange)

    piece = (step + 1) // 2 - 2

    @pl.when(step >= 2)
    def _():
        up_copy(step - 2).wait_recv()

    @pl.when((step >= 3) & (step % 2 == 1))
    def _():
        down_copy(piece).wait_recv()

    add_up(lax.rem(step + steps - 2, steps), jnp.maximum(step - 1, 0))
    add_down(lax.rem(piece + 4, 4), jnp.maximum(piece + 1, 0), (step + 1) % 2)
    down[step // 2, step % 2] = dot_tn(act_ref[...], dm_ref[...]).astype(bf16)
    up[:, :, :, up_columns(step)] = (
        dot(h_t[...], du_ref[...]).astype(bf16).reshape(4, 2, D // 8, FF_TILE)
    )

    @pl.when(step % 2 != core)
    def _():
        down_copy(step // 2).start()

    up_copy(step).start()

    @pl.when(step >= 2)
    def _():
        out_up(step - 2)

    @pl.when((step >= 4) & (step % 2 == 0))
    def _():
        out_down(piece)

    @pl.when(step < 3)
    def _():
        for tap in range(3):
            dw_ref[D * tap : D * tap + D, :] = dot(x_t[...], taps_ref[tap]).astype(bf16)

    @pl.when(step == 3)
    def _():
        attended = jnp.concatenate([o_ref[i] for i in range(o_ref.shape[0])], axis=1)
        dwp_ref[...] = dot_tn(attended, da_ref[...]).astype(bf16)

    @pl.when(step == steps - 1)
    def _():
        add_down(2, 3, 1)
        out_down(2)
        for t in (steps - 2, steps - 1):
            up_copy(t).wait_recv()
            add_up(t, t + 1)
            out_up(t)
        down_copy(3).wait_recv()
        for half in range(2):
            add_down(3, 4, half)
        out_down(3)
        exchange_wait(*exchange)
        for t in range(steps):
            up_copy(t).wait_send()
            for i in range(4):
                up_out(t, i, True).wait()
        for i in range(4):
            down_copy(i).wait_send()
            down_out(i, True).wait()


def weights(act, dm, h, du, x, taps, o, da, sent, blks, collective_id):
    rows = h.shape[0]
    groups = D // 128
    tile = FF_TILE
    steps = FF // tile
    anywhere = pl.BlockSpec(memory_space=pl.ANY)
    third = lambda i: jnp.minimum(i, 2)
    dma = pltpu.SemaphoreType.DMA
    half_down, half_up = (2, FF // 8, D), (2, D // 8, FF)
    return pl.pallas_call(
        functools.partial(weights_kernel, blks),
        grid=(steps,),
        in_specs=[
            pl.BlockSpec((rows, tile), lambda i: (0, i)),
            whole((rows, D)),
            whole((rows, D)),
            pl.BlockSpec((rows, tile), lambda i: (0, i)),
            whole((rows, D)),
            pl.BlockSpec((3, rows, C), lambda i: (third(i), 0, 0)),
            whole((groups, rows, 128)),
            whole((rows, D)),
            anywhere,
        ],
        out_specs=[pl.BlockSpec((3 * D, C), lambda i: (third(i), 0)), whole((D, D))]
        + [anywhere] * 5,
        out_shape=[
            jax.ShapeDtypeStruct(shape, bf16)
            for shape in ((9 * D, C), (D, D), sent.shape, half_down, half_down, half_up, half_up)
        ],
        scratch_shapes=[
            pltpu.VMEM((4, 2, FF // 8, D), bf16),
            pltpu.VMEM((4, 2, D // 8, FF), bf16),
            pltpu.VMEM((5, FF // 8, D), bf16),
            pltpu.VMEM((steps + 1, 4, D // 8, FF_TILE), bf16),
            pltpu.VMEM((D, rows), bf16),
            pltpu.VMEM((D, rows), bf16),
        ]
        + exchange_semaphores(blks)
        + [dma((4,)), dma((4,)), dma((steps,)), dma((steps,)), dma((4,)), dma((steps, 4))],
        compiler_params=exchange_params(blks, 62, collective_id),
        cost_estimate=cost(2 * rows * D * (2 * FF + D + 9 * C), 50 << 20),
        name="weight_grads",
    )(act, dm, h, du, x, taps, o, da, sent)


def qkv_grad_kernel(
    g_ref, wq_ref, wk_ref, wv_ref, h_ref, dx1_ref, x_ref, gain_ref,
    dw_ref, dqb_ref, dvb_ref, dx_ref, sums_ref, h_t, total,
):
    step = pl.program_id(0)

    @pl.when(step == 0)
    def _():
        h_t[...] = h_ref[...].T
        total[...] = jnp.zeros_like(total)

    for part, w_ref in enumerate((wq_ref, wk_ref, wv_ref)):
        lanes = slice(128 * part, 128 * part + 128)
        grad = jnp.concatenate([g_ref[0, :, lanes], g_ref[1, :, lanes]], axis=1)
        total[...] += dot_nt(grad, w_ref[...])
        dw_ref[part] = dot(h_t[...], grad).astype(bf16)
        if part == 0:
            dqb_ref[...] = column_sums(grad.astype(f32))
        if part == 2:
            dvb_ref[...] = column_sums(grad.astype(f32))

    @pl.when(step == pl.num_programs(0) - 1)
    def _():
        grad = total[...]
        normed, scale_inv = layer_stats(x_ref[...].astype(f32))
        dx_ref[...] = dx1_ref[...] + layer_backward(grad, normed, scale_inv, gain_ref[...])
        sums_ref[0:1, :] = column_sums(grad * normed)
        sums_ref[1:2, :] = column_sums(grad)
        sums_ref[2:8, :] = jnp.zeros((6, D), f32)


def qkv_grad(g, weight, h, dx1, x, gain):
    rows = x.shape[0]
    groups = D // 128
    return pl.pallas_call(
        qkv_grad_kernel,
        grid=(groups // 2,),
        in_specs=[
            pl.BlockSpec((2, rows, 384), lambda i: (i, 0, 0)),
            pl.BlockSpec((D, 256), lambda i: (0, i)),
            pl.BlockSpec((D, 256), lambda i: (0, 4 + i)),
            pl.BlockSpec((D, 256), lambda i: (0, 8 + i)),
            whole((rows, D)),
            whole((rows, D)),
            whole((rows, D)),
            whole((1, D)),
        ],
        out_specs=[
            pl.BlockSpec((3, D, 256), lambda i: (0, 0, i)),
            pl.BlockSpec((1, 256), lambda i: (0, i)),
            pl.BlockSpec((1, 256), lambda i: (0, i)),
            whole((rows, D)),
            whole((8, D)),
        ],
        out_shape=[
            jax.ShapeDtypeStruct((3, D, D), bf16),
            jax.ShapeDtypeStruct((1, D), f32),
            jax.ShapeDtypeStruct((1, D), f32),
            jax.ShapeDtypeStruct((rows, D), f32),
            jax.ShapeDtypeStruct((8, D), f32),
        ],
        scratch_shapes=[pltpu.VMEM((D, rows), bf16), pltpu.VMEM((rows, D), f32)],
        compiler_params=params(48),
        cost_estimate=cost(4 * rows * D * 3 * D, 24 << 20),
        name="qkv_norm_grad",
    )(g, weight, weight, weight, h, dx1, x, gain)


def row_segments(rows, rim):
    count = rows // BLOCK
    pieces = []
    for block in range(count):
        first = block * BLOCK - (rim if block == 0 else 0)
        last = (block + 1) * BLOCK + (rim if block == count - 1 else 0)
        pieces.append((first, last - first, block))
    return pieces


def shifted_rows(start, shift, size):
    return pl.ds(pl.multiple_of(start + shift, UNIT), size)


def conv_kernel(widths, x_ref, top_ref, bottom_ref, flags, w_ref, z_ref, sums_ref, x_ext, left, right, centre):
    step = pl.program_id(0)
    rows = x_ref.shape[0]
    extent = rows + 2 * RIM

    @pl.when(step == 0)
    def _():
        x_ext[0:RIM, :] = top_ref[...]
        x_ext[RIM : RIM + rows, :] = x_ref[...]
        x_ext[RIM + rows :, :] = bottom_ref[...]
        left[...] = jnp.zeros_like(left)
        right[...] = jnp.zeros_like(right)

    source = x_ext[...]
    left[8 : 8 + extent, :] = dot(source, w_ref[0:D, :])
    right[8 : 8 + extent, :] = dot(source, w_ref[2 * D : 3 * D, :])
    centre[...] = (
        dot(source, w_ref[D : 2 * D, :])
        + flags[:, 2:3] * left[7 : 7 + extent, :]
        + flags[:, 3:4] * right[9 : 9 + extent, :]
    )
    for first, size, block in row_segments(rows, 0):
        own = slice(first, first + size)
        width = widths[block]
        for tap in range(3):

            @pl.when(step == tap)
            def _(tap=tap, first=first, size=size, own=own, width=width):
                found = centre[shifted_rows(RIM + first, (tap - 1) * width, size), :]
                if tap == 0:
                    z_ref[own, :] = flags[RIM + first : RIM + first + size, 0:1] * found
                elif tap == 1:
                    z_ref[own, :] += found
                else:
                    z_ref[own, :] += flags[RIM + first : RIM + first + size, 1:2] * found

    @pl.when(step == 2)
    def _():
        z = z_ref[...]
        sums_ref[0:1, :] = column_sums(z)
        sums_ref[1:2, :] = column_sums(z * z)
        sums_ref[2:8, :] = jnp.zeros((6, C), f32)


def conv(widths, x, top, bottom, flags, weight):
    rows = x.shape[0]
    extent = rows + 2 * RIM
    return pl.pallas_call(
        conv_kernel,
        grid_spec=pltpu.PrefetchScalarGridSpec(
            num_scalar_prefetch=1,
            grid=(3,),
            in_specs=[
                whole((rows, D)),
                whole((RIM, D)),
                whole((RIM, D)),
                whole((extent, 8)),
                pl.BlockSpec((3 * D, C), lambda i, *_: (i, 0)),
            ],
            out_specs=[whole((rows, C)), whole((8, C))],
            scratch_shapes=[
                pltpu.VMEM((extent, D), bf16),
                pltpu.VMEM((extent + 16, C), f32),
                pltpu.VMEM((extent + 16, C), f32),
                pltpu.VMEM((extent, C), f32),
            ],
        ),
        out_shape=[jax.ShapeDtypeStruct((rows, C), f32), jax.ShapeDtypeStruct((8, C), f32)],
        compiler_params=params(26),
        cost_estimate=cost(2 * extent * 9 * D * C, 8 << 20),
        name="conv",
    )(widths, x, top, bottom, flags, weight)


def spread_kernel(widths, g_ref, top_ref, bottom_ref, flags, out_ref, upper, lower, g_ext):
    rows = g_ref.shape[0]
    extent = rows + 2 * WIDE_RIM
    g_ext[0:WIDE_RIM, :] = top_ref[...].astype(f32)
    g_ext[WIDE_RIM : WIDE_RIM + rows, :] = g_ref[...].astype(f32)
    g_ext[WIDE_RIM + rows :, :] = bottom_ref[...].astype(f32)
    inner = slice(8, extent - 8)
    has_left, has_right = flags[inner, 2:3], flags[inner, 3:4]
    for i, target in enumerate((upper, lower)):
        near = g_ext[:, 2 * i * C : (2 * i + 1) * C]
        far = g_ext[:, (2 * i + 1) * C : (2 * i + 2) * C]
        target[0:8, :] = jnp.zeros((8, C), f32)
        target[extent - 8 :, :] = jnp.zeros((8, C), f32)
        target[inner, :] = (
            (1.0 - 0.25 * has_left) * near[inner, :]
            + (1.0 - 0.25 * has_right) * far[inner, :]
            + 0.25 * has_right * g_ext[9 : extent - 7, 2 * i * C : (2 * i + 1) * C]
            + 0.25 * has_left * g_ext[7 : extent - 9, (2 * i + 1) * C : (2 * i + 2) * C]
        )
    for first, size, block in row_segments(rows, RIM):
        width = widths[block]
        here = WIDE_RIM + first
        has_up, has_down = flags[here : here + size, 0:1], flags[here : here + size, 1:2]
        out_ref[RIM + first : RIM + first + size, :] = (
            (1.0 - 0.25 * has_up) * upper[here : here + size, :]
            + (1.0 - 0.25 * has_down) * lower[here : here + size, :]
            + 0.25 * has_down * upper[shifted_rows(here, width, size), :]
            + 0.25 * has_up * lower[shifted_rows(here, -width, size), :]
        )


def spread(widths, g, top, bottom, flags):
    rows = g.shape[0]
    extent = rows + 2 * WIDE_RIM
    return pl.pallas_call(
        spread_kernel,
        grid_spec=pltpu.PrefetchScalarGridSpec(
            num_scalar_prefetch=1,
            grid=(1,),
            in_specs=[
                whole((rows, D)),
                whole((WIDE_RIM, D)),
                whole((WIDE_RIM, D)),
                whole((extent, 8)),
            ],
            out_specs=whole((rows + 2 * RIM, C)),
            scratch_shapes=[
                pltpu.VMEM((extent, C), f32),
                pltpu.VMEM((extent, C), f32),
                pltpu.VMEM((extent, D), f32),
            ],
        ),
        out_shape=jax.ShapeDtypeStruct((rows + 2 * RIM, C), f32),
        compiler_params=params(24),
        cost_estimate=cost(20 * extent * D, 3 << 20),
        name="upsample_grad",
    )(widths, g, top, bottom, flags)


def batch_kernel(
    widths, z_ref, top_ref, bottom_ref, dact_ref, flags, mean_ref, inv_ref, gain_ref, bias_ref,
    up_ref, normed_ref, dbn_ref, sums_ref, act, mixed,
):
    rows = z_ref.shape[0]
    z = jnp.concatenate([top_ref[...], z_ref[...], bottom_ref[...]], axis=0)
    normed = (z - mean_ref[...]) * inv_ref[...]
    normed_ref[...] = normed
    pre = normed * gain_ref[...] + bias_ref[...]
    cumulative, weighted = gelu_parts(pre)
    act[...] = (pre * cumulative).astype(bf16).astype(f32)
    dbn = dact_ref[...] * (cumulative + weighted)
    dbn_ref[...] = dbn
    own = slice(RIM, RIM + rows)
    sums_ref[0:1, :] = column_sums(dbn[own, :])
    sums_ref[1:2, :] = column_sums(dbn[own, :] * normed[own, :])
    sums_ref[2:8, :] = jnp.zeros((6, C), f32)
    for first, size, block in row_segments(rows, 0):
        width = widths[block]
        here = RIM + first
        outer = slice(here - 8, here + size + 8)
        for i in range(2):
            has = flags[outer, i : i + 1]
            mixed[...] = (1.0 - 0.25 * has) * act[outer, :] + 0.25 * has * act[
                pl.ds(pl.multiple_of(here - 8 + (2 * i - 1) * width, 8), size + 16), :
            ]
            for j in range(2):
                has = flags[here : here + size, 2 + j : 3 + j]
                up_ref[first : first + size, (2 * i + j) * C : (2 * i + j + 1) * C] = (
                    (1.0 - 0.25 * has) * mixed[8 : 8 + size, :]
                    + 0.25 * has * mixed[7 + 2 * j : 7 + 2 * j + size, :]
                ).astype(bf16)


def batch(widths, z, top, bottom, dact, flags, mean, inv, gain, bias):
    rows = z.shape[0]
    extent = rows + 2 * RIM
    return pl.pallas_call(
        batch_kernel,
        grid_spec=pltpu.PrefetchScalarGridSpec(
            num_scalar_prefetch=1,
            grid=(1,),
            in_specs=[
                whole((rows, C)),
                whole((RIM, C)),
                whole((RIM, C)),
                whole((extent, C)),
                whole((extent, 8)),
                whole((1, C)),
                whole((1, C)),
                whole((1, C)),
                whole((1, C)),
            ],
            out_specs=[
                whole((rows, D)),
                whole((extent, C)),
                whole((extent, C)),
                whole((8, C)),
            ],
            scratch_shapes=[pltpu.VMEM((extent, C), f32), pltpu.VMEM((BLOCK + 16, C), f32)],
        ),
        out_shape=[
            jax.ShapeDtypeStruct((rows, D), bf16),
            jax.ShapeDtypeStruct((extent, C), f32),
            jax.ShapeDtypeStruct((extent, C), f32),
            jax.ShapeDtypeStruct((8, C), f32),
        ],
        compiler_params=params(24),
        cost_estimate=cost(60 * extent * C, 4 << 20),
        name="batch_norm",
    )(widths, z, top, bottom, dact, flags, mean, inv, gain, bias)


def conv_grad_kernel(
    widths, dbn_ref, normed_ref, flags, scale_ref, shift_ref, slope_ref, w_ref, og_ref,
    taps, dy_ref, dm_ref, moved,
):
    step = pl.program_id(0)
    rows = og_ref.shape[0]
    extent = rows + 2 * RIM

    @pl.when(step == 0)
    def _():
        dz = scale_ref[...] * (dbn_ref[...] - shift_ref[...] - normed_ref[...] * slope_ref[...])
        dz = dz.astype(bf16).astype(f32)
        dy_ref[...] = og_ref[...].astype(f32)
        moved[0, 0:8, :] = jnp.zeros((8, C), f32)
        moved[0, 8 + extent :, :] = jnp.zeros((8, C), f32)
        moved[0, 8 : 8 + extent, :] = dz
        moved[1, 8 : 8 + extent, :] = flags[:, 3:4] * moved[0, 9 : 9 + extent, :]
        moved[2, 8 : 8 + extent, :] = flags[:, 2:3] * moved[0, 7 : 7 + extent, :]
        for first, size, block in row_segments(rows, 0):
            width = widths[block]
            here = RIM + first
            for row in range(3):
                for col, slot in enumerate((1, 0, 2)):
                    found = moved[slot, pl.ds(pl.multiple_of(8 + here + (1 - row) * width, 8), size), :]
                    if row == 0:
                        found = flags[here : here + size, 1:2] * found
                    if row == 2:
                        found = flags[here : here + size, 0:1] * found
                    taps[3 * row + col, first : first + size, :] = found.astype(bf16)

    for part in range(3):
        dy_ref[...] += dot_nt(taps[3 * step + part], w_ref[D * part : D * part + D, :])

    @pl.when(step == pl.num_programs(0) - 1)
    def _():
        dm_ref[...] = dy_ref[...].astype(bf16)


def conv_grad(widths, dbn, normed, flags, scale, shift, slope, weight, out_grad):
    rows = out_grad.shape[0]
    extent = rows + 2 * RIM
    return pl.pallas_call(
        conv_grad_kernel,
        grid_spec=pltpu.PrefetchScalarGridSpec(
            num_scalar_prefetch=1,
            grid=(3,),
            in_specs=[
                whole((extent, C)),
                whole((extent, C)),
                whole((extent, 8)),
                whole((1, C)),
                whole((1, C)),
                whole((1, C)),
                pl.BlockSpec((3 * D, C), lambda i, *_: (i, 0)),
                whole((rows, D)),
            ],
            out_specs=[whole((9, rows, C)), whole((rows, D)), whole((rows, D))],
            scratch_shapes=[pltpu.VMEM((3, extent + 16, C), f32)],
        ),
        out_shape=[
            jax.ShapeDtypeStruct((9, rows, C), bf16),
            jax.ShapeDtypeStruct((rows, D), f32),
            jax.ShapeDtypeStruct((rows, D), bf16),
        ],
        compiler_params=params(32),
        cost_estimate=cost(2 * rows * 9 * D * C, 12 << 20),
        name="conv_grad",
    )(widths, dbn, normed, flags, scale, shift, slope, weight, out_grad)


def small_sum_kernel(scatter, blks, seqs, rimmed, x_ref, *refs):
    blk, seq = lax.axis_index("blk"), lax.axis_index("seq")
    if rimmed:
        z_ref, out_ref, top, bottom, *refs = refs
    else:
        out_ref, *refs = refs
    first, second, sends, receives, sends2, receives2 = refs[:6]
    barrier = pltpu.get_barrier_semaphore()
    for step in range(1, blks):
        pl.semaphore_signal(
            barrier, inc=1, device_id={"blk": lax.rem(blk + step, blks)}, device_id_type=MESH
        )
    for step in range(1, seqs):
        pl.semaphore_signal(
            barrier, inc=1, device_id={"seq": lax.rem(seq + step, seqs)}, device_id_type=MESH
        )
    pl.semaphore_wait(barrier, blks + seqs - 2)
    copies = []
    for step in range(1, blks):
        to = lax.rem(blk + step, blks)
        copy = pltpu.make_async_remote_copy(
            src_ref=x_ref.at[to] if scatter else x_ref.at[0],
            dst_ref=first.at[blk],
            send_sem=sends.at[step],
            recv_sem=receives.at[step],
            device_id={"blk": to},
            device_id_type=MESH,
        )
        copy.start()
        copies.append(copy)
    if rimmed:
        rims = Rims(blks, z_ref, top, bottom, *refs[6:])
        rims.start()
    first[blk] = x_ref[blk] if scatter else x_ref[0]
    for copy in copies:
        copy.wait()
    total = first[0]
    for i in range(1, blks):
        total = total + first[i]
    second[seq] = total
    copies = []
    for step in range(1, seqs):
        copy = pltpu.make_async_remote_copy(
            src_ref=second.at[seq],
            dst_ref=second.at[seq],
            send_sem=sends2.at[step],
            recv_sem=receives2.at[step],
            device_id={"seq": lax.rem(seq + step, seqs)},
            device_id_type=MESH,
        )
        copy.start()
        copies.append(copy)
    for copy in copies:
        copy.wait()
    total = second[0]
    for i in range(1, seqs):
        total = total + second[i]
    out_ref[...] = total
    if rimmed:
        rims.wait()


def small_sum(x, scatter, collective_id, rimmed=None):
    blks, seqs = lax.axis_size("blk"), lax.axis_size("seq")
    part = x.shape[1:]
    vmem = pl.BlockSpec(memory_space=pltpu.VMEM)
    given, found, extra = [x], [jax.ShapeDtypeStruct(part, f32)], []
    if rimmed is not None:
        given.append(rimmed)
        found += [jax.ShapeDtypeStruct((RIM, rimmed.shape[1]), f32)] * 2
        extra.append(pltpu.VMEM((2, RIM, rimmed.shape[1]), f32))
        extra.append(pltpu.SemaphoreType.DMA((4,)))
    found = pl.pallas_call(
        functools.partial(small_sum_kernel, scatter, blks, seqs, rimmed is not None),
        in_specs=[vmem] * len(given),
        out_specs=[vmem] * len(found),
        out_shape=found,
        scratch_shapes=[
            pltpu.VMEM((blks, *part), f32),
            pltpu.VMEM((seqs, *part), f32),
            pltpu.SemaphoreType.DMA((blks,)),
            pltpu.SemaphoreType.DMA((blks,)),
            pltpu.SemaphoreType.DMA((seqs,)),
            pltpu.SemaphoreType.DMA((seqs,)),
        ]
        + extra,
        compiler_params=params(16, collective_id=collective_id, has_side_effects=True),
        name="small_sum",
    )(*given)
    return found if rimmed is not None else found[0]


LAG = 2
PIECE_ROWS = 64
SLOTS = 3
ROOT = 1


def cuts(size, piece):
    return [slice(first, min(size, first + piece)) for first in range(0, size, piece)]


def pieces_of(index, shape):
    parts, rows, columns = shape
    piece = PIECE_ROWS if columns >= D else 3 * PIECE_ROWS
    return [
        (index, part, row, column)
        for part in range(parts)
        for row in cuts(rows, piece)
        for column in cuts(columns, D)
    ]


class Reducer:
    @staticmethod
    def scratch(shapes, dtypes, staged, halves, units):
        places = []
        for lead in ((4,), (2,), (), (), ()):
            places += [
                pltpu.VMEM(
                    (shape[0],) + ((2,) if lead and index in halves else lead) + shape[1:], dtype
                )
                for index, (shape, dtype) in enumerate(zip(shapes, dtypes))
            ]
        for index in range(len(shapes)):
            _, _, rows, columns = next(unit for unit in units if unit[0] == index)
            size = (rows.stop - rows.start, columns.stop - columns.start)
            size = (SLOTS, 4) + size if index in staged else (1, 1, 16, 128)
            places.append(pltpu.VMEM(size, dtypes[index]))
        total = len(units)
        semaphores = [pltpu.SemaphoreType.DMA((total, 2))] * 2
        semaphores += [pltpu.SemaphoreType.DMA((total,))] * 10
        return places + semaphores

    def __init__(self, seqs, units, staged, halves, ins, outs, refs):
        count = len(ins)
        self.seqs, self.units, self.staged, self.ins, self.outs = seqs, units, staged, ins, outs
        self.halves = halves
        self.sums, self.side, self.last, self.below, self.above, self.slots = [
            refs[i * count : (i + 1) * count] for i in range(6)
        ]
        (self.s2, self.r2, self.load_sem, self.s1, self.r1, self.s3, self.r3, self.sb, self.rb,
         self.sa, self.ra, self.out_sem) = refs[6 * count :]
        blk, self.seq = lax.axis_index("blk"), lax.axis_index("seq")
        self.core, self.x, self.y = blk % 2, (blk // 2) % 2, blk // 4
        self.pair = {"blk": blk + 1 - 2 * self.core}
        self.over_x = {"blk": blk + 2 - 4 * self.x}
        self.over_y = {"blk": blk + 4 - 8 * self.y}
        self.order = {}
        for u, unit in enumerate(units):
            self.order.setdefault(unit[0], []).append(u)

    def send(self, source, target, sent, received, peer):
        return pltpu.make_async_remote_copy(
            src_ref=source, dst_ref=target, send_sem=sent, recv_sem=received,
            device_id=peer, device_id_type=MESH,
        )

    def own(self, u):
        index, part, rows, columns = self.units[u]
        if index in self.staged:
            return self.slots[index].at[self.order[index].index(u) % SLOTS]
        return self.ins[index].at[part, :, self.core, rows, columns]

    def load(self, u):
        index, part, rows, columns = self.units[u]
        return pltpu.make_async_copy(
            self.ins[index].at[part, :, self.core, rows, columns], self.own(u), self.load_sem.at[u]
        )

    def load_half(self, u):
        index, part, rows, columns = self.units[u]
        kept, arrived = self.ins[index]
        return [
            pltpu.make_async_copy(
                kept.at[:, rows, columns], self.sums[index].at[part, :, rows, columns], self.load_sem.at[u]
            ),
            pltpu.make_async_copy(
                arrived.at[:, rows, columns], self.side[index].at[part, :, rows, columns], self.r1.at[u]
            ),
        ]

    def over_x_first(self, u):
        index = self.units[u][0]
        if index in self.halves:
            return self.halves[index] == 0
        return [v for v, unit in enumerate(self.units) if unit[0] not in self.halves].index(u) % 2 == 0

    def first(self, u):
        index, part, rows, columns = self.units[u]
        return self.send(
            self.ins[index].at[part, :, 1 - self.core, rows, columns],
            self.sums[index].at[part, :, rows, columns],
            self.s1.at[u], self.r1.at[u], self.pair,
        )

    def second(self, u):
        index, part, rows, columns = self.units[u]
        copies = []
        for i in range(2):
            x_first = self.over_x_first(u)
            place = 1 - self.x + 2 * i if x_first else 2 * (1 - self.y) + i
            copies.append(
                self.send(
                    self.sums[index].at[part, place, rows, columns],
                    self.side[index].at[part, i, rows, columns],
                    self.s2.at[u, i], self.r2.at[u, i], self.over_x if x_first else self.over_y,
                )
            )
        return copies

    def third(self, u):
        index, part, rows, columns = self.units[u]
        x_first = self.over_x_first(u)
        if index in self.halves:
            place = 1 - self.y if x_first else 1 - self.x
        else:
            place = 2 * (1 - self.y) + self.x if x_first else 2 * self.y + 1 - self.x
        return self.send(
            self.sums[index].at[part, place, rows, columns],
            self.last[index].at[part, rows, columns],
            self.s3.at[u], self.r3.at[u], self.over_y if x_first else self.over_x,
        )

    def result(self, u):
        index, part, rows, columns = self.units[u]
        if index in self.halves:
            return self.sums[index].at[part, self.y if self.over_x_first(u) else self.x, rows, columns]
        return self.sums[index].at[part, 2 * self.y + self.x, rows, columns]

    def down(self, u):
        index, part, rows, columns = self.units[u]
        return self.send(
            self.result(u), self.above[index].at[part, rows, columns],
            self.sa.at[u], self.ra.at[u], {"seq": self.seq - 1},
        )

    def up(self, u):
        index, part, rows, columns = self.units[u]
        return self.send(
            self.result(u), self.below[index].at[part, rows, columns],
            self.sb.at[u], self.rb.at[u], {"seq": self.seq + 1},
        )

    def store(self, u):
        index, part, rows, columns = self.units[u]
        return pltpu.make_async_copy(
            self.result(u), self.outs[index].at[part, rows, columns], self.out_sem.at[u]
        )

    def add_to(self, target, *sources):
        total = target[...].astype(f32)
        for source in sources:
            total = total + source[...].astype(f32)
        target[...] = total.astype(target.dtype)

    def enter(self, u):
        if self.units[u][0] in self.halves:
            for copy in self.load_half(u):
                copy.start()
            return
        self.first(u).start()
        index = self.units[u][0]
        if index in self.staged and self.order[index].index(u) < SLOTS:
            self.load(u).start()

    def stage_near(self, u):
        index, part, rows, columns = self.units[u]
        if index in self.halves:
            return
        if index in self.staged:
            self.load(u).wait()
        self.first(u).wait_recv()
        own = self.own(u)
        for i in range(4):
            self.add_to(self.sums[index].at[part, i, rows, columns], own.at[i])
        if index in self.staged:
            later = self.order[index].index(u) + SLOTS
            if later < len(self.order[index]):
                self.load(self.order[index][later]).start()
        for copy in self.second(u):
            copy.start()

    def stage_side(self, u):
        index, part, rows, columns = self.units[u]
        if index in self.halves:
            for copy in self.load_half(u):
                copy.wait()
            for i in range(2):
                self.add_to(
                    self.sums[index].at[part, i, rows, columns],
                    self.side[index].at[part, i, rows, columns],
                )
            self.third(u).start()
            return
        for i, copy in enumerate(self.second(u)):
            copy.wait_recv()
            keep = 2 * i + self.x if self.over_x_first(u) else 2 * self.y + i
            self.add_to(
                self.sums[index].at[part, keep, rows, columns],
                self.side[index].at[part, i, rows, columns],
            )
        self.third(u).start()

    def stage_last(self, u):
        index, part, rows, columns = self.units[u]
        self.third(u).wait_recv()
        self.add_to(self.result(u), self.last[index].at[part, rows, columns])

        @pl.when(self.seq < ROOT)
        def _():
            self.up(u).start()

        @pl.when(self.seq == self.seqs - 1)
        def _():
            self.down(u).start()

    def stage_chain(self, u, place):
        index, part, rows, columns = self.units[u]

        @pl.when(self.seq == place)
        def _():
            self.down(u).wait_recv()
            self.add_to(self.result(u), self.above[index].at[part, rows, columns])
            self.down(u).start()

    def stage_root(self, u):
        index, part, rows, columns = self.units[u]

        @pl.when(self.seq == ROOT)
        def _():
            self.up(u).wait_recv()
            self.down(u).wait_recv()
            self.add_to(
                self.result(u),
                self.below[index].at[part, rows, columns],
                self.above[index].at[part, rows, columns],
            )
            self.up(u).start()
            self.down(u).start()
            self.store(u).start()

    def stage_spread(self, u, place):
        index, part, rows, columns = self.units[u]

        @pl.when(self.seq == place)
        def _():
            if place < ROOT:
                self.down(u).wait_recv()
                self.up(u).wait_send()
                self.result(u)[...] = self.above[index].at[part, rows, columns][...]
            else:
                self.up(u).wait_recv()
                self.down(u).wait_send()
                self.result(u)[...] = self.below[index].at[part, rows, columns][...]
                if place < self.seqs - 1:
                    self.up(u).start()
            self.store(u).start()

    def stages(self):
        found = [(0, self.stage_near), (LAG, self.stage_side), (2 * LAG, self.stage_last)]
        at = 3 * LAG
        for place in range(self.seqs - 2, ROOT, -1):
            found.append((at, functools.partial(self.stage_chain, place=place)))
            at += LAG
        found.append((at, self.stage_root))
        at += LAG
        for place in range(ROOT):
            found.append((at, functools.partial(self.stage_spread, place=place)))
        for place in range(ROOT + 1, self.seqs):
            found.append((at, functools.partial(self.stage_spread, place=place)))
            at += LAG
        return found

    def steps(self):
        return len(self.units) + self.stages()[-1][0]

    def step(self, t):
        for lag, stage in self.stages():
            if 0 <= t - lag < len(self.units):
                stage(t - lag)

    def finish(self):
        for u in range(len(self.units)):
            if self.units[u][0] not in self.halves:
                self.first(u).wait_send()
                for copy in self.second(u):
                    copy.wait_send()
            self.third(u).wait_send()

            @pl.when(self.seq == ROOT)
            def _(u=u):
                self.down(u).wait_send()
                self.up(u).wait_send()

            @pl.when((self.seq > ROOT) & (self.seq < self.seqs - 1))
            def _(u=u):
                self.up(u).wait_send()

            self.store(u).wait()


STAGED = (2, 3)
HALVES = {0: 0, 1: 1}

AHEAD = 10


def tail_kernel(
    blks, seqs, units, sent, w_ref, h_in, dx1_in, x_in, gain_ref, sums_ref, dub_ref,
    down_in, down_side, up_in, up_side, conv_in, proj_in, dx_out,
    down_out, up_out, conv_out, proj_out, qkv_out, vec_out,
    moved, dw, vectors, h_ref, dx1_ref, x_ref, dx_ref, h_t, w_slots, in_sem, ex_send, ex_recv, ex_own, w_sem, *refs
):
    reducer = Reducer(
        seqs, units, STAGED, HALVES,
        ((down_in, down_side), (up_in, up_side), conv_in, proj_in, dw, vectors),
        (down_out, up_out, conv_out, proj_out, qkv_out, vec_out), refs,
    )
    early = [u for u, unit in enumerate(units) if unit[0] < 4]
    given = [
        pltpu.make_async_copy(source, target, in_sem.at[i])
        for i, (source, target) in enumerate(((h_in, h_ref), (dx1_in, dx1_ref), (x_in, x_ref)))
    ]
    dx_copy = pltpu.make_async_copy(dx_ref, dx_out, in_sem.at[3])
    exchange = (blks, sent, moved, ex_send, ex_recv, ex_own)
    slots = w_slots.shape[0]

    def weight(k):
        part, i = divmod(k, 4)
        first = D * part + 256 * i
        return pltpu.make_async_copy(
            w_ref.at[:, first : first + 256], w_slots.at[k % slots], w_sem.at[k]
        )

    def put(vector, row, index):
        for place in range(8):
            vectors[0, place // 2, place % 2, row : row + 1, :] = vector[:, 128 * index(place) : 128 * index(place) + 128]

    def chunk(k):
        part, i = divmod(k, 4)
        lanes = slice(128 * part, 128 * part + 128)
        weight(k).wait()
        grad = jnp.concatenate([moved[2 * i, :, lanes], moved[2 * i + 1, :, lanes]], axis=1)
        dx_ref[...] += dot_nt(grad, w_slots[k % slots])
        dw[part, :, :, :, 256 * i : 256 * i + 256] = (
            dot(h_t[...], grad).astype(bf16).reshape(4, 2, 128, 256)
        )
        if k + slots < 12:
            weight(k + slots).start()
        if part != 1:
            bias = column_sums(grad.astype(f32))
            place = i + (4 if part else 0)
            for half in range(2):
                vectors[0, place // 2, place % 2, 6 + half : 7 + half, :] = bias[:, 128 * half : 128 * half + 128]
        if i == 3:
            for u, unit in enumerate(units):
                if unit[0] == 4 and unit[1] == part:
                    reducer.enter(u)

    def norm():
        given[1].wait()
        given[2].wait()
        grad = dx_ref[...]
        normed, scale_inv = layer_stats(x_ref[...].astype(f32))
        dx_ref[...] = dx1_ref[...] + layer_backward(grad, normed, scale_inv, gain_ref[...])
        dx_copy.start()
        put(column_sums(grad * normed), 0, lambda place: place)
        put(column_sums(grad), 1, lambda place: place)
        for row in range(4):
            put(sums_ref[row : row + 1, :], 2 + row, lambda place: place)
            put(dub_ref[...], 8 + row, lambda place, row=row: 4 * place + row)
        for place in range(8):
            vectors[0, place // 2, place % 2, 12:16, :] = jnp.zeros((4, 128), f32)
        for u, unit in enumerate(units):
            if unit[0] == 5:
                reducer.enter(u)

    for copy in given:
        copy.start()
    greet(blks, seqs)
    exchange_start(*exchange)
    for u in early:
        reducer.enter(u)
    for k in range(slots):
        weight(k).start()
    given[0].wait()
    h_t[...] = h_ref[...].T
    dx_ref[...] = jnp.zeros_like(dx_ref)
    at = 0
    while at < AHEAD:
        reducer.step(at)
        at += 1
    exchange_wait(*exchange)
    for k in range(12):
        chunk(k)
        if k % 2:
            reducer.step(at)
            at += 1
    norm()
    while at < reducer.steps():
        reducer.step(at)
        at += 1
    reducer.finish()
    dx_copy.wait()


def tail(sent, weight, h, dx1, x, gain, sums, dub, arrays, collective_id):
    blks, seqs = lax.axis_size("blk"), lax.axis_size("seq")
    rows = x.shape[0]
    shapes = [(1, FF // 8, D), (1, D // 8, FF), (1, 9 * D // 8, C), (1, D // 8, D), (3, D // 8, D), (1, 16, 128)]
    dtypes = [bf16] * 5 + [f32]
    found = [pieces_of(index, shape) for index, shape in enumerate(shapes)]
    light = [unit for pair in zip(found[0], found[1]) for unit in pair]
    heavy = found[2] + found[3] + found[4]
    units = []
    for i, unit in enumerate(heavy):
        units += [unit] + light[i * len(light) // len(heavy) : (i + 1) * len(light) // len(heavy)]
    units += found[5]
    anywhere = pl.BlockSpec(memory_space=pl.ANY)
    vmem = pl.BlockSpec(memory_space=pltpu.VMEM)
    return pl.pallas_call(
        functools.partial(tail_kernel, blks, seqs, units),
        in_specs=[anywhere] * 5 + [vmem] * 3 + [anywhere] * 6,
        out_specs=[anywhere] * 7,
        out_shape=[jax.ShapeDtypeStruct((rows, D), f32)]
        + [
            jax.ShapeDtypeStruct(shape, dtype) for shape, dtype in zip(shapes, dtypes)
        ],
        scratch_shapes=[
            pltpu.VMEM(sent.shape, bf16),
            pltpu.VMEM((3, 4, 2, D // 8, D), bf16),
            pltpu.VMEM((1, 4, 2, 16, 128), f32),
            pltpu.VMEM((rows, D), bf16),
            pltpu.VMEM((rows, D), f32),
            pltpu.VMEM((rows, D), bf16),
            pltpu.VMEM((rows, D), f32),
            pltpu.VMEM((D, rows), bf16),
            pltpu.VMEM((3, D, 256), bf16),
            pltpu.SemaphoreType.DMA((4,)),
            pltpu.SemaphoreType.DMA((blks,)),
            pltpu.SemaphoreType.DMA((blks,)),
            pltpu.SemaphoreType.DMA,
            pltpu.SemaphoreType.DMA((12,)),
        ]
        + Reducer.scratch(shapes, dtypes, STAGED, HALVES, units),
        compiler_params=params(63, collective_id=collective_id, has_side_effects=True),
        name="qkv_grad_and_sums",
    )(sent, weight, h, dx1, x, gain, sums, dub, *arrays)


def widen_kernel(counts, *refs):
    matrices = len(refs) - len(counts) - 1 >> 1
    sources, vectors = refs[:matrices], refs[matrices]
    targets, pieces = refs[matrices + 1 : 2 * matrices + 1], refs[2 * matrices + 1 :]
    for source, target in zip(sources[:-1], targets[:-1]):
        target[...] = source[0].astype(f32)
    for part in range(3):
        targets[-1][:, D * part : D * part + D] = sources[-1][part].astype(f32)
    row = 0
    for count, piece in zip(counts, pieces):
        for i in range(count):
            piece[:, 128 * i : 128 * i + 128] = vectors[0, row : row + 1, :]
            row += 1


def widen(arrays, vectors, counts):
    steps = 4
    return pl.pallas_call(
        functools.partial(widen_kernel, counts),
        grid=(steps,),
        in_specs=[
            pl.BlockSpec((a.shape[0], a.shape[1] // steps, a.shape[2]), lambda i: (0, i, 0))
            for a in arrays
        ]
        + [whole(vectors.shape)],
        out_specs=[
            pl.BlockSpec((a.shape[1] // steps, a.shape[0] * a.shape[2]), lambda i: (i, 0))
            for a in arrays
        ]
        + [whole((1, 128 * count)) for count in counts],
        out_shape=[
            jax.ShapeDtypeStruct((a.shape[1], a.shape[0] * a.shape[2]), f32) for a in arrays
        ]
        + [jax.ShapeDtypeStruct((1, 128 * count), f32) for count in counts],
        compiler_params=params(62),
        name="widen",
    )(*arrays, vectors)


def shifted(value, axis, steps):
    count = lax.axis_size(axis)
    leading, last = (max(0, -steps), min(count, count - steps))
    return lax.ppermute(value, axis, [(source, source + steps) for source in range(leading, last)])


def near_blocks(sides_row, keys_own, values_own):
    rows = keys_own.shape[0]
    place, length = lax.axis_index("blk"), rows * lax.axis_size("blk")
    centre = jnp.arange(rows, dtype=jnp.int32)
    segment = image_info(sides_row, place * rows + centre)[0]
    found = []
    for offset in range(-REACH, REACH + 1):
        keys, values = (keys_own, values_own) if offset == 0 else shifted((keys_own, values_own), "blk", -offset)
        positions = (place + offset) * rows + centre
        inside = (positions >= 0) & (positions < length)
        allowed = (segment[:, None] == image_info(sides_row, positions)[0][None, :]) & inside[None, :]
        found.append((offset, keys.reshape(rows, HEADS, HEAD), values.reshape(rows, HEADS, HEAD), allowed))
    return found


def near_scores(queries, keys, allowed):
    scores = jnp.einsum("qhd,khd->hqk", queries, keys, preferred_element_type=f32)
    return jnp.where(allowed[None], scores, masked_score)


def near_attention(near, queries):
    rows = queries.shape[0]
    peak = jnp.full((HEADS, rows), masked_score, f32)
    total = jnp.zeros((HEADS, rows), f32)
    for _, keys, _, allowed in near:
        scores = near_scores(queries, keys, allowed)
        new_peak = jnp.maximum(peak, jnp.max(scores, axis=-1))
        grown = jnp.where(allowed[None], jnp.exp2(scores - new_peak[..., None]), 0.0)
        total = total * jnp.exp2(peak - new_peak) + jnp.sum(grown, axis=-1)
        peak = new_peak
    lse = peak + jnp.log2(total)
    out = jnp.zeros((rows, HEADS, HEAD), f32)
    for _, keys, values, allowed in near:
        scores = near_scores(queries, keys, allowed)
        weights = jnp.where(allowed[None], jnp.exp2(scores - lse[..., None]), 0.0).astype(bf16)
        out = out + jnp.einsum("hqk,khd->qhd", weights, values, preferred_element_type=f32)
    return out.reshape(rows, D).astype(bf16), lse


def near_attention_grad(near, queries, lse, out, grad):
    rows = queries.shape[0]
    grad_heads = grad.reshape(rows, HEADS, HEAD)
    delta = jnp.sum((grad.astype(f32) * out.astype(f32)).reshape(rows, HEADS, HEAD), axis=-1).T
    dq = jnp.zeros((rows, HEADS, HEAD), f32)
    dk = jnp.zeros((rows, HEADS, HEAD), f32)
    dv = jnp.zeros((rows, HEADS, HEAD), f32)
    for offset, keys, values, allowed in near:
        scores = near_scores(queries, keys, allowed)
        weights = jnp.where(allowed[None], jnp.exp2(scores - lse[..., None]), 0.0)
        value_grad = jnp.einsum("qhd,khd->hqk", grad_heads, values, preferred_element_type=f32)
        score_grad = (weights * (value_grad - delta[..., None])).astype(bf16)
        dq = dq + jnp.einsum("hqk,khd->qhd", score_grad, keys, preferred_element_type=f32)
        dk_part = jnp.einsum("hqk,qhd->khd", score_grad, queries, preferred_element_type=f32)
        dv_part = jnp.einsum(
            "hqk,qhd->khd", weights.astype(bf16), grad_heads, preferred_element_type=f32
        )
        if offset:
            dk_part, dv_part = shifted((dk_part.astype(bf16), dv_part.astype(bf16)), "blk", offset)
        dk = dk + dk_part.astype(f32)
        dv = dv + dv_part.astype(f32)
    dq = dq.reshape(rows, D).astype(bf16) * jnp.asarray(HEAD**-0.5, bf16)
    dk = (dk * (1.0 / LOG2E)).reshape(rows, D).astype(bf16)
    return dq, dk, dv.reshape(rows, D).astype(bf16)


def in_groups(*parts):
    rows = parts[0].shape[0]
    stacked = jnp.stack([part.reshape(rows, D // 128, 128) for part in parts], axis=2)
    return stacked.transpose(1, 0, 2, 3).reshape(D // 128, rows, 128 * len(parts))


def from_groups(groups, part):
    picked = groups[:, :, 128 * part : 128 * part + 128]
    return picked.transpose(1, 0, 2).reshape(groups.shape[1], D)


def rims(rows_own, width):
    count = lax.axis_size("blk")
    top = lax.ppermute(rows_own[-width:], "blk", [(i, i + 1) for i in range(count - 1)])
    bottom = lax.ppermute(rows_own[:width], "blk", [(i + 1, i) for i in range(count - 1)])
    return top, bottom


def line(vector):
    return vector.reshape(1, -1)


def shards(
    tokens,
    image_sides,
    ln1_gain,
    ln1_bias,
    qkv_weight,
    qv_bias,
    proj_weight,
    proj_bias,
    ln2_gain,
    ln2_bias,
    up_weight,
    up_bias,
    down_weight,
    down_bias,
    conv_weight,
    bn_gain,
    bn_bias,
    out_grad,
    pup_grad,
):
    x = tokens[0]
    sides_row = image_sides[0]
    rows = x.shape[0]
    blks, seqs = lax.axis_size("blk"), lax.axis_size("seq")
    place = lax.axis_index("blk")
    length = rows * blks
    samples = length * seqs
    by_heads = blks == 8 and HEADS // 2 == blks

    block_starts = jnp.arange(length // BLOCK, dtype=jnp.int32) * BLOCK
    _, block_width, _, _, block_begin = image_info(sides_row, block_starts)
    starts = (block_begin // BLOCK).astype(jnp.int32)
    counts = (block_width * block_width // BLOCK).astype(jnp.int32)
    own_blocks = rows // BLOCK
    widths = lax.dynamic_slice_in_dim(block_width, place * own_blocks, own_blocks)
    wide_positions = place * rows + jnp.arange(-WIDE_RIM, rows + WIDE_RIM, dtype=jnp.int32)
    wide_flags = edge_flags(sides_row, wide_positions)
    flags = wide_flags[WIDE_RIM - RIM : WIDE_RIM + rows + RIM]

    g = pup_grad[0]
    if by_heads:
        h1, g_top, g_bottom, qkv = project_qkv_exchanged(
            x, line(ln1_gain), line(ln1_bias), qkv_weight, line(qv_bias), g, 6
        )
        qkv = qkv.reshape(length, 384)
        o_heads, lse = attention(starts, counts, qkv)
        o_groups = exchange(o_heads.reshape(blks, rows, 128), 7)
    else:
        g_top, g_bottom = rims(g, WIDE_RIM)
        h1, qkv_groups = project_qkv(x, line(ln1_gain), line(ln1_bias), qkv_weight, line(qv_bias))
        queries = from_groups(qkv_groups, 0).reshape(rows, HEADS, HEAD)
        near = near_blocks(sides_row, from_groups(qkv_groups, 1), from_groups(qkv_groups, 2))
        attended, lse = near_attention(near, queries)
        o_groups = in_groups(attended)
    dact = spread(widths, g, g_top, g_bottom, wide_flags)
    x1, h2, act, slope, block_low, top, bottom = mlp(
        o_groups, x, proj_weight, line(proj_bias), line(ln2_gain), line(ln2_bias),
        up_weight, line(up_bias), down_weight, line(down_bias), 8,
    )
    z, z_sums = conv(widths, block_low, top, bottom, flags, conv_weight)
    z_sums, z_top, z_bottom = small_sum(z_sums[None], False, 1, z)
    mean = z_sums[0:1] / samples
    inv = lax.rsqrt(z_sums[1:2] / samples - mean * mean + batch_eps)
    pup_out, normed, dbn, bn_sums = batch(
        widths, z, z_top, z_bottom, dact, flags, mean, inv, line(bn_gain), line(bn_bias)
    )
    bn_sums = small_sum(bn_sums[None], False, 2)

    taps, dy, dm = conv_grad(
        widths, dbn, normed, flags, inv * line(bn_gain), bn_sums[0:1] / samples, bn_sums[1:2] / samples,
        conv_weight, out_grad[0],
    )
    du, up_bias_grad, dx1, da, do_groups, mlp_sums = mlp_grad(
        dy, dm, slope, down_weight, up_weight, x1, line(ln2_gain), proj_weight
    )
    if by_heads:
        conv_weight_grad, proj_grad, do_moved, down_keep, down_send, up_keep, up_send = weights(
            act, dm, h2, du, block_low, taps, o_groups, da, do_groups, blks, 5
        )
        down_side = lax.ppermute(down_send, "blk", [(i, i ^ 2) for i in range(blks)])
        up_side = lax.ppermute(up_send, "blk", [(i, i ^ 4) for i in range(blks)])
        dqkv = attention_grad(starts, counts, qkv, do_moved.reshape(length, 128), o_heads, lse)
        dqkv_groups = dqkv.reshape(blks, rows, 384)
    else:
        down_grad = down_weight_grad_of(act, dm)
        conv_weight_grad = conv_weight_grad_of(block_low, taps)
        up_grad, proj_grad = late_weights(h2, du, o_groups, da)
        grads = near_attention_grad(near, queries, lse, attended, from_groups(do_groups, 0))
        dqkv_groups = in_groups(*grads)

    piece = D // blks
    cuts_of = [piece] * 6 + [2 * piece, 4 * piece]
    if by_heads:
        tokens_grad, *summed = tail(
            dqkv_groups, qkv_weight, h1, dx1, x, line(ln1_gain), mlp_sums, up_bias_grad,
            [
                down_keep, down_side, up_keep, up_side,
                conv_weight_grad.reshape(1, 4, 2, -1, C), proj_grad.reshape(1, 4, 2, -1, D),
            ],
            3,
        )
        tokens_grad, down_grad, up_grad, conv_weight_grad, proj_grad, qkv_weight_grad, *small = widen(
            [tokens_grad[None]] + summed[:5], summed[5], [cut // 128 for cut in cuts_of]
        )
        small = [vector[0] for vector in small]
    else:
        qkv_weight_grad, dqb, dvb, tokens_grad, qkv_sums = qkv_grad(
            dqkv_groups, qkv_weight, h1, dx1, x, line(ln1_gain)
        )

        def scattered(grad):
            part = lax.psum_scatter(grad, "blk", scatter_dimension=0, tiled=True)
            return lax.psum(part, "seq").astype(f32)

        down_grad, up_grad, proj_grad, conv_weight_grad = [
            scattered(grad) for grad in (down_grad, up_grad, proj_grad, conv_weight_grad)
        ]
        qkv_weight_grad = scattered(qkv_weight_grad.transpose(1, 0, 2).reshape(D, 3 * D))
        vectors = [qkv_sums[0], qkv_sums[1], mlp_sums[0], mlp_sums[1], mlp_sums[2], mlp_sums[3]]
        vectors += [jnp.concatenate([dqb[0], dvb[0]]), up_bias_grad[0]]
        stacked = jnp.concatenate([vector.reshape(blks, -1) for vector in vectors], axis=1)
        summed = small_sum(stacked[:, None, :], True, 4)[0]
        ends = [sum(cuts_of[: i + 1]) for i in range(len(cuts_of))]
        small = [summed[end - cut : end] for cut, end in zip(cuts_of, ends)]
    ln1_g, ln1_b, proj_b, ln2_g, ln2_b, down_b, qv_b, up_b = small
    channel_piece = C // blks
    gain_slice = lax.dynamic_slice_in_dim(bn_sums[1], place * channel_piece, channel_piece)
    bias_slice = lax.dynamic_slice_in_dim(bn_sums[0], place * channel_piece, channel_piece)
    return (
        block_low[None],
        pup_out[None],
        tokens_grad[None],
        ln1_g,
        ln1_b,
        qkv_weight_grad,
        qv_b,
        proj_grad,
        proj_b,
        ln2_g,
        ln2_b,
        up_grad,
        up_b,
        down_grad,
        down_b,
        conv_weight_grad,
        gain_slice,
        bias_slice,
    )


def solution(mesh):
    replicated = P()
    packed = P("seq", "blk", None)
    placed = (packed, P("seq", None)) + (replicated,) * 15 + (packed, packed)
    rows, vector = P("blk", None), P("blk")
    return jax.shard_map(
        shards,
        mesh=mesh,
        in_specs=placed,
        out_specs=(
            packed, packed, packed, vector, vector, rows, vector, rows, vector, vector, vector, rows,
            vector, rows, vector, rows, vector, vector,
        ),
        check_vma=False,
    )
```
